32 devices in a mesh: groups: 2 (over y), wide: 4 (over z), tp: 4 (over x, core).
Axes of the slice: x: 2, y: 2, z: 4, core: 2. Of those that a mesh axis runs over, the one named last changes fastest.
Arguments:
- hidden: bfloat16 [4, 64, 8192], P(None, ('groups', 'wide'), 'tp'), parts along dimension 1, may hold values from -6 to 6
- input_norm_gain: bfloat16 [8192], replicated, may hold values from 0.099609375 to 1.8984375
- key_value_weight: bfloat16 [8192, 2, 1024], P(None, None, 'tp'), may hold values from -0.0625 to 0.0625
- key_value_bias: bfloat16 [2, 1024], P(None, 'tp'), may hold values from -3 to 3
- adapter_down_factor: bfloat16 [4, 64, 8192], P('groups', None, 'wide'), parts along dimension 0, may hold values from -0.0625 to 0.0625
- adapter_up_factor: bfloat16 [4, 1024, 64], P('groups', 'tp', 'wide'), parts along dimension 0, may hold values from -0.375 to 0.375
- queries: bfloat16 [4, 64, 8192], P(None, ('groups', 'wide'), 'tp'), parts along dimension 1, may hold values from -180 to 180
- stored_rotated_keys: bfloat16 [64, 512, 1024], P(('groups', 'wide'), None, 'tp'), parts along dimension 0, may hold values from -6 to 6
- stored_value_rows: bfloat16 [64, 512, 1024], P(('groups', 'wide'), None, 'tp'), parts along dimension 0, may hold values from -6 to 6
- lengths: int32 [64], P(('groups', 'wide')), parts along dimension 0, may hold values from 1 to 512, 8192 in all
Outputs:
- new_keys: bfloat16 [4, 64, 1024], P(None, ('groups', 'wide'), 'tp'), parts along dimension 1
- new_values: bfloat16 [4, 64, 1024], P(None, ('groups', 'wide'), 'tp'), parts along dimension 1
- attended: bfloat16 [4, 64, 8192], P(None, ('groups', 'wide'), 'tp'), parts along dimension 1
The draws below stay inside these ranges and needn't reach their ends.
There are 2 independent parts, one for each index of `groups`. The reference program is written for one: setup_inputs(seed, part) draws one part's arguments, and reference() takes and returns one part's arrays. A program takes and returns all parts, laid end to end along the dimension named above; an argument that names none is the same for every part. Nothing has to cross between parts.
Inputs may be any that keep to these rules, and one draw needn't show every extreme that they name: The lengths of each part sum to 8192; some row holds exactly 512 cached positions in every draw.
All inputs are finite; a program needn't handle non-finite values. No bound on the sum of `lengths` on one device may be relied on, other than what follows from the above.
Results may differ from the reference program's by a relative error of at most 0.0095.
Values may be sent and summed in bfloat16 or wider, within the bound.
No kernel may reach another device: no remote copies, remote signals or barrier semaphores. Data moves between devices by JAX's collectives and lax.ppermute only.
A program may use at most 64 MiB of HBM per device.

```python
import math
import jax
import jax.numpy as jnp
import numpy as np
from jax import lax

MODEL_WIDTH = 8192
HQ = 64
KVH = 8
HD = 128
ADAPTER_RANK = 64
STEPS = 4
CACHE = 512
KEY_VALUE_WIDTH = 1024
ROWS = 32


def cached_keys(key):
    return jnp.clip(jax.random.normal(key, (ROWS, CACHE, KVH * HD), jnp.float32), -6.0, 6.0)


def draw_stored_rotated_keys(key, part):
    drawn = cached_keys(key)
    return drawn.astype(jnp.bfloat16)


def draw_queries(key, part):
    key = jax.random.fold_in(key, 5)
    drawn = jnp.clip(jax.random.normal(key, (STEPS, ROWS, HQ * HD), jnp.float32), -6.0, 6.0)
    return drawn.astype(jnp.bfloat16)


def steps_of(stream_key, dims, cuts, least, largest):
    loudness = 1.0
    for axis_at, blocks in cuts:
        draws = jax.random.uniform(jax.random.fold_in(jax.random.fold_in(stream_key, 6), axis_at), (blocks,), jnp.float32, least / len(cuts), largest / len(cuts))
        loudness = loudness * jnp.repeat(jnp.exp(draws), dims[axis_at] // blocks).reshape((-1,) + (1,) * (len(dims) - 1 - axis_at))
    return loudness


def length_profile(number_of, total, most, skew):
    weights = [(1 << 20) // math.isqrt(rank ** skew) + 1 for rank in range(2, number_of + 1)]
    rest, holding = total - most - (number_of - 1), [1] * (number_of - 1)
    while rest > 0:
        movable = [i for i in range(number_of - 1) if holding[i] < most]
        whole, remaining = sum([weights[i] for i in movable]), rest
        for i in movable:
            more = min(most - holding[i], max(1, remaining * weights[i] // whole), rest)
            holding[i] = holding[i] + more
            rest = rest - more
    return np.array([most] + holding)


def ragged(rng, number_of, total, most, lean):
    if number_of == 2:
        one = jax.random.randint(rng, (), max(1, total - most), min(most, total - 1) + 1)
        return jnp.stack([one, total - one])
    sizes = jnp.asarray(length_profile(number_of, total, most, lean), jnp.int32)
    pairs = (number_of - 1) // 2
    giver, receiver = sizes[1:1 + 2 * pairs:2], sizes[2:2 + 2 * pairs:2]
    room = jnp.minimum(giver - 1, most - receiver)
    shifted = jax.random.randint(jax.random.fold_in(rng, 1), (pairs,), 0, 1 << 20) % (room + 1)
    sizes = sizes.at[1:1 + 2 * pairs:2].set(giver - shifted).at[2:2 + 2 * pairs:2].set(receiver + shifted)
    return sizes[jax.random.permutation(jax.random.fold_in(rng, 2), number_of)]


def centred(own_key, shape, scale, limit, cuts=(), held_as=jnp.bfloat16):
    loudness = steps_of(own_key, shape, cuts, -0.22, 0.18) if cuts else 1.0
    array = jax.random.normal(own_key, shape, jnp.float32) * scale * loudness
    return jnp.minimum(jnp.maximum(array, -limit), limit).astype(held_as)


def setup_inputs(seed: int = 0, part: int = 0) -> dict:
    arg_keys = jax.random.split(jax.random.key(seed), 11)
    own_keys = jax.random.split(jax.random.fold_in(arg_keys[10], part), 11)
    hidden = centred(own_keys[0], (STEPS, ROWS, MODEL_WIDTH), 1.0, 6.0, ((1, 4), (2, 4)))
    input_norm_gain = jnp.clip(1.0 + 0.18 * jax.random.normal(arg_keys[1], (MODEL_WIDTH,), jnp.float32), 0.099609375, 1.8984375).astype(jnp.bfloat16)
    key_value_weight = centred(arg_keys[2], (MODEL_WIDTH, 2, KEY_VALUE_WIDTH), MODEL_WIDTH ** -0.5, 0.0625, ((2, 4),))
    key_value_bias = centred(arg_keys[3], (2, KEY_VALUE_WIDTH), 0.5, 3.0, ((1, 4),))
    adapter_down_factor = centred(own_keys[4], (2, ADAPTER_RANK, MODEL_WIDTH), MODEL_WIDTH ** -0.5, 0.0625, ((2, 4),))
    adapter_up_factor = centred(own_keys[5], (2, KEY_VALUE_WIDTH, ADAPTER_RANK), (4 * ADAPTER_RANK) ** -0.5, 0.375, ((1, 4), (2, 4)))
    queries = draw_queries(jax.random.fold_in(jax.random.fold_in(arg_keys[10], part), 71), part)
    stored_rotated_keys = draw_stored_rotated_keys(jax.random.fold_in(jax.random.fold_in(arg_keys[10], part), 71), part)
    stored_value_rows = centred(own_keys[8], (ROWS, CACHE, KEY_VALUE_WIDTH), 1.0, 6.0, ((0, 4), (2, 4)))
    lengths = ragged(own_keys[9], ROWS, ROWS * CACHE // 2, CACHE, 1).astype(jnp.int32)
    return dict(hidden=hidden, input_norm_gain=input_norm_gain, key_value_weight=key_value_weight, key_value_bias=key_value_bias, adapter_down_factor=adapter_down_factor, adapter_up_factor=adapter_up_factor, queries=queries, stored_rotated_keys=stored_rotated_keys, stored_value_rows=stored_value_rows, lengths=lengths)


norm_eps = 1e-06
adapter_scale = 2.0
rope_base = 1000000.0
masked_score = -1e+30

def rotate_keys(key_rows, positions):
    step_count, row_count, row_width = key_rows.shape
    head_count = row_width // HD
    half_dim = HD // 2
    split_keys = key_rows.reshape(step_count, row_count, head_count, HD)
    inv_freq = rope_base ** (-(2.0 * jnp.arange(half_dim, dtype=jnp.float32)) / HD)
    angles = positions.astype(jnp.float32)[:, :, None] * inv_freq
    cosine = jnp.cos(angles)[:, :, None, :]
    sine_part = jnp.sin(angles)[:, :, None, :]
    first_half = split_keys[..., :half_dim]
    second = split_keys[..., half_dim:]
    turned = jnp.concatenate([first_half * cosine - second * sine_part, second * cosine + first_half * sine_part], axis=-1)
    return turned.reshape(step_count, row_count, row_width)

def attend_row(packed):
    query_rows, old_keys, old_values, fresh_keys, fresh_values, row_length = packed
    step_count = query_rows.shape[0]
    cache_span = old_keys.shape[0]
    group_count = old_keys.shape[1] // HD
    per_group = query_rows.shape[1] // HD // group_count
    score_scale = 1.0 / math.sqrt(HD)
    query_split = query_rows.astype(jnp.float32).reshape(step_count, group_count, per_group, HD)
    old_split = old_keys.astype(jnp.float32).reshape(cache_span, group_count, HD)
    old_vsplit = old_values.astype(jnp.float32).reshape(cache_span, group_count, HD)
    fresh_split = fresh_keys.astype(jnp.float32).reshape(step_count, group_count, HD)
    fresh_vsplit = fresh_values.astype(jnp.float32).reshape(step_count, group_count, HD)
    old_scores = jnp.einsum('sgqd,lgd->sgql', query_split, old_split) * score_scale
    fresh_scores = jnp.einsum('sgqd,tgd->sgqt', query_split, fresh_split) * score_scale
    old_live = jnp.arange(cache_span, dtype=jnp.int32) < row_length
    fresh_live = jnp.arange(step_count, dtype=jnp.int32)[None, :] <= jnp.arange(step_count, dtype=jnp.int32)[:, None]
    old_scores = jnp.where(old_live[None, None, None, :], old_scores, masked_score)
    fresh_scores = jnp.where(fresh_live[:, None, None, :], fresh_scores, masked_score)
    score_top = jnp.maximum(lax.optimization_barrier(jnp.max(old_scores, axis=-1, keepdims=True)), lax.optimization_barrier(jnp.max(fresh_scores, axis=-1, keepdims=True)))
    old_exp = jnp.exp(old_scores - score_top)
    fresh_exp = jnp.exp(fresh_scores - score_top)
    totals = lax.optimization_barrier(jnp.sum(old_exp, axis=-1, keepdims=True)) + lax.optimization_barrier(jnp.sum(fresh_exp, axis=-1, keepdims=True))
    old_prob = (old_exp / totals).astype(jnp.bfloat16).astype(jnp.float32)
    fresh_prob = (fresh_exp / totals).astype(jnp.bfloat16).astype(jnp.float32)
    attended = jnp.einsum('sgql,lgd->sgqd', old_prob, old_vsplit) + jnp.einsum('sgqt,tgd->sgqd', fresh_prob, fresh_vsplit)
    return attended.astype(jnp.bfloat16).reshape(step_count, -1)

def reference(hidden, input_norm_gain, key_value_weight, key_value_bias, adapter_down_factor, adapter_up_factor, queries, stored_rotated_keys, stored_value_rows, lengths):
    widened = hidden.astype(jnp.float32)
    mean_square = lax.optimization_barrier(jnp.mean(widened * widened, axis=-1, keepdims=True))
    normed = (widened * lax.rsqrt(mean_square + norm_eps) * input_norm_gain.astype(jnp.float32)).astype(jnp.bfloat16)
    normalized_input_rows = normed.astype(jnp.float32)
    frozen_projection = jnp.einsum('srd,dkc->srkc', normalized_input_rows, key_value_weight.astype(jnp.float32))
    adapter_inner_rows = jnp.einsum('pyz,ioz->pyio', normalized_input_rows, adapter_down_factor.astype(jnp.float32))
    adapter_term = jnp.einsum('qnyo,yeo->qnye', adapter_inner_rows, adapter_up_factor.astype(jnp.float32), precision=lax.Precision.HIGHEST)
    projected_output = frozen_projection + adapter_scale * adapter_term + key_value_bias.astype(jnp.float32)
    positions = lengths[None, :] + jnp.arange(STEPS, dtype=jnp.int32)[:, None]
    new_keys = rotate_keys(projected_output[:, :, 0, :], positions).astype(jnp.bfloat16)
    new_values = projected_output[:, :, 1, :].astype(jnp.bfloat16)
    packed = (jnp.transpose(queries, (1, 0, 2)), stored_rotated_keys, stored_value_rows, jnp.transpose(new_keys, (1, 0, 2)), jnp.transpose(new_values, (1, 0, 2)), lengths)
    attended = lax.map(attend_row, packed)
    return (new_keys, new_values, jnp.transpose(attended, (1, 0, 2)))
```

```python
import functools
import math

import jax
import jax.numpy as jnp
from jax import lax
from jax.sharding import PartitionSpec as P

HD = 128


norm_eps = 1e-06
adapter_scale = 2.0
rope_base = 1000000.0
masked_score = -1e30


def rotate_keys(key_rows, positions):
    step_count, row_count, row_width = key_rows.shape
    head_count = row_width // HD
    half_dim = HD // 2
    split_keys = key_rows.reshape(step_count, row_count, head_count, HD)
    inv_freq = rope_base ** (-(2.0 * jnp.arange(half_dim, dtype=jnp.float32)) / HD)
    angles = positions.astype(jnp.float32)[:, :, None] * inv_freq
    cosine = jnp.cos(angles)[:, :, None, :]
    sine_part = jnp.sin(angles)[:, :, None, :]
    first_half = split_keys[..., :half_dim]
    second = split_keys[..., half_dim:]
    turned = jnp.concatenate(
        [first_half * cosine - second * sine_part, second * cosine + first_half * sine_part],
        axis=-1,
    )
    return turned.reshape(step_count, row_count, row_width)


def attend(queries, stored_rotated_keys, stored_value_rows, new_keys, new_values, lengths):
    step_count, row_count, query_width = queries.shape
    cache_span = stored_rotated_keys.shape[1]
    group_count = stored_rotated_keys.shape[2] // HD
    per_group = query_width // HD // group_count
    score_scale = 1.0 / math.sqrt(HD)
    query_split = queries.reshape(step_count, row_count, group_count, per_group, HD)
    old_keys = stored_rotated_keys.reshape(row_count, cache_span, group_count, HD)
    old_values = stored_value_rows.reshape(row_count, cache_span, group_count, HD)
    fresh_keys = new_keys.reshape(step_count, row_count, group_count, HD)
    fresh_values = new_values.reshape(step_count, row_count, group_count, HD)
    old_scores = (
        jnp.einsum("srgqd,rlgd->srgql", query_split, old_keys, preferred_element_type=jnp.float32)
        * score_scale
    )
    fresh_scores = (
        jnp.einsum("srgqd,trgd->srgqt", query_split, fresh_keys, preferred_element_type=jnp.float32)
        * score_scale
    )
    old_live = jnp.arange(cache_span, dtype=jnp.int32)[None, :] < lengths[:, None]
    fresh_live = (
        jnp.arange(step_count, dtype=jnp.int32)[None, :]
        <= jnp.arange(step_count, dtype=jnp.int32)[:, None]
    )
    old_scores = jnp.where(old_live[None, :, None, None, :], old_scores, masked_score)
    fresh_scores = jnp.where(fresh_live[:, None, None, None, :], fresh_scores, masked_score)
    score_top = jnp.maximum(
        jnp.max(old_scores, axis=-1, keepdims=True), jnp.max(fresh_scores, axis=-1, keepdims=True)
    )
    old_exp = jnp.exp(old_scores - score_top)
    fresh_exp = jnp.exp(fresh_scores - score_top)
    totals = jnp.sum(old_exp, axis=-1, keepdims=True) + jnp.sum(fresh_exp, axis=-1, keepdims=True)
    old_prob = (old_exp / totals).astype(jnp.bfloat16)
    fresh_prob = (fresh_exp / totals).astype(jnp.bfloat16)
    attended = jnp.einsum(
        "srgql,rlgd->srgqd", old_prob, old_values, preferred_element_type=jnp.float32
    )
    attended = attended + jnp.einsum(
        "srgqt,trgd->srgqd", fresh_prob, fresh_values, preferred_element_type=jnp.float32
    )
    return attended.astype(jnp.bfloat16).reshape(step_count, row_count, query_width)


def lora_inner(hidden, scaled_gain_rows, adapter_down_factor, wide_count, tp_count):
    step_count, row_count, part_width = hidden.shape
    if wide_count == tp_count and tp_count == 4:
        there = []
        for w in range(4):
            for t in range(4):
                there.append((w * 4 + t, t * 4 + 2 * ((t // 2) ^ ((w + t) & 1)) + w // 2))
        moved = lax.ppermute(hidden, ("wide", "tp"), there)
        block = lax.axis_index("wide")
        gain_part = lax.dynamic_slice(scaled_gain_rows, (block * part_width,), (part_width,))
        moved = (moved.astype(jnp.float32) * gain_part.astype(jnp.float32)).astype(jnp.bfloat16)
        inner = jnp.einsum(
            "srd,kad->srka", moved, adapter_down_factor, preferred_element_type=jnp.float32
        )
        parts = []
        for j in range(4):
            back = []
            for source, dest in there:
                w, f = source // 4, source % 4
                back.append((dest, w * 4 + (f + j) % 4))
            parts.append(lax.ppermute(inner, ("wide", "tp"), back))
        return parts
    rows = lax.all_gather(hidden, "tp", axis=2, tiled=True).astype(jnp.float32)
    rows = (rows * scaled_gain_rows.astype(jnp.float32)).astype(jnp.bfloat16)
    down = lax.all_gather(adapter_down_factor, "wide", axis=2, tiled=True)
    return [jnp.einsum("srd,kad->srka", rows, down, preferred_element_type=jnp.float32)]


def gather_parts(block, axis, count):
    parts = [block]
    for j in range(1, count):
        parts.append(lax.ppermute(block, axis, [(i, (i + j) % count) for i in range(count)]))
    return parts


def on_device(
    wide_count,
    tp_count,
    hidden,
    input_norm_gain,
    key_value_weight,
    key_value_bias,
    adapter_down_factor,
    adapter_up_factor,
    queries,
    stored_rotated_keys,
    stored_value_rows,
    lengths,
):
    step_count, row_count, part_width = hidden.shape
    inner_parts = lora_inner(hidden, input_norm_gain, adapter_down_factor, wide_count, tp_count)
    width = part_width * tp_count
    me = lax.axis_index("tp")
    my_wide = lax.axis_index("wide")
    square_sum = 0.0
    base = 0.0
    for j, part in enumerate(gather_parts(hidden, "tp", tp_count)):
        start = (me - j) % tp_count * part_width
        part = part.astype(jnp.float32)
        square_sum = square_sum + jnp.sum(part * part, axis=-1)
        gain_part = lax.dynamic_slice(input_norm_gain, (start,), (part_width,))
        scaled = (part * gain_part.astype(jnp.float32)).astype(jnp.bfloat16)
        weight_part = lax.dynamic_slice(
            key_value_weight, (start, 0, 0), (part_width,) + key_value_weight.shape[1:]
        )
        base = base + jnp.einsum(
            "srd,dkc->srkc", scaled, weight_part, preferred_element_type=jnp.float32
        )
    row_scale = lax.rsqrt(square_sum / width + norm_eps)
    inner = sum(inner_parts[1:], inner_parts[0])
    up_parts = gather_parts(adapter_up_factor, "wide", wide_count)
    rank_part = adapter_up_factor.shape[2]
    lora = 0.0
    for j, part in enumerate(up_parts):
        start = (my_wide - j) % wide_count * rank_part
        lora = lora + jnp.einsum(
            "srka,kca->srkc",
            lax.dynamic_slice(inner, (0, 0, 0, start), inner.shape[:3] + (rank_part,)),
            part.astype(jnp.float32),
            precision=lax.Precision.HIGHEST,
        )
    projected_output = (base + adapter_scale * lora) * row_scale[:, :, None, None]
    projected_output = projected_output + key_value_bias.astype(jnp.float32)
    positions = lengths[None, :] + jnp.arange(step_count, dtype=jnp.int32)[:, None]
    new_keys = rotate_keys(projected_output[:, :, 0, :], positions).astype(jnp.bfloat16)
    new_values = projected_output[:, :, 1, :].astype(jnp.bfloat16)
    attended = attend(
        queries, stored_rotated_keys, stored_value_rows, new_keys, new_values, lengths
    )
    return (new_keys, new_values, attended)


def solution(mesh):
    in_specs = (
        P(None, ("groups", "wide"), "tp"),
        P(),
        P(None, None, "tp"),
        P(None, "tp"),
        P("groups", None, "wide"),
        P("groups", "tp", "wide"),
        P(None, ("groups", "wide"), "tp"),
        P(("groups", "wide"), None, "tp"),
        P(("groups", "wide"), None, "tp"),
        P(("groups", "wide")),
    )
    out_specs = (
        P(None, ("groups", "wide"), "tp"),
        P(None, ("groups", "wide"), "tp"),
        P(None, ("groups", "wide"), "tp"),
    )
    body = functools.partial(on_device, mesh.shape["wide"], mesh.shape["tp"])
    return jax.shard_map(
        body, mesh=mesh, in_specs=in_specs, out_specs=out_specs, check_vma=False
    )
```

```python
import functools
import math

import jax
import jax.numpy as jnp
from jax import lax
from jax.experimental import pallas as pl
from jax.experimental.pallas import tpu as pltpu
from jax.sharding import PartitionSpec as P

HD = 128


norm_eps = 1e-06
adapter_scale = 2.0
rope_base = 1000000.0
masked_score = -1e30
score_scale = 1.0 / math.sqrt(HD)

VMEM = pl.BlockSpec(memory_space=pltpu.VMEM)
SMEM = pl.BlockSpec(memory_space=pltpu.SMEM)
HBM = pl.BlockSpec(memory_space=pltpu.HBM)


def query_block(query_ref, group, per_group):
    steps = query_ref.shape[0]
    tiles = []
    for head in range(per_group):
        at = (group * per_group + head) * HD
        for step in range(steps):
            tiles.append(query_ref[step, :, at : at + HD].astype(jnp.float32))
    return jnp.concatenate(tiles, axis=0)


def cache_kernel(
    lengths_ref,
    query_ref,
    key_ref,
    value_ref,
    weight_ref,
    weight_out,
    acc_out,
    top_out,
    total_out,
    cos_out,
    sin_out,
    query_rows,
    key_buffer,
    value_buffer,
    sems,
    weight_sems,
):
    steps, rows, query_width = query_ref.shape
    cache_span = key_ref.shape[1]
    groups = key_ref.shape[2] // HD
    per_group = query_width // HD // groups
    copies = []
    for row in range(rows):
        pair = (
            pltpu.make_async_copy(key_ref.at[row], key_buffer.at[row], sems.at[0, row]),
            pltpu.make_async_copy(value_ref.at[row], value_buffer.at[row], sems.at[1, row]),
        )
        for copy in pair:
            copy.start()
        copies.append(pair)
    pieces = weight_sems.shape[0]
    piece = weight_ref.shape[0] // pieces
    weight_copies = []
    for i in range(pieces):
        at = pl.ds(i * piece, piece)
        copy = pltpu.make_async_copy(weight_ref.at[at], weight_out.at[at], weight_sems.at[i])
        copy.start()
        weight_copies.append(copy)

    for group in range(groups):
        query_rows[group] = query_block(query_ref, group, per_group)

    lane = lax.broadcasted_iota(jnp.int32, (rows, HD), 1)
    half = HD // 2
    second = lane >= half
    index = jnp.where(second, lane - half, lane).astype(jnp.float32)
    inv_freq = jnp.exp(index * (-2.0 * math.log(rope_base) / HD))
    row_index = lax.broadcasted_iota(jnp.int32, (rows, HD), 0)
    row_lengths = jnp.zeros((rows, HD), jnp.int32)
    for row in range(rows):
        row_lengths = jnp.where(row_index == row, lengths_ref[row], row_lengths)
    for step in range(steps):
        angles = (row_lengths + step).astype(jnp.float32) * inv_freq
        sine = jnp.sin(angles)
        cos_out[pl.ds(step * rows, rows)] = jnp.cos(angles)
        sin_out[pl.ds(step * rows, rows)] = jnp.where(second, sine, -sine)

    place = lax.broadcasted_iota(jnp.int32, (steps * per_group, cache_span), 1)
    for row in range(rows):
        for copy in copies[row]:
            copy.wait()
        live = place < lengths_ref[row]
        for group in range(groups):
            at = pl.ds(group * HD, HD)
            mine = pl.ds(row, steps * per_group, stride=rows)
            query = query_rows[group, mine, :].astype(jnp.bfloat16)
            scores = lax.dot_general(
                query,
                key_buffer[row, :, at],
                (((1,), (1,)), ((), ())),
                preferred_element_type=jnp.float32,
            )
            scores = jnp.where(live, scores * score_scale, masked_score)
            top = jnp.max(scores, axis=1, keepdims=True)
            exps = jnp.exp(scores - top)
            total = jnp.sum(exps, axis=1, keepdims=True)
            acc = jnp.dot(
                exps.astype(jnp.bfloat16),
                value_buffer[row, :, at],
                preferred_element_type=jnp.float32,
            )
            acc_out[group, mine, :] = acc
            top_out[group, mine, :] = jnp.broadcast_to(top, acc.shape)
            total_out[group, mine, :] = jnp.broadcast_to(total, acc.shape)
    for copy in weight_copies:
        copy.wait()


def cache_call(lengths, queries, keys, values, weight):
    steps, rows, query_width = queries.shape
    cache_span, key_width = keys.shape[1:]
    groups = key_width // HD
    block = (groups, steps * rows * (query_width // key_width), HD)
    table = (steps * rows, HD)
    pieces = 4
    return pl.pallas_call(
        cache_kernel,
        out_shape=(
            pltpu.VMEM(weight.shape, weight.dtype),
            pltpu.VMEM(block, jnp.float32),
            pltpu.VMEM(block, jnp.float32),
            pltpu.VMEM(block, jnp.float32),
            pltpu.VMEM(table, jnp.float32),
            pltpu.VMEM(table, jnp.float32),
        ),
        in_specs=[SMEM, VMEM, HBM, HBM, HBM],
        out_specs=(VMEM,) * 6,
        scratch_shapes=[
            pltpu.VMEM(block, jnp.float32),
            pltpu.VMEM(keys.shape, keys.dtype),
            pltpu.VMEM(values.shape, values.dtype),
            pltpu.SemaphoreType.DMA((2, rows)),
            pltpu.SemaphoreType.DMA((pieces,)),
        ],
        compiler_params=pltpu.CompilerParams(vmem_limit_bytes=24 << 20),
        cost_estimate=pl.CostEstimate(flops=2 * 67 << 20, bytes_accessed=13 << 20, transcendentals=0),
        name="cache_attention",
    )(lengths, queries, keys, values, weight)


def scaled_chunks(block, gain, start):
    chunks = []
    for i in range(block.shape[1] // HD):
        chunk = block[:, i * HD : (i + 1) * HD]
        chunks.append((chunk * gain[start + i : start + i + 1]).astype(jnp.bfloat16))
    return chunks


def rows_of(ref):
    steps = ref.shape[0]
    return jnp.concatenate([ref[s].astype(jnp.float32) for s in range(steps)], axis=0)


def inner_kernel(count, hidden_ref, gain_ref, down_ref, out_ref, gain_rows):
    width = hidden_ref.shape[2]
    gain_rows[...] = gain_ref[...].astype(jnp.float32)
    start = pl.multiple_of(lax.axis_index("wide") * (width // HD), width // HD)
    gain = gain_rows[pl.ds(start, width // HD)]
    scaled = jnp.concatenate(scaled_chunks(rows_of(hidden_ref), gain, 0), axis=1)
    ranks = down_ref.shape[1]
    for kind in range(down_ref.shape[0]):
        inner = lax.dot_general(
            scaled,
            down_ref[kind],
            (((1,), (1,)), ((), ())),
            preferred_element_type=jnp.float32,
        ).astype(jnp.bfloat16)
        for i in range(count):
            out_ref[i, :, kind * ranks : (kind + 1) * ranks] = inner


def inner_call(count, hidden, gain, down):
    steps, rows, _ = hidden.shape
    kinds, ranks, _ = down.shape
    return pl.pallas_call(
        functools.partial(inner_kernel, count),
        out_shape=jax.ShapeDtypeStruct((count, steps * rows, kinds * ranks), jnp.bfloat16),
        in_specs=[VMEM] * 3,
        out_specs=VMEM,
        scratch_shapes=[pltpu.VMEM(gain.shape, jnp.float32)],
        compiler_params=pltpu.CompilerParams(vmem_limit_bytes=8 << 20),
        name="rank_inner",
    )(hidden, gain, down)


def base_kernel(offsets, gain_ref, weight_ref, *rest):
    parts = rest[: len(offsets)]
    base_out, square_out, gain_rows = rest[len(offsets) :]
    steps, rows, width = parts[0].shape
    count = steps * rows
    kinds, columns = weight_ref.shape[1:]
    flat = weight_ref.reshape(weight_ref.shape[0] * kinds, columns)
    gain_rows[...] = gain_ref[...].astype(jnp.float32)
    me = lax.axis_index("tp")
    lane = lax.broadcasted_iota(jnp.int32, (count, HD), 1)
    low, high = lane // 2, lane // 2 + HD // 2
    even = lane % 2 == 0
    acc = jnp.zeros((kinds * count, columns), jnp.float32)
    squares = jnp.zeros((count, HD), jnp.float32)
    for offset, part in zip(offsets, parts):
        block = me ^ offset
        start = pl.multiple_of(block * (width // HD), width // HD)
        gain = gain_rows[pl.ds(start, width // HD)]
        values = rows_of(part)
        for i in range(width // HD):
            chunk = values[:, i * HD : (i + 1) * HD]
            squares += chunk * chunk
            chunk = chunk * gain[i : i + 1]
            halves = [
                jnp.take_along_axis(chunk, low, axis=1),
                jnp.take_along_axis(chunk, high, axis=1),
            ]
            spread = jnp.concatenate(
                [
                    jnp.concatenate([jnp.where(even, h, 0.0) for h in halves], axis=1),
                    jnp.concatenate([jnp.where(even, 0.0, h) for h in halves], axis=1),
                ],
                axis=0,
            ).astype(jnp.bfloat16)
            at = pl.multiple_of(block * (width * kinds) + i * HD * kinds, HD * kinds)
            acc += jnp.dot(
                spread, flat[pl.ds(at, HD * kinds), :], preferred_element_type=jnp.float32
            )
    base_out[...] = acc
    square_out[...] = jnp.broadcast_to(jnp.sum(squares, axis=1, keepdims=True), squares.shape)


def base_call(offsets, gain, weight, parts):
    steps, rows, _ = parts[0].shape
    kinds, columns = weight.shape[1:]
    return pl.pallas_call(
        functools.partial(base_kernel, offsets),
        out_shape=(
            pltpu.VMEM((kinds * steps * rows, columns), jnp.float32),
            pltpu.VMEM((steps * rows, HD), jnp.float32),
        ),
        in_specs=[VMEM] * (2 + len(parts)),
        out_specs=(VMEM, VMEM),
        scratch_shapes=[pltpu.VMEM(gain.shape, jnp.float32)],
        compiler_params=pltpu.CompilerParams(vmem_limit_bytes=8 << 20),
        cost_estimate=pl.CostEstimate(flops=4 * 134 << 20, bytes_accessed=9 << 20, transcendentals=0),
        name="base_projection",
    )(gain, weight, *parts)


def final_kernel(
    width,
    sources,
    base_ref,
    square_ref,
    inner_ref,
    up_ref,
    bias_ref,
    query_ref,
    acc_ref,
    top_ref,
    total_ref,
    cos_ref,
    sin_ref,
    keys_out,
    values_out,
    attended_out,
):
    steps, rows, query_width = query_ref.shape
    count = steps * rows
    blocks, kinds, rank_part, columns = up_ref.shape
    ranks = blocks * rank_part
    groups = columns // HD
    per_group = query_width // HD // groups
    row_scale = lax.rsqrt(square_ref[:, :1] * (1.0 / width) + norm_eps)
    inner = None
    for source in sources(lax.axis_index("wide")):
        part = inner_ref[source].astype(jnp.float32)
        inner = part if inner is None else inner + part
    high = inner.astype(jnp.bfloat16)
    low = (inner - high.astype(jnp.float32)).astype(jnp.bfloat16)
    bias = bias_ref[...].astype(jnp.float32)
    linear = []
    for kind in range(kinds):
        up = jnp.concatenate([up_ref[i, kind] for i in range(blocks)], axis=0)
        cols = slice(kind * ranks, (kind + 1) * ranks)
        lora = jnp.dot(high[:, cols], up, preferred_element_type=jnp.float32) + jnp.dot(
            low[:, cols], up, preferred_element_type=jnp.float32
        )
        base = base_ref[kind * count : (kind + 1) * count]
        linear.append((base + adapter_scale * lora) * row_scale + bias[kind : kind + 1])
    cosine, sine = cos_ref[...], sin_ref[...]
    size = count * per_group
    line = lax.broadcasted_iota(jnp.int32, (size, count), 0)
    other = lax.broadcasted_iota(jnp.int32, (size, count), 1)
    live = (line % rows == other % rows) & (other // rows <= line // rows % steps)
    for group in range(groups):
        at = slice(group * HD, (group + 1) * HD)
        key = linear[0][:, at]
        key = (key * cosine + pltpu.roll(key, HD // 2, 1) * sine).astype(jnp.bfloat16)
        value = linear[1][:, at].astype(jnp.bfloat16)
        for step in range(steps):
            keys_out[step, :, at] = key[step * rows : (step + 1) * rows]
            values_out[step, :, at] = value[step * rows : (step + 1) * rows]
        query = query_block(query_ref, group, per_group).astype(jnp.bfloat16)
        scores = lax.dot_general(
            query, key, (((1,), (1,)), ((), ())), preferred_element_type=jnp.float32
        )
        scores = jnp.where(live, scores * score_scale, masked_score)
        old_top = top_ref[group][:, :1]
        top = jnp.maximum(old_top, jnp.max(scores, axis=1, keepdims=True))
        exps = jnp.exp(scores - top)
        keep = jnp.exp(old_top - top)
        total = total_ref[group][:, :1] * keep + jnp.sum(exps, axis=1, keepdims=True)
        acc = acc_ref[group] * keep + jnp.dot(
            exps.astype(jnp.bfloat16), value, preferred_element_type=jnp.float32
        )
        attended = (acc / total).astype(jnp.bfloat16)
        for head in range(per_group):
            lanes = pl.ds((group * per_group + head) * HD, HD)
            for step in range(steps):
                tile = (head * steps + step) * rows
                attended_out[step, :, lanes] = attended[tile : tile + rows]


def final_call(width, sources, base, square, inner, up, bias, queries, cached):
    steps, rows, query_width = queries.shape
    columns = up.shape[3]
    small = jax.ShapeDtypeStruct((steps, rows, columns), jnp.bfloat16)
    return pl.pallas_call(
        functools.partial(final_kernel, width, sources),
        out_shape=(small, small, jax.ShapeDtypeStruct(queries.shape, jnp.bfloat16)),
        in_specs=[VMEM] * (6 + len(cached)),
        out_specs=(VMEM,) * 3,
        compiler_params=pltpu.CompilerParams(vmem_limit_bytes=8 << 20),
        name="fresh_attention",
    )(base, square, inner, up, bias, queries, *cached)


def swap(block, offset, count):
    return lax.ppermute(block, "tp", [(i, i ^ offset) for i in range(count)])


def meeting_core(wide_index, tp_index):
    return 2 * ((tp_index // 2) ^ ((wide_index + tp_index) & 1)) + wide_index // 2


def on_device(
    wide_count,
    tp_count,
    hidden,
    input_norm_gain,
    key_value_weight,
    key_value_bias,
    adapter_down_factor,
    adapter_up_factor,
    queries,
    stored_rotated_keys,
    stored_value_rows,
    lengths,
):
    steps, rows, part_width = hidden.shape
    width = part_width * tp_count
    kinds, ranks, down_width = adapter_down_factor.shape
    gain = input_norm_gain.reshape(width // HD, HD)
    up_part = jnp.transpose(adapter_up_factor, (0, 2, 1))
    both = ("wide", "tp")

    direct = wide_count == 4 and tp_count == 4
    if direct:
        there = [(w * 4 + t, t * 4 + meeting_core(w, t)) for w in range(4) for t in range(4)]
        moved = lax.ppermute(hidden, both, there)
    crossed = swap(hidden, 2, tp_count)
    beside = swap(hidden, 1, tp_count)
    weight, *cached = cache_call(
        lengths, queries, stored_rotated_keys, stored_value_rows, key_value_weight
    )
    relayed = swap(crossed, 1, tp_count)
    if direct:
        inner = inner_call(16, moved, gain, adapter_down_factor)
        inner = lax.all_to_all(inner, both, 0, 0)
        up = lax.all_to_all(jnp.broadcast_to(up_part[None], (4,) + up_part.shape), "wide", 0, 0)

        def sources(wide_index):
            return [f * 4 + 2 * ((f // 2) ^ ((wide_index + f) & 1)) + wide_index // 2 for f in range(4)]

    else:
        gathered = lax.all_gather(hidden, "tp", axis=2, tiled=True).astype(jnp.float32)
        scaled = (gathered * input_norm_gain.astype(jnp.float32)).astype(jnp.bfloat16)
        down = lax.all_gather(adapter_down_factor, "wide", axis=2, tiled=True)
        inner = jnp.einsum("srd,kad->srka", scaled, down, preferred_element_type=jnp.float32)
        inner = inner.reshape(1, steps * rows, kinds * ranks)
        up = lax.all_gather(up_part, "wide", axis=1, tiled=True)[None]

        def sources(wide_index):
            return [0]

    base, square = base_call(
        (0, 1, 2, 3), gain, weight, (hidden, beside, crossed, relayed)
    )
    return final_call(width, sources, base, square, inner, up, key_value_bias, queries, cached)


def solution(mesh):
    in_specs = (
        P(None, ("groups", "wide"), "tp"),
        P(),
        P(None, None, "tp"),
        P(None, "tp"),
        P("groups", None, "wide"),
        P("groups", "tp", "wide"),
        P(None, ("groups", "wide"), "tp"),
        P(("groups", "wide"), None, "tp"),
        P(("groups", "wide"), None, "tp"),
        P(("groups", "wide")),
    )
    out_specs = (
        P(None, ("groups", "wide"), "tp"),
        P(None, ("groups", "wide"), "tp"),
        P(None, ("groups", "wide"), "tp"),
    )
    body = functools.partial(on_device, mesh.shape["wide"], mesh.shape["tp"])
    return jax.shard_map(
        body, mesh=mesh, in_specs=in_specs, out_specs=out_specs, check_vma=False
    )
```

```python
import functools
import math

import jax
import jax.numpy as jnp
from jax import lax
from jax.experimental import pallas as pl
from jax.experimental.pallas import tpu as pltpu
from jax.sharding import PartitionSpec as P

HD = 128


norm_eps = 1e-06
adapter_scale = 2.0
rope_base = 1000000.0
masked_score = -1e30
score_scale = 1.0 / math.sqrt(HD)

VMEM = pl.BlockSpec(memory_space=pltpu.VMEM)
HBM = pl.BlockSpec(memory_space=pltpu.HBM)


def query_block(query_ref, group, per_group):
    steps = query_ref.shape[0]
    tiles = []
    for head in range(per_group):
        at = (group * per_group + head) * HD
        for step in range(steps):
            tiles.append(query_ref[step, :, at : at + HD].astype(jnp.float32))
    return jnp.concatenate(tiles, axis=0)


def cache_kernel(
    lengths_ref,
    query_ref,
    key_ref,
    value_ref,
    weight_ref,
    down_ref,
    gain_ref,
    weight_out,
    down_out,
    gain_out,
    query_out,
    acc_out,
    top_out,
    total_out,
    cos_out,
    sin_out,
    lengths,
    queries,
    gain_buffer,
    key_buffer,
    value_buffer,
    small_sems,
    sems,
    weight_sems,
):
    steps, rows, query_width = query_ref.shape
    cache_span = key_ref.shape[1]
    groups = key_ref.shape[2] // HD
    per_group = query_width // HD // groups
    first = [
        pltpu.make_async_copy(lengths_ref, lengths, small_sems.at[0]),
        pltpu.make_async_copy(query_ref, queries, small_sems.at[1]),
    ]
    last = [
        pltpu.make_async_copy(gain_ref, gain_buffer, small_sems.at[2]),
        pltpu.make_async_copy(down_ref, down_out, small_sems.at[3]),
    ]
    copies = []
    for row in range(rows):
        copies.append(
            (
                pltpu.make_async_copy(key_ref.at[row], key_buffer.at[row], sems.at[0, row]),
                pltpu.make_async_copy(value_ref.at[row], value_buffer.at[row], sems.at[1, row]),
            )
        )
    pieces = weight_sems.shape[0]
    piece = weight_ref.shape[0] // pieces
    for i in range(pieces):
        at = pl.ds(i * piece, piece)
        last.append(
            pltpu.make_async_copy(weight_ref.at[at], weight_out.at[at], weight_sems.at[i])
        )
    for copy in first:
        copy.start()
    for pair in copies:
        for copy in pair:
            copy.start()
    for copy in last:
        copy.start()

    first[0].wait()
    lane = lax.broadcasted_iota(jnp.int32, (rows, HD), 1)
    half = HD // 2
    second = lane >= half
    index = jnp.where(second, lane - half, lane).astype(jnp.float32)
    inv_freq = jnp.exp(index * (-2.0 * math.log(rope_base) / HD))
    row_index = lax.broadcasted_iota(jnp.int32, (rows, HD), 0)
    row_lengths = jnp.zeros((rows, HD), jnp.int32)
    for row in range(rows):
        row_lengths = jnp.where(row_index == row, lengths[row], row_lengths)
    for step in range(steps):
        angles = (row_lengths + step).astype(jnp.float32) * inv_freq
        sine = jnp.sin(angles)
        cos_out[pl.ds(step * rows, rows)] = jnp.cos(angles)
        sin_out[pl.ds(step * rows, rows)] = jnp.where(second, sine, -sine)
    first[1].wait()
    for group in range(groups):
        query_out[group] = query_block(queries, group, per_group)

    place = lax.broadcasted_iota(jnp.int32, (steps * per_group, cache_span), 1)
    for row in range(rows):
        for copy in copies[row]:
            copy.wait()
        live = place < lengths[row]
        for group in range(groups):
            at = pl.ds(group * HD, HD)
            mine = pl.ds(row, steps * per_group, stride=rows)
            query = query_out[group, mine, :].astype(jnp.bfloat16)
            scores = lax.dot_general(
                query,
                key_buffer[row, :, at],
                (((1,), (1,)), ((), ())),
                preferred_element_type=jnp.float32,
            )
            scores = jnp.where(live, scores * score_scale, masked_score)
            top = jnp.max(scores, axis=1, keepdims=True)
            exps = jnp.exp(scores - top)
            total = jnp.sum(exps, axis=1, keepdims=True)
            acc = jnp.dot(
                exps.astype(jnp.bfloat16),
                value_buffer[row, :, at],
                preferred_element_type=jnp.float32,
            )
            acc_out[group, mine, :] = acc
            top_out[group, mine, :] = jnp.broadcast_to(top, acc.shape)
            total_out[group, mine, :] = jnp.broadcast_to(total, acc.shape)
    last[0].wait()
    gain_out[...] = gain_buffer[...].astype(jnp.float32)
    for copy in last[1:]:
        copy.wait()


def cache_call(lengths, queries, keys, values, weight, down, gain):
    steps, rows, query_width = queries.shape
    cache_span, key_width = keys.shape[1:]
    groups = key_width // HD
    block = (groups, steps * rows * (query_width // key_width), HD)
    table = (steps * rows, HD)
    pieces = 4
    return pl.pallas_call(
        cache_kernel,
        out_shape=(
            pltpu.VMEM(weight.shape, weight.dtype),
            pltpu.VMEM(down.shape, down.dtype),
            pltpu.VMEM(gain.shape, jnp.float32),
            pltpu.VMEM(block, jnp.float32),
            pltpu.VMEM(block, jnp.float32),
            pltpu.VMEM(block, jnp.float32),
            pltpu.VMEM(block, jnp.float32),
            pltpu.VMEM(table, jnp.float32),
            pltpu.VMEM(table, jnp.float32),
        ),
        in_specs=[HBM] * 7,
        out_specs=(VMEM,) * 9,
        scratch_shapes=[
            pltpu.SMEM(lengths.shape, jnp.int32),
            pltpu.VMEM(queries.shape, queries.dtype),
            pltpu.VMEM(gain.shape, gain.dtype),
            pltpu.VMEM(keys.shape, keys.dtype),
            pltpu.VMEM(values.shape, values.dtype),
            pltpu.SemaphoreType.DMA((4,)),
            pltpu.SemaphoreType.DMA((2, rows)),
            pltpu.SemaphoreType.DMA((pieces,)),
        ],
        compiler_params=pltpu.CompilerParams(vmem_limit_bytes=52 << 20),
        cost_estimate=pl.CostEstimate(flops=2 * 67 << 20, bytes_accessed=13 << 20, transcendentals=0),
        name="cache_attention",
    )(lengths, queries, keys, values, weight, down, gain)


def scaled_chunks(block, gain, start):
    chunks = []
    for i in range(block.shape[1] // HD):
        chunk = block[:, i * HD : (i + 1) * HD]
        chunks.append((chunk * gain[start + i : start + i + 1]).astype(jnp.bfloat16))
    return chunks


def rows_of(ref):
    steps = ref.shape[0]
    return jnp.concatenate([ref[s].astype(jnp.float32) for s in range(steps)], axis=0)


def inner_kernel(hidden_ref, gain_ref, down_ref, up_ref, beside_ref, out_ref, up_out):
    width = hidden_ref.shape[2]
    start = pl.multiple_of(lax.axis_index("wide") * (width // HD), width // HD)
    gain = gain_ref[pl.ds(start, width // HD)]
    scaled = jnp.concatenate(scaled_chunks(rows_of(hidden_ref), gain, 0), axis=1)
    ranks = down_ref.shape[1]
    for kind in range(down_ref.shape[0]):
        out_ref[:, kind * ranks : (kind + 1) * ranks] = lax.dot_general(
            scaled,
            down_ref[kind],
            (((1,), (1,)), ((), ())),
            preferred_element_type=jnp.float32,
        )
    up_out[0] = up_ref[...]
    up_out[1] = beside_ref[...]


def inner_call(hidden, gain, down, up_part, up_beside):
    steps, rows, _ = hidden.shape
    kinds, ranks, _ = down.shape
    return pl.pallas_call(
        inner_kernel,
        out_shape=(
            jax.ShapeDtypeStruct((steps * rows, kinds * ranks), jnp.float32),
            jax.ShapeDtypeStruct((2,) + up_part.shape, up_part.dtype),
        ),
        in_specs=[VMEM] * 5,
        out_specs=(VMEM, VMEM),
        compiler_params=pltpu.CompilerParams(vmem_limit_bytes=8 << 20),
        name="rank_inner",
    )(hidden, gain, down, up_part, up_beside)


def base_kernel(offsets, gain_ref, weight_ref, *rest):
    parts = rest[: len(offsets)]
    base_out, square_out = rest[len(offsets) :]
    steps, rows, width = parts[0].shape
    count = steps * rows
    kinds, columns = weight_ref.shape[1:]
    flat = weight_ref.reshape(weight_ref.shape[0] * kinds, columns)
    me = lax.axis_index("tp")
    lane = lax.broadcasted_iota(jnp.int32, (count, HD), 1)
    low, high = lane // 2, lane // 2 + HD // 2
    even = lane % 2 == 0
    acc = jnp.zeros((kinds * count, columns), jnp.float32)
    squares = jnp.zeros((count, HD), jnp.float32)
    for offset, part in zip(offsets, parts):
        block = me ^ offset
        start = pl.multiple_of(block * (width // HD), width // HD)
        gain = gain_ref[pl.ds(start, width // HD)]
        values = rows_of(part)
        for i in range(width // HD):
            chunk = values[:, i * HD : (i + 1) * HD]
            squares += chunk * chunk
            chunk = chunk * gain[i : i + 1]
            halves = [
                jnp.take_along_axis(chunk, low, axis=1),
                jnp.take_along_axis(chunk, high, axis=1),
            ]
            spread = jnp.concatenate(
                [
                    jnp.concatenate([jnp.where(even, h, 0.0) for h in halves], axis=1),
                    jnp.concatenate([jnp.where(even, 0.0, h) for h in halves], axis=1),
                ],
                axis=0,
            ).astype(jnp.bfloat16)
            at = pl.multiple_of(block * (width * kinds) + i * HD * kinds, HD * kinds)
            acc += jnp.dot(
                spread, flat[pl.ds(at, HD * kinds), :], preferred_element_type=jnp.float32
            )
    base_out[...] = acc
    square_out[...] = jnp.broadcast_to(jnp.sum(squares, axis=1, keepdims=True), squares.shape)


def base_call(offsets, gain, weight, parts):
    steps, rows, _ = parts[0].shape
    kinds, columns = weight.shape[1:]
    return pl.pallas_call(
        functools.partial(base_kernel, offsets),
        out_shape=(
            pltpu.VMEM((kinds * steps * rows, columns), jnp.float32),
            pltpu.VMEM((steps * rows, HD), jnp.float32),
        ),
        in_specs=[VMEM] * (2 + len(parts)),
        out_specs=(VMEM, VMEM),
        compiler_params=pltpu.CompilerParams(vmem_limit_bytes=8 << 20),
        cost_estimate=pl.CostEstimate(flops=4 * 134 << 20, bytes_accessed=9 << 20, transcendentals=0),
        name="base_projection",
    )(gain, weight, *parts)


def final_kernel(width, inner_count, up_count, base_ref, square_ref, bias_ref, *rest):
    query_ref, acc_ref, top_ref, total_ref, cos_ref, sin_ref = rest[:6]
    inner_refs = rest[6 : 6 + inner_count]
    up_refs = rest[6 + inner_count : 6 + inner_count + up_count]
    keys_out, values_out, attended_out = rest[6 + inner_count + up_count :]
    steps, rows, columns = keys_out.shape
    count = steps * rows
    groups, size, _ = query_ref.shape
    per_group = size // count
    kinds = bias_ref.shape[0]
    row_scale = lax.rsqrt(square_ref[:, :1] * (1.0 / width) + norm_eps)
    inner = inner_refs[0][...]
    for ref in inner_refs[1:]:
        inner = inner + ref[...]
    high = inner.astype(jnp.bfloat16)
    low = (inner - high.astype(jnp.float32)).astype(jnp.bfloat16)
    ranks = inner.shape[1] // kinds
    bias = bias_ref[...].astype(jnp.float32)
    linear = []
    for kind in range(kinds):
        if up_count == 1:
            up = up_refs[0][0, kind]
        else:
            me = lax.axis_index("wide")
            pieces = []
            for i in range(4):
                at = (me ^ i) & 1
                near = up_refs[0][at, kind].astype(jnp.float32)
                far = up_refs[1][at, kind].astype(jnp.float32)
                pieces.append(jnp.where(me // 2 == i // 2, near, far))
            up = jnp.concatenate(pieces, axis=0).astype(jnp.bfloat16)
        cols = slice(kind * ranks, (kind + 1) * ranks)
        lora = jnp.dot(high[:, cols], up, preferred_element_type=jnp.float32) + jnp.dot(
            low[:, cols], up, preferred_element_type=jnp.float32
        )
        base = base_ref[kind * count : (kind + 1) * count]
        linear.append((base + adapter_scale * lora) * row_scale + bias[kind : kind + 1])
    cosine, sine = cos_ref[...], sin_ref[...]
    line = lax.broadcasted_iota(jnp.int32, (size, count), 0)
    other = lax.broadcasted_iota(jnp.int32, (size, count), 1)
    live = (line % rows == other % rows) & (other // rows <= line // rows % steps)
    for group in range(groups):
        at = slice(group * HD, (group + 1) * HD)
        key = linear[0][:, at]
        key = (key * cosine + pltpu.roll(key, HD // 2, 1) * sine).astype(jnp.bfloat16)
        value = linear[1][:, at].astype(jnp.bfloat16)
        for step in range(steps):
            keys_out[step, :, at] = key[step * rows : (step + 1) * rows]
            values_out[step, :, at] = value[step * rows : (step + 1) * rows]
        scores = lax.dot_general(
            query_ref[group].astype(jnp.bfloat16),
            key,
            (((1,), (1,)), ((), ())),
            preferred_element_type=jnp.float32,
        )
        scores = jnp.where(live, scores * score_scale, masked_score)
        old_top = top_ref[group][:, :1]
        top = jnp.maximum(old_top, jnp.max(scores, axis=1, keepdims=True))
        exps = jnp.exp(scores - top)
        keep = jnp.exp(old_top - top)
        total = total_ref[group][:, :1] * keep + jnp.sum(exps, axis=1, keepdims=True)
        acc = acc_ref[group] * keep + jnp.dot(
            exps.astype(jnp.bfloat16), value, preferred_element_type=jnp.float32
        )
        attended = (acc / total).astype(jnp.bfloat16)
        for head in range(per_group):
            lanes = pl.ds((group * per_group + head) * HD, HD)
            for step in range(steps):
                tile = (head * steps + step) * rows
                attended_out[step, :, lanes] = attended[tile : tile + rows]


def final_call(shape, width, base, square, bias, cached, inner, up):
    steps, rows, query_width = shape
    small = jax.ShapeDtypeStruct((steps, rows, base.shape[1]), jnp.bfloat16)
    return pl.pallas_call(
        functools.partial(final_kernel, width, len(inner), len(up)),
        out_shape=(small, small, jax.ShapeDtypeStruct(shape, jnp.bfloat16)),
        in_specs=[VMEM] * (3 + len(cached) + len(inner) + len(up)),
        out_specs=(VMEM,) * 3,
        compiler_params=pltpu.CompilerParams(vmem_limit_bytes=8 << 20),
        name="fresh_attention",
    )(base, square, bias, *cached, *inner, *up)


def swap(block, axis, offset, count):
    return lax.ppermute(block, axis, [(i, i ^ offset) for i in range(count)])


def meeting_place():
    pairs = []
    for w in range(4):
        for t in range(4):
            pairs.append((w * 4 + t, t * 4 + 2 * ((t // 2) ^ ((w + t) & 1)) + w // 2))
    return pairs


def on_device(
    wide_count,
    tp_count,
    hidden,
    input_norm_gain,
    key_value_weight,
    key_value_bias,
    adapter_down_factor,
    adapter_up_factor,
    queries,
    stored_rotated_keys,
    stored_value_rows,
    lengths,
):
    steps, rows, part_width = hidden.shape
    width = part_width * tp_count
    kinds, ranks, down_width = adapter_down_factor.shape
    gain = input_norm_gain.reshape(width // HD, HD)
    up_part = jnp.transpose(adapter_up_factor, (0, 2, 1))
    both = ("wide", "tp")

    direct = wide_count == 4 and tp_count == 4
    if direct:
        there = meeting_place()
        moved = lax.ppermute(hidden, both, there)
        up_beside = swap(up_part, "wide", 1, 4)
    crossed = swap(hidden, "tp", 2, tp_count)
    beside = swap(hidden, "tp", 1, tp_count)
    weight, down, gain_rows, *cached = cache_call(
        lengths,
        queries,
        stored_rotated_keys,
        stored_value_rows,
        key_value_weight,
        adapter_down_factor,
        gain,
    )
    relayed, gain_rows = lax.optimization_barrier((crossed, gain_rows))
    relayed = swap(relayed, "tp", 1, tp_count)
    if direct:
        inner, up_pair = inner_call(moved, gain_rows, down, up_part, up_beside)
        inner = lax.ppermute(inner, both, [(b, a) for a, b in there])
        up = [up_pair, swap(up_pair, "wide", 2, 4)]
    else:
        gathered = lax.all_gather(hidden, "tp", axis=2, tiled=True).astype(jnp.float32)
        scaled = (gathered * input_norm_gain.astype(jnp.float32)).astype(jnp.bfloat16)
        all_down = lax.all_gather(adapter_down_factor, "wide", axis=2, tiled=True)
        inner = jnp.einsum("srd,kad->srka", scaled, all_down, preferred_element_type=jnp.float32)
        inner = [inner.reshape(steps * rows, kinds * ranks)]
        up = [lax.all_gather(up_part, "wide", axis=1, tiled=True)[None]]

    base, square = base_call(
        (0, 1, 2, 3), gain_rows, weight, (hidden, beside, crossed, relayed)
    )
    if direct:
        inner, square = lax.optimization_barrier((inner, square))
        inner = [inner] + [swap(inner, "tp", offset, 4) for offset in (2, 3, 1)]
    return final_call(queries.shape, width, base, square, key_value_bias, cached, inner, up)


def solution(mesh):
    in_specs = (
        P(None, ("groups", "wide"), "tp"),
        P(),
        P(None, None, "tp"),
        P(None, "tp"),
        P("groups", None, "wide"),
        P("groups", "tp", "wide"),
        P(None, ("groups", "wide"), "tp"),
        P(("groups", "wide"), None, "tp"),
        P(("groups", "wide"), None, "tp"),
        P(("groups", "wide")),
    )
    out_specs = (
        P(None, ("groups", "wide"), "tp"),
        P(None, ("groups", "wide"), "tp"),
        P(None, ("groups", "wide"), "tp"),
    )
    body = functools.partial(on_device, mesh.shape["wide"], mesh.shape["tp"])
    return jax.shard_map(
        body, mesh=mesh, in_specs=in_specs, out_specs=out_specs, check_vma=False
    )
```

```python
import functools
import math

import jax
import jax.numpy as jnp
from jax import lax
from jax.experimental import pallas as pl
from jax.experimental.pallas import tpu as pltpu
from jax.sharding import PartitionSpec as P

HD = 128


norm_eps = 1e-06
adapter_scale = 2.0
rope_base = 1000000.0
masked_score = -1e30
score_scale = 1.0 / math.sqrt(HD)

VMEM = pl.BlockSpec(memory_space=pltpu.VMEM)
HBM = pl.BlockSpec(memory_space=pltpu.HBM)


def query_block(query_ref, group, per_group):
    steps = query_ref.shape[0]
    tiles = []
    for head in range(per_group):
        at = (group * per_group + head) * HD
        for step in range(steps):
            tiles.append(query_ref[step, :, at : at + HD].astype(jnp.float32))
    return jnp.concatenate(tiles, axis=0)


def weight_block(weight_ref, block, width):
    return weight_ref.at[pl.ds(pl.multiple_of(block * width, width), width)]


def cache_kernel(
    staged,
    lengths_ref,
    query_ref,
    key_ref,
    value_ref,
    down_ref,
    gain_ref,
    up_ref,
    bias_ref,
    weight_ref,
    weight_out,
    down_out,
    gain_out,
    up_out,
    bias_out,
    query_out,
    acc_out,
    top_out,
    total_out,
    cos_out,
    sin_out,
    lengths,
    queries,
    gain_buffer,
    key_buffer,
    value_buffer,
    score_buffer,
    sems,
):
    steps, rows, query_width = query_ref.shape
    cache_span = key_ref.shape[1]
    groups = key_ref.shape[2] // HD
    per_group = query_width // HD // groups
    lines = steps * per_group
    half_rows = rows // 2
    halves = [pl.ds(0, half_rows), pl.ds(half_rows, half_rows)]
    copies = [
        (lengths_ref, lengths),
        (query_ref, queries),
        (key_ref.at[halves[0]], key_buffer.at[halves[0]]),
        (key_ref.at[halves[1]], key_buffer.at[halves[1]]),
        (value_ref.at[halves[0]], value_buffer.at[halves[0]]),
        (value_ref.at[halves[1]], value_buffer.at[halves[1]]),
        (gain_ref, gain_buffer),
        (down_ref, down_out),
        (up_ref, up_out),
        (bias_ref, bias_out),
    ]
    me = lax.axis_index("tp")
    for i, offset in enumerate(staged):
        copies.append((weight_block(weight_ref, me ^ offset, weight_out.shape[1]), weight_out.at[i]))
    copies = [pltpu.make_async_copy(*pair, sems.at[i]) for i, pair in enumerate(copies)]
    for copy in copies:
        copy.start()

    copies[0].wait()
    lane = lax.broadcasted_iota(jnp.int32, (rows, HD), 1)
    half = HD // 2
    second = lane >= half
    index = jnp.where(second, lane - half, lane).astype(jnp.float32)
    inv_freq = jnp.exp(index * (-2.0 * math.log(rope_base) / HD))
    row_index = lax.broadcasted_iota(jnp.int32, (rows, HD), 0)
    row_lengths = jnp.zeros((rows, HD), jnp.int32)
    for row in range(rows):
        row_lengths = jnp.where(row_index == row, lengths[row], row_lengths)
    for step in range(steps):
        angles = (row_lengths + step).astype(jnp.float32) * inv_freq
        sine = jnp.sin(angles)
        cos_out[pl.ds(step * rows, rows)] = jnp.cos(angles)
        sin_out[pl.ds(step * rows, rows)] = jnp.where(second, sine, -sine)
    copies[1].wait()
    for group in range(groups):
        query_out[group] = query_block(queries, group, per_group)

    place = lax.broadcasted_iota(jnp.int32, (lines, cache_span), 1)
    for i in range(2):
        copies[2 + i].wait()
        for row in range(i * half_rows, (i + 1) * half_rows):
            for group in range(groups):
                query = query_out[group, pl.ds(row, lines, stride=rows), :].astype(jnp.bfloat16)
                score_buffer[row * groups + group] = lax.dot_general(
                    query,
                    key_buffer[row, :, pl.ds(group * HD, HD)],
                    (((1,), (1,)), ((), ())),
                    preferred_element_type=jnp.float32,
                )
    for i in range(2):
        copies[4 + i].wait()
        for row in range(i * half_rows, (i + 1) * half_rows):
            live = place < lengths[row]
            for group in range(groups):
                mine = pl.ds(row, lines, stride=rows)
                scores = score_buffer[row * groups + group]
                scores = jnp.where(live, scores * score_scale, masked_score)
                top = jnp.max(scores, axis=1, keepdims=True)
                exps = jnp.exp(scores - top)
                total = jnp.sum(exps, axis=1, keepdims=True)
                acc = jnp.dot(
                    exps.astype(jnp.bfloat16),
                    value_buffer[row, :, pl.ds(group * HD, HD)],
                    preferred_element_type=jnp.float32,
                )
                acc_out[group, mine, :] = acc
                top_out[group, mine, :] = jnp.broadcast_to(top, acc.shape)
                total_out[group, mine, :] = jnp.broadcast_to(total, acc.shape)
    copies[6].wait()
    gain_out[...] = gain_buffer[...].astype(jnp.float32)
    for copy in copies[7:]:
        copy.wait()


def cache_call(staged, part_width, lengths, queries, keys, values, down, gain, up, bias, weight):
    steps, rows, query_width = queries.shape
    cache_span, key_width = keys.shape[1:]
    groups = key_width // HD
    lines = steps * (query_width // key_width)
    block = (groups, lines * rows, HD)
    table = (steps * rows, HD)
    operands = (lengths, queries, keys, values, down, gain, up, bias, weight)
    return pl.pallas_call(
        functools.partial(cache_kernel, staged),
        out_shape=(
            pltpu.VMEM((len(staged), part_width) + weight.shape[1:], weight.dtype),
            pltpu.VMEM(down.shape, down.dtype),
            pltpu.VMEM(gain.shape, jnp.float32),
            pltpu.VMEM(up.shape, up.dtype),
            pltpu.VMEM(bias.shape, bias.dtype),
            pltpu.VMEM(block, jnp.float32),
            pltpu.VMEM(block, jnp.float32),
            pltpu.VMEM(block, jnp.float32),
            pltpu.VMEM(block, jnp.float32),
            pltpu.VMEM(table, jnp.float32),
            pltpu.VMEM(table, jnp.float32),
        ),
        in_specs=[HBM] * len(operands),
        out_specs=(VMEM,) * 11,
        scratch_shapes=[
            pltpu.SMEM(lengths.shape, jnp.int32),
            pltpu.VMEM(queries.shape, queries.dtype),
            pltpu.VMEM(gain.shape, gain.dtype),
            pltpu.VMEM(keys.shape, keys.dtype),
            pltpu.VMEM(values.shape, values.dtype),
            pltpu.VMEM((rows * groups, lines, cache_span), jnp.float32),
            pltpu.SemaphoreType.DMA((10 + len(staged),)),
        ],
        compiler_params=pltpu.CompilerParams(vmem_limit_bytes=16 << 20),
        cost_estimate=pl.CostEstimate(flops=2 * 67 << 20, bytes_accessed=9 << 20, transcendentals=0),
        name="cache_attention",
    )(*[pltpu.with_memory_space_constraint(x, pltpu.HBM) for x in operands])


def scaled_chunks(block, gain, start):
    chunks = []
    for i in range(block.shape[1] // HD):
        chunk = block[:, i * HD : (i + 1) * HD]
        chunks.append((chunk * gain[start + i : start + i + 1]).astype(jnp.bfloat16))
    return chunks


def rows_of(ref):
    steps = ref.shape[0]
    return jnp.concatenate([ref[s].astype(jnp.float32) for s in range(steps)], axis=0)


def inner_kernel(hidden_ref, gain_ref, down_ref, out_ref):
    width = hidden_ref.shape[2]
    start = pl.multiple_of(lax.axis_index("wide") * (width // HD), width // HD)
    gain = gain_ref[pl.ds(start, width // HD)]
    scaled = jnp.concatenate(scaled_chunks(rows_of(hidden_ref), gain, 0), axis=1)
    ranks = down_ref.shape[1]
    for kind in range(down_ref.shape[0]):
        out_ref[:, kind * ranks : (kind + 1) * ranks] = lax.dot_general(
            scaled,
            down_ref[kind],
            (((1,), (1,)), ((), ())),
            preferred_element_type=jnp.float32,
        )


def inner_call(hidden, gain, down):
    steps, rows, _ = hidden.shape
    kinds, ranks, _ = down.shape
    return pl.pallas_call(
        inner_kernel,
        out_shape=jax.ShapeDtypeStruct((steps * rows, kinds * ranks), jnp.float32),
        in_specs=[VMEM] * 3,
        out_specs=VMEM,
        compiler_params=pltpu.CompilerParams(vmem_limit_bytes=8 << 20),
        name="rank_inner",
    )(hidden, gain, down)


def base_kernel(staged, streamed, gain_ref, staged_ref, weight_ref, *rest):
    offsets = staged + streamed
    parts = rest[: len(offsets)]
    base_out, square_out, spread, buffer, sems = rest[len(offsets) :]
    steps, rows, width = parts[0].shape
    count = steps * rows
    kinds, columns = weight_ref.shape[1:]
    me = lax.axis_index("tp")
    copies = []
    for i, offset in enumerate(streamed):
        copy = pltpu.make_async_copy(
            weight_block(weight_ref, me ^ offset, width), buffer.at[i], sems.at[i]
        )
        copy.start()
        copies.append(copy)
    lane = lax.broadcasted_iota(jnp.int32, (count, HD), 1)
    low, high = lane // 2, lane // 2 + HD // 2
    even = lane % 2 == 0
    squares = jnp.zeros((count, HD), jnp.float32)
    acc = None
    for k, (offset, part) in enumerate(zip(offsets, parts)):
        start = pl.multiple_of((me ^ offset) * (width // HD), width // HD)
        gain = gain_ref[pl.ds(start, width // HD)]
        values = rows_of(part)
        for i in range(width // HD):
            chunk = values[:, i * HD : (i + 1) * HD]
            squares += chunk * chunk
            chunk = chunk * gain[i : i + 1]
            for j, index in enumerate((low, high)):
                wide = jnp.take_along_axis(chunk, index, axis=1)
                at = pl.ds((2 * i + j) * HD, HD)
                spread[k, :count, at] = jnp.where(even, wide, 0.0).astype(jnp.bfloat16)
                spread[k, count:, at] = jnp.where(even, 0.0, wide).astype(jnp.bfloat16)
        if k < len(staged):
            block = staged_ref.at[k]
        else:
            copies[k - len(staged)].wait()
            block = buffer.at[k - len(staged)]
        product = jnp.dot(
            spread[k],
            block.reshape(width * kinds, columns)[...],
            preferred_element_type=jnp.float32,
        )
        acc = product if acc is None else acc + product
    base_out[...] = acc
    square_out[...] = jnp.broadcast_to(jnp.sum(squares, axis=1, keepdims=True), squares.shape)


def base_call(staged, streamed, gain, staged_weight, weight, parts):
    steps, rows, width = parts[0].shape
    kinds, columns = weight.shape[1:]
    return pl.pallas_call(
        functools.partial(base_kernel, staged, streamed),
        out_shape=(
            pltpu.VMEM((kinds * steps * rows, columns), jnp.float32),
            pltpu.VMEM((steps * rows, HD), jnp.float32),
        ),
        in_specs=[VMEM, VMEM, HBM] + [VMEM] * len(parts),
        out_specs=(VMEM, VMEM),
        scratch_shapes=[
            pltpu.VMEM((len(parts), kinds * steps * rows, kinds * width), jnp.bfloat16),
            pltpu.VMEM((len(streamed), width, kinds, columns), weight.dtype),
            pltpu.SemaphoreType.DMA((len(streamed),)),
        ],
        compiler_params=pltpu.CompilerParams(vmem_limit_bytes=16 << 20),
        cost_estimate=pl.CostEstimate(flops=4 * 134 << 20, bytes_accessed=9 << 20, transcendentals=0),
        name="base_projection",
    )(gain, staged_weight, pltpu.with_memory_space_constraint(weight, pltpu.HBM), *parts)


def final_kernel(width, inner_count, up_count, base_ref, square_ref, bias_ref, *rest):
    query_ref, acc_ref, top_ref, total_ref, cos_ref, sin_ref = rest[:6]
    inner_refs = rest[6 : 6 + inner_count]
    up_refs = rest[6 + inner_count : 6 + inner_count + up_count]
    keys_out, values_out, attended_out, up_buffer = rest[6 + inner_count + up_count :]
    steps, rows, columns = keys_out.shape
    count = steps * rows
    groups, size, _ = query_ref.shape
    per_group = size // count
    kinds = bias_ref.shape[0]
    row_scale = lax.rsqrt(square_ref[:, :1] * (1.0 / width) + norm_eps)
    inner = inner_refs[0][...]
    for ref in inner_refs[1:]:
        inner = inner + ref[...]
    high = inner.astype(jnp.bfloat16)
    low = (inner - high.astype(jnp.float32)).astype(jnp.bfloat16)
    ranks = inner.shape[1] // kinds
    bias = bias_ref[...].astype(jnp.float32)
    linear = []
    for i, ref in enumerate(up_refs):
        up_buffer[i] = ref[...]
    me = lax.axis_index("wide") if up_count > 1 else 0
    for kind in range(kinds):
        up = jnp.concatenate([up_buffer[me ^ i, kind] for i in range(up_count)], axis=0)
        cols = slice(kind * ranks, (kind + 1) * ranks)
        lora = jnp.dot(high[:, cols], up, preferred_element_type=jnp.float32) + jnp.dot(
            low[:, cols], up, preferred_element_type=jnp.float32
        )
        base = base_ref[kind * count : (kind + 1) * count]
        linear.append((base + adapter_scale * lora) * row_scale + bias[kind : kind + 1])
    cosine, sine = cos_ref[...], sin_ref[...]
    line = lax.broadcasted_iota(jnp.int32, (size, count), 0)
    other = lax.broadcasted_iota(jnp.int32, (size, count), 1)
    live = (line % rows == other % rows) & (other // rows <= line // rows % steps)
    for group in range(groups):
        at = slice(group * HD, (group + 1) * HD)
        key = linear[0][:, at]
        key = (key * cosine + pltpu.roll(key, HD // 2, 1) * sine).astype(jnp.bfloat16)
        value = linear[1][:, at].astype(jnp.bfloat16)
        for step in range(steps):
            keys_out[step, :, at] = key[step * rows : (step + 1) * rows]
            values_out[step, :, at] = value[step * rows : (step + 1) * rows]
        scores = lax.dot_general(
            query_ref[group].astype(jnp.bfloat16),
            key,
            (((1,), (1,)), ((), ())),
            preferred_element_type=jnp.float32,
        )
        scores = jnp.where(live, scores * score_scale, masked_score)
        old_top = top_ref[group][:, :1]
        top = jnp.maximum(old_top, jnp.max(scores, axis=1, keepdims=True))
        exps = jnp.exp(scores - top)
        keep = jnp.exp(old_top - top)
        total = total_ref[group][:, :1] * keep + jnp.sum(exps, axis=1, keepdims=True)
        acc = acc_ref[group] * keep + jnp.dot(
            exps.astype(jnp.bfloat16), value, preferred_element_type=jnp.float32
        )
        attended = (acc / total).astype(jnp.bfloat16)
        for head in range(per_group):
            lanes = pl.ds((group * per_group + head) * HD, HD)
            for step in range(steps):
                tile = (head * steps + step) * rows
                attended_out[step, :, lanes] = attended[tile : tile + rows]


def final_call(shape, width, base, square, bias, cached, inner, up):
    steps, rows, query_width = shape
    small = jax.ShapeDtypeStruct((steps, rows, base.shape[1]), jnp.bfloat16)
    return pl.pallas_call(
        functools.partial(final_kernel, width, len(inner), len(up)),
        out_shape=(small, small, jax.ShapeDtypeStruct(shape, jnp.bfloat16)),
        in_specs=[VMEM] * (3 + len(cached) + len(inner) + len(up)),
        out_specs=(VMEM,) * 3,
        scratch_shapes=[pltpu.VMEM((len(up),) + up[0].shape, up[0].dtype)],
        compiler_params=pltpu.CompilerParams(vmem_limit_bytes=8 << 20),
        name="fresh_attention",
    )(base, square, bias, *cached, *inner, *up)


def swap(block, axis, offset, count):
    return lax.ppermute(block, axis, [(i, i ^ offset) for i in range(count)])


def meeting_place():
    pairs = []
    for w in range(4):
        for t in range(4):
            pairs.append((w * 4 + t, t * 4 + 2 * ((t // 2) ^ ((w + t) & 1)) + w // 2))
    return pairs


def on_device(
    wide_count,
    tp_count,
    hidden,
    input_norm_gain,
    key_value_weight,
    key_value_bias,
    adapter_down_factor,
    adapter_up_factor,
    queries,
    stored_rotated_keys,
    stored_value_rows,
    lengths,
):
    steps, rows, part_width = hidden.shape
    width = part_width * tp_count
    kinds, ranks, down_width = adapter_down_factor.shape
    gain = input_norm_gain.reshape(width // HD, HD)
    up_part = jnp.transpose(adapter_up_factor, (0, 2, 1))
    both = ("wide", "tp")

    direct = wide_count == 4 and tp_count == 4
    parts = [hidden] + [swap(hidden, "tp", offset, tp_count) for offset in (1, 2, 3)]
    if direct:
        there = meeting_place()
        moved = lax.ppermute(hidden, both, there)
        up = [swap(up_part, "wide", offset, 4) for offset in (1, 2, 3)]
    staged, streamed = (0, 1), (2, 3)
    staged_weight, down, gain_rows, my_up, bias, *cached = cache_call(
        staged,
        part_width,
        lengths,
        queries,
        stored_rotated_keys,
        stored_value_rows,
        adapter_down_factor,
        gain,
        up_part,
        key_value_bias,
        key_value_weight,
    )
    if direct:
        inner = inner_call(moved, gain_rows, down)
        inner = lax.ppermute(inner, both, [(b, a) for a, b in there])
        up = [my_up] + up
    else:
        gathered = lax.all_gather(hidden, "tp", axis=2, tiled=True).astype(jnp.float32)
        scaled = (gathered * input_norm_gain.astype(jnp.float32)).astype(jnp.bfloat16)
        all_down = lax.all_gather(adapter_down_factor, "wide", axis=2, tiled=True)
        inner = jnp.einsum("srd,kad->srka", scaled, all_down, preferred_element_type=jnp.float32)
        inner = [inner.reshape(steps * rows, kinds * ranks)]
        up = [lax.all_gather(up_part, "wide", axis=1, tiled=True)]

    base, square = base_call(staged, streamed, gain_rows, staged_weight, key_value_weight, parts)
    if direct:
        inner, square = lax.optimization_barrier((inner, square))
        inner = [inner] + [swap(inner, "tp", offset, 4) for offset in (2, 3, 1)]
    return final_call(queries.shape, width, base, square, bias, cached, inner, up)


def solution(mesh):
    in_specs = (
        P(None, ("groups", "wide"), "tp"),
        P(),
        P(None, None, "tp"),
        P(None, "tp"),
        P("groups", None, "wide"),
        P("groups", "tp", "wide"),
        P(None, ("groups", "wide"), "tp"),
        P(("groups", "wide"), None, "tp"),
        P(("groups", "wide"), None, "tp"),
        P(("groups", "wide")),
    )
    out_specs = (
        P(None, ("groups", "wide"), "tp"),
        P(None, ("groups", "wide"), "tp"),
        P(None, ("groups", "wide"), "tp"),
    )
    body = functools.partial(on_device, mesh.shape["wide"], mesh.shape["tp"])
    return jax.shard_map(
        body, mesh=mesh, in_specs=in_specs, out_specs=out_specs, check_vma=False
    )
```

```python
import functools
import math

import jax
import jax.numpy as jnp
from jax import lax
from jax.experimental import pallas as pl
from jax.experimental.pallas import tpu as pltpu
from jax.sharding import PartitionSpec as P

HD = 128


norm_eps = 1e-06
adapter_scale = 2.0
rope_base = 1000000.0
masked_score = -1e30
score_scale = 1.0 / math.sqrt(HD)

VMEM = pl.BlockSpec(memory_space=pltpu.VMEM)
HBM = pl.BlockSpec(memory_space=pltpu.HBM)


def query_block(query_ref, group, per_group):
    steps = query_ref.shape[0]
    tiles = []
    for head in range(per_group):
        at = (group * per_group + head) * HD
        for step in range(steps):
            tiles.append(query_ref[step, :, at : at + HD].astype(jnp.float32))
    return jnp.concatenate(tiles, axis=0)


def weight_block(weight_ref, block, width):
    return weight_ref.at[pl.ds(pl.multiple_of(block * width, width), width)]


def cache_kernel(
    staged,
    lengths_ref,
    query_ref,
    key_ref,
    value_ref,
    gain_ref,
    bias_ref,
    weight_ref,
    weight_out,
    gain_out,
    bias_out,
    query_out,
    acc_out,
    top_out,
    total_out,
    cos_out,
    sin_out,
    lengths,
    queries,
    gain_buffer,
    key_buffer,
    value_buffer,
    score_buffer,
    sems,
):
    steps, rows, query_width = query_ref.shape
    cache_span = key_ref.shape[1]
    groups = key_ref.shape[2] // HD
    per_group = query_width // HD // groups
    lines = steps * per_group
    half_rows = rows // 2
    halves = [pl.ds(0, half_rows), pl.ds(half_rows, half_rows)]
    copies = [
        (lengths_ref, lengths),
        (query_ref, queries),
        (key_ref.at[halves[0]], key_buffer.at[halves[0]]),
        (key_ref.at[halves[1]], key_buffer.at[halves[1]]),
        (value_ref.at[halves[0]], value_buffer.at[halves[0]]),
        (value_ref.at[halves[1]], value_buffer.at[halves[1]]),
        (gain_ref, gain_buffer),
        (bias_ref, bias_out),
    ]
    me = lax.axis_index("tp")
    for i, offset in enumerate(staged):
        copies.append((weight_block(weight_ref, me ^ offset, weight_out.shape[1]), weight_out.at[i]))
    copies = [pltpu.make_async_copy(*pair, sems.at[i]) for i, pair in enumerate(copies)]
    for copy in copies:
        copy.start()

    copies[0].wait()
    lane = lax.broadcasted_iota(jnp.int32, (rows, HD), 1)
    half = HD // 2
    second = lane >= half
    index = jnp.where(second, lane - half, lane).astype(jnp.float32)
    inv_freq = jnp.exp(index * (-2.0 * math.log(rope_base) / HD))
    row_index = lax.broadcasted_iota(jnp.int32, (rows, HD), 0)
    row_lengths = jnp.zeros((rows, HD), jnp.int32)
    for row in range(rows):
        row_lengths = jnp.where(row_index == row, lengths[row], row_lengths)
    for step in range(steps):
        angles = (row_lengths + step).astype(jnp.float32) * inv_freq
        sine = jnp.sin(angles)
        cos_out[pl.ds(step * rows, rows)] = jnp.cos(angles)
        sin_out[pl.ds(step * rows, rows)] = jnp.where(second, sine, -sine)
    copies[1].wait()
    for group in range(groups):
        query_out[group] = query_block(queries, group, per_group)

    place = lax.broadcasted_iota(jnp.int32, (lines, cache_span), 1)
    for i in range(2):
        copies[2 + i].wait()
        for row in range(i * half_rows, (i + 1) * half_rows):
            for group in range(groups):
                query = query_out[group, pl.ds(row, lines, stride=rows), :].astype(jnp.bfloat16)
                score_buffer[row * groups + group] = lax.dot_general(
                    query,
                    key_buffer[row, :, pl.ds(group * HD, HD)],
                    (((1,), (1,)), ((), ())),
                    preferred_element_type=jnp.float32,
                )
    for i in range(2):
        copies[4 + i].wait()
        for row in range(i * half_rows, (i + 1) * half_rows):
            live = place < lengths[row]
            for group in range(groups):
                mine = pl.ds(row, lines, stride=rows)
                scores = score_buffer[row * groups + group]
                scores = jnp.where(live, scores * score_scale, masked_score)
                top = jnp.max(scores, axis=1, keepdims=True)
                exps = jnp.exp(scores - top)
                total = jnp.sum(exps, axis=1, keepdims=True)
                acc = jnp.dot(
                    exps.astype(jnp.bfloat16),
                    value_buffer[row, :, pl.ds(group * HD, HD)],
                    preferred_element_type=jnp.float32,
                )
                acc_out[group, mine, :] = acc
                top_out[group, mine, :] = jnp.broadcast_to(top, acc.shape)
                total_out[group, mine, :] = jnp.broadcast_to(total, acc.shape)
    copies[6].wait()
    gain_out[...] = gain_buffer[...].astype(jnp.float32)
    for copy in copies[7:]:
        copy.wait()


def cache_call(staged, part_width, lengths, queries, keys, values, gain, bias, weight):
    steps, rows, query_width = queries.shape
    cache_span, key_width = keys.shape[1:]
    groups = key_width // HD
    lines = steps * (query_width // key_width)
    block = (groups, lines * rows, HD)
    table = (steps * rows, HD)
    operands = (lengths, queries, keys, values, gain, bias, weight)
    return pl.pallas_call(
        functools.partial(cache_kernel, staged),
        out_shape=(
            pltpu.VMEM((len(staged), part_width) + weight.shape[1:], weight.dtype),
            pltpu.VMEM(gain.shape, jnp.float32),
            pltpu.VMEM(bias.shape, bias.dtype),
            pltpu.VMEM(block, jnp.float32),
            pltpu.VMEM(block, jnp.float32),
            pltpu.VMEM(block, jnp.float32),
            pltpu.VMEM(block, jnp.float32),
            pltpu.VMEM(table, jnp.float32),
            pltpu.VMEM(table, jnp.float32),
        ),
        in_specs=[HBM] * len(operands),
        out_specs=(VMEM,) * 9,
        scratch_shapes=[
            pltpu.SMEM(lengths.shape, jnp.int32),
            pltpu.VMEM(queries.shape, queries.dtype),
            pltpu.VMEM(gain.shape, gain.dtype),
            pltpu.VMEM(keys.shape, keys.dtype),
            pltpu.VMEM(values.shape, values.dtype),
            pltpu.VMEM((rows * groups, lines, cache_span), jnp.float32),
            pltpu.SemaphoreType.DMA((8 + len(staged),)),
        ],
        compiler_params=pltpu.CompilerParams(vmem_limit_bytes=16 << 20),
        cost_estimate=pl.CostEstimate(flops=2 * 67 << 20, bytes_accessed=9 << 20, transcendentals=0),
        name="cache_attention",
    )(*[pltpu.with_memory_space_constraint(x, pltpu.HBM) for x in operands])


def rows_of(ref):
    return jnp.concatenate([ref[s].astype(jnp.float32) for s in range(ref.shape[0])], axis=0)


def pack_kernel(down_ref, up_ref, out_ref, sems):
    share = out_ref.shape[1]
    width = down_ref.shape[2]
    at = pl.ds(pl.multiple_of(lax.axis_index("tp") * share, share), share)
    down = pltpu.make_async_copy(
        down_ref.at[:, at, :], out_ref.at[:, :, pl.ds(0, width)], sems.at[0]
    )
    up = pltpu.make_async_copy(
        up_ref, out_ref.at[:, :, pl.ds(width, up_ref.shape[2])], sems.at[1]
    )
    down.start()
    up.start()
    down.wait()
    up.wait()


def pack_call(down, up):
    kinds, share, columns = up.shape
    return pl.pallas_call(
        pack_kernel,
        out_shape=pltpu.VMEM((kinds, share, down.shape[2] + columns), down.dtype),
        in_specs=[HBM] * 2,
        out_specs=VMEM,
        scratch_shapes=[pltpu.SemaphoreType.DMA((2,))],
        name="pack_factors",
    )(*[pltpu.with_memory_space_constraint(x, pltpu.HBM) for x in (down, up)])


def inner_kernel(scaled_ref, *rest):
    packs, out_ref = rest[:-1], rest[-1]
    me = lax.axis_index("wide")
    width = scaled_ref.shape[2]
    total = None
    for offset, pack in enumerate(packs):
        part = lax.dot_general(
            scaled_ref[me ^ offset],
            pack[:, :, :width].reshape(out_ref.shape[1], width),
            (((1,), (1,)), ((), ())),
            preferred_element_type=jnp.float32,
        )
        total = part if total is None else total + part
    out_ref[...] = total


def inner_call(scaled, packs):
    kinds, share, _ = packs[0].shape
    return pl.pallas_call(
        inner_kernel,
        out_shape=jax.ShapeDtypeStruct((scaled.shape[1], kinds * share), jnp.float32),
        in_specs=[VMEM] * (1 + len(packs)),
        out_specs=VMEM,
        compiler_params=pltpu.CompilerParams(vmem_limit_bytes=8 << 20),
        name="rank_inner",
    )(scaled, *packs)


def base_kernel(staged, streamed, gain_ref, staged_ref, weight_ref, *rest):
    offsets = staged + streamed
    parts = rest[: len(offsets)]
    base_out, square_out, scaled_out, buffer, sems = rest[len(offsets) :]
    steps, rows, width = parts[0].shape
    count = steps * rows
    kinds, columns = weight_ref.shape[1:]
    chunks = width // HD
    me = lax.axis_index("tp")
    copies = []
    for i, offset in enumerate(streamed):
        copy = pltpu.make_async_copy(
            weight_block(weight_ref, me ^ offset, width), buffer.at[i], sems.at[i]
        )
        copy.start()
        copies.append(copy)
    feature = lax.broadcasted_iota(jnp.int32, (HD, kinds * kinds * HD), 0)
    place = lax.broadcasted_iota(jnp.int32, (HD, kinds * kinds * HD), 1)
    kind = place // (kinds * HD)
    spreader = jnp.where(feature * kinds + kind == place % (kinds * HD), 1.0, 0.0).astype(jnp.bfloat16)
    squares = jnp.zeros((count, HD), jnp.float32)
    acc = jnp.zeros((kinds * count, columns), jnp.float32)
    for k, (offset, part) in enumerate(zip(offsets, parts)):
        start = pl.multiple_of((me ^ offset) * chunks, chunks)
        gain = gain_ref[pl.ds(start, chunks)]
        values = rows_of(part)
        scaled = []
        for i in range(chunks):
            chunk = values[:, i * HD : (i + 1) * HD]
            squares += chunk * chunk
            scaled.append((chunk * gain[i : i + 1]).astype(jnp.bfloat16))
            scaled_out[me ^ offset, :, i * HD : (i + 1) * HD] = scaled[i]
        spread = jnp.dot(
            jnp.concatenate(scaled, axis=0), spreader, preferred_element_type=jnp.float32
        ).astype(jnp.bfloat16)
        if k < len(staged):
            block = staged_ref.at[k]
        else:
            copies[k - len(staged)].wait()
            block = buffer.at[k - len(staged)]
        flat = block.reshape(width * kinds, columns)
        for i in range(chunks):
            lines = spread[i * count : (i + 1) * count]
            lines = jnp.concatenate(
                [lines[:, j * kinds * HD : (j + 1) * kinds * HD] for j in range(kinds)], axis=0
            )
            acc += jnp.dot(
                lines, flat[pl.ds(i * HD * kinds, HD * kinds), :], preferred_element_type=jnp.float32
            )
    base_out[...] = acc
    square_out[...] = jnp.broadcast_to(jnp.sum(squares, axis=1, keepdims=True), squares.shape)


def base_call(staged, streamed, gain, staged_weight, weight, parts):
    steps, rows, width = parts[0].shape
    kinds, columns = weight.shape[1:]
    return pl.pallas_call(
        functools.partial(base_kernel, staged, streamed),
        out_shape=(
            pltpu.VMEM((kinds * steps * rows, columns), jnp.float32),
            pltpu.VMEM((steps * rows, HD), jnp.float32),
            pltpu.VMEM((len(parts), steps * rows, width), jnp.bfloat16),
        ),
        in_specs=[VMEM, VMEM, HBM] + [VMEM] * len(parts),
        out_specs=(VMEM,) * 3,
        scratch_shapes=[
            pltpu.VMEM((len(streamed), width, kinds, columns), weight.dtype),
            pltpu.SemaphoreType.DMA((len(streamed),)),
        ],
        compiler_params=pltpu.CompilerParams(vmem_limit_bytes=16 << 20),
        cost_estimate=pl.CostEstimate(flops=4 * 134 << 20, bytes_accessed=9 << 20, transcendentals=0),
        name="base_projection",
    )(gain, staged_weight, pltpu.with_memory_space_constraint(weight, pltpu.HBM), *parts)


def final_kernel(width, blocks, base_ref, square_ref, bias_ref, *rest):
    query_ref, acc_ref, top_ref, total_ref, cos_ref, sin_ref = rest[:6]
    inner_refs = rest[6 : 6 + blocks]
    up_refs = rest[6 + blocks : 6 + 2 * blocks]
    keys_out, values_out, attended_out, inner_buffer, up_buffer = rest[6 + 2 * blocks :]
    steps, rows, columns = keys_out.shape
    count = steps * rows
    groups, size, _ = query_ref.shape
    per_group = size // count
    kinds, share, pack_width = up_refs[0].shape
    row_scale = lax.rsqrt(square_ref[:, :1] * (1.0 / width) + norm_eps)
    my_tp, my_wide = (lax.axis_index("tp"), lax.axis_index("wide")) if blocks > 1 else (0, 0)
    for i in range(blocks):
        inner_buffer[my_tp ^ i] = inner_refs[i][...]
        up_buffer[my_wide ^ i] = up_refs[i][:, :, pack_width - columns :]
    bias = bias_ref[...].astype(jnp.float32)
    linear = []
    for kind in range(kinds):
        lora = jnp.zeros((count, columns), jnp.float32)
        for i in range(blocks):
            inner = inner_buffer[i, :, kind * share : (kind + 1) * share]
            high = inner.astype(jnp.bfloat16)
            low = (inner - high.astype(jnp.float32)).astype(jnp.bfloat16)
            up = up_buffer[i, kind]
            lora += jnp.dot(high, up, preferred_element_type=jnp.float32)
            lora += jnp.dot(low, up, preferred_element_type=jnp.float32)
        base = base_ref[kind * count : (kind + 1) * count]
        linear.append((base + adapter_scale * lora) * row_scale + bias[kind : kind + 1])
    cosine, sine = cos_ref[...], sin_ref[...]
    line = lax.broadcasted_iota(jnp.int32, (size, count), 0)
    other = lax.broadcasted_iota(jnp.int32, (size, count), 1)
    live = (line % rows == other % rows) & (other // rows <= line // rows % steps)
    for group in range(groups):
        at = slice(group * HD, (group + 1) * HD)
        key = linear[0][:, at]
        key = (key * cosine + pltpu.roll(key, HD // 2, 1) * sine).astype(jnp.bfloat16)
        value = linear[1][:, at].astype(jnp.bfloat16)
        for step in range(steps):
            keys_out[step, :, at] = key[step * rows : (step + 1) * rows]
            values_out[step, :, at] = value[step * rows : (step + 1) * rows]
        scores = lax.dot_general(
            query_ref[group].astype(jnp.bfloat16),
            key,
            (((1,), (1,)), ((), ())),
            preferred_element_type=jnp.float32,
        )
        scores = jnp.where(live, scores * score_scale, masked_score)
        old_top = top_ref[group][:, :1]
        top = jnp.maximum(old_top, jnp.max(scores, axis=1, keepdims=True))
        exps = jnp.exp(scores - top)
        keep = jnp.exp(old_top - top)
        total = total_ref[group][:, :1] * keep + jnp.sum(exps, axis=1, keepdims=True)
        acc = acc_ref[group] * keep + jnp.dot(
            exps.astype(jnp.bfloat16), value, preferred_element_type=jnp.float32
        )
        attended = (acc / total).astype(jnp.bfloat16)
        for head in range(per_group):
            lanes = pl.ds((group * per_group + head) * HD, HD)
            for step in range(steps):
                tile = (head * steps + step) * rows
                attended_out[step, :, lanes] = attended[tile : tile + rows]


def final_call(shape, width, base, square, bias, cached, inner, up):
    steps, rows, query_width = shape
    columns = base.shape[1]
    small = jax.ShapeDtypeStruct((steps, rows, columns), jnp.bfloat16)
    return pl.pallas_call(
        functools.partial(final_kernel, width, len(inner)),
        out_shape=(small, small, jax.ShapeDtypeStruct(shape, jnp.bfloat16)),
        in_specs=[VMEM] * (3 + len(cached) + len(inner) + len(up)),
        out_specs=(VMEM,) * 3,
        scratch_shapes=[
            pltpu.VMEM((len(inner),) + inner[0].shape, jnp.float32),
            pltpu.VMEM((len(up),) + up[0].shape[:2] + (columns,), up[0].dtype),
        ],
        compiler_params=pltpu.CompilerParams(vmem_limit_bytes=8 << 20),
        name="fresh_attention",
    )(base, square, bias, *cached, *inner, *up)


def swap(block, axis, offset, count):
    return lax.ppermute(block, axis, [(i, i ^ offset) for i in range(count)])


def on_device(
    wide_count,
    tp_count,
    hidden,
    input_norm_gain,
    key_value_weight,
    key_value_bias,
    adapter_down_factor,
    adapter_up_factor,
    queries,
    stored_rotated_keys,
    stored_value_rows,
    lengths,
):
    steps, rows, part_width = hidden.shape
    width = part_width * tp_count
    kinds, ranks, down_width = adapter_down_factor.shape
    gain = input_norm_gain.reshape(width // HD, HD)
    up_part = jnp.transpose(adapter_up_factor, (0, 2, 1))
    direct = wide_count == tp_count == 4
    parts = [hidden] + [swap(hidden, "tp", offset, tp_count) for offset in (1, 2, 3)]
    if direct:
        pack = pack_call(adapter_down_factor, up_part)
        packs = [pack] + [swap(pack, "wide", offset, wide_count) for offset in (1, 2, 3)]
    staged, streamed = (0, 1), (2, 3)
    staged_weight, gain_rows, bias, *cached = cache_call(
        staged,
        part_width,
        lengths,
        queries,
        stored_rotated_keys,
        stored_value_rows,
        gain,
        key_value_bias,
        key_value_weight,
    )
    base, square, scaled = base_call(
        staged, streamed, gain_rows, staged_weight, key_value_weight, parts
    )
    if direct:
        inner = inner_call(scaled, packs)
        inner = [inner] + [swap(inner, "tp", offset, tp_count) for offset in (2, 3, 1)]
        inner = [inner[i] for i in (0, 3, 1, 2)]
        up = packs
    else:
        down = lax.all_gather(adapter_down_factor, "wide", axis=2, tiled=True)
        down = down.reshape(kinds * ranks, tp_count, part_width)
        inner = [
            jnp.einsum("brd,kbd->rk", scaled, down, preferred_element_type=jnp.float32)
        ]
        up = [lax.all_gather(up_part, "wide", axis=1, tiled=True)]
    return final_call(queries.shape, width, base, square, bias, cached, inner, up)


def solution(mesh):
    in_specs = (
        P(None, ("groups", "wide"), "tp"),
        P(),
        P(None, None, "tp"),
        P(None, "tp"),
        P("groups", None, "wide"),
        P("groups", "tp", "wide"),
        P(None, ("groups", "wide"), "tp"),
        P(("groups", "wide"), None, "tp"),
        P(("groups", "wide"), None, "tp"),
        P(("groups", "wide")),
    )
    out_specs = (
        P(None, ("groups", "wide"), "tp"),
        P(None, ("groups", "wide"), "tp"),
        P(None, ("groups", "wide"), "tp"),
    )
    body = functools.partial(on_device, mesh.shape["wide"], mesh.shape["tp"])
    return jax.shard_map(
        body, mesh=mesh, in_specs=in_specs, out_specs=out_specs, check_vma=False
    )
```

```python
import functools
import math

import jax
import jax.numpy as jnp
from jax import lax
from jax.experimental import pallas as pl
from jax.experimental.pallas import tpu as pltpu
from jax.sharding import PartitionSpec as P

HD = 128


norm_eps = 1e-06
adapter_scale = 2.0
rope_base = 1000000.0
masked_score = -1e30
score_scale = 1.0 / math.sqrt(HD)

VMEM = pl.BlockSpec(memory_space=pltpu.VMEM)
HBM = pl.BlockSpec(memory_space=pltpu.HBM)


def query_block(query_ref, group, per_group):
    steps = query_ref.shape[0]
    tiles = []
    for head in range(per_group):
        at = (group * per_group + head) * HD
        for step in range(steps):
            tiles.append(query_ref[step, :, at : at + HD].astype(jnp.float32))
    return jnp.concatenate(tiles, axis=0)


def weight_block(weight_ref, block, width):
    return weight_ref.at[pl.ds(pl.multiple_of(block * width, width), width)]


def cache_kernel(
    staged,
    lengths_ref,
    query_ref,
    key_ref,
    value_ref,
    gain_ref,
    bias_ref,
    weight_ref,
    weight_out,
    gain_out,
    bias_out,
    query_out,
    acc_out,
    top_out,
    total_out,
    cos_out,
    sin_out,
    lengths,
    queries,
    gain_buffer,
    key_buffer,
    value_buffer,
    score_buffer,
    sems,
):
    steps, rows, query_width = query_ref.shape
    cache_span = key_ref.shape[1]
    groups = key_ref.shape[2] // HD
    per_group = query_width // HD // groups
    lines = steps * per_group
    half_rows = rows // 2
    halves = [pl.ds(0, half_rows), pl.ds(half_rows, half_rows)]
    copies = [
        (lengths_ref, lengths),
        (query_ref, queries),
        (key_ref.at[halves[0]], key_buffer.at[halves[0]]),
        (key_ref.at[halves[1]], key_buffer.at[halves[1]]),
        (value_ref.at[halves[0]], value_buffer.at[halves[0]]),
        (value_ref.at[halves[1]], value_buffer.at[halves[1]]),
        (gain_ref, gain_buffer),
        (bias_ref, bias_out),
    ]
    me = lax.axis_index("tp")
    for i, offset in enumerate(staged):
        copies.append((weight_block(weight_ref, me ^ offset, weight_out.shape[1]), weight_out.at[i]))
    copies = [pltpu.make_async_copy(*pair, sems.at[i]) for i, pair in enumerate(copies)]
    for copy in copies:
        copy.start()

    copies[0].wait()
    lane = lax.broadcasted_iota(jnp.int32, (rows, HD), 1)
    half = HD // 2
    second = lane >= half
    index = jnp.where(second, lane - half, lane).astype(jnp.float32)
    inv_freq = jnp.exp(index * (-2.0 * math.log(rope_base) / HD))
    row_index = lax.broadcasted_iota(jnp.int32, (rows, HD), 0)
    row_lengths = jnp.zeros((rows, HD), jnp.int32)
    for row in range(rows):
        row_lengths = jnp.where(row_index == row, lengths[row], row_lengths)
    for step in range(steps):
        angles = (row_lengths + step).astype(jnp.float32) * inv_freq
        sine = jnp.sin(angles)
        cos_out[pl.ds(step * rows, rows)] = jnp.cos(angles)
        sin_out[pl.ds(step * rows, rows)] = jnp.where(second, sine, -sine)
    copies[1].wait()
    for group in range(groups):
        query_out[group] = query_block(queries, group, per_group)

    place = lax.broadcasted_iota(jnp.int32, (lines, cache_span), 1)
    for i in range(2):
        copies[2 + i].wait()
        for row in range(i * half_rows, (i + 1) * half_rows):
            for group in range(groups):
                query = query_out[group, pl.ds(row, lines, stride=rows), :].astype(jnp.bfloat16)
                score_buffer[row * groups + group] = lax.dot_general(
                    query,
                    key_buffer[row, :, pl.ds(group * HD, HD)],
                    (((1,), (1,)), ((), ())),
                    preferred_element_type=jnp.float32,
                )
    for i in range(2):
        copies[4 + i].wait()
        for row in range(i * half_rows, (i + 1) * half_rows):
            live = place < lengths[row]
            for group in range(groups):
                mine = pl.ds(row, lines, stride=rows)
                scores = score_buffer[row * groups + group]
                scores = jnp.where(live, scores * score_scale, masked_score)
                top = jnp.max(scores, axis=1, keepdims=True)
                exps = jnp.exp(scores - top)
                total = jnp.sum(exps, axis=1, keepdims=True)
                acc = jnp.dot(
                    exps.astype(jnp.bfloat16),
                    value_buffer[row, :, pl.ds(group * HD, HD)],
                    preferred_element_type=jnp.float32,
                )
                acc_out[group, mine, :] = acc
                top_out[group, mine, :] = jnp.broadcast_to(top, acc.shape)
                total_out[group, mine, :] = jnp.broadcast_to(total, acc.shape)
    copies[6].wait()
    gain_out[...] = gain_buffer[...].astype(jnp.float32)
    for copy in copies[7:]:
        copy.wait()


def cache_call(staged, part_width, lengths, queries, keys, values, gain, bias, weight):
    steps, rows, query_width = queries.shape
    cache_span, key_width = keys.shape[1:]
    groups = key_width // HD
    lines = steps * (query_width // key_width)
    block = (groups, lines * rows, HD)
    table = (steps * rows, HD)
    operands = (lengths, queries, keys, values, gain, bias, weight)
    return pl.pallas_call(
        functools.partial(cache_kernel, staged),
        out_shape=(
            pltpu.VMEM((len(staged), part_width) + weight.shape[1:], weight.dtype),
            pltpu.VMEM(gain.shape, jnp.float32),
            pltpu.VMEM(bias.shape, bias.dtype),
            pltpu.VMEM(block, jnp.float32),
            pltpu.VMEM(block, jnp.float32),
            pltpu.VMEM(block, jnp.float32),
            pltpu.VMEM(block, jnp.float32),
            pltpu.VMEM(table, jnp.float32),
            pltpu.VMEM(table, jnp.float32),
        ),
        in_specs=[HBM] * len(operands),
        out_specs=(VMEM,) * 9,
        scratch_shapes=[
            pltpu.SMEM(lengths.shape, jnp.int32),
            pltpu.VMEM(queries.shape, queries.dtype),
            pltpu.VMEM(gain.shape, gain.dtype),
            pltpu.VMEM(keys.shape, keys.dtype),
            pltpu.VMEM(values.shape, values.dtype),
            pltpu.VMEM((rows * groups, lines, cache_span), jnp.float32),
            pltpu.SemaphoreType.DMA((8 + len(staged),)),
        ],
        compiler_params=pltpu.CompilerParams(vmem_limit_bytes=16 << 20),
        cost_estimate=pl.CostEstimate(flops=2 * 67 << 20, bytes_accessed=9 << 20, transcendentals=0),
        name="cache_attention",
    )(*[pltpu.with_memory_space_constraint(x, pltpu.HBM) for x in operands])


def rows_of(ref):
    return jnp.concatenate([ref[s].astype(jnp.float32) for s in range(ref.shape[0])], axis=0)


def pack_kernel(down_ref, up_ref, out_ref, sems):
    share = out_ref.shape[1]
    width = down_ref.shape[2]
    at = pl.ds(pl.multiple_of(lax.axis_index("tp") * share, share), share)
    down = pltpu.make_async_copy(
        down_ref.at[:, at, :], out_ref.at[:, :, pl.ds(0, width)], sems.at[0]
    )
    up = pltpu.make_async_copy(
        up_ref, out_ref.at[:, :, pl.ds(width, up_ref.shape[2])], sems.at[1]
    )
    down.start()
    up.start()
    down.wait()
    up.wait()


def pack_call(down, up):
    kinds, share, columns = up.shape
    return pl.pallas_call(
        pack_kernel,
        out_shape=pltpu.VMEM((kinds, share, down.shape[2] + columns), down.dtype),
        in_specs=[HBM] * 2,
        out_specs=VMEM,
        scratch_shapes=[pltpu.SemaphoreType.DMA((2,))],
        name="pack_factors",
    )(*[pltpu.with_memory_space_constraint(x, pltpu.HBM) for x in (down, up)])


def inner_kernel(scaled_ref, *rest):
    packs, out_ref = rest[:-1], rest[-1]
    me = lax.axis_index("wide")
    width = scaled_ref.shape[2]
    total = []
    for offset, pack in enumerate(packs):
        total.append(
            lax.dot_general(
                scaled_ref[me ^ offset],
                pack[:, :, :width].reshape(out_ref.shape[1], width),
                (((1,), (1,)), ((), ())),
                preferred_element_type=jnp.float32,
            )
        )
    out_ref[...] = sum(total[1:], total[0])


def inner_call(scaled, packs):
    kinds, share, _ = packs[0].shape
    return pl.pallas_call(
        inner_kernel,
        out_shape=jax.ShapeDtypeStruct((scaled.shape[1], kinds * share), jnp.float32),
        in_specs=[VMEM] * (1 + len(packs)),
        out_specs=VMEM,
        compiler_params=pltpu.CompilerParams(vmem_limit_bytes=8 << 20),
        name="rank_inner",
    )(scaled, *packs)


def project(scaled, block, kinds):
    count, width = scaled.shape
    columns = block.shape[2]
    chunks = width // HD
    group = 4
    feature = lax.broadcasted_iota(jnp.int32, (HD, kinds * kinds * HD), 0)
    place = lax.broadcasted_iota(jnp.int32, (HD, kinds * kinds * HD), 1)
    kind = place // (kinds * HD)
    spreader = jnp.where(feature * kinds + kind == place % (kinds * HD), 1.0, 0.0).astype(jnp.bfloat16)
    stacked = jnp.concatenate([scaled[:, i * HD : (i + 1) * HD] for i in range(chunks)], axis=0)
    spread = jnp.dot(stacked, spreader, preferred_element_type=jnp.float32).astype(jnp.bfloat16)
    flat = block.reshape(width * kinds, columns)
    products = []
    for first in range(0, chunks, group):
        lines = []
        for i in range(first, first + group):
            chunk = spread[i * count : (i + 1) * count]
            lines.append(
                jnp.concatenate(
                    [chunk[:, j * kinds * HD : (j + 1) * kinds * HD] for j in range(kinds)], axis=0
                )
            )
        at = pl.ds(first * HD * kinds, group * HD * kinds)
        products.append(
            jnp.dot(jnp.concatenate(lines, axis=1), flat[at, :], preferred_element_type=jnp.float32)
        )
    return sum(products[1:], products[0])


def near_kernel(near, far, gain_ref, near_ref, weight_ref, *rest):
    offsets = near + far
    parts = rest[: len(offsets)]
    base_out, square_out, scaled_out, weight_out, sems = rest[len(offsets) :]
    steps, rows, width = parts[0].shape
    count = steps * rows
    kinds = weight_ref.shape[1]
    chunks = width // HD
    me = lax.axis_index("tp")
    copies = []
    for i, offset in enumerate(far):
        copy = pltpu.make_async_copy(
            weight_block(weight_ref, me ^ offset, width), weight_out.at[i], sems.at[i]
        )
        copy.start()
        copies.append(copy)
    squares = jnp.zeros((count, HD), jnp.float32)
    for offset, part in zip(offsets, parts):
        start = pl.multiple_of((me ^ offset) * chunks, chunks)
        gain = gain_ref[pl.ds(start, chunks)]
        values = rows_of(part)
        for i in range(chunks):
            chunk = values[:, i * HD : (i + 1) * HD]
            squares += chunk * chunk
            scaled_out[me ^ offset, :, i * HD : (i + 1) * HD] = (chunk * gain[i : i + 1]).astype(jnp.bfloat16)
    square_out[...] = jnp.broadcast_to(jnp.sum(squares, axis=1, keepdims=True), squares.shape)
    acc = None
    for k, offset in enumerate(near):
        product = project(scaled_out[me ^ offset], near_ref.at[k], kinds)
        acc = product if acc is None else acc + product
    base_out[...] = acc
    for copy in copies:
        copy.wait()


def near_call(near, far, gain, near_weight, weight, parts):
    steps, rows, width = parts[0].shape
    kinds, columns = weight.shape[1:]
    return pl.pallas_call(
        functools.partial(near_kernel, near, far),
        out_shape=(
            pltpu.VMEM((kinds * steps * rows, columns), jnp.float32),
            pltpu.VMEM((steps * rows, HD), jnp.float32),
            pltpu.VMEM((len(parts), steps * rows, width), jnp.bfloat16),
            pltpu.VMEM((len(far), width, kinds, columns), weight.dtype),
        ),
        in_specs=[VMEM, VMEM, HBM] + [VMEM] * len(parts),
        out_specs=(VMEM,) * 4,
        scratch_shapes=[pltpu.SemaphoreType.DMA((len(far),))],
        compiler_params=pltpu.CompilerParams(vmem_limit_bytes=16 << 20),
        cost_estimate=pl.CostEstimate(flops=2 * 134 << 20, bytes_accessed=5 << 20, transcendentals=0),
        name="near_projection",
    )(gain, near_weight, pltpu.with_memory_space_constraint(weight, pltpu.HBM), *parts)


def far_kernel(far, base_ref, scaled_ref, weight_ref, *rest):
    packs = rest[:-2]
    base_out, up_out = rest[-2:]
    kinds, share, pack_width = packs[0].shape
    columns = base_out.shape[1]
    me = lax.axis_index("wide") if len(packs) > 1 else 0
    up_out[...] = jnp.zeros_like(up_out)
    for offset, pack in enumerate(packs):
        for kind in range(kinds):
            at = pl.multiple_of(((me ^ offset) * kinds + kind) * share, share)
            up_out[pl.ds(at, share), kind * columns : (kind + 1) * columns] = pack[
                kind, :, pack_width - columns :
            ]
    acc = base_ref[...]
    tp = lax.axis_index("tp")
    for k, offset in enumerate(far):
        acc = acc + project(scaled_ref[tp ^ offset], weight_ref.at[k], kinds)
    base_out[...] = acc


def far_call(far, base, scaled, weight, packs):
    kinds, share, _ = packs[0].shape
    return pl.pallas_call(
        functools.partial(far_kernel, far),
        out_shape=(
            pltpu.VMEM(base.shape, base.dtype),
            pltpu.VMEM((len(packs) * kinds * share, kinds * base.shape[1]), jnp.bfloat16),
        ),
        in_specs=[VMEM] * (3 + len(packs)),
        out_specs=(VMEM,) * 2,
        compiler_params=pltpu.CompilerParams(vmem_limit_bytes=16 << 20),
        cost_estimate=pl.CostEstimate(flops=2 * 134 << 20, bytes_accessed=5 << 20, transcendentals=0),
        name="far_projection",
    )(base, scaled, weight, *packs)


def final_kernel(width, blocks, base_ref, square_ref, up_ref, bias_ref, *rest):
    query_ref, acc_ref, top_ref, total_ref, cos_ref, sin_ref = rest[:6]
    inner_refs = rest[6 : 6 + blocks]
    keys_out, values_out, attended_out, inner_buffer = rest[6 + blocks :]
    steps, rows, columns = keys_out.shape
    count = steps * rows
    groups, size, _ = query_ref.shape
    per_group = size // count
    kinds = bias_ref.shape[0]
    row_scale = lax.rsqrt(square_ref[:, :1] * (1.0 / width) + norm_eps)
    me = lax.axis_index("tp") if blocks > 1 else 0
    for i in range(blocks):
        inner_buffer[me ^ i] = inner_refs[i][...]
    inner = jnp.concatenate([inner_buffer[i] for i in range(blocks)], axis=1)
    high = inner.astype(jnp.bfloat16)
    low = (inner - high.astype(jnp.float32)).astype(jnp.bfloat16)
    lora = jnp.dot(
        jnp.concatenate([high, low], axis=0), up_ref[...], preferred_element_type=jnp.float32
    )
    lora = lora[:count] + lora[count:]
    bias = bias_ref[...].astype(jnp.float32)
    linear = []
    for kind in range(kinds):
        base = base_ref[kind * count : (kind + 1) * count]
        part = lora[:, kind * columns : (kind + 1) * columns]
        linear.append((base + adapter_scale * part) * row_scale + bias[kind : kind + 1])
    cosine, sine = cos_ref[...], sin_ref[...]
    line = lax.broadcasted_iota(jnp.int32, (size, count), 0)
    other = lax.broadcasted_iota(jnp.int32, (size, count), 1)
    live = (line % rows == other % rows) & (other // rows <= line // rows % steps)
    for group in range(groups):
        at = slice(group * HD, (group + 1) * HD)
        key = linear[0][:, at]
        key = (key * cosine + pltpu.roll(key, HD // 2, 1) * sine).astype(jnp.bfloat16)
        value = linear[1][:, at].astype(jnp.bfloat16)
        for step in range(steps):
            keys_out[step, :, at] = key[step * rows : (step + 1) * rows]
            values_out[step, :, at] = value[step * rows : (step + 1) * rows]
        scores = lax.dot_general(
            query_ref[group].astype(jnp.bfloat16),
            key,
            (((1,), (1,)), ((), ())),
            preferred_element_type=jnp.float32,
        )
        scores = jnp.where(live, scores * score_scale, masked_score)
        old_top = top_ref[group][:, :1]
        top = jnp.maximum(old_top, jnp.max(scores, axis=1, keepdims=True))
        exps = jnp.exp(scores - top)
        keep = jnp.exp(old_top - top)
        total = total_ref[group][:, :1] * keep + jnp.sum(exps, axis=1, keepdims=True)
        acc = acc_ref[group] * keep + jnp.dot(
            exps.astype(jnp.bfloat16), value, preferred_element_type=jnp.float32
        )
        attended = (acc / total).astype(jnp.bfloat16)
        for head in range(per_group):
            lanes = pl.ds((group * per_group + head) * HD, HD)
            for step in range(steps):
                tile = (head * steps + step) * rows
                attended_out[step, :, lanes] = attended[tile : tile + rows]


def final_call(shape, width, base, square, up, bias, cached, inner):
    steps, rows, query_width = shape
    columns = base.shape[1]
    small = jax.ShapeDtypeStruct((steps, rows, columns), jnp.bfloat16)
    return pl.pallas_call(
        functools.partial(final_kernel, width, len(inner)),
        out_shape=(small, small, jax.ShapeDtypeStruct(shape, jnp.bfloat16)),
        in_specs=[VMEM] * (4 + len(cached) + len(inner)),
        out_specs=(VMEM,) * 3,
        scratch_shapes=[pltpu.VMEM((len(inner),) + inner[0].shape, jnp.float32)],
        compiler_params=pltpu.CompilerParams(vmem_limit_bytes=8 << 20),
        name="fresh_attention",
    )(base, square, up, bias, *cached, *inner)


def swap(block, axis, offset, count):
    return lax.ppermute(block, axis, [(i, i ^ offset) for i in range(count)])


def on_device(
    wide_count,
    tp_count,
    hidden,
    input_norm_gain,
    key_value_weight,
    key_value_bias,
    adapter_down_factor,
    adapter_up_factor,
    queries,
    stored_rotated_keys,
    stored_value_rows,
    lengths,
):
    steps, rows, part_width = hidden.shape
    width = part_width * tp_count
    kinds, ranks, down_width = adapter_down_factor.shape
    gain = input_norm_gain.reshape(width // HD, HD)
    up_part = jnp.transpose(adapter_up_factor, (0, 2, 1))
    direct = wide_count == tp_count == 4
    parts = [hidden] + [swap(hidden, "tp", offset, tp_count) for offset in (1, 2, 3)]
    if direct:
        pack = pack_call(adapter_down_factor, up_part)
        second = swap(pack, "wide", 2, wide_count)
        first = swap(pack, "wide", 1, wide_count)
    near, far = (0, 1), (2, 3)
    near_weight, gain_rows, bias, *cached = cache_call(
        near,
        part_width,
        lengths,
        queries,
        stored_rotated_keys,
        stored_value_rows,
        gain,
        key_value_bias,
        key_value_weight,
    )
    if direct:
        relayed, gain_rows = lax.optimization_barrier((second, gain_rows))
        packs = [pack, first, second, swap(relayed, "wide", 1, wide_count)]
    base, square, scaled, far_weight = near_call(
        near, far, gain_rows, near_weight, key_value_weight, parts
    )
    if direct:
        inner = inner_call(scaled, packs)
        inner, scaled = lax.optimization_barrier((inner, scaled))
        inner = [inner] + [swap(inner, "tp", offset, tp_count) for offset in (1, 2, 3)]
    else:
        down = lax.all_gather(adapter_down_factor, "wide", axis=2, tiled=True)
        down = down.reshape(kinds * ranks, tp_count, part_width)
        inner = [
            jnp.einsum("brd,kbd->rk", scaled, down, preferred_element_type=jnp.float32)
        ]
        packs = [lax.all_gather(up_part, "wide", axis=1, tiled=True)]
    base, up = far_call(far, base, scaled, far_weight, packs)
    return final_call(queries.shape, width, base, square, up, bias, cached, inner)


def solution(mesh):
    in_specs = (
        P(None, ("groups", "wide"), "tp"),
        P(),
        P(None, None, "tp"),
        P(None, "tp"),
        P("groups", None, "wide"),
        P("groups", "tp", "wide"),
        P(None, ("groups", "wide"), "tp"),
        P(("groups", "wide"), None, "tp"),
        P(("groups", "wide"), None, "tp"),
        P(("groups", "wide")),
    )
    out_specs = (
        P(None, ("groups", "wide"), "tp"),
        P(None, ("groups", "wide"), "tp"),
        P(None, ("groups", "wide"), "tp"),
    )
    body = functools.partial(on_device, mesh.shape["wide"], mesh.shape["tp"])
    return jax.shard_map(
        body, mesh=mesh, in_specs=in_specs, out_specs=out_specs, check_vma=False
    )
```

```python
import functools
import math

import jax
import jax.numpy as jnp
from jax import lax
from jax.experimental import pallas as pl
from jax.experimental.pallas import tpu as pltpu
from jax.sharding import PartitionSpec as P

HD = 128


norm_eps = 1e-06
adapter_scale = 2.0
rope_base = 1000000.0
masked_score = -1e30
score_scale = 1.0 / math.sqrt(HD)

VMEM = pl.BlockSpec(memory_space=pltpu.VMEM)
HBM = pl.BlockSpec(memory_space=pltpu.HBM)


def query_block(query_ref, group, per_group):
    steps = query_ref.shape[0]
    tiles = []
    for head in range(per_group):
        at = (group * per_group + head) * HD
        for step in range(steps):
            tiles.append(query_ref[step, :, at : at + HD].astype(jnp.float32))
    return jnp.concatenate(tiles, axis=0)


def cache_kernel(
    lengths_ref,
    query_ref,
    key_ref,
    value_ref,
    gain_ref,
    bias_ref,
    hidden_ref,
    gain_out,
    bias_out,
    hidden_out,
    query_out,
    acc_out,
    top_out,
    total_out,
    cos_out,
    sin_out,
    lengths,
    queries,
    gain_buffer,
    key_buffer,
    value_buffer,
    score_buffer,
    sems,
):
    steps, rows, query_width = query_ref.shape
    cache_span = key_ref.shape[1]
    groups = key_ref.shape[2] // HD
    per_group = query_width // HD // groups
    lines = steps * per_group
    half_rows = rows // 2
    halves = [pl.ds(0, half_rows), pl.ds(half_rows, half_rows)]
    copies = [
        (lengths_ref, lengths),
        (query_ref, queries),
        (key_ref.at[halves[0]], key_buffer.at[halves[0]]),
        (key_ref.at[halves[1]], key_buffer.at[halves[1]]),
        (value_ref.at[halves[0]], value_buffer.at[halves[0]]),
        (value_ref.at[halves[1]], value_buffer.at[halves[1]]),
        (gain_ref, gain_buffer),
        (bias_ref, bias_out),
        (hidden_ref, hidden_out),
    ]
    copies = [pltpu.make_async_copy(*pair, sems.at[i]) for i, pair in enumerate(copies)]
    for copy in copies:
        copy.start()

    copies[0].wait()
    lane = lax.broadcasted_iota(jnp.int32, (rows, HD), 1)
    half = HD // 2
    second = lane >= half
    index = jnp.where(second, lane - half, lane).astype(jnp.float32)
    inv_freq = jnp.exp(index * (-2.0 * math.log(rope_base) / HD))
    row_index = lax.broadcasted_iota(jnp.int32, (rows, HD), 0)
    row_lengths = jnp.zeros((rows, HD), jnp.int32)
    for row in range(rows):
        row_lengths = jnp.where(row_index == row, lengths[row], row_lengths)
    for step in range(steps):
        angles = (row_lengths + step).astype(jnp.float32) * inv_freq
        sine = jnp.sin(angles)
        cos_out[pl.ds(step * rows, rows)] = jnp.cos(angles)
        sin_out[pl.ds(step * rows, rows)] = jnp.where(second, sine, -sine)
    copies[1].wait()
    for group in range(groups):
        query_out[group] = query_block(queries, group, per_group)

    place = lax.broadcasted_iota(jnp.int32, (lines, cache_span), 1)
    for i in range(2):
        copies[2 + i].wait()
        for row in range(i * half_rows, (i + 1) * half_rows):
            for group in range(groups):
                query = query_out[group, pl.ds(row, lines, stride=rows), :].astype(jnp.bfloat16)
                score_buffer[row * groups + group] = lax.dot_general(
                    query,
                    key_buffer[row, :, pl.ds(group * HD, HD)],
                    (((1,), (1,)), ((), ())),
                    preferred_element_type=jnp.float32,
                )
    for i in range(2):
        copies[4 + i].wait()
        for row in range(i * half_rows, (i + 1) * half_rows):
            live = place < lengths[row]
            for group in range(groups):
                mine = pl.ds(row, lines, stride=rows)
                scores = score_buffer[row * groups + group]
                scores = jnp.where(live, scores * score_scale, masked_score)
                top = jnp.max(scores, axis=1, keepdims=True)
                exps = jnp.exp(scores - top)
                total = jnp.sum(exps, axis=1, keepdims=True)
                acc = jnp.dot(
                    exps.astype(jnp.bfloat16),
                    value_buffer[row, :, pl.ds(group * HD, HD)],
                    preferred_element_type=jnp.float32,
                )
                acc_out[group, mine, :] = acc
                top_out[group, mine, :] = jnp.broadcast_to(top, acc.shape)
                total_out[group, mine, :] = jnp.broadcast_to(total, acc.shape)
    copies[6].wait()
    gain_out[...] = gain_buffer[...].astype(jnp.float32)
    for copy in copies[7:]:
        copy.wait()


def cache_call(lengths, queries, keys, values, gain, bias, hidden):
    steps, rows, query_width = queries.shape
    cache_span, key_width = keys.shape[1:]
    groups = key_width // HD
    lines = steps * (query_width // key_width)
    block = (groups, lines * rows, HD)
    table = (steps * rows, HD)
    operands = (lengths, queries, keys, values, gain, bias, hidden)
    return pl.pallas_call(
        cache_kernel,
        out_shape=(
            pltpu.VMEM(gain.shape, jnp.float32),
            pltpu.VMEM(bias.shape, bias.dtype),
            pltpu.VMEM(hidden.shape, hidden.dtype),
            pltpu.VMEM(block, jnp.float32),
            pltpu.VMEM(block, jnp.float32),
            pltpu.VMEM(block, jnp.float32),
            pltpu.VMEM(block, jnp.float32),
            pltpu.VMEM(table, jnp.float32),
            pltpu.VMEM(table, jnp.float32),
        ),
        in_specs=[HBM] * len(operands),
        out_specs=(VMEM,) * 9,
        scratch_shapes=[
            pltpu.SMEM(lengths.shape, jnp.int32),
            pltpu.VMEM(queries.shape, queries.dtype),
            pltpu.VMEM(gain.shape, gain.dtype),
            pltpu.VMEM(keys.shape, keys.dtype),
            pltpu.VMEM(values.shape, values.dtype),
            pltpu.VMEM((rows * groups, lines, cache_span), jnp.float32),
            pltpu.SemaphoreType.DMA((9,)),
        ],
        compiler_params=pltpu.CompilerParams(vmem_limit_bytes=16 << 20),
        cost_estimate=pl.CostEstimate(flops=2 * 67 << 20, bytes_accessed=5 << 20, transcendentals=0),
        name="cache_attention",
    )(*[pltpu.with_memory_space_constraint(x, pltpu.HBM) for x in operands])


def rows_of(ref):
    return jnp.concatenate([ref[s].astype(jnp.float32) for s in range(ref.shape[0])], axis=0)


def pack_kernel(down_ref, up_ref, out_ref, sems):
    share = out_ref.shape[1]
    width = down_ref.shape[2]
    at = pl.ds(pl.multiple_of(lax.axis_index("tp") * share, share), share)
    down = pltpu.make_async_copy(
        down_ref.at[:, at, :], out_ref.at[:, :, pl.ds(0, width)], sems.at[0]
    )
    up = pltpu.make_async_copy(
        up_ref, out_ref.at[:, :, pl.ds(width, up_ref.shape[2])], sems.at[1]
    )
    down.start()
    up.start()
    down.wait()
    up.wait()


def pack_call(down, up):
    kinds, share, columns = up.shape
    return pl.pallas_call(
        pack_kernel,
        out_shape=pltpu.VMEM((kinds, share, down.shape[2] + columns), down.dtype),
        in_specs=[HBM] * 2,
        out_specs=VMEM,
        scratch_shapes=[pltpu.SemaphoreType.DMA((2,))],
        name="pack_factors",
    )(*[pltpu.with_memory_space_constraint(x, pltpu.HBM) for x in (down, up)])


def inner_kernel(scaled_ref, *rest):
    packs, out_ref = rest[:-1], rest[-1]
    me = lax.axis_index("wide")
    width = scaled_ref.shape[1] // len(packs)
    total = []
    for offset, pack in enumerate(packs):
        total.append(
            lax.dot_general(
                scaled_ref[:, pl.ds(pl.multiple_of((me ^ offset) * width, width), width)],
                pack[:, :, :width].reshape(out_ref.shape[1], width),
                (((1,), (1,)), ((), ())),
                preferred_element_type=jnp.float32,
            )
        )
    out_ref[...] = sum(total[1:], total[0])


def inner_call(scaled, packs):
    kinds, share, _ = packs[0].shape
    return pl.pallas_call(
        inner_kernel,
        out_shape=jax.ShapeDtypeStruct((scaled.shape[0], kinds * share), jnp.float32),
        in_specs=[VMEM] * (1 + len(packs)),
        out_specs=VMEM,
        compiler_params=pltpu.CompilerParams(vmem_limit_bytes=8 << 20),
        name="rank_inner",
    )(scaled, *packs)


def scale_kernel(gain_ref, *rest):
    parts = rest[:-2]
    scaled_out, square_out = rest[-2:]
    steps, rows, width = parts[0].shape
    chunks = width // HD
    me = lax.axis_index("tp")
    squares = jnp.zeros(square_out.shape, jnp.float32)
    for offset, part in enumerate(parts):
        block = me ^ offset
        gain = gain_ref[pl.ds(pl.multiple_of(block * chunks, chunks), chunks)]
        values = rows_of(part)
        scaled = []
        for i in range(chunks):
            chunk = values[:, i * HD : (i + 1) * HD]
            squares += chunk * chunk
            scaled.append((chunk * gain[i : i + 1]).astype(jnp.bfloat16))
        at = pl.ds(pl.multiple_of(block * width, width), width)
        scaled_out[:, at] = jnp.concatenate(scaled, axis=1)
    square_out[...] = jnp.broadcast_to(jnp.sum(squares, axis=1, keepdims=True), squares.shape)


def scale_call(gain, parts):
    steps, rows, width = parts[0].shape
    return pl.pallas_call(
        scale_kernel,
        out_shape=(
            pltpu.VMEM((steps * rows, len(parts) * width), jnp.bfloat16),
            pltpu.VMEM((steps * rows, HD), jnp.float32),
        ),
        in_specs=[VMEM] * (1 + len(parts)),
        out_specs=(VMEM,) * 2,
        compiler_params=pltpu.CompilerParams(vmem_limit_bytes=8 << 20),
        name="scale_features",
    )(gain, *parts)


def up_kernel(*refs):
    packs, up_out = refs[:-1], refs[-1]
    kinds, share, pack_width = packs[0].shape
    columns = up_out.shape[1] // kinds
    me = lax.axis_index("wide") if len(packs) > 1 else 0
    up_out[...] = jnp.zeros_like(up_out)
    for offset, pack in enumerate(packs):
        for kind in range(kinds):
            at = pl.multiple_of(((me ^ offset) * kinds + kind) * share, share)
            up_out[pl.ds(at, share), kind * columns : (kind + 1) * columns] = pack[
                kind, :, pack_width - columns :
            ]


def final_kernel(width, blocks, base_ref, square_ref, bias_ref, *rest):
    query_ref, acc_ref, top_ref, total_ref, cos_ref, sin_ref = rest[:6]
    inner_refs = rest[6 : 6 + blocks]
    packs = rest[6 + blocks : 6 + 2 * blocks]
    keys_out, values_out, attended_out, inner_buffer, up_ref = rest[6 + 2 * blocks :]
    up_kernel(*packs, up_ref)
    steps, rows, columns = keys_out.shape
    count = steps * rows
    groups, size, _ = query_ref.shape
    per_group = size // count
    kinds = bias_ref.shape[0]
    row_scale = lax.rsqrt(square_ref[:, :1] * (1.0 / width) + norm_eps)
    me = lax.axis_index("tp") if blocks > 1 else 0
    for i in range(blocks):
        inner_buffer[me ^ i] = inner_refs[i][...]
    inner = jnp.concatenate([inner_buffer[i] for i in range(blocks)], axis=1)
    high = inner.astype(jnp.bfloat16)
    low = (inner - high.astype(jnp.float32)).astype(jnp.bfloat16)
    lora = jnp.dot(
        jnp.concatenate([high, low], axis=0), up_ref[...], preferred_element_type=jnp.float32
    )
    lora = lora[:count] + lora[count:]
    bias = bias_ref[...].astype(jnp.float32)
    linear = []
    for kind in range(kinds):
        base = base_ref[kind]
        part = lora[:, kind * columns : (kind + 1) * columns]
        linear.append((base + adapter_scale * part) * row_scale + bias[kind : kind + 1])
    cosine, sine = cos_ref[...], sin_ref[...]
    line = lax.broadcasted_iota(jnp.int32, (size, count), 0)
    other = lax.broadcasted_iota(jnp.int32, (size, count), 1)
    live = (line % rows == other % rows) & (other // rows <= line // rows % steps)
    for group in range(groups):
        at = slice(group * HD, (group + 1) * HD)
        key = linear[0][:, at]
        key = (key * cosine + pltpu.roll(key, HD // 2, 1) * sine).astype(jnp.bfloat16)
        value = linear[1][:, at].astype(jnp.bfloat16)
        for step in range(steps):
            keys_out[step, :, at] = key[step * rows : (step + 1) * rows]
            values_out[step, :, at] = value[step * rows : (step + 1) * rows]
        scores = lax.dot_general(
            query_ref[group].astype(jnp.bfloat16),
            key,
            (((1,), (1,)), ((), ())),
            preferred_element_type=jnp.float32,
        )
        scores = jnp.where(live, scores * score_scale, masked_score)
        old_top = top_ref[group][:, :1]
        top = jnp.maximum(old_top, jnp.max(scores, axis=1, keepdims=True))
        exps = jnp.exp(scores - top)
        keep = jnp.exp(old_top - top)
        total = total_ref[group][:, :1] * keep + jnp.sum(exps, axis=1, keepdims=True)
        acc = acc_ref[group] * keep + jnp.dot(
            exps.astype(jnp.bfloat16), value, preferred_element_type=jnp.float32
        )
        attended = (acc / total).astype(jnp.bfloat16)
        for head in range(per_group):
            lanes = pl.ds((group * per_group + head) * HD, HD)
            for step in range(steps):
                tile = (head * steps + step) * rows
                attended_out[step, :, lanes] = attended[tile : tile + rows]


def final_call(shape, width, base, square, bias, cached, inner, packs):
    steps, rows, query_width = shape
    kinds, share, _ = packs[0].shape
    columns = base.shape[2]
    small = jax.ShapeDtypeStruct((steps, rows, columns), jnp.bfloat16)
    return pl.pallas_call(
        functools.partial(final_kernel, width, len(inner)),
        out_shape=(small, small, jax.ShapeDtypeStruct(shape, jnp.bfloat16)),
        in_specs=[VMEM] * (3 + len(cached) + len(inner) + len(packs)),
        out_specs=(VMEM,) * 3,
        scratch_shapes=[
            pltpu.VMEM((len(inner),) + inner[0].shape, jnp.float32),
            pltpu.VMEM((len(packs) * kinds * share, kinds * columns), jnp.bfloat16),
        ],
        compiler_params=pltpu.CompilerParams(vmem_limit_bytes=8 << 20),
        name="fresh_attention",
    )(base, square, bias, *cached, *inner, *packs)


def swap(block, axis, offset, count):
    return lax.ppermute(block, axis, [(i, i ^ offset) for i in range(count)])


def on_device(
    wide_count,
    tp_count,
    hidden,
    input_norm_gain,
    key_value_weight,
    key_value_bias,
    adapter_down_factor,
    adapter_up_factor,
    queries,
    stored_rotated_keys,
    stored_value_rows,
    lengths,
):
    steps, rows, part_width = hidden.shape
    width = part_width * tp_count
    kinds, ranks, down_width = adapter_down_factor.shape
    gain = input_norm_gain.reshape(width // HD, HD)
    up_part = jnp.transpose(adapter_up_factor, (0, 2, 1))
    direct = wide_count == tp_count == 4
    beside = swap(hidden, "tp", 1, tp_count)
    crossed = swap(hidden, "tp", 2, tp_count)
    if direct:
        pack = pack_call(adapter_down_factor, up_part)
        packs = [pack] + [swap(pack, "wide", offset, wide_count) for offset in (1, 2, 3)]
    gain_rows, bias, near, *cached = cache_call(
        lengths, queries, stored_rotated_keys, stored_value_rows, gain, key_value_bias, hidden
    )
    relayed, gain_rows = lax.optimization_barrier((crossed, gain_rows))
    relayed = swap(relayed, "tp", 1, tp_count)
    scaled, square = scale_call(gain_rows, (near, beside, crossed, relayed))
    base = jnp.einsum("md,dkc->kmc", scaled, key_value_weight, preferred_element_type=jnp.float32)
    if direct:
        inner = inner_call(scaled, packs)
        inner = [inner] + [swap(inner, "tp", offset, tp_count) for offset in (1, 2, 3)]
    else:
        down = lax.all_gather(adapter_down_factor, "wide", axis=2, tiled=True)
        down = down.reshape(kinds * ranks, width)
        inner = [jnp.einsum("rd,kd->rk", scaled, down, preferred_element_type=jnp.float32)]
        packs = [lax.all_gather(up_part, "wide", axis=1, tiled=True)]
    return final_call(queries.shape, width, base, square, bias, cached, inner, packs)


def solution(mesh):
    in_specs = (
        P(None, ("groups", "wide"), "tp"),
        P(),
        P(None, None, "tp"),
        P(None, "tp"),
        P("groups", None, "wide"),
        P("groups", "tp", "wide"),
        P(None, ("groups", "wide"), "tp"),
        P(("groups", "wide"), None, "tp"),
        P(("groups", "wide"), None, "tp"),
        P(("groups", "wide")),
    )
    out_specs = (
        P(None, ("groups", "wide"), "tp"),
        P(None, ("groups", "wide"), "tp"),
        P(None, ("groups", "wide"), "tp"),
    )
    body = functools.partial(on_device, mesh.shape["wide"], mesh.shape["tp"])
    return jax.shard_map(
        body, mesh=mesh, in_specs=in_specs, out_specs=out_specs, check_vma=False
    )
```

```python
import functools
import math

import jax
import jax.numpy as jnp
from jax import lax
from jax.experimental import pallas as pl
from jax.experimental.pallas import tpu as pltpu
from jax.sharding import PartitionSpec as P

HD = 128


norm_eps = 1e-06
adapter_scale = 2.0
rope_base = 1000000.0
masked_score = -1e30
score_scale = 1.0 / math.sqrt(HD)

VMEM = pl.BlockSpec(memory_space=pltpu.VMEM)
HBM = pl.BlockSpec(memory_space=pltpu.HBM)


def query_block(query_ref, group, per_group):
    steps = query_ref.shape[0]
    tiles = []
    for head in range(per_group):
        at = (group * per_group + head) * HD
        for step in range(steps):
            tiles.append(query_ref[step, :, at : at + HD].astype(jnp.float32))
    return jnp.concatenate(tiles, axis=0)


def cache_kernel(
    near,
    far,
    lengths_ref,
    query_ref,
    key_ref,
    value_ref,
    gain_ref,
    bias_ref,
    hidden_ref,
    weight_ref,
    near_out,
    far_out,
    gain_out,
    bias_out,
    hidden_out,
    query_out,
    acc_out,
    top_out,
    total_out,
    cos_out,
    sin_out,
    lengths,
    queries,
    gain_buffer,
    key_buffer,
    value_buffer,
    score_buffer,
    sems,
):
    steps, rows, query_width = query_ref.shape
    cache_span = key_ref.shape[1]
    groups = key_ref.shape[2] // HD
    per_group = query_width // HD // groups
    lines = steps * per_group
    half_rows = rows // 2
    halves = [pl.ds(0, half_rows), pl.ds(half_rows, half_rows)]
    copies = [
        (lengths_ref, lengths),
        (query_ref, queries),
        (key_ref.at[halves[0]], key_buffer.at[halves[0]]),
        (key_ref.at[halves[1]], key_buffer.at[halves[1]]),
        (value_ref.at[halves[0]], value_buffer.at[halves[0]]),
        (value_ref.at[halves[1]], value_buffer.at[halves[1]]),
        (gain_ref, gain_buffer),
        (bias_ref, bias_out),
        (hidden_ref, hidden_out),
    ]
    me = lax.axis_index("tp")
    width = hidden_ref.shape[2]
    for offsets, out in ((near, near_out), (far, far_out)):
        for i, offset in enumerate(offsets):
            block = pl.ds(pl.multiple_of((me ^ offset) * width, width), width)
            copies.append((weight_ref.at[block], out.at[pl.ds(i * width, width)]))
    copies = [pltpu.make_async_copy(*pair, sems.at[i]) for i, pair in enumerate(copies)]
    for copy in copies:
        copy.start()

    copies[0].wait()
    lane = lax.broadcasted_iota(jnp.int32, (rows, HD), 1)
    half = HD // 2
    second = lane >= half
    index = jnp.where(second, lane - half, lane).astype(jnp.float32)
    inv_freq = jnp.exp(index * (-2.0 * math.log(rope_base) / HD))
    row_index = lax.broadcasted_iota(jnp.int32, (rows, HD), 0)
    row_lengths = jnp.zeros((rows, HD), jnp.int32)
    for row in range(rows):
        row_lengths = jnp.where(row_index == row, lengths[row], row_lengths)
    for step in range(steps):
        angles = (row_lengths + step).astype(jnp.float32) * inv_freq
        sine = jnp.sin(angles)
        cos_out[pl.ds(step * rows, rows)] = jnp.cos(angles)
        sin_out[pl.ds(step * rows, rows)] = jnp.where(second, sine, -sine)
    copies[1].wait()
    for group in range(groups):
        query_out[group] = query_block(queries, group, per_group)

    place = lax.broadcasted_iota(jnp.int32, (lines, cache_span), 1)
    for i in range(2):
        copies[2 + i].wait()
        for row in range(i * half_rows, (i + 1) * half_rows):
            for group in range(groups):
                query = query_out[group, pl.ds(row, lines, stride=rows), :].astype(jnp.bfloat16)
                score_buffer[row * groups + group] = lax.dot_general(
                    query,
                    key_buffer[row, :, pl.ds(group * HD, HD)],
                    (((1,), (1,)), ((), ())),
                    preferred_element_type=jnp.float32,
                )
    for i in range(2):
        copies[4 + i].wait()
        for row in range(i * half_rows, (i + 1) * half_rows):
            live = place < lengths[row]
            for group in range(groups):
                mine = pl.ds(row, lines, stride=rows)
                scores = score_buffer[row * groups + group]
                scores = jnp.where(live, scores * score_scale, masked_score)
                top = jnp.max(scores, axis=1, keepdims=True)
                exps = jnp.exp(scores - top)
                total = jnp.sum(exps, axis=1, keepdims=True)
                acc = jnp.dot(
                    exps.astype(jnp.bfloat16),
                    value_buffer[row, :, pl.ds(group * HD, HD)],
                    preferred_element_type=jnp.float32,
                )
                acc_out[group, mine, :] = acc
                top_out[group, mine, :] = jnp.broadcast_to(top, acc.shape)
                total_out[group, mine, :] = jnp.broadcast_to(total, acc.shape)
    copies[6].wait()
    gain_out[...] = gain_buffer[...].astype(jnp.float32)
    for copy in copies[7:]:
        copy.wait()


def cache_call(near, far, lengths, queries, keys, values, gain, bias, hidden, weight):
    steps, rows, query_width = queries.shape
    cache_span, key_width = keys.shape[1:]
    groups = key_width // HD
    lines = steps * (query_width // key_width)
    block = (groups, lines * rows, HD)
    table = (steps * rows, HD)
    operands = (lengths, queries, keys, values, gain, bias, hidden, weight)
    part = hidden.shape[2]
    return pl.pallas_call(
        functools.partial(cache_kernel, near, far),
        out_shape=(
            pltpu.VMEM((len(near) * part,) + weight.shape[1:], weight.dtype),
            pltpu.VMEM((len(far) * part,) + weight.shape[1:], weight.dtype),
            pltpu.VMEM(gain.shape, jnp.float32),
            pltpu.VMEM(bias.shape, bias.dtype),
            pltpu.VMEM(hidden.shape, hidden.dtype),
            pltpu.VMEM(block, jnp.float32),
            pltpu.VMEM(block, jnp.float32),
            pltpu.VMEM(block, jnp.float32),
            pltpu.VMEM(block, jnp.float32),
            pltpu.VMEM(table, jnp.float32),
            pltpu.VMEM(table, jnp.float32),
        ),
        in_specs=[HBM] * len(operands),
        out_specs=(VMEM,) * 11,
        scratch_shapes=[
            pltpu.SMEM(lengths.shape, jnp.int32),
            pltpu.VMEM(queries.shape, queries.dtype),
            pltpu.VMEM(gain.shape, gain.dtype),
            pltpu.VMEM(keys.shape, keys.dtype),
            pltpu.VMEM(values.shape, values.dtype),
            pltpu.VMEM((rows * groups, lines, cache_span), jnp.float32),
            pltpu.SemaphoreType.DMA((9 + len(near) + len(far),)),
        ],
        compiler_params=pltpu.CompilerParams(vmem_limit_bytes=16 << 20),
        cost_estimate=pl.CostEstimate(flops=2 * 67 << 20, bytes_accessed=13 << 20, transcendentals=0),
        name="cache_attention",
    )(*[pltpu.with_memory_space_constraint(x, pltpu.HBM) for x in operands])


def rows_of(ref):
    return jnp.concatenate([ref[s].astype(jnp.float32) for s in range(ref.shape[0])], axis=0)


def pack_kernel(down_ref, up_ref, out_ref, sems):
    share = out_ref.shape[1]
    width = down_ref.shape[2]
    at = pl.ds(pl.multiple_of(lax.axis_index("tp") * share, share), share)
    down = pltpu.make_async_copy(
        down_ref.at[:, at, :], out_ref.at[:, :, pl.ds(0, width)], sems.at[0]
    )
    up = pltpu.make_async_copy(
        up_ref, out_ref.at[:, :, pl.ds(width, up_ref.shape[2])], sems.at[1]
    )
    down.start()
    up.start()
    down.wait()
    up.wait()


def pack_call(down, up):
    kinds, share, columns = up.shape
    return pl.pallas_call(
        pack_kernel,
        out_shape=pltpu.VMEM((kinds, share, down.shape[2] + columns), down.dtype),
        in_specs=[HBM] * 2,
        out_specs=VMEM,
        scratch_shapes=[pltpu.SemaphoreType.DMA((2,))],
        name="pack_factors",
    )(*[pltpu.with_memory_space_constraint(x, pltpu.HBM) for x in (down, up)])


def inner_kernel(scaled_ref, *rest):
    packs, out_ref = rest[:-1], rest[-1]
    me = lax.axis_index("wide")
    width = scaled_ref.shape[1] // len(packs)
    total = []
    for offset, pack in enumerate(packs):
        total.append(
            lax.dot_general(
                scaled_ref[:, pl.ds(pl.multiple_of((me ^ offset) * width, width), width)],
                pack[:, :, :width].reshape(out_ref.shape[1], width),
                (((1,), (1,)), ((), ())),
                preferred_element_type=jnp.float32,
            )
        )
    out_ref[...] = sum(total[1:], total[0])


def inner_call(scaled, packs):
    kinds, share, _ = packs[0].shape
    return pl.pallas_call(
        inner_kernel,
        out_shape=jax.ShapeDtypeStruct((scaled.shape[0], kinds * share), jnp.float32),
        in_specs=[VMEM] * (1 + len(packs)),
        out_specs=VMEM,
        compiler_params=pltpu.CompilerParams(vmem_limit_bytes=8 << 20),
        name="rank_inner",
    )(scaled, *packs)


def scale_kernel(near_count, gain_ref, *rest):
    parts = rest[:-4]
    scaled_out, near_out, far_out, square_out = rest[-4:]
    steps, rows, width = parts[0].shape
    chunks = width // HD
    me = lax.axis_index("tp")
    squares = jnp.zeros(square_out.shape, jnp.float32)
    for offset, part in enumerate(parts):
        block = me ^ offset
        gain = gain_ref[pl.ds(pl.multiple_of(block * chunks, chunks), chunks)]
        values = rows_of(part)
        scaled = []
        for i in range(chunks):
            chunk = values[:, i * HD : (i + 1) * HD]
            squares += chunk * chunk
            scaled.append((chunk * gain[i : i + 1]).astype(jnp.bfloat16))
        at = pl.ds(pl.multiple_of(block * width, width), width)
        scaled = jnp.concatenate(scaled, axis=1)
        scaled_out[:, at] = scaled
        out, i = (near_out, offset) if offset < near_count else (far_out, offset - near_count)
        out[:, i * width : (i + 1) * width] = scaled
    square_out[...] = jnp.broadcast_to(jnp.sum(squares, axis=1, keepdims=True), squares.shape)


def scale_call(near_count, gain, parts):
    steps, rows, width = parts[0].shape
    return pl.pallas_call(
        functools.partial(scale_kernel, near_count),
        out_shape=(
            pltpu.VMEM((steps * rows, len(parts) * width), jnp.bfloat16),
            pltpu.VMEM((steps * rows, near_count * width), jnp.bfloat16),
            pltpu.VMEM((steps * rows, (len(parts) - near_count) * width), jnp.bfloat16),
            pltpu.VMEM((steps * rows, HD), jnp.float32),
        ),
        in_specs=[VMEM] * (1 + len(parts)),
        out_specs=(VMEM,) * 4,
        compiler_params=pltpu.CompilerParams(vmem_limit_bytes=8 << 20),
        name="scale_features",
    )(gain, *parts)


def up_kernel(*refs):
    packs, up_out = refs[:-1], refs[-1]
    kinds, share, pack_width = packs[0].shape
    columns = up_out.shape[1] // kinds
    me = lax.axis_index("wide") if len(packs) > 1 else 0
    up_out[...] = jnp.zeros_like(up_out)
    for offset, pack in enumerate(packs):
        for kind in range(kinds):
            at = pl.multiple_of(((me ^ offset) * kinds + kind) * share, share)
            up_out[pl.ds(at, share), kind * columns : (kind + 1) * columns] = pack[
                kind, :, pack_width - columns :
            ]


def final_kernel(width, blocks, near_ref, far_ref, square_ref, bias_ref, *rest):
    query_ref, acc_ref, top_ref, total_ref, cos_ref, sin_ref = rest[:6]
    inner_refs = rest[6 : 6 + blocks]
    packs = rest[6 + blocks : 6 + 2 * blocks]
    keys_out, values_out, attended_out, inner_buffer, up_ref = rest[6 + 2 * blocks :]
    up_kernel(*packs, up_ref)
    steps, rows, columns = keys_out.shape
    count = steps * rows
    groups, size, _ = query_ref.shape
    per_group = size // count
    kinds = bias_ref.shape[0]
    row_scale = lax.rsqrt(square_ref[:, :1] * (1.0 / width) + norm_eps)
    me = lax.axis_index("tp") if blocks > 1 else 0
    for i in range(blocks):
        inner_buffer[me ^ i] = inner_refs[i][...]
    inner = jnp.concatenate([inner_buffer[i] for i in range(blocks)], axis=1)
    high = inner.astype(jnp.bfloat16)
    low = (inner - high.astype(jnp.float32)).astype(jnp.bfloat16)
    lora = jnp.dot(
        jnp.concatenate([high, low], axis=0), up_ref[...], preferred_element_type=jnp.float32
    )
    lora = lora[:count] + lora[count:]
    bias = bias_ref[...].astype(jnp.float32)
    linear = []
    for kind in range(kinds):
        base = near_ref[kind] + far_ref[kind]
        part = lora[:, kind * columns : (kind + 1) * columns]
        linear.append((base + adapter_scale * part) * row_scale + bias[kind : kind + 1])
    cosine, sine = cos_ref[...], sin_ref[...]
    line = lax.broadcasted_iota(jnp.int32, (size, count), 0)
    other = lax.broadcasted_iota(jnp.int32, (size, count), 1)
    live = (line % rows == other % rows) & (other // rows <= line // rows % steps)
    for group in range(groups):
        at = slice(group * HD, (group + 1) * HD)
        key = linear[0][:, at]
        key = (key * cosine + pltpu.roll(key, HD // 2, 1) * sine).astype(jnp.bfloat16)
        value = linear[1][:, at].astype(jnp.bfloat16)
        for step in range(steps):
            keys_out[step, :, at] = key[step * rows : (step + 1) * rows]
            values_out[step, :, at] = value[step * rows : (step + 1) * rows]
        scores = lax.dot_general(
            query_ref[group].astype(jnp.bfloat16),
            key,
            (((1,), (1,)), ((), ())),
            preferred_element_type=jnp.float32,
        )
        scores = jnp.where(live, scores * score_scale, masked_score)
        old_top = top_ref[group][:, :1]
        top = jnp.maximum(old_top, jnp.max(scores, axis=1, keepdims=True))
        exps = jnp.exp(scores - top)
        keep = jnp.exp(old_top - top)
        total = total_ref[group][:, :1] * keep + jnp.sum(exps, axis=1, keepdims=True)
        acc = acc_ref[group] * keep + jnp.dot(
            exps.astype(jnp.bfloat16), value, preferred_element_type=jnp.float32
        )
        attended = (acc / total).astype(jnp.bfloat16)
        for head in range(per_group):
            lanes = pl.ds((group * per_group + head) * HD, HD)
            for step in range(steps):
                tile = (head * steps + step) * rows
                attended_out[step, :, lanes] = attended[tile : tile + rows]


def final_call(shape, width, near, far, square, bias, cached, inner, packs):
    steps, rows, query_width = shape
    kinds, share, _ = packs[0].shape
    columns = near.shape[2]
    small = jax.ShapeDtypeStruct((steps, rows, columns), jnp.bfloat16)
    return pl.pallas_call(
        functools.partial(final_kernel, width, len(inner)),
        out_shape=(small, small, jax.ShapeDtypeStruct(shape, jnp.bfloat16)),
        in_specs=[VMEM] * (4 + len(cached) + len(inner) + len(packs)),
        out_specs=(VMEM,) * 3,
        scratch_shapes=[
            pltpu.VMEM((len(inner),) + inner[0].shape, jnp.float32),
            pltpu.VMEM((len(packs) * kinds * share, kinds * columns), jnp.bfloat16),
        ],
        compiler_params=pltpu.CompilerParams(vmem_limit_bytes=8 << 20),
        name="fresh_attention",
    )(near, far, square, bias, *cached, *inner, *packs)


def swap(block, axis, offset, count):
    return lax.ppermute(block, axis, [(i, i ^ offset) for i in range(count)])


def on_device(
    wide_count,
    tp_count,
    hidden,
    input_norm_gain,
    key_value_weight,
    key_value_bias,
    adapter_down_factor,
    adapter_up_factor,
    queries,
    stored_rotated_keys,
    stored_value_rows,
    lengths,
):
    steps, rows, part_width = hidden.shape
    width = part_width * tp_count
    kinds, ranks, down_width = adapter_down_factor.shape
    gain = input_norm_gain.reshape(width // HD, HD)
    up_part = jnp.transpose(adapter_up_factor, (0, 2, 1))
    direct = wide_count == tp_count == 4
    beside = swap(hidden, "tp", 1, tp_count)
    crossed = swap(hidden, "tp", 2, tp_count)
    if direct:
        pack = pack_call(adapter_down_factor, up_part)
        second = swap(pack, "wide", 2, wide_count)
        first = swap(pack, "wide", 1, wide_count)
    near, far = (0, 1), (2, 3)
    near_weight, far_weight, gain_rows, bias, mine, *cached = cache_call(
        near,
        far,
        lengths,
        queries,
        stored_rotated_keys,
        stored_value_rows,
        gain,
        key_value_bias,
        hidden,
        key_value_weight,
    )
    relayed, gain_rows = lax.optimization_barrier((crossed, gain_rows))
    relayed = swap(relayed, "tp", 1, tp_count)
    if direct:
        third, gain_rows = lax.optimization_barrier((second, gain_rows))
        relayed, first = lax.optimization_barrier((relayed, first))
        packs = [pack, first, second, swap(third, "wide", 1, wide_count)]
    scaled, near_scaled, far_scaled, square = scale_call(
        len(near), gain_rows, (mine, beside, crossed, relayed)
    )
    if direct:
        inner = inner_call(scaled, packs)
        inner, far_scaled = lax.optimization_barrier((inner, far_scaled))
        inner = [inner] + [swap(inner, "tp", offset, tp_count) for offset in (1, 2, 3)]
    else:
        down = lax.all_gather(adapter_down_factor, "wide", axis=2, tiled=True)
        down = down.reshape(kinds * ranks, width)
        inner = [jnp.einsum("rd,kd->rk", scaled, down, preferred_element_type=jnp.float32)]
        packs = [lax.all_gather(up_part, "wide", axis=1, tiled=True)]
    near_base, far_base = [
        jnp.einsum("md,dkc->kmc", x, y, preferred_element_type=jnp.float32)
        for x, y in ((near_scaled, near_weight), (far_scaled, far_weight))
    ]
    return final_call(
        queries.shape, width, near_base, far_base, square, bias, cached, inner, packs
    )


def solution(mesh):
    in_specs = (
        P(None, ("groups", "wide"), "tp"),
        P(),
        P(None, None, "tp"),
        P(None, "tp"),
        P("groups", None, "wide"),
        P("groups", "tp", "wide"),
        P(None, ("groups", "wide"), "tp"),
        P(("groups", "wide"), None, "tp"),
        P(("groups", "wide"), None, "tp"),
        P(("groups", "wide")),
    )
    out_specs = (
        P(None, ("groups", "wide"), "tp"),
        P(None, ("groups", "wide"), "tp"),
        P(None, ("groups", "wide"), "tp"),
    )
    body = functools.partial(on_device, mesh.shape["wide"], mesh.shape["tp"])
    return jax.shard_map(
        body, mesh=mesh, in_specs=in_specs, out_specs=out_specs, check_vma=False
    )
```

```python
import functools
import math

import jax
import jax.numpy as jnp
from jax import lax
from jax.experimental import pallas as pl
from jax.experimental.pallas import tpu as pltpu
from jax.sharding import PartitionSpec as P

HD = 128


norm_eps = 1e-06
adapter_scale = 2.0
rope_base = 1000000.0
masked_score = -1e30
score_scale = 1.0 / math.sqrt(HD)

VMEM = pl.BlockSpec(memory_space=pltpu.VMEM)
HBM = pl.BlockSpec(memory_space=pltpu.HBM)


def query_block(query_ref, group, per_group):
    steps = query_ref.shape[0]
    tiles = []
    for head in range(per_group):
        at = (group * per_group + head) * HD
        for step in range(steps):
            tiles.append(query_ref[step, :, at : at + HD].astype(jnp.float32))
    return jnp.concatenate(tiles, axis=0)


def cache_kernel(
    near,
    far,
    lengths_ref,
    query_ref,
    key_ref,
    value_ref,
    gain_ref,
    bias_ref,
    hidden_ref,
    weight_ref,
    near_out,
    far_out,
    gain_out,
    bias_out,
    hidden_out,
    query_out,
    acc_out,
    top_out,
    total_out,
    cos_out,
    sin_out,
    lengths,
    queries,
    gain_buffer,
    key_buffer,
    value_buffer,
    score_buffer,
    sems,
):
    steps, rows, query_width = query_ref.shape
    cache_span = key_ref.shape[1]
    groups = key_ref.shape[2] // HD
    per_group = query_width // HD // groups
    lines = steps * per_group
    half_rows = rows // 2
    halves = [pl.ds(0, half_rows), pl.ds(half_rows, half_rows)]
    copies = [
        (lengths_ref, lengths),
        (query_ref, queries),
        (key_ref.at[halves[0]], key_buffer.at[halves[0]]),
        (key_ref.at[halves[1]], key_buffer.at[halves[1]]),
        (value_ref.at[halves[0]], value_buffer.at[halves[0]]),
        (value_ref.at[halves[1]], value_buffer.at[halves[1]]),
        (gain_ref, gain_buffer),
        (bias_ref, bias_out),
        (hidden_ref, hidden_out),
    ]
    me = lax.axis_index("tp")
    width = hidden_ref.shape[2]
    for offsets, out in ((near, near_out), (far, far_out)):
        for i, offset in enumerate(offsets):
            block = pl.ds(pl.multiple_of((me ^ offset) * width, width), width)
            copies.append((weight_ref.at[block], out.at[pl.ds(i * width, width)]))
    copies = [pltpu.make_async_copy(*pair, sems.at[i]) for i, pair in enumerate(copies)]
    for copy in copies:
        copy.start()

    copies[0].wait()
    lane = lax.broadcasted_iota(jnp.int32, (rows, HD), 1)
    half = HD // 2
    second = lane >= half
    index = jnp.where(second, lane - half, lane).astype(jnp.float32)
    inv_freq = jnp.exp(index * (-2.0 * math.log(rope_base) / HD))
    row_index = lax.broadcasted_iota(jnp.int32, (rows, HD), 0)
    row_lengths = jnp.zeros((rows, HD), jnp.int32)
    for row in range(rows):
        row_lengths = jnp.where(row_index == row, lengths[row], row_lengths)
    for step in range(steps):
        angles = (row_lengths + step).astype(jnp.float32) * inv_freq
        sine = jnp.sin(angles)
        cos_out[pl.ds(step * rows, rows)] = jnp.cos(angles)
        sin_out[pl.ds(step * rows, rows)] = jnp.where(second, sine, -sine)
    copies[1].wait()
    for group in range(groups):
        query_out[group] = query_block(queries, group, per_group)

    place = lax.broadcasted_iota(jnp.int32, (lines, cache_span), 1)
    for i in range(2):
        copies[2 + i].wait()
        for row in range(i * half_rows, (i + 1) * half_rows):
            for group in range(groups):
                query = query_out[group, pl.ds(row, lines, stride=rows), :].astype(jnp.bfloat16)
                score_buffer[row * groups + group] = lax.dot_general(
                    query,
                    key_buffer[row, :, pl.ds(group * HD, HD)],
                    (((1,), (1,)), ((), ())),
                    preferred_element_type=jnp.float32,
                )
    for i in range(2):
        copies[4 + i].wait()
        for row in range(i * half_rows, (i + 1) * half_rows):
            live = place < lengths[row]
            for group in range(groups):
                mine = pl.ds(row, lines, stride=rows)
                scores = score_buffer[row * groups + group]
                scores = jnp.where(live, scores * score_scale, masked_score)
                top = jnp.max(scores, axis=1, keepdims=True)
                exps = jnp.exp(scores - top)
                total = jnp.sum(exps, axis=1, keepdims=True)
                acc = jnp.dot(
                    exps.astype(jnp.bfloat16),
                    value_buffer[row, :, pl.ds(group * HD, HD)],
                    preferred_element_type=jnp.float32,
                )
                acc_out[group, mine, :] = acc
                top_out[group, mine, :] = jnp.broadcast_to(top, acc.shape)
                total_out[group, mine, :] = jnp.broadcast_to(total, acc.shape)
    copies[6].wait()
    gain_out[...] = gain_buffer[...].astype(jnp.float32)
    for copy in copies[7:]:
        copy.wait()


def cache_call(near, far, lengths, queries, keys, values, gain, bias, hidden, weight):
    steps, rows, query_width = queries.shape
    cache_span, key_width = keys.shape[1:]
    groups = key_width // HD
    lines = steps * (query_width // key_width)
    block = (groups, lines * rows, HD)
    table = (steps * rows, HD)
    operands = (lengths, queries, keys, values, gain, bias, hidden, weight)
    part = hidden.shape[2]
    return pl.pallas_call(
        functools.partial(cache_kernel, near, far),
        out_shape=(
            pltpu.VMEM((len(near) * part,) + weight.shape[1:], weight.dtype),
            pltpu.VMEM((len(far) * part,) + weight.shape[1:], weight.dtype),
            pltpu.VMEM(gain.shape, jnp.float32),
            pltpu.VMEM(bias.shape, bias.dtype),
            pltpu.VMEM(hidden.shape, hidden.dtype),
            pltpu.VMEM(block, jnp.float32),
            pltpu.VMEM(block, jnp.float32),
            pltpu.VMEM(block, jnp.float32),
            pltpu.VMEM(block, jnp.float32),
            pltpu.VMEM(table, jnp.float32),
            pltpu.VMEM(table, jnp.float32),
        ),
        in_specs=[HBM] * len(operands),
        out_specs=(VMEM,) * 11,
        scratch_shapes=[
            pltpu.SMEM(lengths.shape, jnp.int32),
            pltpu.VMEM(queries.shape, queries.dtype),
            pltpu.VMEM(gain.shape, gain.dtype),
            pltpu.VMEM(keys.shape, keys.dtype),
            pltpu.VMEM(values.shape, values.dtype),
            pltpu.VMEM((rows * groups, lines, cache_span), jnp.float32),
            pltpu.SemaphoreType.DMA((9 + len(near) + len(far),)),
        ],
        compiler_params=pltpu.CompilerParams(vmem_limit_bytes=16 << 20),
        cost_estimate=pl.CostEstimate(flops=2 * 67 << 20, bytes_accessed=13 << 20, transcendentals=0),
        name="cache_attention",
    )(*[pltpu.with_memory_space_constraint(x, pltpu.HBM) for x in operands])


def rows_of(ref):
    return jnp.concatenate([ref[s].astype(jnp.float32) for s in range(ref.shape[0])], axis=0)


def pack_kernel(down_ref, up_ref, out_ref, sems):
    share = out_ref.shape[1]
    width = down_ref.shape[2]
    at = pl.ds(pl.multiple_of(lax.axis_index("tp") * share, share), share)
    down = pltpu.make_async_copy(
        down_ref.at[:, at, :], out_ref.at[:, :, pl.ds(0, width)], sems.at[0]
    )
    up = pltpu.make_async_copy(
        up_ref, out_ref.at[:, :, pl.ds(width, up_ref.shape[2])], sems.at[1]
    )
    down.start()
    up.start()
    down.wait()
    up.wait()


def pack_call(down, up):
    kinds, share, columns = up.shape
    return pl.pallas_call(
        pack_kernel,
        out_shape=pltpu.VMEM((kinds, share, down.shape[2] + columns), down.dtype),
        in_specs=[HBM] * 2,
        out_specs=VMEM,
        scratch_shapes=[pltpu.SemaphoreType.DMA((2,))],
        name="pack_factors",
    )(*[pltpu.with_memory_space_constraint(x, pltpu.HBM) for x in (down, up)])


def inner_kernel(scaled_ref, *rest):
    packs, out_ref = rest[:-1], rest[-1]
    me = lax.axis_index("wide")
    width = scaled_ref.shape[1] // len(packs)
    total = []
    for offset, pack in enumerate(packs):
        total.append(
            lax.dot_general(
                scaled_ref[:, pl.ds(pl.multiple_of((me ^ offset) * width, width), width)],
                pack[:, :, :width].reshape(out_ref.shape[2], width),
                (((1,), (1,)), ((), ())),
                preferred_element_type=jnp.float32,
            )
        )
    total = sum(total[1:], total[0])
    for i in range(out_ref.shape[0]):
        out_ref[i] = total


def inner_call(scaled, packs):
    kinds, share, _ = packs[0].shape
    return pl.pallas_call(
        inner_kernel,
        out_shape=jax.ShapeDtypeStruct((len(packs), scaled.shape[0], kinds * share), jnp.float32),
        in_specs=[VMEM] * (1 + len(packs)),
        out_specs=VMEM,
        compiler_params=pltpu.CompilerParams(vmem_limit_bytes=8 << 20),
        name="rank_inner",
    )(scaled, *packs)


def scale_kernel(near_count, gain_ref, *rest):
    parts = rest[:-4]
    scaled_out, near_out, far_out, square_out = rest[-4:]
    steps, rows, width = parts[0].shape
    chunks = width // HD
    me = lax.axis_index("tp")
    squares = jnp.zeros(square_out.shape, jnp.float32)
    for offset, part in enumerate(parts):
        block = me ^ offset
        gain = gain_ref[pl.ds(pl.multiple_of(block * chunks, chunks), chunks)]
        values = rows_of(part)
        scaled = []
        for i in range(chunks):
            chunk = values[:, i * HD : (i + 1) * HD]
            squares += chunk * chunk
            scaled.append((chunk * gain[i : i + 1]).astype(jnp.bfloat16))
        at = pl.ds(pl.multiple_of(block * width, width), width)
        scaled = jnp.concatenate(scaled, axis=1)
        scaled_out[:, at] = scaled
        out, i = (near_out, offset) if offset < near_count else (far_out, offset - near_count)
        out[:, i * width : (i + 1) * width] = scaled
    square_out[...] = jnp.broadcast_to(jnp.sum(squares, axis=1, keepdims=True), squares.shape)


def scale_call(near_count, gain, parts):
    steps, rows, width = parts[0].shape
    return pl.pallas_call(
        functools.partial(scale_kernel, near_count),
        out_shape=(
            pltpu.VMEM((steps * rows, len(parts) * width), jnp.bfloat16),
            pltpu.VMEM((steps * rows, near_count * width), jnp.bfloat16),
            pltpu.VMEM((steps * rows, (len(parts) - near_count) * width), jnp.bfloat16),
            pltpu.VMEM((steps * rows, HD), jnp.float32),
        ),
        in_specs=[VMEM] * (1 + len(parts)),
        out_specs=(VMEM,) * 4,
        compiler_params=pltpu.CompilerParams(vmem_limit_bytes=8 << 20),
        name="scale_features",
    )(gain, *parts)


def up_kernel(*refs):
    packs, up_out = refs[:-1], refs[-1]
    kinds, share, pack_width = packs[0].shape
    columns = up_out.shape[1] // kinds
    me = lax.axis_index("wide") if len(packs) > 1 else 0
    up_out[...] = jnp.zeros_like(up_out)
    for offset, pack in enumerate(packs):
        for kind in range(kinds):
            at = pl.multiple_of(((me ^ offset) * kinds + kind) * share, share)
            up_out[pl.ds(at, share), kind * columns : (kind + 1) * columns] = pack[
                kind, :, pack_width - columns :
            ]


def final_kernel(width, blocks, near_ref, far_ref, square_ref, bias_ref, *rest):
    query_ref, acc_ref, top_ref, total_ref, cos_ref, sin_ref = rest[:6]
    inner_ref = rest[6]
    packs = rest[7 : 7 + blocks]
    keys_out, values_out, attended_out, up_ref = rest[7 + blocks :]
    up_kernel(*packs, up_ref)
    steps, rows, columns = keys_out.shape
    count = steps * rows
    groups, size, _ = query_ref.shape
    per_group = size // count
    kinds = bias_ref.shape[0]
    row_scale = lax.rsqrt(square_ref[:, :1] * (1.0 / width) + norm_eps)
    inner = jnp.concatenate([inner_ref[i] for i in range(blocks)], axis=1)
    high = inner.astype(jnp.bfloat16)
    low = (inner - high.astype(jnp.float32)).astype(jnp.bfloat16)
    lora = jnp.dot(
        jnp.concatenate([high, low], axis=0), up_ref[...], preferred_element_type=jnp.float32
    )
    lora = lora[:count] + lora[count:]
    bias = bias_ref[...].astype(jnp.float32)
    linear = []
    for kind in range(kinds):
        base = near_ref[kind] + far_ref[kind]
        part = lora[:, kind * columns : (kind + 1) * columns]
        linear.append((base + adapter_scale * part) * row_scale + bias[kind : kind + 1])
    cosine, sine = cos_ref[...], sin_ref[...]
    line = lax.broadcasted_iota(jnp.int32, (size, count), 0)
    other = lax.broadcasted_iota(jnp.int32, (size, count), 1)
    live = (line % rows == other % rows) & (other // rows <= line // rows % steps)
    for group in range(groups):
        at = slice(group * HD, (group + 1) * HD)
        key = linear[0][:, at]
        key = (key * cosine + pltpu.roll(key, HD // 2, 1) * sine).astype(jnp.bfloat16)
        value = linear[1][:, at].astype(jnp.bfloat16)
        for step in range(steps):
            keys_out[step, :, at] = key[step * rows : (step + 1) * rows]
            values_out[step, :, at] = value[step * rows : (step + 1) * rows]
        scores = lax.dot_general(
            query_ref[group].astype(jnp.bfloat16),
            key,
            (((1,), (1,)), ((), ())),
            preferred_element_type=jnp.float32,
        )
        scores = jnp.where(live, scores * score_scale, masked_score)
        old_top = top_ref[group][:, :1]
        top = jnp.maximum(old_top, jnp.max(scores, axis=1, keepdims=True))
        exps = jnp.exp(scores - top)
        keep = jnp.exp(old_top - top)
        total = total_ref[group][:, :1] * keep + jnp.sum(exps, axis=1, keepdims=True)
        acc = acc_ref[group] * keep + jnp.dot(
            exps.astype(jnp.bfloat16), value, preferred_element_type=jnp.float32
        )
        attended = (acc / total).astype(jnp.bfloat16)
        for head in range(per_group):
            lanes = pl.ds((group * per_group + head) * HD, HD)
            for step in range(steps):
                tile = (head * steps + step) * rows
                attended_out[step, :, lanes] = attended[tile : tile + rows]


def final_call(shape, width, near, far, square, bias, cached, inner, packs):
    steps, rows, query_width = shape
    kinds, share, _ = packs[0].shape
    columns = near.shape[2]
    small = jax.ShapeDtypeStruct((steps, rows, columns), jnp.bfloat16)
    return pl.pallas_call(
        functools.partial(final_kernel, width, len(packs)),
        out_shape=(small, small, jax.ShapeDtypeStruct(shape, jnp.bfloat16)),
        in_specs=[VMEM] * (5 + len(cached) + len(packs)),
        out_specs=(VMEM,) * 3,
        scratch_shapes=[
            pltpu.VMEM((len(packs) * kinds * share, kinds * columns), jnp.bfloat16),
        ],
        compiler_params=pltpu.CompilerParams(vmem_limit_bytes=8 << 20),
        name="fresh_attention",
    )(near, far, square, bias, *cached, inner, *packs)


def swap(block, axis, offset, count):
    return lax.ppermute(block, axis, [(i, i ^ offset) for i in range(count)])


def on_device(
    wide_count,
    tp_count,
    hidden,
    input_norm_gain,
    key_value_weight,
    key_value_bias,
    adapter_down_factor,
    adapter_up_factor,
    queries,
    stored_rotated_keys,
    stored_value_rows,
    lengths,
):
    steps, rows, part_width = hidden.shape
    width = part_width * tp_count
    kinds, ranks, down_width = adapter_down_factor.shape
    gain = input_norm_gain.reshape(width // HD, HD)
    up_part = jnp.transpose(adapter_up_factor, (0, 2, 1))
    direct = wide_count == tp_count == 4
    beside = swap(hidden, "tp", 1, tp_count)
    crossed = swap(hidden, "tp", 2, tp_count)
    across = swap(hidden, "tp", 3, tp_count)
    if direct:
        pack = pack_call(adapter_down_factor, up_part)
        second = swap(pack, "wide", 2, wide_count)
        first = swap(pack, "wide", 1, wide_count)
    near, far = (0, 1), (2, 3)
    near_weight, far_weight, gain_rows, bias, mine, *cached = cache_call(
        near,
        far,
        lengths,
        queries,
        stored_rotated_keys,
        stored_value_rows,
        gain,
        key_value_bias,
        hidden,
        key_value_weight,
    )
    if direct:
        third, gain_rows = lax.optimization_barrier((second, gain_rows))
        across, first = lax.optimization_barrier((across, first))
        packs = [pack, first, second, swap(third, "wide", 1, wide_count)]
    scaled, near_scaled, far_scaled, square = scale_call(
        len(near), gain_rows, (mine, beside, crossed, across)
    )
    if direct:
        inner = inner_call(scaled, packs)
        inner = lax.all_to_all(inner, "tp", 0, 0)
    else:
        down = lax.all_gather(adapter_down_factor, "wide", axis=2, tiled=True)
        down = down.reshape(kinds * ranks, width)
        inner = jnp.einsum("rd,kd->rk", scaled, down, preferred_element_type=jnp.float32)[None]
        packs = [lax.all_gather(up_part, "wide", axis=1, tiled=True)]
    near_base, far_base = [
        jnp.einsum("md,dkc->kmc", x, y, preferred_element_type=jnp.float32)
        for x, y in ((near_scaled, near_weight), (far_scaled, far_weight))
    ]
    return final_call(
        queries.shape, width, near_base, far_base, square, bias, cached, inner, packs
    )


def solution(mesh):
    in_specs = (
        P(None, ("groups", "wide"), "tp"),
        P(),
        P(None, None, "tp"),
        P(None, "tp"),
        P("groups", None, "wide"),
        P("groups", "tp", "wide"),
        P(None, ("groups", "wide"), "tp"),
        P(("groups", "wide"), None, "tp"),
        P(("groups", "wide"), None, "tp"),
        P(("groups", "wide")),
    )
    out_specs = (
        P(None, ("groups", "wide"), "tp"),
        P(None, ("groups", "wide"), "tp"),
        P(None, ("groups", "wide"), "tp"),
    )
    body = functools.partial(on_device, mesh.shape["wide"], mesh.shape["tp"])
    return jax.shard_map(
        body, mesh=mesh, in_specs=in_specs, out_specs=out_specs, check_vma=False
    )
```

```python
import functools
import math

import jax
import jax.numpy as jnp
from jax import lax
from jax.experimental import pallas as pl
from jax.experimental.pallas import tpu as pltpu
from jax.sharding import PartitionSpec as P

HD = 128


norm_eps = 1e-06
adapter_scale = 2.0
rope_base = 1000000.0
masked_score = -1e30
score_scale = 1.0 / math.sqrt(HD)

VMEM = pl.BlockSpec(memory_space=pltpu.VMEM)
HBM = pl.BlockSpec(memory_space=pltpu.HBM)


def query_block(query_ref, group, per_group):
    steps = query_ref.shape[0]
    tiles = []
    for head in range(per_group):
        at = (group * per_group + head) * HD
        for step in range(steps):
            tiles.append(query_ref[step, :, at : at + HD].astype(jnp.float32))
    return jnp.concatenate(tiles, axis=0)


def copy_blocks(offsets, width, weight_ref, out_ref, sems):
    me = lax.axis_index("tp")
    copies = []
    for i, offset in enumerate(offsets):
        block = pl.ds(pl.multiple_of((me ^ offset) * width, width), width)
        copies.append(
            pltpu.make_async_copy(
                weight_ref.at[block], out_ref.at[pl.ds(i * width, width)], sems.at[i]
            )
        )
        copies[-1].start()
    return copies


def cache_kernel(
    near,
    lengths_ref,
    query_ref,
    key_ref,
    value_ref,
    gain_ref,
    bias_ref,
    hidden_ref,
    weight_ref,
    near_out,
    gain_out,
    bias_out,
    hidden_out,
    query_out,
    acc_out,
    top_out,
    total_out,
    cos_out,
    sin_out,
    lengths,
    queries,
    gain_buffer,
    key_buffer,
    value_buffer,
    score_buffer,
    sems,
    weight_sems,
):
    steps, rows, query_width = query_ref.shape
    cache_span = key_ref.shape[1]
    groups = key_ref.shape[2] // HD
    per_group = query_width // HD // groups
    lines = steps * per_group
    half_rows = rows // 2
    halves = [pl.ds(0, half_rows), pl.ds(half_rows, half_rows)]
    copies = [
        (lengths_ref, lengths),
        (query_ref, queries),
        (key_ref.at[halves[0]], key_buffer.at[halves[0]]),
        (key_ref.at[halves[1]], key_buffer.at[halves[1]]),
        (value_ref.at[halves[0]], value_buffer.at[halves[0]]),
        (value_ref.at[halves[1]], value_buffer.at[halves[1]]),
        (gain_ref, gain_buffer),
        (bias_ref, bias_out),
        (hidden_ref, hidden_out),
    ]
    copies = [pltpu.make_async_copy(*pair, sems.at[i]) for i, pair in enumerate(copies)]
    for copy in copies:
        copy.start()
    copies += copy_blocks(near, hidden_ref.shape[2], weight_ref, near_out, weight_sems)

    copies[0].wait()
    lane = lax.broadcasted_iota(jnp.int32, (rows, HD), 1)
    half = HD // 2
    second = lane >= half
    index = jnp.where(second, lane - half, lane).astype(jnp.float32)
    inv_freq = jnp.exp(index * (-2.0 * math.log(rope_base) / HD))
    row_index = lax.broadcasted_iota(jnp.int32, (rows, HD), 0)
    row_lengths = jnp.zeros((rows, HD), jnp.int32)
    for row in range(rows):
        row_lengths = jnp.where(row_index == row, lengths[row], row_lengths)
    for step in range(steps):
        angles = (row_lengths + step).astype(jnp.float32) * inv_freq
        sine = jnp.sin(angles)
        cos_out[pl.ds(step * rows, rows)] = jnp.cos(angles)
        sin_out[pl.ds(step * rows, rows)] = jnp.where(second, sine, -sine)
    copies[1].wait()
    for group in range(groups):
        query_out[group] = query_block(queries, group, per_group)

    place = lax.broadcasted_iota(jnp.int32, (lines, cache_span), 1)
    for i in range(2):
        copies[2 + i].wait()
        for row in range(i * half_rows, (i + 1) * half_rows):
            for group in range(groups):
                query = query_out[group, pl.ds(row, lines, stride=rows), :].astype(jnp.bfloat16)
                score_buffer[row * groups + group] = lax.dot_general(
                    query,
                    key_buffer[row, :, pl.ds(group * HD, HD)],
                    (((1,), (1,)), ((), ())),
                    preferred_element_type=jnp.float32,
                )
    for i in range(2):
        copies[4 + i].wait()
        for row in range(i * half_rows, (i + 1) * half_rows):
            live = place < lengths[row]
            for group in range(groups):
                mine = pl.ds(row, lines, stride=rows)
                scores = score_buffer[row * groups + group]
                scores = jnp.where(live, scores * score_scale, masked_score)
                top = jnp.max(scores, axis=1, keepdims=True)
                exps = jnp.exp(scores - top)
                total = jnp.sum(exps, axis=1, keepdims=True)
                acc = jnp.dot(
                    exps.astype(jnp.bfloat16),
                    value_buffer[row, :, pl.ds(group * HD, HD)],
                    preferred_element_type=jnp.float32,
                )
                acc_out[group, mine, :] = acc
                top_out[group, mine, :] = jnp.broadcast_to(top, acc.shape)
                total_out[group, mine, :] = jnp.broadcast_to(total, acc.shape)
    copies[6].wait()
    gain_out[...] = gain_buffer[...].astype(jnp.float32)
    for copy in copies[7:]:
        copy.wait()


def cache_call(near, lengths, queries, keys, values, gain, bias, hidden, weight):
    steps, rows, query_width = queries.shape
    cache_span, key_width = keys.shape[1:]
    groups = key_width // HD
    lines = steps * (query_width // key_width)
    block = (groups, lines * rows, HD)
    table = (steps * rows, HD)
    operands = (lengths, queries, keys, values, gain, bias, hidden, weight)
    part = hidden.shape[2]
    return pl.pallas_call(
        functools.partial(cache_kernel, near),
        out_shape=(
            pltpu.VMEM((len(near) * part,) + weight.shape[1:], weight.dtype),
            pltpu.VMEM(gain.shape, jnp.float32),
            pltpu.VMEM(bias.shape, bias.dtype),
            pltpu.VMEM(hidden.shape, hidden.dtype),
            pltpu.VMEM(block, jnp.float32),
            pltpu.VMEM(block, jnp.float32),
            pltpu.VMEM(block, jnp.float32),
            pltpu.VMEM(block, jnp.float32),
            pltpu.VMEM(table, jnp.float32),
            pltpu.VMEM(table, jnp.float32),
        ),
        in_specs=[HBM] * len(operands),
        out_specs=(VMEM,) * 10,
        scratch_shapes=[
            pltpu.SMEM(lengths.shape, jnp.int32),
            pltpu.VMEM(queries.shape, queries.dtype),
            pltpu.VMEM(gain.shape, gain.dtype),
            pltpu.VMEM(keys.shape, keys.dtype),
            pltpu.VMEM(values.shape, values.dtype),
            pltpu.VMEM((rows * groups, lines, cache_span), jnp.float32),
            pltpu.SemaphoreType.DMA((9,)),
            pltpu.SemaphoreType.DMA((len(near),)),
        ],
        compiler_params=pltpu.CompilerParams(vmem_limit_bytes=16 << 20),
        cost_estimate=pl.CostEstimate(flops=2 * 67 << 20, bytes_accessed=9 << 20, transcendentals=0),
        name="cache_attention",
    )(*[pltpu.with_memory_space_constraint(x, pltpu.HBM) for x in operands])


def rows_of(ref):
    return jnp.concatenate([ref[s].astype(jnp.float32) for s in range(ref.shape[0])], axis=0)


def pack_kernel(down_ref, up_ref, out_ref, sems):
    share = out_ref.shape[1]
    width = down_ref.shape[2]
    at = pl.ds(pl.multiple_of(lax.axis_index("tp") * share, share), share)
    down = pltpu.make_async_copy(
        down_ref.at[:, at, :], out_ref.at[:, :, pl.ds(0, width)], sems.at[0]
    )
    up = pltpu.make_async_copy(
        up_ref, out_ref.at[:, :, pl.ds(width, up_ref.shape[2])], sems.at[1]
    )
    down.start()
    up.start()
    down.wait()
    up.wait()


def pack_call(down, up):
    kinds, share, columns = up.shape
    return pl.pallas_call(
        pack_kernel,
        out_shape=pltpu.VMEM((kinds, share, down.shape[2] + columns), down.dtype),
        in_specs=[HBM] * 2,
        out_specs=VMEM,
        scratch_shapes=[pltpu.SemaphoreType.DMA((2,))],
        name="pack_factors",
    )(*[pltpu.with_memory_space_constraint(x, pltpu.HBM) for x in (down, up)])


def inner_kernel(scaled_ref, *rest):
    packs, out_ref = rest[:-1], rest[-1]
    me = lax.axis_index("wide")
    width = scaled_ref.shape[1] // len(packs)
    total = []
    for offset, pack in enumerate(packs):
        total.append(
            lax.dot_general(
                scaled_ref[:, pl.ds(pl.multiple_of((me ^ offset) * width, width), width)],
                pack[:, :, :width].reshape(out_ref.shape[1], width),
                (((1,), (1,)), ((), ())),
                preferred_element_type=jnp.float32,
            )
        )
    out_ref[...] = sum(total[1:], total[0])


def inner_call(scaled, packs):
    kinds, share, _ = packs[0].shape
    return pl.pallas_call(
        inner_kernel,
        out_shape=jax.ShapeDtypeStruct((scaled.shape[0], kinds * share), jnp.float32),
        in_specs=[VMEM] * (1 + len(packs)),
        out_specs=VMEM,
        compiler_params=pltpu.CompilerParams(vmem_limit_bytes=8 << 20),
        name="rank_inner",
    )(scaled, *packs)


def scale_kernel(near, far, weight_ref, gain_ref, *rest):
    parts = rest[:-6]
    scaled_out, near_out, far_out, square_out, weight_out, sems = rest[-6:]
    steps, rows, width = parts[0].shape
    chunks = width // HD
    copies = copy_blocks(far, width, weight_ref, weight_out, sems)
    me = lax.axis_index("tp")
    squares = jnp.zeros(square_out.shape, jnp.float32)
    for k, (offset, part) in enumerate(zip(near + far, parts)):
        block = me ^ offset
        gain = gain_ref[pl.ds(pl.multiple_of(block * chunks, chunks), chunks)]
        values = rows_of(part)
        scaled = []
        for i in range(chunks):
            chunk = values[:, i * HD : (i + 1) * HD]
            squares += chunk * chunk
            scaled.append((chunk * gain[i : i + 1]).astype(jnp.bfloat16))
        at = pl.ds(pl.multiple_of(block * width, width), width)
        scaled = jnp.concatenate(scaled, axis=1)
        scaled_out[:, at] = scaled
        out, i = (near_out, k) if k < len(near) else (far_out, k - len(near))
        out[:, i * width : (i + 1) * width] = scaled
    square_out[...] = jnp.broadcast_to(jnp.sum(squares, axis=1, keepdims=True), squares.shape)
    for copy in copies:
        copy.wait()


def scale_call(near, far, weight, gain, parts):
    steps, rows, width = parts[0].shape
    return pl.pallas_call(
        functools.partial(scale_kernel, near, far),
        out_shape=(
            pltpu.VMEM((steps * rows, len(parts) * width), jnp.bfloat16),
            pltpu.VMEM((steps * rows, len(near) * width), jnp.bfloat16),
            pltpu.VMEM((steps * rows, len(far) * width), jnp.bfloat16),
            pltpu.VMEM((steps * rows, HD), jnp.float32),
            pltpu.VMEM((len(far) * width,) + weight.shape[1:], weight.dtype),
        ),
        in_specs=[HBM] + [VMEM] * (1 + len(parts)),
        out_specs=(VMEM,) * 5,
        scratch_shapes=[pltpu.SemaphoreType.DMA((len(far),))],
        compiler_params=pltpu.CompilerParams(vmem_limit_bytes=8 << 20),
        cost_estimate=pl.CostEstimate(flops=0, bytes_accessed=5 << 20, transcendentals=0),
        name="scale_features",
    )(pltpu.with_memory_space_constraint(weight, pltpu.HBM), gain, *parts)


def up_kernel(*refs):
    packs, up_out = refs[:-1], refs[-1]
    kinds, share, pack_width = packs[0].shape
    columns = up_out.shape[1] // kinds
    me = lax.axis_index("wide") if len(packs) > 1 else 0
    up_out[...] = jnp.zeros_like(up_out)
    for offset, pack in enumerate(packs):
        for kind in range(kinds):
            at = pl.multiple_of(((me ^ offset) * kinds + kind) * share, share)
            up_out[pl.ds(at, share), kind * columns : (kind + 1) * columns] = pack[
                kind, :, pack_width - columns :
            ]


def final_kernel(width, blocks, near_ref, far_ref, square_ref, bias_ref, *rest):
    query_ref, acc_ref, top_ref, total_ref, cos_ref, sin_ref = rest[:6]
    inner_refs = rest[6 : 6 + blocks]
    packs = rest[6 + blocks : 6 + 2 * blocks]
    keys_out, values_out, attended_out, inner_buffer, up_ref = rest[6 + 2 * blocks :]
    up_kernel(*packs, up_ref)
    steps, rows, columns = keys_out.shape
    count = steps * rows
    groups, size, _ = query_ref.shape
    per_group = size // count
    kinds = bias_ref.shape[0]
    row_scale = lax.rsqrt(square_ref[:, :1] * (1.0 / width) + norm_eps)
    me = lax.axis_index("tp") if blocks > 1 else 0
    for i in range(blocks):
        inner_buffer[me ^ i] = inner_refs[i][...]
    inner = jnp.concatenate([inner_buffer[i] for i in range(blocks)], axis=1)
    high = inner.astype(jnp.bfloat16)
    low = (inner - high.astype(jnp.float32)).astype(jnp.bfloat16)
    lora = jnp.dot(
        jnp.concatenate([high, low], axis=0), up_ref[...], preferred_element_type=jnp.float32
    )
    lora = lora[:count] + lora[count:]
    bias = bias_ref[...].astype(jnp.float32)
    linear = []
    for kind in range(kinds):
        base = near_ref[kind] + far_ref[kind]
        part = lora[:, kind * columns : (kind + 1) * columns]
        linear.append((base + adapter_scale * part) * row_scale + bias[kind : kind + 1])
    cosine, sine = cos_ref[...], sin_ref[...]
    line = lax.broadcasted_iota(jnp.int32, (size, count), 0)
    other = lax.broadcasted_iota(jnp.int32, (size, count), 1)
    live = (line % rows == other % rows) & (other // rows <= line // rows % steps)
    for group in range(groups):
        at = slice(group * HD, (group + 1) * HD)
        key = linear[0][:, at]
        key = (key * cosine + pltpu.roll(key, HD // 2, 1) * sine).astype(jnp.bfloat16)
        value = linear[1][:, at].astype(jnp.bfloat16)
        for step in range(steps):
            keys_out[step, :, at] = key[step * rows : (step + 1) * rows]
            values_out[step, :, at] = value[step * rows : (step + 1) * rows]
        scores = lax.dot_general(
            query_ref[group].astype(jnp.bfloat16),
            key,
            (((1,), (1,)), ((), ())),
            preferred_element_type=jnp.float32,
        )
        scores = jnp.where(live, scores * score_scale, masked_score)
        old_top = top_ref[group][:, :1]
        top = jnp.maximum(old_top, jnp.max(scores, axis=1, keepdims=True))
        exps = jnp.exp(scores - top)
        keep = jnp.exp(old_top - top)
        total = total_ref[group][:, :1] * keep + jnp.sum(exps, axis=1, keepdims=True)
        acc = acc_ref[group] * keep + jnp.dot(
            exps.astype(jnp.bfloat16), value, preferred_element_type=jnp.float32
        )
        attended = (acc / total).astype(jnp.bfloat16)
        for head in range(per_group):
            lanes = pl.ds((group * per_group + head) * HD, HD)
            for step in range(steps):
                tile = (head * steps + step) * rows
                attended_out[step, :, lanes] = attended[tile : tile + rows]


def final_call(shape, width, near, far, square, bias, cached, inner, packs):
    steps, rows, query_width = shape
    kinds, share, _ = packs[0].shape
    columns = near.shape[2]
    small = jax.ShapeDtypeStruct((steps, rows, columns), jnp.bfloat16)
    return pl.pallas_call(
        functools.partial(final_kernel, width, len(inner)),
        out_shape=(small, small, jax.ShapeDtypeStruct(shape, jnp.bfloat16)),
        in_specs=[VMEM] * (4 + len(cached) + len(inner) + len(packs)),
        out_specs=(VMEM,) * 3,
        scratch_shapes=[
            pltpu.VMEM((len(inner),) + inner[0].shape, jnp.float32),
            pltpu.VMEM((len(packs) * kinds * share, kinds * columns), jnp.bfloat16),
        ],
        compiler_params=pltpu.CompilerParams(vmem_limit_bytes=8 << 20),
        name="fresh_attention",
    )(near, far, square, bias, *cached, *inner, *packs)


def swap(block, axis, offset, count):
    return lax.ppermute(block, axis, [(i, i ^ offset) for i in range(count)])


def on_device(
    wide_count,
    tp_count,
    hidden,
    input_norm_gain,
    key_value_weight,
    key_value_bias,
    adapter_down_factor,
    adapter_up_factor,
    queries,
    stored_rotated_keys,
    stored_value_rows,
    lengths,
):
    steps, rows, part_width = hidden.shape
    width = part_width * tp_count
    kinds, ranks, down_width = adapter_down_factor.shape
    gain = input_norm_gain.reshape(width // HD, HD)
    up_part = jnp.transpose(adapter_up_factor, (0, 2, 1))
    direct = wide_count == tp_count == 4
    tp_parts = [swap(hidden, "tp", offset, tp_count) for offset in (1, 2, 3)]
    if direct:
        pack = pack_call(adapter_down_factor, up_part)
        second = swap(pack, "wide", 2, wide_count)
        first = swap(pack, "wide", 1, wide_count)
    near, far = (0, 1), (2, 3)
    near_weight, gain_rows, bias, mine, *cached = cache_call(
        near,
        lengths,
        queries,
        stored_rotated_keys,
        stored_value_rows,
        gain,
        key_value_bias,
        hidden,
        key_value_weight,
    )
    if direct:
        third, gain_rows = lax.optimization_barrier((second, gain_rows))
        packs = [pack, first, second, swap(third, "wide", 1, wide_count)]
    scaled, near_scaled, far_scaled, square, far_weight = scale_call(
        near, far, key_value_weight, gain_rows, [mine] + tp_parts
    )
    if direct:
        inner = inner_call(scaled, packs)
        inner, far_scaled = lax.optimization_barrier((inner, far_scaled))
        inner = [inner] + [swap(inner, "tp", offset, tp_count) for offset in (1, 2, 3)]
    else:
        down = lax.all_gather(adapter_down_factor, "wide", axis=2, tiled=True)
        down = down.reshape(kinds * ranks, width)
        inner = [jnp.einsum("rd,kd->rk", scaled, down, preferred_element_type=jnp.float32)]
        packs = [lax.all_gather(up_part, "wide", axis=1, tiled=True)]
    near_base, far_base = [
        jnp.einsum("md,dkc->kmc", x, y, preferred_element_type=jnp.float32)
        for x, y in ((near_scaled, near_weight), (far_scaled, far_weight))
    ]
    return final_call(
        queries.shape, width, near_base, far_base, square, bias, cached, inner, packs
    )


def solution(mesh):
    in_specs = (
        P(None, ("groups", "wide"), "tp"),
        P(),
        P(None, None, "tp"),
        P(None, "tp"),
        P("groups", None, "wide"),
        P("groups", "tp", "wide"),
        P(None, ("groups", "wide"), "tp"),
        P(("groups", "wide"), None, "tp"),
        P(("groups", "wide"), None, "tp"),
        P(("groups", "wide")),
    )
    out_specs = (
        P(None, ("groups", "wide"), "tp"),
        P(None, ("groups", "wide"), "tp"),
        P(None, ("groups", "wide"), "tp"),
    )
    body = functools.partial(on_device, mesh.shape["wide"], mesh.shape["tp"])
    return jax.shard_map(
        body, mesh=mesh, in_specs=in_specs, out_specs=out_specs, check_vma=False
    )
```

```python
import functools
import math

import jax
import jax.numpy as jnp
from jax import lax
from jax.experimental import pallas as pl
from jax.experimental.pallas import tpu as pltpu
from jax.sharding import PartitionSpec as P

HD = 128


norm_eps = 1e-06
adapter_scale = 2.0
rope_base = 1000000.0
masked_score = -1e30
score_scale = 1.0 / math.sqrt(HD)

VMEM = pl.BlockSpec(memory_space=pltpu.VMEM)
HBM = pl.BlockSpec(memory_space=pltpu.HBM)


def query_block(query_ref, group, per_group):
    steps = query_ref.shape[0]
    tiles = []
    for head in range(per_group):
        at = (group * per_group + head) * HD
        for step in range(steps):
            tiles.append(query_ref[step, :, at : at + HD].astype(jnp.float32))
    return jnp.concatenate(tiles, axis=0)


def copy_blocks(offsets, width, weight_ref, out_ref, sems):
    me = lax.axis_index("tp")
    copies = []
    for i, offset in enumerate(offsets):
        block = pl.ds(pl.multiple_of((me ^ offset) * width, width), width)
        copies.append(
            pltpu.make_async_copy(
                weight_ref.at[block], out_ref.at[pl.ds(i * width, width)], sems.at[i]
            )
        )
        copies[-1].start()
    return copies


def cache_kernel(
    near,
    lengths_ref,
    query_ref,
    key_ref,
    value_ref,
    gain_ref,
    bias_ref,
    hidden_ref,
    down_ref,
    up_ref,
    weight_ref,
    near_out,
    gain_out,
    bias_out,
    hidden_out,
    down_out,
    up_out,
    query_out,
    acc_out,
    top_out,
    total_out,
    cos_out,
    sin_out,
    lengths,
    queries,
    gain_buffer,
    key_buffer,
    value_buffer,
    score_buffer,
    sems,
    weight_sems,
):
    steps, rows, query_width = query_ref.shape
    cache_span = key_ref.shape[1]
    groups = key_ref.shape[2] // HD
    per_group = query_width // HD // groups
    lines = steps * per_group
    half_rows = rows // 2
    halves = [pl.ds(0, half_rows), pl.ds(half_rows, half_rows)]
    copies = [
        (lengths_ref, lengths),
        (query_ref, queries),
        (key_ref.at[halves[0]], key_buffer.at[halves[0]]),
        (key_ref.at[halves[1]], key_buffer.at[halves[1]]),
        (value_ref.at[halves[0]], value_buffer.at[halves[0]]),
        (value_ref.at[halves[1]], value_buffer.at[halves[1]]),
        (gain_ref, gain_buffer),
        (bias_ref, bias_out),
        (hidden_ref, hidden_out),
        (down_ref, down_out),
        (up_ref, up_out),
    ]
    copies = [pltpu.make_async_copy(*pair, sems.at[i]) for i, pair in enumerate(copies)]
    for copy in copies:
        copy.start()
    copies += copy_blocks(near, hidden_ref.shape[2], weight_ref, near_out, weight_sems)

    copies[0].wait()
    lane = lax.broadcasted_iota(jnp.int32, (rows, HD), 1)
    half = HD // 2
    second = lane >= half
    index = jnp.where(second, lane - half, lane).astype(jnp.float32)
    inv_freq = jnp.exp(index * (-2.0 * math.log(rope_base) / HD))
    row_index = lax.broadcasted_iota(jnp.int32, (rows, HD), 0)
    row_lengths = jnp.zeros((rows, HD), jnp.int32)
    for row in range(rows):
        row_lengths = jnp.where(row_index == row, lengths[row], row_lengths)
    for step in range(steps):
        angles = (row_lengths + step).astype(jnp.float32) * inv_freq
        sine = jnp.sin(angles)
        cos_out[pl.ds(step * rows, rows)] = jnp.cos(angles)
        sin_out[pl.ds(step * rows, rows)] = jnp.where(second, sine, -sine)
    copies[1].wait()
    for group in range(groups):
        query_out[group] = query_block(queries, group, per_group)

    place = lax.broadcasted_iota(jnp.int32, (lines, cache_span), 1)
    for i in range(2):
        copies[2 + i].wait()
        for row in range(i * half_rows, (i + 1) * half_rows):
            for group in range(groups):
                query = query_out[group, pl.ds(row, lines, stride=rows), :].astype(jnp.bfloat16)
                score_buffer[row * groups + group] = lax.dot_general(
                    query,
                    key_buffer[row, :, pl.ds(group * HD, HD)],
                    (((1,), (1,)), ((), ())),
                    preferred_element_type=jnp.float32,
                )
    for i in range(2):
        copies[4 + i].wait()
        for row in range(i * half_rows, (i + 1) * half_rows):
            live = place < lengths[row]
            for group in range(groups):
                mine = pl.ds(row, lines, stride=rows)
                scores = score_buffer[row * groups + group]
                scores = jnp.where(live, scores * score_scale, masked_score)
                top = jnp.max(scores, axis=1, keepdims=True)
                exps = jnp.exp(scores - top)
                total = jnp.sum(exps, axis=1, keepdims=True)
                acc = jnp.dot(
                    exps.astype(jnp.bfloat16),
                    value_buffer[row, :, pl.ds(group * HD, HD)],
                    preferred_element_type=jnp.float32,
                )
                acc_out[group, mine, :] = acc
                top_out[group, mine, :] = jnp.broadcast_to(top, acc.shape)
                total_out[group, mine, :] = jnp.broadcast_to(total, acc.shape)
    copies[6].wait()
    gain_out[...] = gain_buffer[...].astype(jnp.float32)
    for copy in copies[7:]:
        copy.wait()


def cache_call(near, lengths, queries, keys, values, gain, bias, hidden, down, up, weight):
    steps, rows, query_width = queries.shape
    cache_span, key_width = keys.shape[1:]
    groups = key_width // HD
    lines = steps * (query_width // key_width)
    block = (groups, lines * rows, HD)
    table = (steps * rows, HD)
    operands = (lengths, queries, keys, values, gain, bias, hidden, down, up, weight)
    part = hidden.shape[2]
    return pl.pallas_call(
        functools.partial(cache_kernel, near),
        out_shape=(
            pltpu.VMEM((len(near) * part,) + weight.shape[1:], weight.dtype),
            pltpu.VMEM(gain.shape, jnp.float32),
            pltpu.VMEM(bias.shape, bias.dtype),
            pltpu.VMEM(hidden.shape, hidden.dtype),
            pltpu.VMEM(down.shape, down.dtype),
            pltpu.VMEM(up.shape, up.dtype),
            pltpu.VMEM(block, jnp.float32),
            pltpu.VMEM(block, jnp.float32),
            pltpu.VMEM(block, jnp.float32),
            pltpu.VMEM(block, jnp.float32),
            pltpu.VMEM(table, jnp.float32),
            pltpu.VMEM(table, jnp.float32),
        ),
        in_specs=[HBM] * len(operands),
        out_specs=(VMEM,) * 12,
        scratch_shapes=[
            pltpu.SMEM(lengths.shape, jnp.int32),
            pltpu.VMEM(queries.shape, queries.dtype),
            pltpu.VMEM(gain.shape, gain.dtype),
            pltpu.VMEM(keys.shape, keys.dtype),
            pltpu.VMEM(values.shape, values.dtype),
            pltpu.VMEM((rows * groups, lines, cache_span), jnp.float32),
            pltpu.SemaphoreType.DMA((11,)),
            pltpu.SemaphoreType.DMA((len(near),)),
        ],
        compiler_params=pltpu.CompilerParams(vmem_limit_bytes=16 << 20),
        cost_estimate=pl.CostEstimate(flops=2 * 67 << 20, bytes_accessed=9 << 20, transcendentals=0),
        name="cache_attention",
    )(*[pltpu.with_memory_space_constraint(x, pltpu.HBM) for x in operands])


def rows_of(ref):
    return jnp.concatenate([ref[s].astype(jnp.float32) for s in range(ref.shape[0])], axis=0)


def inner_kernel(hidden_ref, gain_ref, down_ref, up_ref, beside_ref, out_ref, up_out):
    width = hidden_ref.shape[2]
    chunks = width // HD
    start = pl.multiple_of(lax.axis_index("wide") * chunks, chunks)
    gain = gain_ref[pl.ds(start, chunks)]
    values = rows_of(hidden_ref)
    scaled = [
        (values[:, i * HD : (i + 1) * HD] * gain[i : i + 1]).astype(jnp.bfloat16)
        for i in range(chunks)
    ]
    scaled = jnp.concatenate(scaled, axis=1)
    kinds, ranks, _ = down_ref.shape
    for kind in range(kinds):
        out_ref[:, kind * ranks : (kind + 1) * ranks] = lax.dot_general(
            scaled,
            down_ref[kind],
            (((1,), (1,)), ((), ())),
            preferred_element_type=jnp.float32,
        )
    up_out[0] = up_ref[...]
    up_out[1] = beside_ref[...]


def inner_call(hidden, gain, down, up, beside):
    steps, rows, _ = hidden.shape
    kinds, ranks, _ = down.shape
    return pl.pallas_call(
        inner_kernel,
        out_shape=(
            pltpu.VMEM((steps * rows, kinds * ranks), jnp.float32),
            pltpu.VMEM((2,) + up.shape, up.dtype),
        ),
        in_specs=[VMEM] * 5,
        out_specs=(VMEM,) * 2,
        compiler_params=pltpu.CompilerParams(vmem_limit_bytes=8 << 20),
        name="rank_inner",
    )(hidden, gain, down, up, beside)


def scale_kernel(near, far, weight_ref, gain_ref, *rest):
    parts = rest[:-5]
    near_out, far_out, square_out, weight_out, sems = rest[-5:]
    steps, rows, width = parts[0].shape
    chunks = width // HD
    copies = copy_blocks(far, width, weight_ref, weight_out, sems)
    me = lax.axis_index("tp")
    squares = jnp.zeros(square_out.shape, jnp.float32)
    for k, (offset, part) in enumerate(zip(near + far, parts)):
        block = me ^ offset
        gain = gain_ref[pl.ds(pl.multiple_of(block * chunks, chunks), chunks)]
        values = rows_of(part)
        scaled = []
        for i in range(chunks):
            chunk = values[:, i * HD : (i + 1) * HD]
            squares += chunk * chunk
            scaled.append((chunk * gain[i : i + 1]).astype(jnp.bfloat16))
        scaled = jnp.concatenate(scaled, axis=1)
        out, i = (near_out, k) if k < len(near) else (far_out, k - len(near))
        out[:, i * width : (i + 1) * width] = scaled
    square_out[...] = jnp.broadcast_to(jnp.sum(squares, axis=1, keepdims=True), squares.shape)
    for copy in copies:
        copy.wait()


def scale_call(near, far, weight, gain, parts):
    steps, rows, width = parts[0].shape
    return pl.pallas_call(
        functools.partial(scale_kernel, near, far),
        out_shape=(
            pltpu.VMEM((steps * rows, len(near) * width), jnp.bfloat16),
            pltpu.VMEM((steps * rows, len(far) * width), jnp.bfloat16),
            pltpu.VMEM((steps * rows, HD), jnp.float32),
            pltpu.VMEM((len(far) * width,) + weight.shape[1:], weight.dtype),
        ),
        in_specs=[HBM] + [VMEM] * (1 + len(parts)),
        out_specs=(VMEM,) * 4,
        scratch_shapes=[pltpu.SemaphoreType.DMA((len(far),))],
        compiler_params=pltpu.CompilerParams(vmem_limit_bytes=8 << 20),
        cost_estimate=pl.CostEstimate(flops=0, bytes_accessed=5 << 20, transcendentals=0),
        name="scale_features",
    )(pltpu.with_memory_space_constraint(weight, pltpu.HBM), gain, *parts)


def lay_out(ups, out_ref):
    kinds, share, columns = ups[0].shape
    me = lax.axis_index("wide") if len(ups) > 1 else 0
    out_ref[...] = jnp.zeros_like(out_ref)
    for offset, up in enumerate(ups):
        for kind in range(kinds):
            at = pl.multiple_of((kind * len(ups) + (me ^ offset)) * share, share)
            out_ref[pl.ds(at, share), kind * columns : (kind + 1) * columns] = up[kind]


def final_kernel(width, inner_count, up_count, near_ref, far_ref, square_ref, bias_ref, *rest):
    query_ref, acc_ref, top_ref, total_ref, cos_ref, sin_ref = rest[:6]
    inner_refs = rest[6 : 6 + inner_count]
    up_refs = rest[6 + inner_count : 6 + inner_count + up_count]
    keys_out, values_out, attended_out, up_ref = rest[6 + inner_count + up_count :]
    lay_out([ref.at[i] for ref in up_refs for i in range(ref.shape[0])], up_ref)
    steps, rows, columns = keys_out.shape
    count = steps * rows
    groups, size, _ = query_ref.shape
    per_group = size // count
    kinds = bias_ref.shape[0]
    row_scale = lax.rsqrt(square_ref[:, :1] * (1.0 / width) + norm_eps)
    inner = inner_refs[0][...]
    for ref in inner_refs[1:]:
        inner = inner + ref[...]
    high = inner.astype(jnp.bfloat16)
    low = (inner - high.astype(jnp.float32)).astype(jnp.bfloat16)
    lora = jnp.dot(
        jnp.concatenate([high, low], axis=0), up_ref[...], preferred_element_type=jnp.float32
    )
    lora = lora[:count] + lora[count:]
    bias = bias_ref[...].astype(jnp.float32)
    linear = []
    for kind in range(kinds):
        base = near_ref[kind] + far_ref[kind]
        part = lora[:, kind * columns : (kind + 1) * columns]
        linear.append((base + adapter_scale * part) * row_scale + bias[kind : kind + 1])
    cosine, sine = cos_ref[...], sin_ref[...]
    line = lax.broadcasted_iota(jnp.int32, (size, count), 0)
    other = lax.broadcasted_iota(jnp.int32, (size, count), 1)
    live = (line % rows == other % rows) & (other // rows <= line // rows % steps)
    for group in range(groups):
        at = slice(group * HD, (group + 1) * HD)
        key = linear[0][:, at]
        key = (key * cosine + pltpu.roll(key, HD // 2, 1) * sine).astype(jnp.bfloat16)
        value = linear[1][:, at].astype(jnp.bfloat16)
        for step in range(steps):
            keys_out[step, :, at] = key[step * rows : (step + 1) * rows]
            values_out[step, :, at] = value[step * rows : (step + 1) * rows]
        scores = lax.dot_general(
            query_ref[group].astype(jnp.bfloat16),
            key,
            (((1,), (1,)), ((), ())),
            preferred_element_type=jnp.float32,
        )
        scores = jnp.where(live, scores * score_scale, masked_score)
        old_top = top_ref[group][:, :1]
        top = jnp.maximum(old_top, jnp.max(scores, axis=1, keepdims=True))
        exps = jnp.exp(scores - top)
        keep = jnp.exp(old_top - top)
        total = total_ref[group][:, :1] * keep + jnp.sum(exps, axis=1, keepdims=True)
        acc = acc_ref[group] * keep + jnp.dot(
            exps.astype(jnp.bfloat16), value, preferred_element_type=jnp.float32
        )
        attended = (acc / total).astype(jnp.bfloat16)
        for head in range(per_group):
            lanes = pl.ds((group * per_group + head) * HD, HD)
            for step in range(steps):
                tile = (head * steps + step) * rows
                attended_out[step, :, lanes] = attended[tile : tile + rows]


def final_call(shape, width, near, far, square, bias, cached, inner, ups):
    steps, rows, query_width = shape
    kinds, _, columns = near.shape
    small = jax.ShapeDtypeStruct((steps, rows, columns), jnp.bfloat16)
    return pl.pallas_call(
        functools.partial(final_kernel, width, len(inner), len(ups)),
        out_shape=(small, small, jax.ShapeDtypeStruct(shape, jnp.bfloat16)),
        in_specs=[VMEM] * (4 + len(cached) + len(inner) + len(ups)),
        out_specs=(VMEM,) * 3,
        scratch_shapes=[pltpu.VMEM((inner[0].shape[1], kinds * columns), jnp.bfloat16)],
        compiler_params=pltpu.CompilerParams(vmem_limit_bytes=8 << 20),
        name="fresh_attention",
    )(near, far, square, bias, *cached, *inner, *ups)


def swap(block, axis, offset, count):
    return lax.ppermute(block, axis, [(i, i ^ offset) for i in range(count)])


def meeting_place():
    pairs = []
    for w in range(4):
        for t in range(4):
            pairs.append((w * 4 + t, t * 4 + 2 * ((t // 2) ^ ((w + t) & 1)) + w // 2))
    return pairs


def on_device(
    wide_count,
    tp_count,
    hidden,
    input_norm_gain,
    key_value_weight,
    key_value_bias,
    adapter_down_factor,
    adapter_up_factor,
    queries,
    stored_rotated_keys,
    stored_value_rows,
    lengths,
):
    steps, rows, part_width = hidden.shape
    width = part_width * tp_count
    kinds, ranks, down_width = adapter_down_factor.shape
    gain = input_norm_gain.reshape(width // HD, HD)
    up_part = jnp.transpose(adapter_up_factor, (0, 2, 1))
    direct = wide_count == tp_count == 4
    both = ("wide", "tp")
    if direct:
        there = meeting_place()
        moved = lax.ppermute(hidden, both, there)
        up_beside = swap(up_part, "wide", 1, wide_count)
    tp_parts = [swap(hidden, "tp", offset, tp_count) for offset in (1, 2, 3)]
    near, far = (0, 1), (2, 3)
    near_weight, gain_rows, bias, mine, my_down, my_up, *cached = cache_call(
        near,
        lengths,
        queries,
        stored_rotated_keys,
        stored_value_rows,
        gain,
        key_value_bias,
        hidden,
        adapter_down_factor,
        up_part,
        key_value_weight,
    )
    if direct:
        inner, up_pair = inner_call(moved, gain_rows, my_down, my_up, up_beside)
        inner = lax.ppermute(inner, both, [(b, a) for a, b in there])
        gain_rows, up_pair = lax.optimization_barrier((gain_rows, up_pair))
        ups = [up_pair, swap(up_pair, "wide", 2, wide_count)]
    near_scaled, far_scaled, square, far_weight = scale_call(
        near, far, key_value_weight, gain_rows, [mine] + tp_parts
    )
    if direct:
        inner, far_scaled, near_scaled = lax.optimization_barrier(
            (inner, far_scaled, near_scaled)
        )
        inner = [inner] + [swap(inner, "tp", offset, tp_count) for offset in (1, 2, 3)]
    else:
        rows_full = lax.all_gather(hidden, "tp", axis=2, tiled=True).astype(jnp.float32)
        rows_full = (rows_full * input_norm_gain.astype(jnp.float32)).astype(jnp.bfloat16)
        down = lax.all_gather(adapter_down_factor, "wide", axis=2, tiled=True)
        inner = jnp.einsum("srd,kad->srka", rows_full, down, preferred_element_type=jnp.float32)
        inner = [inner.reshape(steps * rows, kinds * ranks)]
        ups = [lax.all_gather(up_part, "wide", axis=1, tiled=True)[None]]
    near_base, far_base = [
        jnp.einsum("md,dkc->kmc", x, y, preferred_element_type=jnp.float32)
        for x, y in ((near_scaled, near_weight), (far_scaled, far_weight))
    ]
    return final_call(queries.shape, width, near_base, far_base, square, bias, cached, inner, ups)


def solution(mesh):
    in_specs = (
        P(None, ("groups", "wide"), "tp"),
        P(),
        P(None, None, "tp"),
        P(None, "tp"),
        P("groups", None, "wide"),
        P("groups", "tp", "wide"),
        P(None, ("groups", "wide"), "tp"),
        P(("groups", "wide"), None, "tp"),
        P(("groups", "wide"), None, "tp"),
        P(("groups", "wide")),
    )
    out_specs = (
        P(None, ("groups", "wide"), "tp"),
        P(None, ("groups", "wide"), "tp"),
        P(None, ("groups", "wide"), "tp"),
    )
    body = functools.partial(on_device, mesh.shape["wide"], mesh.shape["tp"])
    return jax.shard_map(
        body, mesh=mesh, in_specs=in_specs, out_specs=out_specs, check_vma=False
    )
```

```python
import functools
import math

import jax
import jax.numpy as jnp
from jax import lax
from jax.experimental import pallas as pl
from jax.experimental.pallas import tpu as pltpu
from jax.sharding import PartitionSpec as P

HD = 128


norm_eps = 1e-06
adapter_scale = 2.0
rope_base = 1000000.0
masked_score = -1e30
score_scale = 1.0 / math.sqrt(HD)

VMEM = pl.BlockSpec(memory_space=pltpu.VMEM)
HBM = pl.BlockSpec(memory_space=pltpu.HBM)


def query_block(query_ref, group, per_group):
    steps = query_ref.shape[0]
    tiles = []
    for head in range(per_group):
        at = (group * per_group + head) * HD
        for step in range(steps):
            tiles.append(query_ref[step, :, at : at + HD].astype(jnp.float32))
    return jnp.concatenate(tiles, axis=0)


def copy_blocks(offsets, width, weight_ref, out_ref, sems):
    me = lax.axis_index("tp")
    copies = []
    for i, offset in enumerate(offsets):
        block = pl.ds(pl.multiple_of((me ^ offset) * width, width), width)
        copies.append(
            pltpu.make_async_copy(
                weight_ref.at[block], out_ref.at[pl.ds(i * width, width)], sems.at[i]
            )
        )
        copies[-1].start()
    return copies


def cache_kernel(
    near,
    lengths_ref,
    query_ref,
    key_ref,
    value_ref,
    gain_ref,
    bias_ref,
    hidden_ref,
    down_ref,
    weight_ref,
    near_out,
    gain_out,
    bias_out,
    hidden_out,
    down_out,
    query_out,
    acc_out,
    top_out,
    total_out,
    cos_out,
    sin_out,
    lengths,
    queries,
    gain_buffer,
    key_buffer,
    value_buffer,
    score_buffer,
    sems,
    weight_sems,
):
    steps, rows, query_width = query_ref.shape
    cache_span = key_ref.shape[1]
    groups = key_ref.shape[2] // HD
    per_group = query_width // HD // groups
    lines = steps * per_group
    half_rows = rows // 2
    halves = [pl.ds(0, half_rows), pl.ds(half_rows, half_rows)]
    copies = [
        (lengths_ref, lengths),
        (query_ref, queries),
        (key_ref.at[halves[0]], key_buffer.at[halves[0]]),
        (key_ref.at[halves[1]], key_buffer.at[halves[1]]),
        (value_ref.at[halves[0]], value_buffer.at[halves[0]]),
        (value_ref.at[halves[1]], value_buffer.at[halves[1]]),
        (gain_ref, gain_buffer),
        (bias_ref, bias_out),
        (hidden_ref, hidden_out),
        (down_ref, down_out),
    ]
    copies = [pltpu.make_async_copy(*pair, sems.at[i]) for i, pair in enumerate(copies)]
    for copy in copies:
        copy.start()
    copies += copy_blocks(near, hidden_ref.shape[2], weight_ref, near_out, weight_sems)

    copies[0].wait()
    lane = lax.broadcasted_iota(jnp.int32, (rows, HD), 1)
    half = HD // 2
    second = lane >= half
    index = jnp.where(second, lane - half, lane).astype(jnp.float32)
    inv_freq = jnp.exp(index * (-2.0 * math.log(rope_base) / HD))
    row_index = lax.broadcasted_iota(jnp.int32, (rows, HD), 0)
    row_lengths = jnp.zeros((rows, HD), jnp.int32)
    for row in range(rows):
        row_lengths = jnp.where(row_index == row, lengths[row], row_lengths)
    for step in range(steps):
        angles = (row_lengths + step).astype(jnp.float32) * inv_freq
        sine = jnp.sin(angles)
        cos_out[pl.ds(step * rows, rows)] = jnp.cos(angles)
        sin_out[pl.ds(step * rows, rows)] = jnp.where(second, sine, -sine)
    copies[1].wait()
    for group in range(groups):
        query_out[group] = query_block(queries, group, per_group)

    place = lax.broadcasted_iota(jnp.int32, (lines, cache_span), 1)
    for i in range(2):
        copies[2 + i].wait()
        for row in range(i * half_rows, (i + 1) * half_rows):
            for group in range(groups):
                query = query_out[group, pl.ds(row, lines, stride=rows), :].astype(jnp.bfloat16)
                score_buffer[row * groups + group] = lax.dot_general(
                    query,
                    key_buffer[row, :, pl.ds(group * HD, HD)],
                    (((1,), (1,)), ((), ())),
                    preferred_element_type=jnp.float32,
                )
    for i in range(2):
        copies[4 + i].wait()
        for row in range(i * half_rows, (i + 1) * half_rows):
            live = place < lengths[row]
            for group in range(groups):
                mine = pl.ds(row, lines, stride=rows)
                scores = score_buffer[row * groups + group]
                scores = jnp.where(live, scores * score_scale, masked_score)
                top = jnp.max(scores, axis=1, keepdims=True)
                exps = jnp.exp(scores - top)
                total = jnp.sum(exps, axis=1, keepdims=True)
                acc = jnp.dot(
                    exps.astype(jnp.bfloat16),
                    value_buffer[row, :, pl.ds(group * HD, HD)],
                    preferred_element_type=jnp.float32,
                )
                acc_out[group, mine, :] = acc
                top_out[group, mine, :] = jnp.broadcast_to(top, acc.shape)
                total_out[group, mine, :] = jnp.broadcast_to(total, acc.shape)
    copies[6].wait()
    gain_out[...] = gain_buffer[...].astype(jnp.float32)
    for copy in copies[7:]:
        copy.wait()


def cache_call(near, lengths, queries, keys, values, gain, bias, hidden, down, weight):
    steps, rows, query_width = queries.shape
    cache_span, key_width = keys.shape[1:]
    groups = key_width // HD
    lines = steps * (query_width // key_width)
    block = (groups, lines * rows, HD)
    table = (steps * rows, HD)
    operands = (lengths, queries, keys, values, gain, bias, hidden, down, weight)
    part = hidden.shape[2]
    return pl.pallas_call(
        functools.partial(cache_kernel, near),
        out_shape=(
            pltpu.VMEM((len(near) * part,) + weight.shape[1:], weight.dtype),
            pltpu.VMEM(gain.shape, jnp.float32),
            pltpu.VMEM(bias.shape, bias.dtype),
            pltpu.VMEM(hidden.shape, hidden.dtype),
            pltpu.VMEM(down.shape, down.dtype),
            pltpu.VMEM(block, jnp.float32),
            pltpu.VMEM(block, jnp.float32),
            pltpu.VMEM(block, jnp.float32),
            pltpu.VMEM(block, jnp.float32),
            pltpu.VMEM(table, jnp.float32),
            pltpu.VMEM(table, jnp.float32),
        ),
        in_specs=[HBM] * len(operands),
        out_specs=(VMEM,) * 11,
        scratch_shapes=[
            pltpu.SMEM(lengths.shape, jnp.int32),
            pltpu.VMEM(queries.shape, queries.dtype),
            pltpu.VMEM(gain.shape, gain.dtype),
            pltpu.VMEM(keys.shape, keys.dtype),
            pltpu.VMEM(values.shape, values.dtype),
            pltpu.VMEM((rows * groups, lines, cache_span), jnp.float32),
            pltpu.SemaphoreType.DMA((10,)),
            pltpu.SemaphoreType.DMA((len(near),)),
        ],
        compiler_params=pltpu.CompilerParams(vmem_limit_bytes=16 << 20),
        cost_estimate=pl.CostEstimate(flops=2 * 67 << 20, bytes_accessed=9 << 20, transcendentals=0),
        name="cache_attention",
    )(*[pltpu.with_memory_space_constraint(x, pltpu.HBM) for x in operands])


def rows_of(ref):
    return jnp.concatenate([ref[s].astype(jnp.float32) for s in range(ref.shape[0])], axis=0)


def pack_kernel(down_ref, up_ref, out_ref, sems):
    share = out_ref.shape[1]
    width = down_ref.shape[2]
    at = pl.ds(pl.multiple_of(lax.axis_index("tp") * share, share), share)
    down = pltpu.make_async_copy(
        down_ref.at[:, at, :], out_ref.at[:, :, pl.ds(0, width)], sems.at[0]
    )
    up = pltpu.make_async_copy(
        up_ref, out_ref.at[:, :, pl.ds(width, up_ref.shape[2])], sems.at[1]
    )
    down.start()
    up.start()
    down.wait()
    up.wait()


def pack_call(down, up):
    kinds, share, columns = up.shape
    return pl.pallas_call(
        pack_kernel,
        out_shape=pltpu.VMEM((kinds, share, down.shape[2] + columns), down.dtype),
        in_specs=[HBM] * 2,
        out_specs=VMEM,
        scratch_shapes=[pltpu.SemaphoreType.DMA((2,))],
        name="pack_factors",
    )(*[pltpu.with_memory_space_constraint(x, pltpu.HBM) for x in (down, up)])


def visiting_kernel(shares, hidden_ref, gain_ref, down_ref, out_ref):
    chunks = hidden_ref.shape[2] // HD
    start = pl.multiple_of(lax.axis_index("wide") * chunks, chunks)
    gain = gain_ref[pl.ds(start, chunks)]
    values = rows_of(hidden_ref)
    scaled = [
        (values[:, i * HD : (i + 1) * HD] * gain[i : i + 1]).astype(jnp.bfloat16)
        for i in range(chunks)
    ]
    kinds, ranks, _ = down_ref.shape
    share = ranks // shares
    down = [
        down_ref[kind, i * share : (i + 1) * share] for i in range(shares) for kind in range(kinds)
    ]
    out_ref[...] = lax.dot_general(
        jnp.concatenate(scaled, axis=1),
        jnp.concatenate(down, axis=0),
        (((1,), (1,)), ((), ())),
        preferred_element_type=jnp.float32,
    )


def visiting_call(shares, hidden, gain, down):
    steps, rows, _ = hidden.shape
    kinds, ranks, _ = down.shape
    return pl.pallas_call(
        functools.partial(visiting_kernel, shares),
        out_shape=pltpu.VMEM((steps * rows, kinds * ranks), jnp.float32),
        in_specs=[VMEM] * 3,
        out_specs=VMEM,
        compiler_params=pltpu.CompilerParams(vmem_limit_bytes=8 << 20),
        name="visiting_rows",
    )(hidden, gain, down)


def inner_kernel(shares, scaled_ref, far_ref, *rest):
    packs, out_ref = rest[:-1], rest[-1]
    me = lax.axis_index("wide")
    kinds, share, pack_width = packs[0].shape
    width = scaled_ref.shape[1] // shares
    total = []
    for offset, pack in enumerate(packs):
        total.append(
            lax.dot_general(
                scaled_ref[:, pl.ds(pl.multiple_of((me ^ offset) * width, width), width)],
                pack[:, :, :width].reshape(kinds * share, width),
                (((1,), (1,)), ((), ())),
                preferred_element_type=jnp.float32,
            )
        )
    total = jnp.concatenate([sum(total[1:], total[0])] * shares, axis=1)
    lane = lax.broadcasted_iota(jnp.int32, total.shape, 1)
    mine = lane // (kinds * share) == lax.axis_index("tp")
    out_ref[...] = jnp.where(mine, total, 0.0) + far_ref[...]


def inner_call(scaled, far, packs):
    return pl.pallas_call(
        functools.partial(inner_kernel, len(packs) + 1),
        out_shape=pltpu.VMEM(far.shape, jnp.float32),
        in_specs=[VMEM] * (2 + len(packs)),
        out_specs=VMEM,
        compiler_params=pltpu.CompilerParams(vmem_limit_bytes=8 << 20),
        name="rank_inner",
    )(scaled, far, *packs)


def scale_kernel(near, far, weight_ref, gain_ref, *rest):
    parts = rest[:-6]
    scaled_out, near_out, far_out, square_out, weight_out, sems = rest[-6:]
    steps, rows, width = parts[0].shape
    chunks = width // HD
    copies = copy_blocks(far, width, weight_ref, weight_out, sems)
    me = lax.axis_index("tp")
    squares = jnp.zeros(square_out.shape, jnp.float32)
    for k, (offset, part) in enumerate(zip(near + far, parts)):
        block = me ^ offset
        gain = gain_ref[pl.ds(pl.multiple_of(block * chunks, chunks), chunks)]
        values = rows_of(part)
        scaled = []
        for i in range(chunks):
            chunk = values[:, i * HD : (i + 1) * HD]
            squares += chunk * chunk
            scaled.append((chunk * gain[i : i + 1]).astype(jnp.bfloat16))
        at = pl.ds(pl.multiple_of(block * width, width), width)
        scaled = jnp.concatenate(scaled, axis=1)
        scaled_out[:, at] = scaled
        out, i = (near_out, k) if k < len(near) else (far_out, k - len(near))
        out[:, i * width : (i + 1) * width] = scaled
    square_out[...] = jnp.broadcast_to(jnp.sum(squares, axis=1, keepdims=True), squares.shape)
    for copy in copies:
        copy.wait()


def scale_call(near, far, weight, gain, parts):
    steps, rows, width = parts[0].shape
    return pl.pallas_call(
        functools.partial(scale_kernel, near, far),
        out_shape=(
            pltpu.VMEM((steps * rows, len(parts) * width), jnp.bfloat16),
            pltpu.VMEM((steps * rows, len(near) * width), jnp.bfloat16),
            pltpu.VMEM((steps * rows, len(far) * width), jnp.bfloat16),
            pltpu.VMEM((steps * rows, HD), jnp.float32),
            pltpu.VMEM((len(far) * width,) + weight.shape[1:], weight.dtype),
        ),
        in_specs=[HBM] + [VMEM] * (1 + len(parts)),
        out_specs=(VMEM,) * 5,
        scratch_shapes=[pltpu.SemaphoreType.DMA((len(far),))],
        compiler_params=pltpu.CompilerParams(vmem_limit_bytes=8 << 20),
        cost_estimate=pl.CostEstimate(flops=0, bytes_accessed=5 << 20, transcendentals=0),
        name="scale_features",
    )(pltpu.with_memory_space_constraint(weight, pltpu.HBM), gain, *parts)


def up_kernel(*refs):
    packs, up_out = refs[:-1], refs[-1]
    kinds, share, _ = packs[0].shape
    columns = up_out.shape[1] // kinds
    me = lax.axis_index("wide") if len(packs) > 1 else 0
    up_out[...] = jnp.zeros_like(up_out)
    for offset, pack in enumerate(packs):
        for kind in range(kinds):
            at = pl.multiple_of(((me ^ offset) * kinds + kind) * share, share)
            up_out[pl.ds(at, share), kind * columns : (kind + 1) * columns] = pack[
                kind, :, pack.shape[2] - columns :
            ]


def final_kernel(width, inner_count, up_count, near_ref, far_ref, square_ref, bias_ref, *rest):
    query_ref, acc_ref, top_ref, total_ref, cos_ref, sin_ref = rest[:6]
    inner_refs = rest[6 : 6 + inner_count]
    packs = rest[6 + inner_count : 6 + inner_count + up_count]
    keys_out, values_out, attended_out, up_ref = rest[6 + inner_count + up_count :]
    up_kernel(*packs, up_ref)
    steps, rows, columns = keys_out.shape
    count = steps * rows
    groups, size, _ = query_ref.shape
    per_group = size // count
    kinds = bias_ref.shape[0]
    row_scale = lax.rsqrt(square_ref[:, :1] * (1.0 / width) + norm_eps)
    inner = inner_refs[0][...]
    for ref in inner_refs[1:]:
        inner = inner + ref[...]
    high = inner.astype(jnp.bfloat16)
    low = (inner - high.astype(jnp.float32)).astype(jnp.bfloat16)
    lora = jnp.dot(
        jnp.concatenate([high, low], axis=0), up_ref[...], preferred_element_type=jnp.float32
    )
    lora = lora[:count] + lora[count:]
    bias = bias_ref[...].astype(jnp.float32)
    linear = []
    for kind in range(kinds):
        base = near_ref[kind] + far_ref[kind]
        part = lora[:, kind * columns : (kind + 1) * columns]
        linear.append((base + adapter_scale * part) * row_scale + bias[kind : kind + 1])
    cosine, sine = cos_ref[...], sin_ref[...]
    line = lax.broadcasted_iota(jnp.int32, (size, count), 0)
    other = lax.broadcasted_iota(jnp.int32, (size, count), 1)
    live = (line % rows == other % rows) & (other // rows <= line // rows % steps)
    for group in range(groups):
        at = slice(group * HD, (group + 1) * HD)
        key = linear[0][:, at]
        key = (key * cosine + pltpu.roll(key, HD // 2, 1) * sine).astype(jnp.bfloat16)
        value = linear[1][:, at].astype(jnp.bfloat16)
        for step in range(steps):
            keys_out[step, :, at] = key[step * rows : (step + 1) * rows]
            values_out[step, :, at] = value[step * rows : (step + 1) * rows]
        scores = lax.dot_general(
            query_ref[group].astype(jnp.bfloat16),
            key,
            (((1,), (1,)), ((), ())),
            preferred_element_type=jnp.float32,
        )
        scores = jnp.where(live, scores * score_scale, masked_score)
        old_top = top_ref[group][:, :1]
        top = jnp.maximum(old_top, jnp.max(scores, axis=1, keepdims=True))
        exps = jnp.exp(scores - top)
        keep = jnp.exp(old_top - top)
        total = total_ref[group][:, :1] * keep + jnp.sum(exps, axis=1, keepdims=True)
        acc = acc_ref[group] * keep + jnp.dot(
            exps.astype(jnp.bfloat16), value, preferred_element_type=jnp.float32
        )
        attended = (acc / total).astype(jnp.bfloat16)
        for head in range(per_group):
            lanes = pl.ds((group * per_group + head) * HD, HD)
            for step in range(steps):
                tile = (head * steps + step) * rows
                attended_out[step, :, lanes] = attended[tile : tile + rows]


def final_call(shape, width, near, far, square, bias, cached, inner, packs):
    steps, rows, query_width = shape
    kinds, _, columns = near.shape
    small = jax.ShapeDtypeStruct((steps, rows, columns), jnp.bfloat16)
    return pl.pallas_call(
        functools.partial(final_kernel, width, len(inner), len(packs)),
        out_shape=(small, small, jax.ShapeDtypeStruct(shape, jnp.bfloat16)),
        in_specs=[VMEM] * (4 + len(cached) + len(inner) + len(packs)),
        out_specs=(VMEM,) * 3,
        scratch_shapes=[pltpu.VMEM((inner[0].shape[1], kinds * columns), jnp.bfloat16)],
        compiler_params=pltpu.CompilerParams(vmem_limit_bytes=8 << 20),
        name="fresh_attention",
    )(near, far, square, bias, *cached, *inner, *packs)


def swap(block, axis, offset, count):
    return lax.ppermute(block, axis, [(i, i ^ offset) for i in range(count)])


def on_device(
    wide_count,
    tp_count,
    hidden,
    input_norm_gain,
    key_value_weight,
    key_value_bias,
    adapter_down_factor,
    adapter_up_factor,
    queries,
    stored_rotated_keys,
    stored_value_rows,
    lengths,
):
    steps, rows, part_width = hidden.shape
    width = part_width * tp_count
    kinds, ranks, down_width = adapter_down_factor.shape
    gain = input_norm_gain.reshape(width // HD, HD)
    up_part = jnp.transpose(adapter_up_factor, (0, 2, 1))
    direct = wide_count == tp_count == 4
    if direct:
        pack = pack_call(adapter_down_factor, up_part)
        second = swap(pack, "wide", 2, wide_count)
        first = swap(pack, "wide", 1, wide_count)
        there = [(3, 15), (12, 0), (6, 9), (9, 6)]
        visitors = lax.ppermute(hidden, ("wide", "tp"), there)
    crossed = swap(hidden, "tp", 2, tp_count)
    beside = swap(hidden, "tp", 1, tp_count)
    near, far = (0, 1), (2, 3)
    near_weight, gain_rows, bias, mine, my_down, *cached = cache_call(
        near,
        lengths,
        queries,
        stored_rotated_keys,
        stored_value_rows,
        gain,
        key_value_bias,
        hidden,
        adapter_down_factor,
        key_value_weight,
    )
    relayed, gain_rows = lax.optimization_barrier((crossed, gain_rows))
    relayed = swap(relayed, "tp", 1, tp_count)
    if direct:
        inner = visiting_call(tp_count, visitors, gain_rows, my_down)
        inner = lax.ppermute(inner, ("wide", "tp"), [(b, a) for a, b in there])
        packs = [pack, first, second, swap(up_part, "wide", 3, wide_count)]
    scaled, near_scaled, far_scaled, square, far_weight = scale_call(
        near, far, key_value_weight, gain_rows, (mine, beside, crossed, relayed)
    )
    if direct:
        inner = inner_call(scaled, inner, packs[:3])
        inner, near_scaled, far_scaled = lax.optimization_barrier(
            (inner, near_scaled, far_scaled)
        )
        inner = [inner] + [swap(inner, "tp", offset, tp_count) for offset in (3, 2, 1)]
    else:
        down = lax.all_gather(adapter_down_factor, "wide", axis=2, tiled=True)
        down = down.reshape(kinds * ranks, width)
        inner = [jnp.einsum("rd,kd->rk", scaled, down, preferred_element_type=jnp.float32)]
        packs = [lax.all_gather(up_part, "wide", axis=1, tiled=True)]
    near_base, far_base = [
        jnp.einsum("md,dkc->kmc", x, y, preferred_element_type=jnp.float32)
        for x, y in ((near_scaled, near_weight), (far_scaled, far_weight))
    ]
    return final_call(
        queries.shape, width, near_base, far_base, square, bias, cached, inner, packs
    )


def solution(mesh):
    in_specs = (
        P(None, ("groups", "wide"), "tp"),
        P(),
        P(None, None, "tp"),
        P(None, "tp"),
        P("groups", None, "wide"),
        P("groups", "tp", "wide"),
        P(None, ("groups", "wide"), "tp"),
        P(("groups", "wide"), None, "tp"),
        P(("groups", "wide"), None, "tp"),
        P(("groups", "wide")),
    )
    out_specs = (
        P(None, ("groups", "wide"), "tp"),
        P(None, ("groups", "wide"), "tp"),
        P(None, ("groups", "wide"), "tp"),
    )
    body = functools.partial(on_device, mesh.shape["wide"], mesh.shape["tp"])
    return jax.shard_map(
        body, mesh=mesh, in_specs=in_specs, out_specs=out_specs, check_vma=False
    )
```

```python
import functools
import math

import jax
import jax.numpy as jnp
from jax import lax
from jax.experimental import pallas as pl
from jax.experimental.pallas import tpu as pltpu
from jax.sharding import PartitionSpec as P

HD = 128


norm_eps = 1e-06
adapter_scale = 2.0
rope_base = 1000000.0
masked_score = -1e30
score_scale = 1.0 / math.sqrt(HD)

VMEM = pl.BlockSpec(memory_space=pltpu.VMEM)
HBM = pl.BlockSpec(memory_space=pltpu.HBM)


def query_block(query_ref, group, per_group):
    steps = query_ref.shape[0]
    tiles = []
    for head in range(per_group):
        at = (group * per_group + head) * HD
        for step in range(steps):
            tiles.append(query_ref[step, :, at : at + HD].astype(jnp.float32))
    return jnp.concatenate(tiles, axis=0)


def copy_blocks(offsets, width, weight_ref, out_ref, sems):
    me = lax.axis_index("tp")
    copies = []
    for i, offset in enumerate(offsets):
        block = pl.ds(pl.multiple_of((me ^ offset) * width, width), width)
        copies.append(
            pltpu.make_async_copy(
                weight_ref.at[block], out_ref.at[pl.ds(i * width, width)], sems.at[i]
            )
        )
        copies[-1].start()
    return copies


def cache_kernel(
    near,
    lengths_ref,
    query_ref,
    key_ref,
    value_ref,
    gain_ref,
    bias_ref,
    hidden_ref,
    weight_ref,
    near_out,
    gain_out,
    bias_out,
    hidden_out,
    query_out,
    acc_out,
    top_out,
    total_out,
    cos_out,
    sin_out,
    lengths,
    queries,
    gain_buffer,
    key_buffer,
    value_buffer,
    score_buffer,
    sems,
    weight_sems,
):
    steps, rows, query_width = query_ref.shape
    cache_span = key_ref.shape[1]
    groups = key_ref.shape[2] // HD
    per_group = query_width // HD // groups
    lines = steps * per_group
    half_rows = rows // 2
    halves = [pl.ds(0, half_rows), pl.ds(half_rows, half_rows)]
    copies = [
        (lengths_ref, lengths),
        (query_ref, queries),
        (key_ref.at[halves[0]], key_buffer.at[halves[0]]),
        (key_ref.at[halves[1]], key_buffer.at[halves[1]]),
        (value_ref.at[halves[0]], value_buffer.at[halves[0]]),
        (value_ref.at[halves[1]], value_buffer.at[halves[1]]),
        (gain_ref, gain_buffer),
        (bias_ref, bias_out),
        (hidden_ref, hidden_out),
    ]
    copies = [pltpu.make_async_copy(*pair, sems.at[i]) for i, pair in enumerate(copies)]
    for copy in copies:
        copy.start()
    copies += copy_blocks(near, hidden_ref.shape[2], weight_ref, near_out, weight_sems)

    copies[0].wait()
    lane = lax.broadcasted_iota(jnp.int32, (rows, HD), 1)
    half = HD // 2
    second = lane >= half
    index = jnp.where(second, lane - half, lane).astype(jnp.float32)
    inv_freq = jnp.exp(index * (-2.0 * math.log(rope_base) / HD))
    row_index = lax.broadcasted_iota(jnp.int32, (rows, HD), 0)
    row_lengths = jnp.zeros((rows, HD), jnp.int32)
    for row in range(rows):
        row_lengths = jnp.where(row_index == row, lengths[row], row_lengths)
    for step in range(steps):
        angles = (row_lengths + step).astype(jnp.float32) * inv_freq
        sine = jnp.sin(angles)
        cos_out[pl.ds(step * rows, rows)] = jnp.cos(angles)
        sin_out[pl.ds(step * rows, rows)] = jnp.where(second, sine, -sine)
    copies[1].wait()
    for group in range(groups):
        query_out[group] = query_block(queries, group, per_group)

    place = lax.broadcasted_iota(jnp.int32, (lines, cache_span), 1)
    for i in range(2):
        copies[2 + i].wait()
        for row in range(i * half_rows, (i + 1) * half_rows):
            for group in range(groups):
                query = query_out[group, pl.ds(row, lines, stride=rows), :].astype(jnp.bfloat16)
                score_buffer[row * groups + group] = lax.dot_general(
                    query,
                    key_buffer[row, :, pl.ds(group * HD, HD)],
                    (((1,), (1,)), ((), ())),
                    preferred_element_type=jnp.float32,
                )
    for i in range(2):
        copies[4 + i].wait()
        for row in range(i * half_rows, (i + 1) * half_rows):
            live = place < lengths[row]
            for group in range(groups):
                mine = pl.ds(row, lines, stride=rows)
                scores = score_buffer[row * groups + group]
                scores = jnp.where(live, scores * score_scale, masked_score)
                top = jnp.max(scores, axis=1, keepdims=True)
                exps = jnp.exp(scores - top)
                total = jnp.sum(exps, axis=1, keepdims=True)
                acc = jnp.dot(
                    exps.astype(jnp.bfloat16),
                    value_buffer[row, :, pl.ds(group * HD, HD)],
                    preferred_element_type=jnp.float32,
                )
                acc_out[group, mine, :] = acc
                top_out[group, mine, :] = jnp.broadcast_to(top, acc.shape)
                total_out[group, mine, :] = jnp.broadcast_to(total, acc.shape)
    copies[6].wait()
    gain_out[...] = gain_buffer[...].astype(jnp.float32)
    for copy in copies[7:]:
        copy.wait()


def cache_call(near, lengths, queries, keys, values, gain, bias, hidden, weight):
    steps, rows, query_width = queries.shape
    cache_span, key_width = keys.shape[1:]
    groups = key_width // HD
    lines = steps * (query_width // key_width)
    block = (groups, lines * rows, HD)
    table = (steps * rows, HD)
    operands = (lengths, queries, keys, values, gain, bias, hidden, weight)
    part = hidden.shape[2]
    return pl.pallas_call(
        functools.partial(cache_kernel, near),
        out_shape=(
            pltpu.VMEM((len(near) * part,) + weight.shape[1:], weight.dtype),
            pltpu.VMEM(gain.shape, jnp.float32),
            pltpu.VMEM(bias.shape, bias.dtype),
            pltpu.VMEM(hidden.shape, hidden.dtype),
            pltpu.VMEM(block, jnp.float32),
            pltpu.VMEM(block, jnp.float32),
            pltpu.VMEM(block, jnp.float32),
            pltpu.VMEM(block, jnp.float32),
            pltpu.VMEM(table, jnp.float32),
            pltpu.VMEM(table, jnp.float32),
        ),
        in_specs=[HBM] * len(operands),
        out_specs=(VMEM,) * 10,
        scratch_shapes=[
            pltpu.SMEM(lengths.shape, jnp.int32),
            pltpu.VMEM(queries.shape, queries.dtype),
            pltpu.VMEM(gain.shape, gain.dtype),
            pltpu.VMEM(keys.shape, keys.dtype),
            pltpu.VMEM(values.shape, values.dtype),
            pltpu.VMEM((rows * groups, lines, cache_span), jnp.float32),
            pltpu.SemaphoreType.DMA((9,)),
            pltpu.SemaphoreType.DMA((len(near),)),
        ],
        compiler_params=pltpu.CompilerParams(vmem_limit_bytes=16 << 20),
        cost_estimate=pl.CostEstimate(flops=2 * 67 << 20, bytes_accessed=9 << 20, transcendentals=0),
        name="cache_attention",
    )(*[pltpu.with_memory_space_constraint(x, pltpu.HBM) for x in operands])


def rows_of(ref):
    return jnp.concatenate([ref[s].astype(jnp.float32) for s in range(ref.shape[0])], axis=0)


def pack_kernel(down_ref, up_ref, out_ref, sems):
    share = out_ref.shape[1]
    width = down_ref.shape[2]
    at = pl.ds(pl.multiple_of(lax.axis_index("tp") * share, share), share)
    down = pltpu.make_async_copy(
        down_ref.at[:, at, :], out_ref.at[:, :, pl.ds(0, width)], sems.at[0]
    )
    up = pltpu.make_async_copy(
        up_ref, out_ref.at[:, :, pl.ds(width, up_ref.shape[2])], sems.at[1]
    )
    down.start()
    up.start()
    down.wait()
    up.wait()


def pack_call(down, up):
    kinds, share, columns = up.shape
    return pl.pallas_call(
        pack_kernel,
        out_shape=pltpu.VMEM((kinds, share, down.shape[2] + columns), down.dtype),
        in_specs=[HBM] * 2,
        out_specs=VMEM,
        scratch_shapes=[pltpu.SemaphoreType.DMA((2,))],
        name="pack_factors",
    )(*[pltpu.with_memory_space_constraint(x, pltpu.HBM) for x in (down, up)])


def inner_kernel(scaled_ref, *rest):
    packs, out_ref = rest[:-1], rest[-1]
    me = lax.axis_index("wide")
    shares = len(packs)
    kinds, share, _ = packs[0].shape
    width = scaled_ref.shape[1] // shares
    total = []
    for offset, pack in enumerate(packs):
        total.append(
            lax.dot_general(
                scaled_ref[:, pl.ds(pl.multiple_of((me ^ offset) * width, width), width)],
                pack[:, :, :width].reshape(kinds * share, width),
                (((1,), (1,)), ((), ())),
                preferred_element_type=jnp.float32,
            )
        )
    total = jnp.concatenate([sum(total[1:], total[0])] * shares, axis=1)
    lane = lax.broadcasted_iota(jnp.int32, total.shape, 1)
    out_ref[...] = jnp.where(lane // (kinds * share) == lax.axis_index("tp"), total, 0.0)


def inner_call(scaled, packs):
    kinds, share, _ = packs[0].shape
    return pl.pallas_call(
        inner_kernel,
        out_shape=pltpu.VMEM((scaled.shape[0], len(packs) * kinds * share), jnp.float32),
        in_specs=[VMEM] * (1 + len(packs)),
        out_specs=VMEM,
        compiler_params=pltpu.CompilerParams(vmem_limit_bytes=8 << 20),
        name="rank_inner",
    )(scaled, *packs)


def scale_kernel(near, far, weight_ref, gain_ref, *rest):
    parts = rest[:-6]
    scaled_out, near_out, far_out, square_out, weight_out, sems = rest[-6:]
    steps, rows, width = parts[0].shape
    chunks = width // HD
    copies = copy_blocks(far, width, weight_ref, weight_out, sems)
    me = lax.axis_index("tp")
    squares = jnp.zeros(square_out.shape, jnp.float32)
    for k, (offset, part) in enumerate(zip(near + far, parts)):
        block = me ^ offset
        gain = gain_ref[pl.ds(pl.multiple_of(block * chunks, chunks), chunks)]
        values = rows_of(part)
        scaled = []
        for i in range(chunks):
            chunk = values[:, i * HD : (i + 1) * HD]
            squares += chunk * chunk
            scaled.append((chunk * gain[i : i + 1]).astype(jnp.bfloat16))
        at = pl.ds(pl.multiple_of(block * width, width), width)
        scaled = jnp.concatenate(scaled, axis=1)
        scaled_out[:, at] = scaled
        out, i = (near_out, k) if k < len(near) else (far_out, k - len(near))
        out[:, i * width : (i + 1) * width] = scaled
    square_out[...] = jnp.broadcast_to(jnp.sum(squares, axis=1, keepdims=True), squares.shape)
    for copy in copies:
        copy.wait()


def scale_call(near, far, weight, gain, parts):
    steps, rows, width = parts[0].shape
    return pl.pallas_call(
        functools.partial(scale_kernel, near, far),
        out_shape=(
            pltpu.VMEM((steps * rows, len(parts) * width), jnp.bfloat16),
            pltpu.VMEM((steps * rows, len(near) * width), jnp.bfloat16),
            pltpu.VMEM((steps * rows, len(far) * width), jnp.bfloat16),
            pltpu.VMEM((steps * rows, HD), jnp.float32),
            pltpu.VMEM((len(far) * width,) + weight.shape[1:], weight.dtype),
        ),
        in_specs=[HBM] + [VMEM] * (1 + len(parts)),
        out_specs=(VMEM,) * 5,
        scratch_shapes=[pltpu.SemaphoreType.DMA((len(far),))],
        compiler_params=pltpu.CompilerParams(vmem_limit_bytes=8 << 20),
        cost_estimate=pl.CostEstimate(flops=0, bytes_accessed=5 << 20, transcendentals=0),
        name="scale_features",
    )(pltpu.with_memory_space_constraint(weight, pltpu.HBM), gain, *parts)


def up_kernel(*refs):
    packs, up_out = refs[:-1], refs[-1]
    kinds, share, pack_width = packs[0].shape
    columns = up_out.shape[1] // kinds
    me = lax.axis_index("wide") if len(packs) > 1 else 0
    up_out[...] = jnp.zeros_like(up_out)
    for offset, pack in enumerate(packs):
        for kind in range(kinds):
            at = pl.multiple_of(((me ^ offset) * kinds + kind) * share, share)
            up_out[pl.ds(at, share), kind * columns : (kind + 1) * columns] = pack[
                kind, :, pack_width - columns :
            ]


def final_kernel(width, inner_count, up_count, near_ref, far_ref, square_ref, bias_ref, *rest):
    query_ref, acc_ref, top_ref, total_ref, cos_ref, sin_ref = rest[:6]
    inner_refs = rest[6 : 6 + inner_count]
    packs = rest[6 + inner_count : 6 + inner_count + up_count]
    keys_out, values_out, attended_out, up_ref = rest[6 + inner_count + up_count :]
    up_kernel(*packs, up_ref)
    steps, rows, columns = keys_out.shape
    count = steps * rows
    groups, size, _ = query_ref.shape
    per_group = size // count
    kinds = bias_ref.shape[0]
    row_scale = lax.rsqrt(square_ref[:, :1] * (1.0 / width) + norm_eps)
    inner = inner_refs[0][...]
    for ref in inner_refs[1:]:
        inner = inner + ref[...]
    high = inner.astype(jnp.bfloat16)
    low = (inner - high.astype(jnp.float32)).astype(jnp.bfloat16)
    lora = jnp.dot(
        jnp.concatenate([high, low], axis=0), up_ref[...], preferred_element_type=jnp.float32
    )
    lora = lora[:count] + lora[count:]
    bias = bias_ref[...].astype(jnp.float32)
    linear = []
    for kind in range(kinds):
        base = near_ref[kind] + far_ref[kind]
        part = lora[:, kind * columns : (kind + 1) * columns]
        linear.append((base + adapter_scale * part) * row_scale + bias[kind : kind + 1])
    cosine, sine = cos_ref[...], sin_ref[...]
    line = lax.broadcasted_iota(jnp.int32, (size, count), 0)
    other = lax.broadcasted_iota(jnp.int32, (size, count), 1)
    live = (line % rows == other % rows) & (other // rows <= line // rows % steps)
    for group in range(groups):
        at = slice(group * HD, (group + 1) * HD)
        key = linear[0][:, at]
        key = (key * cosine + pltpu.roll(key, HD // 2, 1) * sine).astype(jnp.bfloat16)
        value = linear[1][:, at].astype(jnp.bfloat16)
        for step in range(steps):
            keys_out[step, :, at] = key[step * rows : (step + 1) * rows]
            values_out[step, :, at] = value[step * rows : (step + 1) * rows]
        scores = lax.dot_general(
            query_ref[group].astype(jnp.bfloat16),
            key,
            (((1,), (1,)), ((), ())),
            preferred_element_type=jnp.float32,
        )
        scores = jnp.where(live, scores * score_scale, masked_score)
        old_top = top_ref[group][:, :1]
        top = jnp.maximum(old_top, jnp.max(scores, axis=1, keepdims=True))
        exps = jnp.exp(scores - top)
        keep = jnp.exp(old_top - top)
        total = total_ref[group][:, :1] * keep + jnp.sum(exps, axis=1, keepdims=True)
        acc = acc_ref[group] * keep + jnp.dot(
            exps.astype(jnp.bfloat16), value, preferred_element_type=jnp.float32
        )
        attended = (acc / total).astype(jnp.bfloat16)
        for head in range(per_group):
            lanes = pl.ds((group * per_group + head) * HD, HD)
            for step in range(steps):
                tile = (head * steps + step) * rows
                attended_out[step, :, lanes] = attended[tile : tile + rows]


def final_call(shape, width, near, far, square, bias, cached, inner, packs):
    steps, rows, query_width = shape
    kinds, _, columns = near.shape
    small = jax.ShapeDtypeStruct((steps, rows, columns), jnp.bfloat16)
    return pl.pallas_call(
        functools.partial(final_kernel, width, len(inner), len(packs)),
        out_shape=(small, small, jax.ShapeDtypeStruct(shape, jnp.bfloat16)),
        in_specs=[VMEM] * (4 + len(cached) + len(inner) + len(packs)),
        out_specs=(VMEM,) * 3,
        scratch_shapes=[pltpu.VMEM((inner[0].shape[1], kinds * columns), jnp.bfloat16)],
        compiler_params=pltpu.CompilerParams(vmem_limit_bytes=8 << 20),
        name="fresh_attention",
    )(near, far, square, bias, *cached, *inner, *packs)


def dot(rows, weight):
    return jnp.einsum("md,dkc->kmc", rows, weight, preferred_element_type=jnp.float32)


def swap(block, axis, offset, count):
    return lax.ppermute(block, axis, [(i, i ^ offset) for i in range(count)])


def on_device(
    wide_count,
    tp_count,
    hidden,
    input_norm_gain,
    key_value_weight,
    key_value_bias,
    adapter_down_factor,
    adapter_up_factor,
    queries,
    stored_rotated_keys,
    stored_value_rows,
    lengths,
):
    steps, rows, part_width = hidden.shape
    width = part_width * tp_count
    kinds, ranks, down_width = adapter_down_factor.shape
    gain = input_norm_gain.reshape(width // HD, HD)
    up_part = jnp.transpose(adapter_up_factor, (0, 2, 1))
    direct = wide_count == tp_count == 4
    tp_parts = [swap(hidden, "tp", offset, tp_count) for offset in (1, 2, 3)]
    if direct:
        pack = pack_call(adapter_down_factor, up_part)
        second = swap(pack, "wide", 2, wide_count)
        first = swap(pack, "wide", 1, wide_count)
    near, far = (0, 1), (2, 3)
    near_weight, gain_rows, bias, mine, *cached = cache_call(
        near,
        lengths,
        queries,
        stored_rotated_keys,
        stored_value_rows,
        gain,
        key_value_bias,
        hidden,
        key_value_weight,
    )
    if direct:
        third, gain_rows = lax.optimization_barrier((second, gain_rows))
        packs = [pack, first, second, swap(third, "wide", 1, wide_count)]
    scaled, near_scaled, far_scaled, square, far_weight = scale_call(
        near, far, key_value_weight, gain_rows, [mine] + tp_parts
    )
    if direct:
        near_base = dot(near_scaled, near_weight)
        scaled, near_base = lax.optimization_barrier((scaled, near_base))
        inner = inner_call(scaled, packs)
        inner = inner + swap(inner, "tp", 1, tp_count)
        inner, far_scaled = lax.optimization_barrier((inner, far_scaled))
        inner = [inner, swap(inner, "tp", 2, tp_count)]
    else:
        near_base = dot(near_scaled, near_weight)
        down = lax.all_gather(adapter_down_factor, "wide", axis=2, tiled=True)
        down = down.reshape(kinds * ranks, width)
        inner = [jnp.einsum("rd,kd->rk", scaled, down, preferred_element_type=jnp.float32)]
        packs = [lax.all_gather(up_part, "wide", axis=1, tiled=True)]
    far_base = dot(far_scaled, far_weight)
    return final_call(
        queries.shape, width, near_base, far_base, square, bias, cached, inner, packs
    )


def solution(mesh):
    in_specs = (
        P(None, ("groups", "wide"), "tp"),
        P(),
        P(None, None, "tp"),
        P(None, "tp"),
        P("groups", None, "wide"),
        P("groups", "tp", "wide"),
        P(None, ("groups", "wide"), "tp"),
        P(("groups", "wide"), None, "tp"),
        P(("groups", "wide"), None, "tp"),
        P(("groups", "wide")),
    )
    out_specs = (
        P(None, ("groups", "wide"), "tp"),
        P(None, ("groups", "wide"), "tp"),
        P(None, ("groups", "wide"), "tp"),
    )
    body = functools.partial(on_device, mesh.shape["wide"], mesh.shape["tp"])
    return jax.shard_map(
        body, mesh=mesh, in_specs=in_specs, out_specs=out_specs, check_vma=False
    )
```

```python
import functools
import math

import jax
import jax.numpy as jnp
from jax import lax
from jax.experimental import pallas as pl
from jax.experimental.pallas import tpu as pltpu
from jax.sharding import PartitionSpec as P

HD = 128


norm_eps = 1e-06
adapter_scale = 2.0
rope_base = 1000000.0
masked_score = -1e30
score_scale = 1.0 / math.sqrt(HD)

VMEM = pl.BlockSpec(memory_space=pltpu.VMEM)
HBM = pl.BlockSpec(memory_space=pltpu.HBM)


def query_block(query_ref, group, per_group):
    steps = query_ref.shape[0]
    tiles = []
    for head in range(per_group):
        at = (group * per_group + head) * HD
        for step in range(steps):
            tiles.append(query_ref[step, :, at : at + HD].astype(jnp.float32))
    return jnp.concatenate(tiles, axis=0)


def copy_blocks(offsets, width, weight_ref, out_ref, sems):
    me = lax.axis_index("tp")
    copies = []
    for i, offset in enumerate(offsets):
        block = pl.ds(pl.multiple_of((me ^ offset) * width, width), width)
        copies.append(
            pltpu.make_async_copy(
                weight_ref.at[block], out_ref.at[pl.ds(i * width, width)], sems.at[i]
            )
        )
        copies[-1].start()
    return copies


def cache_kernel(
    near,
    lengths_ref,
    query_ref,
    key_ref,
    value_ref,
    gain_ref,
    bias_ref,
    hidden_ref,
    weight_ref,
    near_out,
    gain_out,
    bias_out,
    hidden_out,
    query_out,
    acc_out,
    top_out,
    total_out,
    cos_out,
    sin_out,
    lengths,
    queries,
    gain_buffer,
    key_buffer,
    value_buffer,
    score_buffer,
    sems,
    weight_sems,
):
    steps, rows, query_width = query_ref.shape
    cache_span = key_ref.shape[1]
    groups = key_ref.shape[2] // HD
    per_group = query_width // HD // groups
    lines = steps * per_group
    half_rows = rows // 2
    halves = [pl.ds(0, half_rows), pl.ds(half_rows, half_rows)]
    copies = [
        (lengths_ref, lengths),
        (query_ref, queries),
        (key_ref.at[halves[0]], key_buffer.at[halves[0]]),
        (key_ref.at[halves[1]], key_buffer.at[halves[1]]),
        (value_ref.at[halves[0]], value_buffer.at[halves[0]]),
        (value_ref.at[halves[1]], value_buffer.at[halves[1]]),
        (gain_ref, gain_buffer),
        (bias_ref, bias_out),
        (hidden_ref, hidden_out),
    ]
    copies = [pltpu.make_async_copy(*pair, sems.at[i]) for i, pair in enumerate(copies)]
    for copy in copies:
        copy.start()
    copies += copy_blocks(near, hidden_ref.shape[2], weight_ref, near_out, weight_sems)

    copies[0].wait()
    lane = lax.broadcasted_iota(jnp.int32, (rows, HD), 1)
    half = HD // 2
    second = lane >= half
    index = jnp.where(second, lane - half, lane).astype(jnp.float32)
    inv_freq = jnp.exp(index * (-2.0 * math.log(rope_base) / HD))
    row_index = lax.broadcasted_iota(jnp.int32, (rows, HD), 0)
    row_lengths = jnp.zeros((rows, HD), jnp.int32)
    for row in range(rows):
        row_lengths = jnp.where(row_index == row, lengths[row], row_lengths)
    for step in range(steps):
        angles = (row_lengths + step).astype(jnp.float32) * inv_freq
        sine = jnp.sin(angles)
        cos_out[pl.ds(step * rows, rows)] = jnp.cos(angles)
        sin_out[pl.ds(step * rows, rows)] = jnp.where(second, sine, -sine)
    copies[1].wait()
    for group in range(groups):
        query_out[group] = query_block(queries, group, per_group)

    place = lax.broadcasted_iota(jnp.int32, (lines, cache_span), 1)
    for i in range(2):
        copies[2 + i].wait()
        for row in range(i * half_rows, (i + 1) * half_rows):
            for group in range(groups):
                query = query_out[group, pl.ds(row, lines, stride=rows), :].astype(jnp.bfloat16)
                score_buffer[row * groups + group] = lax.dot_general(
                    query,
                    key_buffer[row, :, pl.ds(group * HD, HD)],
                    (((1,), (1,)), ((), ())),
                    preferred_element_type=jnp.float32,
                )
    for i in range(2):
        copies[4 + i].wait()
        for row in range(i * half_rows, (i + 1) * half_rows):
            live = place < lengths[row]
            for group in range(groups):
                mine = pl.ds(row, lines, stride=rows)
                scores = score_buffer[row * groups + group]
                scores = jnp.where(live, scores * score_scale, masked_score)
                top = jnp.max(scores, axis=1, keepdims=True)
                exps = jnp.exp(scores - top)
                total = jnp.sum(exps, axis=1, keepdims=True)
                acc = jnp.dot(
                    exps.astype(jnp.bfloat16),
                    value_buffer[row, :, pl.ds(group * HD, HD)],
                    preferred_element_type=jnp.float32,
                )
                acc_out[group, mine, :] = acc
                top_out[group, mine, :] = jnp.broadcast_to(top, acc.shape)
                total_out[group, mine, :] = jnp.broadcast_to(total, acc.shape)
    copies[6].wait()
    gain_out[...] = gain_buffer[...].astype(jnp.float32)
    for copy in copies[7:]:
        copy.wait()


def cache_call(near, lengths, queries, keys, values, gain, bias, hidden, weight):
    steps, rows, query_width = queries.shape
    cache_span, key_width = keys.shape[1:]
    groups = key_width // HD
    lines = steps * (query_width // key_width)
    block = (groups, lines * rows, HD)
    table = (steps * rows, HD)
    operands = (lengths, queries, keys, values, gain, bias, hidden, weight)
    part = hidden.shape[2]
    return pl.pallas_call(
        functools.partial(cache_kernel, near),
        out_shape=(
            pltpu.VMEM((len(near) * part,) + weight.shape[1:], weight.dtype),
            pltpu.VMEM(gain.shape, jnp.float32),
            pltpu.VMEM(bias.shape, bias.dtype),
            pltpu.VMEM(hidden.shape, hidden.dtype),
            pltpu.VMEM(block, jnp.float32),
            pltpu.VMEM(block, jnp.float32),
            pltpu.VMEM(block, jnp.float32),
            pltpu.VMEM(block, jnp.float32),
            pltpu.VMEM(table, jnp.float32),
            pltpu.VMEM(table, jnp.float32),
        ),
        in_specs=[HBM] * len(operands),
        out_specs=(VMEM,) * 10,
        scratch_shapes=[
            pltpu.SMEM(lengths.shape, jnp.int32),
            pltpu.VMEM(queries.shape, queries.dtype),
            pltpu.VMEM(gain.shape, gain.dtype),
            pltpu.VMEM(keys.shape, keys.dtype),
            pltpu.VMEM(values.shape, values.dtype),
            pltpu.VMEM((rows * groups, lines, cache_span), jnp.float32),
            pltpu.SemaphoreType.DMA((9,)),
            pltpu.SemaphoreType.DMA((len(near),)),
        ],
        compiler_params=pltpu.CompilerParams(vmem_limit_bytes=16 << 20),
        cost_estimate=pl.CostEstimate(flops=2 * 67 << 20, bytes_accessed=9 << 20, transcendentals=0),
        name="cache_attention",
    )(*[pltpu.with_memory_space_constraint(x, pltpu.HBM) for x in operands])


def rows_of(ref):
    return jnp.concatenate([ref[s].astype(jnp.float32) for s in range(ref.shape[0])], axis=0)


def pack_kernel(down_ref, up_ref, out_ref, sems):
    share = out_ref.shape[1]
    width = down_ref.shape[2]
    at = pl.ds(pl.multiple_of(lax.axis_index("tp") * share, share), share)
    down = pltpu.make_async_copy(
        down_ref.at[:, at, :], out_ref.at[:, :, pl.ds(0, width)], sems.at[0]
    )
    up = pltpu.make_async_copy(
        up_ref, out_ref.at[:, :, pl.ds(width, up_ref.shape[2])], sems.at[1]
    )
    down.start()
    up.start()
    down.wait()
    up.wait()


def pack_call(down, up):
    kinds, share, columns = up.shape
    return pl.pallas_call(
        pack_kernel,
        out_shape=pltpu.VMEM((kinds, share, down.shape[2] + columns), down.dtype),
        in_specs=[HBM] * 2,
        out_specs=VMEM,
        scratch_shapes=[pltpu.SemaphoreType.DMA((2,))],
        name="pack_factors",
    )(*[pltpu.with_memory_space_constraint(x, pltpu.HBM) for x in (down, up)])


def inner_kernel(scaled_ref, *rest):
    packs, out_ref = rest[:-1], rest[-1]
    me = lax.axis_index("wide")
    width = scaled_ref.shape[1] // len(packs)
    total = []
    for offset, pack in enumerate(packs):
        total.append(
            lax.dot_general(
                scaled_ref[:, pl.ds(pl.multiple_of((me ^ offset) * width, width), width)],
                pack[:, :, :width].reshape(out_ref.shape[1], width),
                (((1,), (1,)), ((), ())),
                preferred_element_type=jnp.float32,
            )
        )
    out_ref[...] = sum(total[1:], total[0])


def inner_call(scaled, packs):
    kinds, share, _ = packs[0].shape
    return pl.pallas_call(
        inner_kernel,
        out_shape=jax.ShapeDtypeStruct((scaled.shape[0], kinds * share), jnp.float32),
        in_specs=[VMEM] * (1 + len(packs)),
        out_specs=VMEM,
        compiler_params=pltpu.CompilerParams(vmem_limit_bytes=8 << 20),
        name="rank_inner",
    )(scaled, *packs)


def scale_kernel(near, far, weight_ref, gain_ref, *rest):
    parts = rest[:-6]
    scaled_out, near_out, far_out, square_out, weight_out, sems = rest[-6:]
    steps, rows, width = parts[0].shape
    chunks = width // HD
    copies = copy_blocks(far, width, weight_ref, weight_out, sems)
    me = lax.axis_index("tp")
    squares = jnp.zeros(square_out.shape, jnp.float32)
    for k, (offset, part) in enumerate(zip(near + far, parts)):
        block = me ^ offset
        gain = gain_ref[pl.ds(pl.multiple_of(block * chunks, chunks), chunks)]
        values = rows_of(part)
        scaled = []
        for i in range(chunks):
            chunk = values[:, i * HD : (i + 1) * HD]
            squares += chunk * chunk
            scaled.append((chunk * gain[i : i + 1]).astype(jnp.bfloat16))
        at = pl.ds(pl.multiple_of(block * width, width), width)
        scaled = jnp.concatenate(scaled, axis=1)
        scaled_out[:, at] = scaled
        out, i = (near_out, k) if k < len(near) else (far_out, k - len(near))
        out[:, i * width : (i + 1) * width] = scaled
    square_out[...] = jnp.broadcast_to(jnp.sum(squares, axis=1, keepdims=True), squares.shape)
    for copy in copies:
        copy.wait()


def scale_call(near, far, weight, gain, parts):
    steps, rows, width = parts[0].shape
    return pl.pallas_call(
        functools.partial(scale_kernel, near, far),
        out_shape=(
            pltpu.VMEM((steps * rows, len(parts) * width), jnp.bfloat16),
            pltpu.VMEM((steps * rows, len(near) * width), jnp.bfloat16),
            pltpu.VMEM((steps * rows, len(far) * width), jnp.bfloat16),
            pltpu.VMEM((steps * rows, HD), jnp.float32),
            pltpu.VMEM((len(far) * width,) + weight.shape[1:], weight.dtype),
        ),
        in_specs=[HBM] + [VMEM] * (1 + len(parts)),
        out_specs=(VMEM,) * 5,
        scratch_shapes=[pltpu.SemaphoreType.DMA((len(far),))],
        compiler_params=pltpu.CompilerParams(vmem_limit_bytes=8 << 20),
        cost_estimate=pl.CostEstimate(flops=0, bytes_accessed=5 << 20, transcendentals=0),
        name="scale_features",
    )(pltpu.with_memory_space_constraint(weight, pltpu.HBM), gain, *parts)


def up_kernel(*refs):
    packs, up_out = refs[:-1], refs[-1]
    kinds, share, pack_width = packs[0].shape
    columns = up_out.shape[1] // kinds
    me = lax.axis_index("wide") if len(packs) > 1 else 0
    up_out[...] = jnp.zeros_like(up_out)
    for offset, pack in enumerate(packs):
        for kind in range(kinds):
            at = pl.multiple_of(((me ^ offset) * kinds + kind) * share, share)
            up_out[pl.ds(at, share), kind * columns : (kind + 1) * columns] = pack[
                kind, :, pack_width - columns :
            ]


def final_kernel(width, blocks, near_ref, far_ref, square_ref, bias_ref, *rest):
    query_ref, acc_ref, top_ref, total_ref, cos_ref, sin_ref = rest[:6]
    inner_refs = rest[6 : 6 + blocks]
    packs = rest[6 + blocks : 6 + 2 * blocks]
    keys_out, values_out, attended_out, inner_buffer, up_ref = rest[6 + 2 * blocks :]
    up_kernel(*packs, up_ref)
    steps, rows, columns = keys_out.shape
    count = steps * rows
    groups, size, _ = query_ref.shape
    per_group = size // count
    kinds = bias_ref.shape[0]
    row_scale = lax.rsqrt(square_ref[:, :1] * (1.0 / width) + norm_eps)
    me = lax.axis_index("tp") if blocks > 1 else 0
    for i in range(blocks):
        inner_buffer[me ^ i] = inner_refs[i][...]
    inner = jnp.concatenate([inner_buffer[i] for i in range(blocks)], axis=1)
    high = inner.astype(jnp.bfloat16)
    low = (inner - high.astype(jnp.float32)).astype(jnp.bfloat16)
    lora = jnp.dot(
        jnp.concatenate([high, low], axis=0), up_ref[...], preferred_element_type=jnp.float32
    )
    lora = lora[:count] + lora[count:]
    bias = bias_ref[...].astype(jnp.float32)
    linear = []
    for kind in range(kinds):
        base = near_ref[kind] + far_ref[kind]
        part = lora[:, kind * columns : (kind + 1) * columns]
        linear.append((base + adapter_scale * part) * row_scale + bias[kind : kind + 1])
    cosine, sine = cos_ref[...], sin_ref[...]
    line = lax.broadcasted_iota(jnp.int32, (size, count), 0)
    other = lax.broadcasted_iota(jnp.int32, (size, count), 1)
    live = (line % rows == other % rows) & (other // rows <= line // rows % steps)
    for group in range(groups):
        at = slice(group * HD, (group + 1) * HD)
        key = linear[0][:, at]
        key = (key * cosine + pltpu.roll(key, HD // 2, 1) * sine).astype(jnp.bfloat16)
        value = linear[1][:, at].astype(jnp.bfloat16)
        for step in range(steps):
            keys_out[step, :, at] = key[step * rows : (step + 1) * rows]
            values_out[step, :, at] = value[step * rows : (step + 1) * rows]
        scores = lax.dot_general(
            query_ref[group].astype(jnp.bfloat16),
            key,
            (((1,), (1,)), ((), ())),
            preferred_element_type=jnp.float32,
        )
        scores = jnp.where(live, scores * score_scale, masked_score)
        old_top = top_ref[group][:, :1]
        top = jnp.maximum(old_top, jnp.max(scores, axis=1, keepdims=True))
        exps = jnp.exp(scores - top)
        keep = jnp.exp(old_top - top)
        total = total_ref[group][:, :1] * keep + jnp.sum(exps, axis=1, keepdims=True)
        acc = acc_ref[group] * keep + jnp.dot(
            exps.astype(jnp.bfloat16), value, preferred_element_type=jnp.float32
        )
        attended = (acc / total).astype(jnp.bfloat16)
        for head in range(per_group):
            lanes = pl.ds((group * per_group + head) * HD, HD)
            for step in range(steps):
                tile = (head * steps + step) * rows
                attended_out[step, :, lanes] = attended[tile : tile + rows]


def final_call(shape, width, near, far, square, bias, cached, inner, packs):
    steps, rows, query_width = shape
    kinds, share, _ = packs[0].shape
    columns = near.shape[2]
    small = jax.ShapeDtypeStruct((steps, rows, columns), jnp.bfloat16)
    return pl.pallas_call(
        functools.partial(final_kernel, width, len(inner)),
        out_shape=(small, small, jax.ShapeDtypeStruct(shape, jnp.bfloat16)),
        in_specs=[VMEM] * (4 + len(cached) + len(inner) + len(packs)),
        out_specs=(VMEM,) * 3,
        scratch_shapes=[
            pltpu.VMEM((len(inner),) + inner[0].shape, jnp.float32),
            pltpu.VMEM((len(packs) * kinds * share, kinds * columns), jnp.bfloat16),
        ],
        compiler_params=pltpu.CompilerParams(vmem_limit_bytes=8 << 20),
        name="fresh_attention",
    )(near, far, square, bias, *cached, *inner, *packs)


def swap(block, axis, offset, count):
    return lax.ppermute(block, axis, [(i, i ^ offset) for i in range(count)])


def on_device(
    wide_count,
    tp_count,
    hidden,
    input_norm_gain,
    key_value_weight,
    key_value_bias,
    adapter_down_factor,
    adapter_up_factor,
    queries,
    stored_rotated_keys,
    stored_value_rows,
    lengths,
):
    steps, rows, part_width = hidden.shape
    width = part_width * tp_count
    kinds, ranks, down_width = adapter_down_factor.shape
    gain = input_norm_gain.reshape(width // HD, HD)
    up_part = jnp.transpose(adapter_up_factor, (0, 2, 1))
    direct = wide_count == tp_count == 4
    if direct:
        pack = pack_call(adapter_down_factor, up_part)
        second = swap(pack, "wide", 2, wide_count)
        first = swap(pack, "wide", 1, wide_count)
    beside, crossed = [swap(hidden, "tp", offset, tp_count) for offset in (1, 2)]
    near, far = (0, 1), (2, 3)
    near_weight, gain_rows, bias, mine, *cached = cache_call(
        near,
        lengths,
        queries,
        stored_rotated_keys,
        stored_value_rows,
        gain,
        key_value_bias,
        hidden,
        key_value_weight,
    )
    if direct:
        third, gain_rows = lax.optimization_barrier((second, gain_rows))
        packs = [pack, first, second, swap(third, "wide", 1, wide_count)]
        relayed, first, beside = lax.optimization_barrier((crossed, first, beside))
        packs[1] = first
    else:
        relayed = crossed
    relayed, gain_rows = lax.optimization_barrier((relayed, gain_rows))
    relayed = swap(relayed, "tp", 1, tp_count)
    scaled, near_scaled, far_scaled, square, far_weight = scale_call(
        near, far, key_value_weight, gain_rows, (mine, beside, crossed, relayed)
    )
    if direct:
        inner = inner_call(scaled, packs)
        inner, far_scaled = lax.optimization_barrier((inner, far_scaled))
        inner = [inner] + [swap(inner, "tp", offset, tp_count) for offset in (1, 2, 3)]
    else:
        down = lax.all_gather(adapter_down_factor, "wide", axis=2, tiled=True)
        down = down.reshape(kinds * ranks, width)
        inner = [jnp.einsum("rd,kd->rk", scaled, down, preferred_element_type=jnp.float32)]
        packs = [lax.all_gather(up_part, "wide", axis=1, tiled=True)]
    near_base, far_base = [
        jnp.einsum("md,dkc->kmc", x, y, preferred_element_type=jnp.float32)
        for x, y in ((near_scaled, near_weight), (far_scaled, far_weight))
    ]
    return final_call(
        queries.shape, width, near_base, far_base, square, bias, cached, inner, packs
    )


def solution(mesh):
    in_specs = (
        P(None, ("groups", "wide"), "tp"),
        P(),
        P(None, None, "tp"),
        P(None, "tp"),
        P("groups", None, "wide"),
        P("groups", "tp", "wide"),
        P(None, ("groups", "wide"), "tp"),
        P(("groups", "wide"), None, "tp"),
        P(("groups", "wide"), None, "tp"),
        P(("groups", "wide")),
    )
    out_specs = (
        P(None, ("groups", "wide"), "tp"),
        P(None, ("groups", "wide"), "tp"),
        P(None, ("groups", "wide"), "tp"),
    )
    body = functools.partial(on_device, mesh.shape["wide"], mesh.shape["tp"])
    return jax.shard_map(
        body, mesh=mesh, in_specs=in_specs, out_specs=out_specs, check_vma=False
    )
```

```python
import functools
import math

import jax
import jax.numpy as jnp
from jax import lax
from jax.experimental import pallas as pl
from jax.experimental.pallas import tpu as pltpu
from jax.sharding import PartitionSpec as P

HD = 128


norm_eps = 1e-06
adapter_scale = 2.0
rope_base = 1000000.0
masked_score = -1e30
score_scale = 1.0 / math.sqrt(HD)

VMEM = pl.BlockSpec(memory_space=pltpu.VMEM)
HBM = pl.BlockSpec(memory_space=pltpu.HBM)


def query_block(query_ref, group, per_group):
    steps = query_ref.shape[0]
    tiles = []
    for head in range(per_group):
        at = (group * per_group + head) * HD
        for step in range(steps):
            tiles.append(query_ref[step, :, at : at + HD].astype(jnp.float32))
    return jnp.concatenate(tiles, axis=0)


def copy_blocks(offsets, width, weight_ref, out_ref, sems):
    me = lax.axis_index("tp")
    copies = []
    for i, offset in enumerate(offsets):
        block = pl.ds(pl.multiple_of((me ^ offset) * width, width), width)
        copies.append(
            pltpu.make_async_copy(
                weight_ref.at[block], out_ref.at[pl.ds(i * width, width)], sems.at[i]
            )
        )
        copies[-1].start()
    return copies


def cache_kernel(
    near,
    lengths_ref,
    query_ref,
    key_ref,
    value_ref,
    gain_ref,
    bias_ref,
    hidden_ref,
    weight_ref,
    near_out,
    gain_out,
    bias_out,
    hidden_out,
    query_rows,
    query_out,
    acc_out,
    top_out,
    total_out,
    cos_out,
    sin_out,
    lengths,
    queries,
    gain_buffer,
    key_buffer,
    value_buffer,
    score_buffer,
    sems,
    weight_sems,
):
    steps, rows, query_width = query_ref.shape
    cache_span = key_ref.shape[1]
    groups = key_ref.shape[2] // HD
    per_group = query_width // HD // groups
    lines = steps * per_group
    half_rows = rows // 2
    halves = [pl.ds(0, half_rows), pl.ds(half_rows, half_rows)]
    copies = [
        (lengths_ref, lengths),
        (query_ref, queries),
        (key_ref.at[halves[0]], key_buffer.at[halves[0]]),
        (key_ref.at[halves[1]], key_buffer.at[halves[1]]),
        (value_ref.at[halves[0]], value_buffer.at[halves[0]]),
        (value_ref.at[halves[1]], value_buffer.at[halves[1]]),
        (gain_ref, gain_buffer),
        (bias_ref, bias_out),
        (hidden_ref, hidden_out),
    ]
    copies = [pltpu.make_async_copy(*pair, sems.at[i]) for i, pair in enumerate(copies)]
    for copy in copies:
        copy.start()
    copies += copy_blocks(near, hidden_ref.shape[2], weight_ref, near_out, weight_sems)

    copies[0].wait()
    lane = lax.broadcasted_iota(jnp.int32, (rows, HD), 1)
    half = HD // 2
    second = lane >= half
    index = jnp.where(second, lane - half, lane).astype(jnp.float32)
    inv_freq = jnp.exp(index * (-2.0 * math.log(rope_base) / HD))
    row_index = lax.broadcasted_iota(jnp.int32, (rows, HD), 0)
    row_lengths = jnp.zeros((rows, HD), jnp.int32)
    for row in range(rows):
        row_lengths = jnp.where(row_index == row, lengths[row], row_lengths)
    for step in range(steps):
        angles = (row_lengths + step).astype(jnp.float32) * inv_freq
        sine = jnp.sin(angles)
        cos_out[pl.ds(step * rows, rows)] = jnp.cos(angles)
        sin_out[pl.ds(step * rows, rows)] = jnp.where(second, sine, -sine)
    copies[1].wait()
    for group in range(groups):
        query_rows[group] = query_block(queries, group, per_group)
        query_out[group] = query_rows[group].astype(jnp.bfloat16)

    place = lax.broadcasted_iota(jnp.int32, (lines, cache_span), 1)
    for i in range(2):
        copies[2 + i].wait()
        for row in range(i * half_rows, (i + 1) * half_rows):
            for group in range(groups):
                query = query_rows[group, pl.ds(row, lines, stride=rows), :].astype(jnp.bfloat16)
                score_buffer[row * groups + group] = lax.dot_general(
                    query,
                    key_buffer[row, :, pl.ds(group * HD, HD)],
                    (((1,), (1,)), ((), ())),
                    preferred_element_type=jnp.float32,
                )
    for i in range(2):
        copies[4 + i].wait()
        for row in range(i * half_rows, (i + 1) * half_rows):
            live = place < lengths[row]
            for group in range(groups):
                mine = pl.ds(row, lines, stride=rows)
                scores = score_buffer[row * groups + group]
                scores = jnp.where(live, scores * score_scale, masked_score)
                top = jnp.max(scores, axis=1, keepdims=True)
                exps = jnp.exp(scores - top)
                total = jnp.sum(exps, axis=1, keepdims=True)
                acc = jnp.dot(
                    exps.astype(jnp.bfloat16),
                    value_buffer[row, :, pl.ds(group * HD, HD)],
                    preferred_element_type=jnp.float32,
                )
                acc_out[group, mine, :] = acc
                top_out[group, mine, :] = jnp.broadcast_to(top, acc.shape)
                total_out[group, mine, :] = jnp.broadcast_to(total, acc.shape)
    copies[6].wait()
    gain_out[...] = gain_buffer[...].astype(jnp.float32)
    for copy in copies[7:]:
        copy.wait()


def cache_call(near, lengths, queries, keys, values, gain, bias, hidden, weight):
    steps, rows, query_width = queries.shape
    cache_span, key_width = keys.shape[1:]
    groups = key_width // HD
    lines = steps * (query_width // key_width)
    block = (groups, lines * rows, HD)
    table = (steps * rows, HD)
    operands = (lengths, queries, keys, values, gain, bias, hidden, weight)
    part = hidden.shape[2]
    return pl.pallas_call(
        functools.partial(cache_kernel, near),
        out_shape=(
            pltpu.VMEM((len(near) * part,) + weight.shape[1:], weight.dtype),
            pltpu.VMEM(gain.shape, jnp.float32),
            pltpu.VMEM(bias.shape, bias.dtype),
            pltpu.VMEM(hidden.shape, hidden.dtype),
            pltpu.VMEM(block, jnp.float32),
            pltpu.VMEM(block, jnp.bfloat16),
            pltpu.VMEM(block, jnp.float32),
            pltpu.VMEM(block, jnp.float32),
            pltpu.VMEM(block, jnp.float32),
            pltpu.VMEM(table, jnp.float32),
            pltpu.VMEM(table, jnp.float32),
        ),
        in_specs=[HBM] * len(operands),
        out_specs=(VMEM,) * 11,
        scratch_shapes=[
            pltpu.SMEM(lengths.shape, jnp.int32),
            pltpu.VMEM(queries.shape, queries.dtype),
            pltpu.VMEM(gain.shape, gain.dtype),
            pltpu.VMEM(keys.shape, keys.dtype),
            pltpu.VMEM(values.shape, values.dtype),
            pltpu.VMEM((rows * groups, lines, cache_span), jnp.float32),
            pltpu.SemaphoreType.DMA((9,)),
            pltpu.SemaphoreType.DMA((len(near),)),
        ],
        compiler_params=pltpu.CompilerParams(vmem_limit_bytes=16 << 20),
        cost_estimate=pl.CostEstimate(flops=2 * 67 << 20, bytes_accessed=9 << 20, transcendentals=0),
        name="cache_attention",
    )(*[pltpu.with_memory_space_constraint(x, pltpu.HBM) for x in operands])


def rows_of(ref):
    return jnp.concatenate([ref[s].astype(jnp.float32) for s in range(ref.shape[0])], axis=0)


def pack_kernel(down_ref, up_ref, out_ref, sems):
    share = out_ref.shape[1]
    width = down_ref.shape[2]
    at = pl.ds(pl.multiple_of(lax.axis_index("tp") * share, share), share)
    down = pltpu.make_async_copy(
        down_ref.at[:, at, :], out_ref.at[:, :, pl.ds(0, width)], sems.at[0]
    )
    up = pltpu.make_async_copy(
        up_ref, out_ref.at[:, :, pl.ds(width, up_ref.shape[2])], sems.at[1]
    )
    down.start()
    up.start()
    down.wait()
    up.wait()


def pack_call(down, up):
    kinds, share, columns = up.shape
    return pl.pallas_call(
        pack_kernel,
        out_shape=pltpu.VMEM((kinds, share, down.shape[2] + columns), down.dtype),
        in_specs=[HBM] * 2,
        out_specs=VMEM,
        scratch_shapes=[pltpu.SemaphoreType.DMA((2,))],
        name="pack_factors",
    )(*[pltpu.with_memory_space_constraint(x, pltpu.HBM) for x in (down, up)])


def inner_kernel(scaled_ref, *rest):
    packs, out_ref = rest[:-1], rest[-1]
    me = lax.axis_index("wide")
    width = scaled_ref.shape[1] // len(packs)
    total = []
    for offset, pack in enumerate(packs):
        total.append(
            lax.dot_general(
                scaled_ref[:, pl.ds(pl.multiple_of((me ^ offset) * width, width), width)],
                pack[:, :, :width].reshape(out_ref.shape[1], width),
                (((1,), (1,)), ((), ())),
                preferred_element_type=jnp.float32,
            )
        )
    out_ref[...] = sum(total[1:], total[0])


def inner_call(scaled, packs):
    kinds, share, _ = packs[0].shape
    return pl.pallas_call(
        inner_kernel,
        out_shape=jax.ShapeDtypeStruct((scaled.shape[0], kinds * share), jnp.float32),
        in_specs=[VMEM] * (1 + len(packs)),
        out_specs=VMEM,
        compiler_params=pltpu.CompilerParams(vmem_limit_bytes=8 << 20),
        name="rank_inner",
    )(scaled, *packs)


def scale_kernel(near, far, weight_ref, gain_ref, *rest):
    parts = rest[:-6]
    scaled_out, near_out, far_out, square_out, weight_out, sems = rest[-6:]
    steps, rows, width = parts[0].shape
    chunks = width // HD
    copies = copy_blocks(far, width, weight_ref, weight_out, sems)
    me = lax.axis_index("tp")
    squares = jnp.zeros(square_out.shape, jnp.float32)
    for k, (offset, part) in enumerate(zip(near + far, parts)):
        block = me ^ offset
        gain = gain_ref[pl.ds(pl.multiple_of(block * chunks, chunks), chunks)]
        values = rows_of(part)
        scaled = []
        for i in range(chunks):
            chunk = values[:, i * HD : (i + 1) * HD]
            squares += chunk * chunk
            scaled.append((chunk * gain[i : i + 1]).astype(jnp.bfloat16))
        at = pl.ds(pl.multiple_of(block * width, width), width)
        scaled = jnp.concatenate(scaled, axis=1)
        scaled_out[:, at] = scaled
        out, i = (near_out, k) if k < len(near) else (far_out, k - len(near))
        out[:, i * width : (i + 1) * width] = scaled
    square_out[...] = jnp.broadcast_to(jnp.sum(squares, axis=1, keepdims=True), squares.shape)
    for copy in copies:
        copy.wait()


def scale_call(near, far, weight, gain, parts):
    steps, rows, width = parts[0].shape
    return pl.pallas_call(
        functools.partial(scale_kernel, near, far),
        out_shape=(
            pltpu.VMEM((steps * rows, len(parts) * width), jnp.bfloat16),
            pltpu.VMEM((steps * rows, len(near) * width), jnp.bfloat16),
            pltpu.VMEM((steps * rows, len(far) * width), jnp.bfloat16),
            pltpu.VMEM((steps * rows, HD), jnp.float32),
            pltpu.VMEM((len(far) * width,) + weight.shape[1:], weight.dtype),
        ),
        in_specs=[HBM] + [VMEM] * (1 + len(parts)),
        out_specs=(VMEM,) * 5,
        scratch_shapes=[pltpu.SemaphoreType.DMA((len(far),))],
        compiler_params=pltpu.CompilerParams(vmem_limit_bytes=8 << 20),
        cost_estimate=pl.CostEstimate(flops=0, bytes_accessed=5 << 20, transcendentals=0),
        name="scale_features",
    )(pltpu.with_memory_space_constraint(weight, pltpu.HBM), gain, *parts)


def up_kernel(*refs):
    packs, up_out = refs[:-1], refs[-1]
    kinds, share, pack_width = packs[0].shape
    columns = up_out.shape[1] // kinds
    me = lax.axis_index("wide") if len(packs) > 1 else 0
    up_out[...] = jnp.zeros_like(up_out)
    for offset, pack in enumerate(packs):
        for kind in range(kinds):
            at = pl.multiple_of(((me ^ offset) * kinds + kind) * share, share)
            up_out[pl.ds(at, share), kind * columns : (kind + 1) * columns] = pack[
                kind, :, pack_width - columns :
            ]


def up_call(packs, columns):
    kinds, share, _ = packs[0].shape
    return pl.pallas_call(
        up_kernel,
        out_shape=pltpu.VMEM((len(packs) * kinds * share, kinds * columns), packs[0].dtype),
        in_specs=[VMEM] * len(packs),
        out_specs=VMEM,
        compiler_params=pltpu.CompilerParams(vmem_limit_bytes=8 << 20),
        name="lay_out_up",
    )(*packs)


def final_kernel(width, blocks, near_ref, far_ref, square_ref, bias_ref, *rest):
    query_ref, acc_ref, top_ref, total_ref, cos_ref, sin_ref = rest[:6]
    inner_refs = rest[6 : 6 + blocks]
    up_ref, keys_out, values_out, attended_out, inner_buffer = rest[6 + blocks :]
    steps, rows, columns = keys_out.shape
    count = steps * rows
    groups, size, _ = query_ref.shape
    per_group = size // count
    kinds = bias_ref.shape[0]
    row_scale = lax.rsqrt(square_ref[:, :1] * (1.0 / width) + norm_eps)
    me = lax.axis_index("tp") if blocks > 1 else 0
    for i in range(blocks):
        inner_buffer[me ^ i] = inner_refs[i][...]
    inner = jnp.concatenate([inner_buffer[i] for i in range(blocks)], axis=1)
    high = inner.astype(jnp.bfloat16)
    low = (inner - high.astype(jnp.float32)).astype(jnp.bfloat16)
    lora = jnp.dot(
        jnp.concatenate([high, low], axis=0), up_ref[...], preferred_element_type=jnp.float32
    )
    lora = lora[:count] + lora[count:]
    bias = bias_ref[...].astype(jnp.float32)
    linear = []
    for kind in range(kinds):
        base = near_ref[kind] + far_ref[kind]
        part = lora[:, kind * columns : (kind + 1) * columns]
        linear.append((base + adapter_scale * part) * row_scale + bias[kind : kind + 1])
    cosine, sine = cos_ref[...], sin_ref[...]
    line = lax.broadcasted_iota(jnp.int32, (size, count), 0)
    other = lax.broadcasted_iota(jnp.int32, (size, count), 1)
    live = (line % rows == other % rows) & (other // rows <= line // rows % steps)
    for group in range(groups):
        at = slice(group * HD, (group + 1) * HD)
        key = linear[0][:, at]
        key = (key * cosine + pltpu.roll(key, HD // 2, 1) * sine).astype(jnp.bfloat16)
        value = linear[1][:, at].astype(jnp.bfloat16)
        for step in range(steps):
            keys_out[step, :, at] = key[step * rows : (step + 1) * rows]
            values_out[step, :, at] = value[step * rows : (step + 1) * rows]
        scores = lax.dot_general(
            query_ref[group],
            key,
            (((1,), (1,)), ((), ())),
            preferred_element_type=jnp.float32,
        )
        scores = jnp.where(live, scores * score_scale, masked_score)
        old_top = top_ref[group][:, :1]
        top = jnp.maximum(old_top, jnp.max(scores, axis=1, keepdims=True))
        exps = jnp.exp(scores - top)
        keep = jnp.exp(old_top - top)
        total = total_ref[group][:, :1] * keep + jnp.sum(exps, axis=1, keepdims=True)
        acc = acc_ref[group] * keep + jnp.dot(
            exps.astype(jnp.bfloat16), value, preferred_element_type=jnp.float32
        )
        attended = (acc / total).astype(jnp.bfloat16)
        for head in range(per_group):
            lanes = pl.ds((group * per_group + head) * HD, HD)
            for step in range(steps):
                tile = (head * steps + step) * rows
                attended_out[step, :, lanes] = attended[tile : tile + rows]


def final_call(shape, width, near, far, square, bias, cached, inner, up):
    steps, rows, query_width = shape
    columns = near.shape[2]
    small = jax.ShapeDtypeStruct((steps, rows, columns), jnp.bfloat16)
    return pl.pallas_call(
        functools.partial(final_kernel, width, len(inner)),
        out_shape=(small, small, jax.ShapeDtypeStruct(shape, jnp.bfloat16)),
        in_specs=[VMEM] * (5 + len(cached) + len(inner)),
        out_specs=(VMEM,) * 3,
        scratch_shapes=[pltpu.VMEM((len(inner),) + inner[0].shape, jnp.float32)],
        compiler_params=pltpu.CompilerParams(vmem_limit_bytes=8 << 20),
        name="fresh_attention",
    )(near, far, square, bias, *cached, *inner, up)


def swap(block, axis, offset, count):
    return lax.ppermute(block, axis, [(i, i ^ offset) for i in range(count)])


def on_device(
    wide_count,
    tp_count,
    hidden,
    input_norm_gain,
    key_value_weight,
    key_value_bias,
    adapter_down_factor,
    adapter_up_factor,
    queries,
    stored_rotated_keys,
    stored_value_rows,
    lengths,
):
    steps, rows, part_width = hidden.shape
    width = part_width * tp_count
    kinds, ranks, down_width = adapter_down_factor.shape
    gain = input_norm_gain.reshape(width // HD, HD)
    up_part = jnp.transpose(adapter_up_factor, (0, 2, 1))
    direct = wide_count == tp_count == 4
    tp_parts = [swap(hidden, "tp", offset, tp_count) for offset in (1, 2, 3)]
    if direct:
        pack = pack_call(adapter_down_factor, up_part)
        second = swap(pack, "wide", 2, wide_count)
        first = swap(pack, "wide", 1, wide_count)
    near, far = (0, 1), (2, 3)
    near_weight, gain_rows, bias, mine, _, *cached = cache_call(
        near,
        lengths,
        queries,
        stored_rotated_keys,
        stored_value_rows,
        gain,
        key_value_bias,
        hidden,
        key_value_weight,
    )
    if direct:
        third, gain_rows = lax.optimization_barrier((second, gain_rows))
        packs = [pack, first, second, swap(third, "wide", 1, wide_count)]
    scaled, near_scaled, far_scaled, square, far_weight = scale_call(
        near, far, key_value_weight, gain_rows, [mine] + tp_parts
    )
    if direct:
        inner = inner_call(scaled, packs)
        inner, far_scaled, packs = lax.optimization_barrier((inner, far_scaled, packs))
        inner = [inner] + [swap(inner, "tp", offset, tp_count) for offset in (1, 2, 3)]
    else:
        down = lax.all_gather(adapter_down_factor, "wide", axis=2, tiled=True)
        down = down.reshape(kinds * ranks, width)
        inner = [jnp.einsum("rd,kd->rk", scaled, down, preferred_element_type=jnp.float32)]
        packs = [lax.all_gather(up_part, "wide", axis=1, tiled=True)]
    near_base, far_base = [
        jnp.einsum("md,dkc->kmc", x, y, preferred_element_type=jnp.float32)
        for x, y in ((near_scaled, near_weight), (far_scaled, far_weight))
    ]
    up = up_call(packs, bias.shape[1])
    return final_call(
        queries.shape, width, near_base, far_base, square, bias, cached, inner, up
    )


def solution(mesh):
    in_specs = (
        P(None, ("groups", "wide"), "tp"),
        P(),
        P(None, None, "tp"),
        P(None, "tp"),
        P("groups", None, "wide"),
        P("groups", "tp", "wide"),
        P(None, ("groups", "wide"), "tp"),
        P(("groups", "wide"), None, "tp"),
        P(("groups", "wide"), None, "tp"),
        P(("groups", "wide")),
    )
    out_specs = (
        P(None, ("groups", "wide"), "tp"),
        P(None, ("groups", "wide"), "tp"),
        P(None, ("groups", "wide"), "tp"),
    )
    body = functools.partial(on_device, mesh.shape["wide"], mesh.shape["tp"])
    return jax.shard_map(
        body, mesh=mesh, in_specs=in_specs, out_specs=out_specs, check_vma=False
    )
```

```python
import functools
import math

import jax
import jax.numpy as jnp
from jax import lax
from jax.experimental import pallas as pl
from jax.experimental.pallas import tpu as pltpu
from jax.sharding import PartitionSpec as P

HD = 128


norm_eps = 1e-06
adapter_scale = 2.0
rope_base = 1000000.0
masked_score = -1e30
score_scale = 1.0 / math.sqrt(HD)

VMEM = pl.BlockSpec(memory_space=pltpu.VMEM)
HBM = pl.BlockSpec(memory_space=pltpu.HBM)


def query_block(query_ref, group, per_group):
    steps = query_ref.shape[0]
    tiles = []
    for head in range(per_group):
        at = (group * per_group + head) * HD
        for step in range(steps):
            tiles.append(query_ref[step, :, at : at + HD].astype(jnp.float32))
    return jnp.concatenate(tiles, axis=0)


def copy_blocks(offsets, width, weight_ref, out_ref, sems):
    me = lax.axis_index("tp")
    copies = []
    for i, offset in enumerate(offsets):
        block = pl.ds(pl.multiple_of((me ^ offset) * width, width), width)
        copies.append(
            pltpu.make_async_copy(
                weight_ref.at[block], out_ref.at[pl.ds(i * width, width)], sems.at[i]
            )
        )
        copies[-1].start()
    return copies


def cache_kernel(
    lengths_ref,
    query_ref,
    key_ref,
    value_ref,
    gain_ref,
    bias_ref,
    hidden_ref,
    gain_out,
    bias_out,
    hidden_out,
    query_rows,
    query_out,
    acc_out,
    top_out,
    total_out,
    cos_out,
    sin_out,
    lengths,
    queries,
    gain_buffer,
    key_buffer,
    value_buffer,
    score_buffer,
    sems,
):
    steps, rows, query_width = query_ref.shape
    cache_span = key_ref.shape[1]
    groups = key_ref.shape[2] // HD
    per_group = query_width // HD // groups
    lines = steps * per_group
    half_rows = rows // 2
    halves = [pl.ds(0, half_rows), pl.ds(half_rows, half_rows)]
    copies = [
        (lengths_ref, lengths),
        (query_ref, queries),
        (key_ref.at[halves[0]], key_buffer.at[halves[0]]),
        (key_ref.at[halves[1]], key_buffer.at[halves[1]]),
        (value_ref.at[halves[0]], value_buffer.at[halves[0]]),
        (value_ref.at[halves[1]], value_buffer.at[halves[1]]),
        (gain_ref, gain_buffer),
        (bias_ref, bias_out),
        (hidden_ref, hidden_out),
    ]
    copies = [pltpu.make_async_copy(*pair, sems.at[i]) for i, pair in enumerate(copies)]
    for copy in copies:
        copy.start()

    copies[0].wait()
    lane = lax.broadcasted_iota(jnp.int32, (rows, HD), 1)
    half = HD // 2
    second = lane >= half
    index = jnp.where(second, lane - half, lane).astype(jnp.float32)
    inv_freq = jnp.exp(index * (-2.0 * math.log(rope_base) / HD))
    row_index = lax.broadcasted_iota(jnp.int32, (rows, HD), 0)
    row_lengths = jnp.zeros((rows, HD), jnp.int32)
    for row in range(rows):
        row_lengths = jnp.where(row_index == row, lengths[row], row_lengths)
    for step in range(steps):
        angles = (row_lengths + step).astype(jnp.float32) * inv_freq
        sine = jnp.sin(angles)
        cos_out[pl.ds(step * rows, rows)] = jnp.cos(angles)
        sin_out[pl.ds(step * rows, rows)] = jnp.where(second, sine, -sine)
    copies[1].wait()
    for group in range(groups):
        query_rows[group] = query_block(queries, group, per_group)
        query_out[group] = query_rows[group].astype(jnp.bfloat16)

    place = lax.broadcasted_iota(jnp.int32, (lines, cache_span), 1)
    for i in range(2):
        copies[2 + i].wait()
        for row in range(i * half_rows, (i + 1) * half_rows):
            for group in range(groups):
                query = query_rows[group, pl.ds(row, lines, stride=rows), :].astype(jnp.bfloat16)
                score_buffer[row * groups + group] = lax.dot_general(
                    query,
                    key_buffer[row, :, pl.ds(group * HD, HD)],
                    (((1,), (1,)), ((), ())),
                    preferred_element_type=jnp.float32,
                )
    for i in range(2):
        copies[4 + i].wait()
        for row in range(i * half_rows, (i + 1) * half_rows):
            live = place < lengths[row]
            for group in range(groups):
                mine = pl.ds(row, lines, stride=rows)
                scores = score_buffer[row * groups + group]
                scores = jnp.where(live, scores * score_scale, masked_score)
                top = jnp.max(scores, axis=1, keepdims=True)
                exps = jnp.exp(scores - top)
                total = jnp.sum(exps, axis=1, keepdims=True)
                acc = jnp.dot(
                    exps.astype(jnp.bfloat16),
                    value_buffer[row, :, pl.ds(group * HD, HD)],
                    preferred_element_type=jnp.float32,
                )
                acc_out[group, mine, :] = acc
                top_out[group, mine, :] = jnp.broadcast_to(top, acc.shape)
                total_out[group, mine, :] = jnp.broadcast_to(total, acc.shape)
    copies[6].wait()
    gain_out[...] = gain_buffer[...].astype(jnp.float32)
    for copy in copies[7:]:
        copy.wait()


def cache_call(lengths, queries, keys, values, gain, bias, hidden):
    steps, rows, query_width = queries.shape
    cache_span, key_width = keys.shape[1:]
    groups = key_width // HD
    lines = steps * (query_width // key_width)
    block = (groups, lines * rows, HD)
    table = (steps * rows, HD)
    operands = (lengths, queries, keys, values, gain, bias, hidden)
    return pl.pallas_call(
        cache_kernel,
        out_shape=(
            pltpu.VMEM(gain.shape, jnp.float32),
            pltpu.VMEM(bias.shape, bias.dtype),
            pltpu.VMEM(hidden.shape, hidden.dtype),
            pltpu.VMEM(block, jnp.float32),
            pltpu.VMEM(block, jnp.bfloat16),
            pltpu.VMEM(block, jnp.float32),
            pltpu.VMEM(block, jnp.float32),
            pltpu.VMEM(block, jnp.float32),
            pltpu.VMEM(table, jnp.float32),
            pltpu.VMEM(table, jnp.float32),
        ),
        in_specs=[HBM] * len(operands),
        out_specs=(VMEM,) * 10,
        scratch_shapes=[
            pltpu.SMEM(lengths.shape, jnp.int32),
            pltpu.VMEM(queries.shape, queries.dtype),
            pltpu.VMEM(gain.shape, gain.dtype),
            pltpu.VMEM(keys.shape, keys.dtype),
            pltpu.VMEM(values.shape, values.dtype),
            pltpu.VMEM((rows * groups, lines, cache_span), jnp.float32),
            pltpu.SemaphoreType.DMA((9,)),
        ],
        compiler_params=pltpu.CompilerParams(vmem_limit_bytes=16 << 20),
        cost_estimate=pl.CostEstimate(flops=2 * 67 << 20, bytes_accessed=5 << 20, transcendentals=0),
        name="cache_attention",
    )(*[pltpu.with_memory_space_constraint(x, pltpu.HBM) for x in operands])


def rows_of(ref):
    return jnp.concatenate([ref[s].astype(jnp.float32) for s in range(ref.shape[0])], axis=0)


def pack_kernel(down_ref, up_ref, out_ref, sems):
    share = out_ref.shape[1]
    width = down_ref.shape[2]
    at = pl.ds(pl.multiple_of(lax.axis_index("tp") * share, share), share)
    down = pltpu.make_async_copy(
        down_ref.at[:, at, :], out_ref.at[:, :, pl.ds(0, width)], sems.at[0]
    )
    up = pltpu.make_async_copy(
        up_ref, out_ref.at[:, :, pl.ds(width, up_ref.shape[2])], sems.at[1]
    )
    down.start()
    up.start()
    down.wait()
    up.wait()


def pack_call(down, up):
    kinds, share, columns = up.shape
    return pl.pallas_call(
        pack_kernel,
        out_shape=pltpu.VMEM((kinds, share, down.shape[2] + columns), down.dtype),
        in_specs=[HBM] * 2,
        out_specs=VMEM,
        scratch_shapes=[pltpu.SemaphoreType.DMA((2,))],
        name="pack_factors",
    )(*[pltpu.with_memory_space_constraint(x, pltpu.HBM) for x in (down, up)])


def scaled_block(part, gain_ref, block):
    steps, rows, width = part.shape
    chunks = width // HD
    gain = gain_ref[pl.ds(pl.multiple_of(block * chunks, chunks), chunks)]
    values = rows_of(part)
    squares = jnp.zeros((steps * rows, HD), jnp.float32)
    scaled = []
    for i in range(chunks):
        chunk = values[:, i * HD : (i + 1) * HD]
        squares += chunk * chunk
        scaled.append((chunk * gain[i : i + 1]).astype(jnp.bfloat16))
    return jnp.concatenate(scaled, axis=1), squares


def scale_kernel(near, far, weight_ref, gain_ref, *rest):
    scaled_out, near_out, far_out, square_out, near_weight, far_weight, near_sems, far_sems = rest[-8:]
    parts = rest[:-8]
    width = parts[0].shape[2]
    copies = copy_blocks(near, width, weight_ref, near_weight, near_sems)
    copies += copy_blocks(far, width, weight_ref, far_weight, far_sems)
    me = lax.axis_index("tp")
    offsets = near + far
    total = None
    for k, part in enumerate(parts):
        block = me ^ offsets[k]
        scaled, squares = scaled_block(part, gain_ref, block)
        total = squares if total is None else total + squares
        scaled_out[:, pl.ds(pl.multiple_of(block * width, width), width)] = scaled
        if k < len(near):
            near_out[:, k * width : (k + 1) * width] = scaled
        else:
            i = k - len(near)
            far_out[:, i * width : (i + 1) * width] = scaled
    at = pl.ds(pl.multiple_of((me ^ offsets[-1]) * width, width), width)
    scaled_out[:, at] = jnp.zeros_like(scaled)
    square_out[...] = total
    for copy in copies:
        copy.wait()


def scale_call(near, far, weight, gain, parts):
    steps, rows, width = parts[0].shape
    count = steps * rows
    return pl.pallas_call(
        functools.partial(scale_kernel, near, far),
        out_shape=(
            pltpu.VMEM((count, (len(near) + len(far)) * width), jnp.bfloat16),
            pltpu.VMEM((count, len(near) * width), jnp.bfloat16),
            pltpu.VMEM((count, (len(far) - 1) * width), jnp.bfloat16),
            pltpu.VMEM((count, HD), jnp.float32),
            pltpu.VMEM((len(near) * width,) + weight.shape[1:], weight.dtype),
            pltpu.VMEM((len(far) * width,) + weight.shape[1:], weight.dtype),
        ),
        in_specs=[HBM] + [VMEM] * (1 + len(parts)),
        out_specs=(VMEM,) * 6,
        scratch_shapes=[
            pltpu.SemaphoreType.DMA((len(near),)),
            pltpu.SemaphoreType.DMA((len(far),)),
        ],
        compiler_params=pltpu.CompilerParams(vmem_limit_bytes=8 << 20),
        cost_estimate=pl.CostEstimate(flops=0, bytes_accessed=9 << 20, transcendentals=0),
        name="scale_features",
    )(pltpu.with_memory_space_constraint(weight, pltpu.HBM), gain, *parts)


def inner_kernel(last, scaled_ref, far_ref, square_ref, gain_ref, part_ref, *rest):
    far_out, square_out = rest[-2:]
    packs, inner_out = (rest[:-3], rest[-3]) if len(rest) > 2 else ((), None)
    block = lax.axis_index("tp") ^ last
    late, squares = scaled_block(part_ref, gain_ref, block)
    width = late.shape[1]
    far_out[:, : far_ref.shape[1]] = far_ref[...]
    far_out[:, far_ref.shape[1] :] = late
    squares = jnp.sum(squares + square_ref[...], axis=1, keepdims=True)
    square_out[...] = jnp.broadcast_to(squares, square_out.shape)
    if not packs:
        return
    me = lax.axis_index("wide")
    total = []
    for offset, pack in enumerate(packs):
        mine = me ^ offset
        early = scaled_ref[:, pl.ds(pl.multiple_of(mine * width, width), width)]
        total.append(
            lax.dot_general(
                jnp.where(mine == block, late, early),
                pack[:, :, :width].reshape(inner_out.shape[1], width),
                (((1,), (1,)), ((), ())),
                preferred_element_type=jnp.float32,
            )
        )
    inner_out[...] = sum(total[1:], total[0])


def inner_call(last, scaled, far, square, gain, part, packs):
    count, width = far.shape[0], part.shape[2]
    shapes = [
        pltpu.VMEM((count, far.shape[1] + width), far.dtype),
        pltpu.VMEM(square.shape, jnp.float32),
    ]
    if packs:
        kinds, share, _ = packs[0].shape
        shapes = [pltpu.VMEM((count, kinds * share), jnp.float32)] + shapes
    return pl.pallas_call(
        functools.partial(inner_kernel, last),
        out_shape=tuple(shapes),
        in_specs=[VMEM] * (5 + len(packs)),
        out_specs=(VMEM,) * len(shapes),
        compiler_params=pltpu.CompilerParams(vmem_limit_bytes=8 << 20),
        name="rank_inner",
    )(scaled, far, square, gain, part, *packs)


def up_kernel(*refs):
    packs, up_out = refs[:-1], refs[-1]
    kinds, share, pack_width = packs[0].shape
    columns = up_out.shape[1] // kinds
    me = lax.axis_index("wide") if len(packs) > 1 else 0
    up_out[...] = jnp.zeros_like(up_out)
    for offset, pack in enumerate(packs):
        for kind in range(kinds):
            at = pl.multiple_of(((me ^ offset) * kinds + kind) * share, share)
            up_out[pl.ds(at, share), kind * columns : (kind + 1) * columns] = pack[
                kind, :, pack_width - columns :
            ]


def up_call(packs, columns):
    kinds, share, _ = packs[0].shape
    return pl.pallas_call(
        up_kernel,
        out_shape=pltpu.VMEM((len(packs) * kinds * share, kinds * columns), packs[0].dtype),
        in_specs=[VMEM] * len(packs),
        out_specs=VMEM,
        compiler_params=pltpu.CompilerParams(vmem_limit_bytes=8 << 20),
        name="lay_out_up",
    )(*packs)


def final_kernel(width, blocks, near_ref, far_ref, square_ref, bias_ref, *rest):
    query_ref, acc_ref, top_ref, total_ref, cos_ref, sin_ref = rest[:6]
    inner_refs = rest[6 : 6 + blocks]
    up_ref, keys_out, values_out, attended_out, inner_buffer = rest[6 + blocks :]
    steps, rows, columns = keys_out.shape
    count = steps * rows
    groups, size, _ = query_ref.shape
    per_group = size // count
    kinds = bias_ref.shape[0]
    row_scale = lax.rsqrt(square_ref[:, :1] * (1.0 / width) + norm_eps)
    me = lax.axis_index("tp") if blocks > 1 else 0
    for i in range(blocks):
        inner_buffer[me ^ i] = inner_refs[i][...]
    inner = jnp.concatenate([inner_buffer[i] for i in range(blocks)], axis=1)
    high = inner.astype(jnp.bfloat16)
    low = (inner - high.astype(jnp.float32)).astype(jnp.bfloat16)
    lora = jnp.dot(
        jnp.concatenate([high, low], axis=0), up_ref[...], preferred_element_type=jnp.float32
    )
    lora = lora[:count] + lora[count:]
    bias = bias_ref[...].astype(jnp.float32)
    linear = []
    for kind in range(kinds):
        base = near_ref[kind] + far_ref[kind]
        part = lora[:, kind * columns : (kind + 1) * columns]
        linear.append((base + adapter_scale * part) * row_scale + bias[kind : kind + 1])
    cosine, sine = cos_ref[...], sin_ref[...]
    line = lax.broadcasted_iota(jnp.int32, (size, count), 0)
    other = lax.broadcasted_iota(jnp.int32, (size, count), 1)
    live = (line % rows == other % rows) & (other // rows <= line // rows % steps)
    for group in range(groups):
        at = slice(group * HD, (group + 1) * HD)
        key = linear[0][:, at]
        key = (key * cosine + pltpu.roll(key, HD // 2, 1) * sine).astype(jnp.bfloat16)
        value = linear[1][:, at].astype(jnp.bfloat16)
        for step in range(steps):
            keys_out[step, :, at] = key[step * rows : (step + 1) * rows]
            values_out[step, :, at] = value[step * rows : (step + 1) * rows]
        scores = lax.dot_general(
            query_ref[group],
            key,
            (((1,), (1,)), ((), ())),
            preferred_element_type=jnp.float32,
        )
        scores = jnp.where(live, scores * score_scale, masked_score)
        old_top = top_ref[group][:, :1]
        top = jnp.maximum(old_top, jnp.max(scores, axis=1, keepdims=True))
        exps = jnp.exp(scores - top)
        keep = jnp.exp(old_top - top)
        total = total_ref[group][:, :1] * keep + jnp.sum(exps, axis=1, keepdims=True)
        acc = acc_ref[group] * keep + jnp.dot(
            exps.astype(jnp.bfloat16), value, preferred_element_type=jnp.float32
        )
        attended = (acc / total).astype(jnp.bfloat16)
        for head in range(per_group):
            lanes = pl.ds((group * per_group + head) * HD, HD)
            for step in range(steps):
                tile = (head * steps + step) * rows
                attended_out[step, :, lanes] = attended[tile : tile + rows]


def final_call(shape, width, near, far, square, bias, cached, inner, up):
    steps, rows, query_width = shape
    columns = near.shape[2]
    small = jax.ShapeDtypeStruct((steps, rows, columns), jnp.bfloat16)
    return pl.pallas_call(
        functools.partial(final_kernel, width, len(inner)),
        out_shape=(small, small, jax.ShapeDtypeStruct(shape, jnp.bfloat16)),
        in_specs=[VMEM] * (5 + len(cached) + len(inner)),
        out_specs=(VMEM,) * 3,
        scratch_shapes=[pltpu.VMEM((len(inner),) + inner[0].shape, jnp.float32)],
        compiler_params=pltpu.CompilerParams(vmem_limit_bytes=8 << 20),
        name="fresh_attention",
    )(near, far, square, bias, *cached, *inner, up)


def dot(rows, weight):
    return jnp.einsum("md,dkc->kmc", rows, weight, preferred_element_type=jnp.float32)


def swap(block, axis, offset, count):
    return lax.ppermute(block, axis, [(i, i ^ offset) for i in range(count)])


def on_device(
    wide_count,
    tp_count,
    hidden,
    input_norm_gain,
    key_value_weight,
    key_value_bias,
    adapter_down_factor,
    adapter_up_factor,
    queries,
    stored_rotated_keys,
    stored_value_rows,
    lengths,
):
    steps, rows, part_width = hidden.shape
    width = part_width * tp_count
    kinds, ranks, down_width = adapter_down_factor.shape
    gain = input_norm_gain.reshape(width // HD, HD)
    up_part = jnp.transpose(adapter_up_factor, (0, 2, 1))
    direct = wide_count == tp_count == 4
    tp_parts = [swap(hidden, "tp", offset, tp_count) for offset in (1, 2, 3)]
    if direct:
        pack = pack_call(adapter_down_factor, up_part)
        second = swap(pack, "wide", 2, wide_count)
        first = swap(pack, "wide", 1, wide_count)
    near, far = (0, 1), (2, 3)
    gain_rows, bias, mine, _, *cached = cache_call(
        lengths, queries, stored_rotated_keys, stored_value_rows, gain, key_value_bias, hidden
    )
    if direct:
        third, gain_rows = lax.optimization_barrier((second, gain_rows))
        packs = [pack, first, second, swap(third, "wide", 1, wide_count)]
    scaled, near_scaled, far_scaled, square, near_weight, far_weight = scale_call(
        near, far, key_value_weight, gain_rows, [mine] + tp_parts[:2]
    )
    near_base = dot(near_scaled, near_weight)
    if direct:
        scaled, near_base = lax.optimization_barrier((scaled, near_base))
        inner, far_scaled, square = inner_call(
            far[-1], scaled, far_scaled, square, gain_rows, tp_parts[2], packs
        )
        inner, far_scaled, packs = lax.optimization_barrier((inner, far_scaled, packs))
        inner = [inner] + [swap(inner, "tp", offset, tp_count) for offset in (1, 2, 3)]
    else:
        far_scaled, square = inner_call(
            far[-1], scaled, far_scaled, square, gain_rows, tp_parts[2], []
        )
        down = lax.all_gather(adapter_down_factor, "wide", axis=2, tiled=True)
        rows_full = lax.all_gather(hidden, "tp", axis=2, tiled=True).astype(jnp.float32)
        rows_full = (rows_full * input_norm_gain.astype(jnp.float32)).astype(jnp.bfloat16)
        inner = jnp.einsum("srd,kad->srka", rows_full, down, preferred_element_type=jnp.float32)
        inner = [inner.reshape(steps * rows, kinds * ranks)]
        packs = [lax.all_gather(up_part, "wide", axis=1, tiled=True)]
    far_base = dot(far_scaled, far_weight)
    up = up_call(packs, bias.shape[1])
    return final_call(
        queries.shape, width, near_base, far_base, square, bias, cached, inner, up
    )


def solution(mesh):
    in_specs = (
        P(None, ("groups", "wide"), "tp"),
        P(),
        P(None, None, "tp"),
        P(None, "tp"),
        P("groups", None, "wide"),
        P("groups", "tp", "wide"),
        P(None, ("groups", "wide"), "tp"),
        P(("groups", "wide"), None, "tp"),
        P(("groups", "wide"), None, "tp"),
        P(("groups", "wide")),
    )
    out_specs = (
        P(None, ("groups", "wide"), "tp"),
        P(None, ("groups", "wide"), "tp"),
        P(None, ("groups", "wide"), "tp"),
    )
    body = functools.partial(on_device, mesh.shape["wide"], mesh.shape["tp"])
    return jax.shard_map(
        body, mesh=mesh, in_specs=in_specs, out_specs=out_specs, check_vma=False
    )
```

```python
import functools
import math

import jax
import jax.numpy as jnp
from jax import lax
from jax.experimental import pallas as pl
from jax.experimental.pallas import tpu as pltpu
from jax.sharding import PartitionSpec as P

HD = 128


norm_eps = 1e-06
adapter_scale = 2.0
rope_base = 1000000.0
masked_score = -1e30
score_scale = 1.0 / math.sqrt(HD)

VMEM = pl.BlockSpec(memory_space=pltpu.VMEM)
HBM = pl.BlockSpec(memory_space=pltpu.HBM)


def query_block(query_ref, group, per_group):
    steps = query_ref.shape[0]
    tiles = []
    for head in range(per_group):
        at = (group * per_group + head) * HD
        for step in range(steps):
            tiles.append(query_ref[step, :, at : at + HD].astype(jnp.float32))
    return jnp.concatenate(tiles, axis=0)


def copy_blocks(offsets, width, weight_ref, out_ref, sems):
    me = lax.axis_index("tp")
    copies = []
    for i, offset in enumerate(offsets):
        block = pl.ds(pl.multiple_of((me ^ offset) * width, width), width)
        copies.append(
            pltpu.make_async_copy(
                weight_ref.at[block], out_ref.at[pl.ds(i * width, width)], sems.at[i]
            )
        )
        copies[-1].start()
    return copies


def cache_kernel(
    lengths_ref,
    query_ref,
    key_ref,
    value_ref,
    gain_ref,
    bias_ref,
    hidden_ref,
    gain_out,
    bias_out,
    hidden_out,
    query_out,
    acc_out,
    top_out,
    total_out,
    lengths,
    queries,
    gain_buffer,
    key_buffer,
    value_buffer,
    score_buffer,
    sems,
):
    steps, rows, query_width = query_ref.shape
    cache_span = key_ref.shape[1]
    groups = key_ref.shape[2] // HD
    per_group = query_width // HD // groups
    lines = steps * per_group
    half_rows = rows // 2
    halves = [pl.ds(0, half_rows), pl.ds(half_rows, half_rows)]
    copies = [
        (lengths_ref, lengths),
        (query_ref, queries),
        (key_ref.at[halves[0]], key_buffer.at[halves[0]]),
        (key_ref.at[halves[1]], key_buffer.at[halves[1]]),
        (value_ref.at[halves[0]], value_buffer.at[halves[0]]),
        (value_ref.at[halves[1]], value_buffer.at[halves[1]]),
        (gain_ref, gain_buffer),
        (bias_ref, bias_out),
        (hidden_ref, hidden_out),
    ]
    copies = [pltpu.make_async_copy(*pair, sems.at[i]) for i, pair in enumerate(copies)]
    for copy in copies:
        copy.start()

    copies[0].wait()
    copies[1].wait()
    for group in range(groups):
        query_out[group] = query_block(queries, group, per_group)

    place = lax.broadcasted_iota(jnp.int32, (lines, cache_span), 1)
    for i in range(2):
        copies[2 + i].wait()
        for row in range(i * half_rows, (i + 1) * half_rows):
            for group in range(groups):
                query = query_out[group, pl.ds(row, lines, stride=rows), :].astype(jnp.bfloat16)
                score_buffer[row * groups + group] = lax.dot_general(
                    query,
                    key_buffer[row, :, pl.ds(group * HD, HD)],
                    (((1,), (1,)), ((), ())),
                    preferred_element_type=jnp.float32,
                )
    for i in range(2):
        copies[4 + i].wait()
        for row in range(i * half_rows, (i + 1) * half_rows):
            live = place < lengths[row]
            for group in range(groups):
                mine = pl.ds(row, lines, stride=rows)
                scores = score_buffer[row * groups + group]
                scores = jnp.where(live, scores * score_scale, masked_score)
                top = jnp.max(scores, axis=1, keepdims=True)
                exps = jnp.exp(scores - top)
                total = jnp.sum(exps, axis=1, keepdims=True)
                acc = jnp.dot(
                    exps.astype(jnp.bfloat16),
                    value_buffer[row, :, pl.ds(group * HD, HD)],
                    preferred_element_type=jnp.float32,
                )
                acc_out[group, mine, :] = acc
                top_out[group, mine, :] = jnp.broadcast_to(top, acc.shape)
                total_out[group, mine, :] = jnp.broadcast_to(total, acc.shape)
    copies[6].wait()
    gain_out[...] = gain_buffer[...].astype(jnp.float32)
    for copy in copies[7:]:
        copy.wait()


def cache_call(lengths, queries, keys, values, gain, bias, hidden):
    steps, rows, query_width = queries.shape
    cache_span, key_width = keys.shape[1:]
    groups = key_width // HD
    lines = steps * (query_width // key_width)
    block = (groups, lines * rows, HD)
    operands = (lengths, queries, keys, values, gain, bias, hidden)
    return pl.pallas_call(
        cache_kernel,
        out_shape=(
            pltpu.VMEM(gain.shape, jnp.float32),
            pltpu.VMEM(bias.shape, bias.dtype),
            pltpu.VMEM(hidden.shape, hidden.dtype),
            pltpu.VMEM(block, jnp.float32),
            pltpu.VMEM(block, jnp.float32),
            pltpu.VMEM(block, jnp.float32),
            pltpu.VMEM(block, jnp.float32),
        ),
        in_specs=[HBM] * len(operands),
        out_specs=(VMEM,) * 7,
        scratch_shapes=[
            pltpu.SMEM(lengths.shape, jnp.int32),
            pltpu.VMEM(queries.shape, queries.dtype),
            pltpu.VMEM(gain.shape, gain.dtype),
            pltpu.VMEM(keys.shape, keys.dtype),
            pltpu.VMEM(values.shape, values.dtype),
            pltpu.VMEM((rows * groups, lines, cache_span), jnp.float32),
            pltpu.SemaphoreType.DMA((9,)),
        ],
        compiler_params=pltpu.CompilerParams(vmem_limit_bytes=16 << 20),
        cost_estimate=pl.CostEstimate(flops=2 * 67 << 20, bytes_accessed=5 << 20, transcendentals=0),
        name="cache_attention",
    )(*[pltpu.with_memory_space_constraint(x, pltpu.HBM) for x in operands])


def rows_of(ref):
    return jnp.concatenate([ref[s].astype(jnp.float32) for s in range(ref.shape[0])], axis=0)


def pack_kernel(down_ref, up_ref, out_ref, sems):
    share = out_ref.shape[1]
    width = down_ref.shape[2]
    at = pl.ds(pl.multiple_of(lax.axis_index("tp") * share, share), share)
    down = pltpu.make_async_copy(
        down_ref.at[:, at, :], out_ref.at[:, :, pl.ds(0, width)], sems.at[0]
    )
    up = pltpu.make_async_copy(
        up_ref, out_ref.at[:, :, pl.ds(width, up_ref.shape[2])], sems.at[1]
    )
    down.start()
    up.start()
    down.wait()
    up.wait()


def pack_call(down, up):
    kinds, share, columns = up.shape
    return pl.pallas_call(
        pack_kernel,
        out_shape=pltpu.VMEM((kinds, share, down.shape[2] + columns), down.dtype),
        in_specs=[HBM] * 2,
        out_specs=VMEM,
        scratch_shapes=[pltpu.SemaphoreType.DMA((2,))],
        name="pack_factors",
    )(*[pltpu.with_memory_space_constraint(x, pltpu.HBM) for x in (down, up)])


def scaled_block(part, gain_ref, block):
    steps, rows, width = part.shape
    chunks = width // HD
    gain = gain_ref[pl.ds(pl.multiple_of(block * chunks, chunks), chunks)]
    values = rows_of(part)
    squares = jnp.zeros((steps * rows, HD), jnp.float32)
    scaled = []
    for i in range(chunks):
        chunk = values[:, i * HD : (i + 1) * HD]
        squares += chunk * chunk
        scaled.append((chunk * gain[i : i + 1]).astype(jnp.bfloat16))
    return jnp.concatenate(scaled, axis=1), squares


def rotation_tables(lengths, steps, rows, cos_out, sin_out):
    lane = lax.broadcasted_iota(jnp.int32, (rows, HD), 1)
    half = HD // 2
    second = lane >= half
    index = jnp.where(second, lane - half, lane).astype(jnp.float32)
    inv_freq = jnp.exp(index * (-2.0 * math.log(rope_base) / HD))
    row_index = lax.broadcasted_iota(jnp.int32, (rows, HD), 0)
    row_lengths = jnp.zeros((rows, HD), jnp.int32)
    for row in range(rows):
        row_lengths = jnp.where(row_index == row, lengths[row], row_lengths)
    for step in range(steps):
        angles = (row_lengths + step).astype(jnp.float32) * inv_freq
        sine = jnp.sin(angles)
        cos_out[pl.ds(step * rows, rows)] = jnp.cos(angles)
        sin_out[pl.ds(step * rows, rows)] = jnp.where(second, sine, -sine)


def scale_kernel(near, far, lengths_ref, weight_ref, gain_ref, *rest):
    scaled_out, near_out, far_out, square_out, near_weight, far_weight, cos_out, sin_out = rest[-12:-4]
    lengths, length_sem, near_sems, far_sems = rest[-4:]
    parts = rest[:-12]
    steps, rows, width = parts[0].shape
    length_copy = pltpu.make_async_copy(lengths_ref, lengths, length_sem)
    length_copy.start()
    copies = copy_blocks(near, width, weight_ref, near_weight, near_sems)
    copies += copy_blocks(far, width, weight_ref, far_weight, far_sems)
    me = lax.axis_index("tp")
    offsets = near + far
    total = None
    for k, part in enumerate(parts):
        block = me ^ offsets[k]
        scaled, squares = scaled_block(part, gain_ref, block)
        total = squares if total is None else total + squares
        scaled_out[:, pl.ds(pl.multiple_of(block * width, width), width)] = scaled
        if k < len(near):
            near_out[:, k * width : (k + 1) * width] = scaled
        else:
            i = k - len(near)
            far_out[:, i * width : (i + 1) * width] = scaled
    at = pl.ds(pl.multiple_of((me ^ offsets[-1]) * width, width), width)
    scaled_out[:, at] = jnp.zeros_like(scaled)
    square_out[...] = total
    length_copy.wait()
    rotation_tables(lengths, steps, rows, cos_out, sin_out)
    for copy in copies:
        copy.wait()


def scale_call(near, far, lengths, weight, gain, parts):
    steps, rows, width = parts[0].shape
    count = steps * rows
    return pl.pallas_call(
        functools.partial(scale_kernel, near, far),
        out_shape=(
            pltpu.VMEM((count, (len(near) + len(far)) * width), jnp.bfloat16),
            pltpu.VMEM((count, len(near) * width), jnp.bfloat16),
            pltpu.VMEM((count, (len(far) - 1) * width), jnp.bfloat16),
            pltpu.VMEM((count, HD), jnp.float32),
            pltpu.VMEM((len(near) * width,) + weight.shape[1:], weight.dtype),
            pltpu.VMEM((len(far) * width,) + weight.shape[1:], weight.dtype),
            pltpu.VMEM((count, HD), jnp.float32),
            pltpu.VMEM((count, HD), jnp.float32),
        ),
        in_specs=[HBM] * 2 + [VMEM] * (1 + len(parts)),
        out_specs=(VMEM,) * 8,
        scratch_shapes=[
            pltpu.SMEM(lengths.shape, jnp.int32),
            pltpu.SemaphoreType.DMA,
            pltpu.SemaphoreType.DMA((len(near),)),
            pltpu.SemaphoreType.DMA((len(far),)),
        ],
        compiler_params=pltpu.CompilerParams(vmem_limit_bytes=8 << 20),
        cost_estimate=pl.CostEstimate(flops=0, bytes_accessed=9 << 20, transcendentals=0),
        name="scale_features",
    )(*[pltpu.with_memory_space_constraint(x, pltpu.HBM) for x in (lengths, weight)], gain, *parts)


def inner_kernel(last, scaled_ref, far_ref, square_ref, gain_ref, part_ref, *rest):
    far_out, square_out = rest[-2:]
    packs, inner_out = (rest[:-3], rest[-3]) if len(rest) > 2 else ((), None)
    block = lax.axis_index("tp") ^ last
    late, squares = scaled_block(part_ref, gain_ref, block)
    width = late.shape[1]
    far_out[:, : far_ref.shape[1]] = far_ref[...]
    far_out[:, far_ref.shape[1] :] = late
    squares = jnp.sum(squares + square_ref[...], axis=1, keepdims=True)
    square_out[...] = jnp.broadcast_to(squares, square_out.shape)
    if not packs:
        return
    me = lax.axis_index("wide")
    total = []
    for offset, pack in enumerate(packs):
        mine = me ^ offset
        early = scaled_ref[:, pl.ds(pl.multiple_of(mine * width, width), width)]
        total.append(
            lax.dot_general(
                jnp.where(mine == block, late, early),
                pack[:, :, :width].reshape(inner_out.shape[1], width),
                (((1,), (1,)), ((), ())),
                preferred_element_type=jnp.float32,
            )
        )
    inner_out[...] = sum(total[1:], total[0])


def inner_call(last, scaled, far, square, gain, part, packs):
    count, width = far.shape[0], part.shape[2]
    shapes = [
        pltpu.VMEM((count, far.shape[1] + width), far.dtype),
        pltpu.VMEM(square.shape, jnp.float32),
    ]
    if packs:
        kinds, share, _ = packs[0].shape
        shapes = [pltpu.VMEM((count, kinds * share), jnp.float32)] + shapes
    return pl.pallas_call(
        functools.partial(inner_kernel, last),
        out_shape=tuple(shapes),
        in_specs=[VMEM] * (5 + len(packs)),
        out_specs=(VMEM,) * len(shapes),
        compiler_params=pltpu.CompilerParams(vmem_limit_bytes=8 << 20),
        name="rank_inner",
    )(scaled, far, square, gain, part, *packs)


def up_kernel(*refs):
    packs, up_out = refs[:-1], refs[-1]
    kinds, share, pack_width = packs[0].shape
    columns = up_out.shape[1] // kinds
    me = lax.axis_index("wide") if len(packs) > 1 else 0
    up_out[...] = jnp.zeros_like(up_out)
    for offset, pack in enumerate(packs):
        for kind in range(kinds):
            at = pl.multiple_of(((me ^ offset) * kinds + kind) * share, share)
            up_out[pl.ds(at, share), kind * columns : (kind + 1) * columns] = pack[
                kind, :, pack_width - columns :
            ]


def up_call(packs, columns):
    kinds, share, _ = packs[0].shape
    return pl.pallas_call(
        up_kernel,
        out_shape=pltpu.VMEM((len(packs) * kinds * share, kinds * columns), packs[0].dtype),
        in_specs=[VMEM] * len(packs),
        out_specs=VMEM,
        compiler_params=pltpu.CompilerParams(vmem_limit_bytes=8 << 20),
        name="lay_out_up",
    )(*packs)


def final_kernel(width, blocks, near_ref, far_ref, square_ref, bias_ref, *rest):
    query_ref, acc_ref, top_ref, total_ref, cos_ref, sin_ref = rest[:6]
    inner_refs = rest[6 : 6 + blocks]
    up_ref, keys_out, values_out, attended_out, inner_buffer = rest[6 + blocks :]
    steps, rows, columns = keys_out.shape
    count = steps * rows
    groups, size, _ = query_ref.shape
    per_group = size // count
    kinds = bias_ref.shape[0]
    row_scale = lax.rsqrt(square_ref[:, :1] * (1.0 / width) + norm_eps)
    me = lax.axis_index("tp") if blocks > 1 else 0
    for i in range(blocks):
        inner_buffer[me ^ i] = inner_refs[i][...]
    inner = jnp.concatenate([inner_buffer[i] for i in range(blocks)], axis=1)
    high = inner.astype(jnp.bfloat16)
    low = (inner - high.astype(jnp.float32)).astype(jnp.bfloat16)
    lora = jnp.dot(
        jnp.concatenate([high, low], axis=0), up_ref[...], preferred_element_type=jnp.float32
    )
    lora = lora[:count] + lora[count:]
    bias = bias_ref[...].astype(jnp.float32)
    linear = []
    for kind in range(kinds):
        base = near_ref[kind] + far_ref[kind]
        part = lora[:, kind * columns : (kind + 1) * columns]
        linear.append((base + adapter_scale * part) * row_scale + bias[kind : kind + 1])
    cosine, sine = cos_ref[...], sin_ref[...]
    line = lax.broadcasted_iota(jnp.int32, (size, count), 0)
    other = lax.broadcasted_iota(jnp.int32, (size, count), 1)
    live = (line % rows == other % rows) & (other // rows <= line // rows % steps)
    for group in range(groups):
        at = slice(group * HD, (group + 1) * HD)
        key = linear[0][:, at]
        key = (key * cosine + pltpu.roll(key, HD // 2, 1) * sine).astype(jnp.bfloat16)
        value = linear[1][:, at].astype(jnp.bfloat16)
        for step in range(steps):
            keys_out[step, :, at] = key[step * rows : (step + 1) * rows]
            values_out[step, :, at] = value[step * rows : (step + 1) * rows]
        scores = lax.dot_general(
            query_ref[group].astype(jnp.bfloat16),
            key,
            (((1,), (1,)), ((), ())),
            preferred_element_type=jnp.float32,
        )
        scores = jnp.where(live, scores * score_scale, masked_score)
        old_top = top_ref[group][:, :1]
        top = jnp.maximum(old_top, jnp.max(scores, axis=1, keepdims=True))
        exps = jnp.exp(scores - top)
        keep = jnp.exp(old_top - top)
        total = total_ref[group][:, :1] * keep + jnp.sum(exps, axis=1, keepdims=True)
        acc = acc_ref[group] * keep + jnp.dot(
            exps.astype(jnp.bfloat16), value, preferred_element_type=jnp.float32
        )
        attended = (acc / total).astype(jnp.bfloat16)
        for head in range(per_group):
            lanes = pl.ds((group * per_group + head) * HD, HD)
            for step in range(steps):
                tile = (head * steps + step) * rows
                attended_out[step, :, lanes] = attended[tile : tile + rows]


def final_call(shape, width, near, far, square, bias, cached, inner, up):
    steps, rows, query_width = shape
    columns = near.shape[2]
    small = jax.ShapeDtypeStruct((steps, rows, columns), jnp.bfloat16)
    return pl.pallas_call(
        functools.partial(final_kernel, width, len(inner)),
        out_shape=(small, small, jax.ShapeDtypeStruct(shape, jnp.bfloat16)),
        in_specs=[VMEM] * (5 + len(cached) + len(inner)),
        out_specs=(VMEM,) * 3,
        scratch_shapes=[pltpu.VMEM((len(inner),) + inner[0].shape, jnp.float32)],
        compiler_params=pltpu.CompilerParams(vmem_limit_bytes=8 << 20),
        name="fresh_attention",
    )(near, far, square, bias, *cached, *inner, up)


def dot(rows, weight):
    return jnp.einsum("md,dkc->kmc", rows, weight, preferred_element_type=jnp.float32)


def swap(block, axis, offset, count):
    return lax.ppermute(block, axis, [(i, i ^ offset) for i in range(count)])


def on_device(
    wide_count,
    tp_count,
    hidden,
    input_norm_gain,
    key_value_weight,
    key_value_bias,
    adapter_down_factor,
    adapter_up_factor,
    queries,
    stored_rotated_keys,
    stored_value_rows,
    lengths,
):
    steps, rows, part_width = hidden.shape
    width = part_width * tp_count
    kinds, ranks, down_width = adapter_down_factor.shape
    gain = input_norm_gain.reshape(width // HD, HD)
    up_part = jnp.transpose(adapter_up_factor, (0, 2, 1))
    direct = wide_count == tp_count == 4
    tp_parts = [swap(hidden, "tp", offset, tp_count) for offset in (1, 2, 3)]
    if direct:
        pack = pack_call(adapter_down_factor, up_part)
        second = swap(pack, "wide", 2, wide_count)
        first = swap(pack, "wide", 1, wide_count)
    near, far = (0, 1), (2, 3)
    gain_rows, bias, mine, *cached = cache_call(
        lengths, queries, stored_rotated_keys, stored_value_rows, gain, key_value_bias, hidden
    )
    if direct:
        third, gain_rows = lax.optimization_barrier((second, gain_rows))
        packs = [pack, first, second, swap(third, "wide", 1, wide_count)]
    scaled, near_scaled, far_scaled, square, near_weight, far_weight, *tables = scale_call(
        near, far, lengths, key_value_weight, gain_rows, [mine] + tp_parts[:2]
    )
    near_base = dot(near_scaled, near_weight)
    if direct:
        scaled, near_base = lax.optimization_barrier((scaled, near_base))
        inner, far_scaled, square = inner_call(
            far[-1], scaled, far_scaled, square, gain_rows, tp_parts[2], packs
        )
        inner, far_scaled, packs = lax.optimization_barrier((inner, far_scaled, packs))
        inner = [inner] + [swap(inner, "tp", offset, tp_count) for offset in (1, 2, 3)]
    else:
        far_scaled, square = inner_call(
            far[-1], scaled, far_scaled, square, gain_rows, tp_parts[2], []
        )
        down = lax.all_gather(adapter_down_factor, "wide", axis=2, tiled=True)
        rows_full = lax.all_gather(hidden, "tp", axis=2, tiled=True).astype(jnp.float32)
        rows_full = (rows_full * input_norm_gain.astype(jnp.float32)).astype(jnp.bfloat16)
        inner = jnp.einsum("srd,kad->srka", rows_full, down, preferred_element_type=jnp.float32)
        inner = [inner.reshape(steps * rows, kinds * ranks)]
        packs = [lax.all_gather(up_part, "wide", axis=1, tiled=True)]
    far_base = dot(far_scaled, far_weight)
    up = up_call(packs, bias.shape[1])
    return final_call(
        queries.shape, width, near_base, far_base, square, bias, cached + tables, inner, up
    )


def solution(mesh):
    in_specs = (
        P(None, ("groups", "wide"), "tp"),
        P(),
        P(None, None, "tp"),
        P(None, "tp"),
        P("groups", None, "wide"),
        P("groups", "tp", "wide"),
        P(None, ("groups", "wide"), "tp"),
        P(("groups", "wide"), None, "tp"),
        P(("groups", "wide"), None, "tp"),
        P(("groups", "wide")),
    )
    out_specs = (
        P(None, ("groups", "wide"), "tp"),
        P(None, ("groups", "wide"), "tp"),
        P(None, ("groups", "wide"), "tp"),
    )
    body = functools.partial(on_device, mesh.shape["wide"], mesh.shape["tp"])
    return jax.shard_map(
        body, mesh=mesh, in_specs=in_specs, out_specs=out_specs, check_vma=False
    )
```

```python
import functools
import math

import jax
import jax.numpy as jnp
from jax import lax
from jax.experimental import pallas as pl
from jax.experimental.pallas import tpu as pltpu
from jax.sharding import PartitionSpec as P

HD = 128


norm_eps = 1e-06
adapter_scale = 2.0
rope_base = 1000000.0
masked_score = -1e30
score_scale = 1.0 / math.sqrt(HD)

VMEM = pl.BlockSpec(memory_space=pltpu.VMEM)
HBM = pl.BlockSpec(memory_space=pltpu.HBM)


def query_block(query_ref, group, per_group):
    steps = query_ref.shape[0]
    tiles = []
    for head in range(per_group):
        at = (group * per_group + head) * HD
        for step in range(steps):
            tiles.append(query_ref[step, :, at : at + HD].astype(jnp.float32))
    return jnp.concatenate(tiles, axis=0)


def copy_blocks(offsets, width, weight_ref, out_ref, sems):
    me = lax.axis_index("tp")
    copies = []
    for i, offset in enumerate(offsets):
        block = pl.ds(pl.multiple_of((me ^ offset) * width, width), width)
        copies.append(
            pltpu.make_async_copy(
                weight_ref.at[block], out_ref.at[pl.ds(i * width, width)], sems.at[i]
            )
        )
        copies[-1].start()
    return copies


def cache_kernel(
    near,
    lengths_ref,
    query_ref,
    key_ref,
    value_ref,
    gain_ref,
    bias_ref,
    hidden_ref,
    weight_ref,
    near_out,
    gain_out,
    bias_out,
    hidden_out,
    query_out,
    acc_out,
    top_out,
    total_out,
    lengths,
    queries,
    gain_buffer,
    key_buffer,
    value_buffer,
    score_buffer,
    sems,
    weight_sems,
):
    steps, rows, query_width = query_ref.shape
    cache_span = key_ref.shape[1]
    groups = key_ref.shape[2] // HD
    per_group = query_width // HD // groups
    lines = steps * per_group
    half_rows = rows // 2
    halves = [pl.ds(0, half_rows), pl.ds(half_rows, half_rows)]
    copies = [
        (lengths_ref, lengths),
        (query_ref, queries),
        (key_ref.at[halves[0]], key_buffer.at[halves[0]]),
        (key_ref.at[halves[1]], key_buffer.at[halves[1]]),
        (value_ref.at[halves[0]], value_buffer.at[halves[0]]),
        (value_ref.at[halves[1]], value_buffer.at[halves[1]]),
        (gain_ref, gain_buffer),
        (bias_ref, bias_out),
        (hidden_ref, hidden_out),
    ]
    copies = [pltpu.make_async_copy(*pair, sems.at[i]) for i, pair in enumerate(copies)]
    for copy in copies:
        copy.start()
    copies += copy_blocks(near, hidden_ref.shape[2], weight_ref, near_out, weight_sems)

    copies[0].wait()
    copies[1].wait()
    for group in range(groups):
        query_out[group] = query_block(queries, group, per_group)

    place = lax.broadcasted_iota(jnp.int32, (lines, cache_span), 1)
    for i in range(2):
        copies[2 + i].wait()
        for row in range(i * half_rows, (i + 1) * half_rows):
            for group in range(groups):
                query = query_out[group, pl.ds(row, lines, stride=rows), :].astype(jnp.bfloat16)
                score_buffer[row * groups + group] = lax.dot_general(
                    query,
                    key_buffer[row, :, pl.ds(group * HD, HD)],
                    (((1,), (1,)), ((), ())),
                    preferred_element_type=jnp.float32,
                )
    for i in range(2):
        copies[4 + i].wait()
        for row in range(i * half_rows, (i + 1) * half_rows):
            live = place < lengths[row]
            for group in range(groups):
                mine = pl.ds(row, lines, stride=rows)
                scores = score_buffer[row * groups + group]
                scores = jnp.where(live, scores * score_scale, masked_score)
                top = jnp.max(scores, axis=1, keepdims=True)
                exps = jnp.exp(scores - top)
                total = jnp.sum(exps, axis=1, keepdims=True)
                acc = jnp.dot(
                    exps.astype(jnp.bfloat16),
                    value_buffer[row, :, pl.ds(group * HD, HD)],
                    preferred_element_type=jnp.float32,
                )
                acc_out[group, mine, :] = acc
                top_out[group, mine, :] = jnp.broadcast_to(top, acc.shape)
                total_out[group, mine, :] = jnp.broadcast_to(total, acc.shape)
    copies[6].wait()
    gain_out[...] = gain_buffer[...].astype(jnp.float32)
    for copy in copies[7:]:
        copy.wait()


def cache_call(near, lengths, queries, keys, values, gain, bias, hidden, weight):
    steps, rows, query_width = queries.shape
    cache_span, key_width = keys.shape[1:]
    groups = key_width // HD
    lines = steps * (query_width // key_width)
    block = (groups, lines * rows, HD)
    operands = (lengths, queries, keys, values, gain, bias, hidden, weight)
    near_weight = (len(near) * hidden.shape[2],) + weight.shape[1:]
    return pl.pallas_call(
        functools.partial(cache_kernel, near),
        out_shape=(
            pltpu.VMEM(near_weight, weight.dtype),
            pltpu.VMEM(gain.shape, jnp.float32),
            pltpu.VMEM(bias.shape, bias.dtype),
            pltpu.VMEM(hidden.shape, hidden.dtype),
            pltpu.VMEM(block, jnp.float32),
            pltpu.VMEM(block, jnp.float32),
            pltpu.VMEM(block, jnp.float32),
            pltpu.VMEM(block, jnp.float32),
        ),
        in_specs=[HBM] * len(operands),
        out_specs=(VMEM,) * 8,
        scratch_shapes=[
            pltpu.SMEM(lengths.shape, jnp.int32),
            pltpu.VMEM(queries.shape, queries.dtype),
            pltpu.VMEM(gain.shape, gain.dtype),
            pltpu.VMEM(keys.shape, keys.dtype),
            pltpu.VMEM(values.shape, values.dtype),
            pltpu.VMEM((rows * groups, lines, cache_span), jnp.float32),
            pltpu.SemaphoreType.DMA((9,)),
            pltpu.SemaphoreType.DMA((len(near),)),
        ],
        compiler_params=pltpu.CompilerParams(vmem_limit_bytes=16 << 20),
        cost_estimate=pl.CostEstimate(flops=2 * 67 << 20, bytes_accessed=5 << 20, transcendentals=0),
        name="cache_attention",
    )(*[pltpu.with_memory_space_constraint(x, pltpu.HBM) for x in operands])


def rows_of(ref):
    return jnp.concatenate([ref[s].astype(jnp.float32) for s in range(ref.shape[0])], axis=0)


def pack_kernel(down_ref, up_ref, out_ref, sems):
    share = out_ref.shape[1]
    width = down_ref.shape[2]
    at = pl.ds(pl.multiple_of(lax.axis_index("tp") * share, share), share)
    copies = [(up_ref, out_ref.at[:, :, pl.ds(width, up_ref.shape[2])])]
    half = width // 2
    for kind in range(down_ref.shape[0]):
        for first in (0, half):
            lanes = pl.ds(first, half)
            copies.append((down_ref.at[kind, at, lanes], out_ref.at[kind, :, lanes]))
    copies = [pltpu.make_async_copy(*pair, sems.at[i]) for i, pair in enumerate(copies)]
    for copy in copies:
        copy.start()
    for copy in copies:
        copy.wait()


def pack_call(down, up):
    kinds, share, columns = up.shape
    return pl.pallas_call(
        pack_kernel,
        out_shape=pltpu.VMEM((kinds, share, down.shape[2] + columns), down.dtype),
        in_specs=[HBM] * 2,
        out_specs=VMEM,
        scratch_shapes=[pltpu.SemaphoreType.DMA((1 + 2 * kinds,))],
        name="pack_factors",
    )(*[pltpu.with_memory_space_constraint(x, pltpu.HBM) for x in (down, up)])


def scaled_block(part, gain_ref, block):
    steps, rows, width = part.shape
    chunks = width // HD
    gain = gain_ref[pl.ds(pl.multiple_of(block * chunks, chunks), chunks)]
    values = rows_of(part)
    squares = jnp.zeros((steps * rows, HD), jnp.float32)
    scaled = []
    for i in range(chunks):
        chunk = values[:, i * HD : (i + 1) * HD]
        squares += chunk * chunk
        scaled.append((chunk * gain[i : i + 1]).astype(jnp.bfloat16))
    return jnp.concatenate(scaled, axis=1), squares


def rotation_tables(lengths, steps, rows, cos_out, sin_out):
    lane = lax.broadcasted_iota(jnp.int32, (rows, HD), 1)
    half = HD // 2
    second = lane >= half
    index = jnp.where(second, lane - half, lane).astype(jnp.float32)
    inv_freq = jnp.exp(index * (-2.0 * math.log(rope_base) / HD))
    row_index = lax.broadcasted_iota(jnp.int32, (rows, HD), 0)
    row_lengths = jnp.zeros((rows, HD), jnp.int32)
    for row in range(rows):
        row_lengths = jnp.where(row_index == row, lengths[row], row_lengths)
    for step in range(steps):
        angles = (row_lengths + step).astype(jnp.float32) * inv_freq
        sine = jnp.sin(angles)
        cos_out[pl.ds(step * rows, rows)] = jnp.cos(angles)
        sin_out[pl.ds(step * rows, rows)] = jnp.where(second, sine, -sine)


def scale_kernel(near, far, lengths_ref, weight_ref, gain_ref, *rest):
    scaled_out, near_out, far_out, square_out, far_weight, cos_out, sin_out = rest[-10:-3]
    lengths, length_sem, far_sems = rest[-3:]
    parts = rest[:-10]
    steps, rows, width = parts[0].shape
    length_copy = pltpu.make_async_copy(lengths_ref, lengths, length_sem)
    length_copy.start()
    copies = copy_blocks(far, width, weight_ref, far_weight, far_sems)
    me = lax.axis_index("tp")
    offsets = near + far
    total = None
    for k, part in enumerate(parts):
        block = me ^ offsets[k]
        scaled, squares = scaled_block(part, gain_ref, block)
        total = squares if total is None else total + squares
        scaled_out[:, pl.ds(pl.multiple_of(block * width, width), width)] = scaled
        if k < len(near):
            near_out[:, k * width : (k + 1) * width] = scaled
        else:
            i = k - len(near)
            far_out[:, i * width : (i + 1) * width] = scaled
    at = pl.ds(pl.multiple_of((me ^ offsets[-1]) * width, width), width)
    scaled_out[:, at] = jnp.zeros_like(scaled)
    square_out[...] = total
    length_copy.wait()
    rotation_tables(lengths, steps, rows, cos_out, sin_out)
    for copy in copies:
        copy.wait()


def scale_call(near, far, lengths, weight, gain, parts):
    steps, rows, width = parts[0].shape
    count = steps * rows
    return pl.pallas_call(
        functools.partial(scale_kernel, near, far),
        out_shape=(
            pltpu.VMEM((count, (len(near) + len(far)) * width), jnp.bfloat16),
            pltpu.VMEM((count, len(near) * width), jnp.bfloat16),
            pltpu.VMEM((count, (len(far) - 1) * width), jnp.bfloat16),
            pltpu.VMEM((count, HD), jnp.float32),
            pltpu.VMEM((len(far) * width,) + weight.shape[1:], weight.dtype),
            pltpu.VMEM((count, HD), jnp.float32),
            pltpu.VMEM((count, HD), jnp.float32),
        ),
        in_specs=[HBM] * 2 + [VMEM] * (1 + len(parts)),
        out_specs=(VMEM,) * 7,
        scratch_shapes=[
            pltpu.SMEM(lengths.shape, jnp.int32),
            pltpu.SemaphoreType.DMA,
            pltpu.SemaphoreType.DMA((len(far),)),
        ],
        compiler_params=pltpu.CompilerParams(vmem_limit_bytes=8 << 20),
        cost_estimate=pl.CostEstimate(flops=0, bytes_accessed=9 << 20, transcendentals=0),
        name="scale_features",
    )(*[pltpu.with_memory_space_constraint(x, pltpu.HBM) for x in (lengths, weight)], gain, *parts)


def inner_kernel(last, scaled_ref, far_ref, square_ref, gain_ref, part_ref, *rest):
    far_out, square_out = rest[-2:]
    packs, inner_out = (rest[:-3], rest[-3]) if len(rest) > 2 else ((), None)
    block = lax.axis_index("tp") ^ last
    late, squares = scaled_block(part_ref, gain_ref, block)
    width = late.shape[1]
    far_out[:, : far_ref.shape[1]] = far_ref[...]
    far_out[:, far_ref.shape[1] :] = late
    squares = jnp.sum(squares + square_ref[...], axis=1, keepdims=True)
    square_out[...] = jnp.broadcast_to(squares, square_out.shape)
    if not packs:
        return
    me = lax.axis_index("wide")
    total = []
    for offset, pack in enumerate(packs):
        mine = me ^ offset
        early = scaled_ref[:, pl.ds(pl.multiple_of(mine * width, width), width)]
        total.append(
            lax.dot_general(
                jnp.where(mine == block, late, early),
                pack[:, :, :width].reshape(pack.shape[0] * pack.shape[1], width),
                (((1,), (1,)), ((), ())),
                preferred_element_type=jnp.float32,
            )
        )
    total = sum(total[1:], total[0])
    lines = inner_out.shape[0]
    inner_out[...] = jnp.concatenate(
        [total[i : i + lines] for i in range(0, total.shape[0], lines)], axis=1
    )


def inner_call(last, scaled, far, square, gain, part, packs):
    count, width = far.shape[0], part.shape[2]
    shapes = [
        pltpu.VMEM((count, far.shape[1] + width), far.dtype),
        pltpu.VMEM(square.shape, jnp.float32),
    ]
    if packs:
        kinds, share, _ = packs[0].shape
        shapes = [pltpu.VMEM((count * kinds * share // HD, HD), jnp.float32)] + shapes
    return pl.pallas_call(
        functools.partial(inner_kernel, last),
        out_shape=tuple(shapes),
        in_specs=[VMEM] * (5 + len(packs)),
        out_specs=(VMEM,) * len(shapes),
        compiler_params=pltpu.CompilerParams(vmem_limit_bytes=8 << 20),
        name="rank_inner",
    )(scaled, far, square, gain, part, *packs)


def up_kernel(*refs):
    packs, up_out = refs[:-1], refs[-1]
    kinds, share, pack_width = packs[0].shape
    columns = up_out.shape[1] // kinds
    me = lax.axis_index("wide") if len(packs) > 1 else 0
    up_out[...] = jnp.zeros_like(up_out)
    for offset, pack in enumerate(packs):
        for kind in range(kinds):
            at = pl.multiple_of(((me ^ offset) * kinds + kind) * share, share)
            up_out[pl.ds(at, share), kind * columns : (kind + 1) * columns] = pack[
                kind, :, pack_width - columns :
            ]


def up_call(packs, columns):
    kinds, share, _ = packs[0].shape
    return pl.pallas_call(
        up_kernel,
        out_shape=pltpu.VMEM((len(packs) * kinds * share, kinds * columns), packs[0].dtype),
        in_specs=[VMEM] * len(packs),
        out_specs=VMEM,
        compiler_params=pltpu.CompilerParams(vmem_limit_bytes=8 << 20),
        name="lay_out_up",
    )(*packs)


def final_kernel(width, blocks, near_ref, far_ref, square_ref, bias_ref, *rest):
    query_ref, acc_ref, top_ref, total_ref, cos_ref, sin_ref = rest[:6]
    inner_refs = rest[6 : 6 + blocks]
    up_ref, keys_out, values_out, attended_out, inner_buffer = rest[6 + blocks :]
    steps, rows, columns = keys_out.shape
    count = steps * rows
    groups, size, _ = query_ref.shape
    per_group = size // count
    kinds = bias_ref.shape[0]
    row_scale = lax.rsqrt(square_ref[:, :1] * (1.0 / width) + norm_eps)
    me = lax.axis_index("tp") if blocks > 1 else 0
    for i in range(blocks):
        inner_buffer[me ^ i] = inner_refs[i][...]
    lines = inner_buffer.shape[1]
    share = inner_buffer.shape[2] * lines // count
    inner = jnp.concatenate(
        [
            jnp.concatenate(
                [inner_buffer[i, :, j * share : (j + 1) * share] for i in range(blocks)], axis=1
            )
            for j in range(count // lines)
        ],
        axis=0,
    )
    high = inner.astype(jnp.bfloat16)
    low = (inner - high.astype(jnp.float32)).astype(jnp.bfloat16)
    lora = jnp.dot(
        jnp.concatenate([high, low], axis=0), up_ref[...], preferred_element_type=jnp.float32
    )
    lora = lora[:count] + lora[count:]
    bias = bias_ref[...].astype(jnp.float32)
    linear = []
    for kind in range(kinds):
        base = near_ref[kind] + far_ref[kind]
        part = lora[:, kind * columns : (kind + 1) * columns]
        linear.append((base + adapter_scale * part) * row_scale + bias[kind : kind + 1])
    cosine, sine = cos_ref[...], sin_ref[...]
    line = lax.broadcasted_iota(jnp.int32, (size, count), 0)
    other = lax.broadcasted_iota(jnp.int32, (size, count), 1)
    live = (line % rows == other % rows) & (other // rows <= line // rows % steps)
    for group in range(groups):
        at = slice(group * HD, (group + 1) * HD)
        key = linear[0][:, at]
        key = (key * cosine + pltpu.roll(key, HD // 2, 1) * sine).astype(jnp.bfloat16)
        value = linear[1][:, at].astype(jnp.bfloat16)
        for step in range(steps):
            keys_out[step, :, at] = key[step * rows : (step + 1) * rows]
            values_out[step, :, at] = value[step * rows : (step + 1) * rows]
        scores = lax.dot_general(
            query_ref[group].astype(jnp.bfloat16),
            key,
            (((1,), (1,)), ((), ())),
            preferred_element_type=jnp.float32,
        )
        scores = jnp.where(live, scores * score_scale, masked_score)
        old_top = top_ref[group][:, :1]
        top = jnp.maximum(old_top, jnp.max(scores, axis=1, keepdims=True))
        exps = jnp.exp(scores - top)
        keep = jnp.exp(old_top - top)
        total = total_ref[group][:, :1] * keep + jnp.sum(exps, axis=1, keepdims=True)
        acc = acc_ref[group] * keep + jnp.dot(
            exps.astype(jnp.bfloat16), value, preferred_element_type=jnp.float32
        )
        attended = (acc / total).astype(jnp.bfloat16)
        for head in range(per_group):
            lanes = pl.ds((group * per_group + head) * HD, HD)
            for step in range(steps):
                tile = (head * steps + step) * rows
                attended_out[step, :, lanes] = attended[tile : tile + rows]


def final_call(shape, width, near, far, square, bias, cached, inner, up):
    steps, rows, query_width = shape
    columns = near.shape[2]
    small = jax.ShapeDtypeStruct((steps, rows, columns), jnp.bfloat16)
    return pl.pallas_call(
        functools.partial(final_kernel, width, len(inner)),
        out_shape=(small, small, jax.ShapeDtypeStruct(shape, jnp.bfloat16)),
        in_specs=[VMEM] * (5 + len(cached) + len(inner)),
        out_specs=(VMEM,) * 3,
        scratch_shapes=[pltpu.VMEM((len(inner),) + inner[0].shape, jnp.float32)],
        compiler_params=pltpu.CompilerParams(vmem_limit_bytes=8 << 20),
        name="fresh_attention",
    )(near, far, square, bias, *cached, *inner, up)


def dot(rows, weight):
    return jnp.einsum("md,dkc->kmc", rows, weight, preferred_element_type=jnp.float32)


def swap(block, axis, offset, count):
    return lax.ppermute(block, axis, [(i, i ^ offset) for i in range(count)])


def on_device(
    wide_count,
    tp_count,
    hidden,
    input_norm_gain,
    key_value_weight,
    key_value_bias,
    adapter_down_factor,
    adapter_up_factor,
    queries,
    stored_rotated_keys,
    stored_value_rows,
    lengths,
):
    steps, rows, part_width = hidden.shape
    width = part_width * tp_count
    kinds, ranks, down_width = adapter_down_factor.shape
    gain = input_norm_gain.reshape(width // HD, HD)
    up_part = jnp.transpose(adapter_up_factor, (0, 2, 1))
    direct = wide_count == tp_count == 4
    tp_parts = [swap(hidden, "tp", offset, tp_count) for offset in (1, 2, 3)]
    if direct:
        pack = pack_call(adapter_down_factor, up_part)
        second = swap(pack, "wide", 2, wide_count)
        first = swap(pack, "wide", 1, wide_count)
    near, far = (0, 1), (2, 3)
    near_weight, gain_rows, bias, mine, *cached = cache_call(
        near,
        lengths,
        queries,
        stored_rotated_keys,
        stored_value_rows,
        gain,
        key_value_bias,
        hidden,
        key_value_weight,
    )
    if direct:
        third, gain_rows = lax.optimization_barrier((second, gain_rows))
        packs = [pack, first, second, swap(third, "wide", 1, wide_count)]
    scaled, near_scaled, far_scaled, square, far_weight, *tables = scale_call(
        near, far, lengths, key_value_weight, gain_rows, [mine] + tp_parts[:2]
    )
    near_base = dot(near_scaled, near_weight)
    if direct:
        scaled, near_base = lax.optimization_barrier((scaled, near_base))
        inner, far_scaled, square = inner_call(
            far[-1], scaled, far_scaled, square, gain_rows, tp_parts[2], packs
        )
        inner, far_scaled, packs = lax.optimization_barrier((inner, far_scaled, packs))
        inner = [inner] + [swap(inner, "tp", offset, tp_count) for offset in (1, 2, 3)]
    else:
        far_scaled, square = inner_call(
            far[-1], scaled, far_scaled, square, gain_rows, tp_parts[2], []
        )
        down = lax.all_gather(adapter_down_factor, "wide", axis=2, tiled=True)
        rows_full = lax.all_gather(hidden, "tp", axis=2, tiled=True).astype(jnp.float32)
        rows_full = (rows_full * input_norm_gain.astype(jnp.float32)).astype(jnp.bfloat16)
        inner = jnp.einsum("srd,kad->srka", rows_full, down, preferred_element_type=jnp.float32)
        inner = [inner.reshape(steps * rows, kinds * ranks)]
        packs = [lax.all_gather(up_part, "wide", axis=1, tiled=True)]
    far_base = dot(far_scaled, far_weight)
    up = up_call(packs, bias.shape[1])
    return final_call(
        queries.shape, width, near_base, far_base, square, bias, cached + tables, inner, up
    )


def solution(mesh):
    in_specs = (
        P(None, ("groups", "wide"), "tp"),
        P(),
        P(None, None, "tp"),
        P(None, "tp"),
        P("groups", None, "wide"),
        P("groups", "tp", "wide"),
        P(None, ("groups", "wide"), "tp"),
        P(("groups", "wide"), None, "tp"),
        P(("groups", "wide"), None, "tp"),
        P(("groups", "wide")),
    )
    out_specs = (
        P(None, ("groups", "wide"), "tp"),
        P(None, ("groups", "wide"), "tp"),
        P(None, ("groups", "wide"), "tp"),
    )
    body = functools.partial(on_device, mesh.shape["wide"], mesh.shape["tp"])
    return jax.shard_map(
        body, mesh=mesh, in_specs=in_specs, out_specs=out_specs, check_vma=False
    )
```

```python
import functools
import math

import jax
import jax.numpy as jnp
from jax import lax
from jax.experimental import pallas as pl
from jax.experimental.pallas import tpu as pltpu
from jax.sharding import PartitionSpec as P

HD = 128


norm_eps = 1e-06
adapter_scale = 2.0
rope_base = 1000000.0
masked_score = -1e30
score_scale = 1.0 / math.sqrt(HD)

VMEM = pl.BlockSpec(memory_space=pltpu.VMEM)
HBM = pl.BlockSpec(memory_space=pltpu.HBM)


def query_block(query_ref, group, per_group):
    steps = query_ref.shape[0]
    tiles = []
    for head in range(per_group):
        at = (group * per_group + head) * HD
        for step in range(steps):
            tiles.append(query_ref[step, :, at : at + HD].astype(jnp.float32))
    return jnp.concatenate(tiles, axis=0)


def copy_blocks(offsets, width, weight_ref, out_ref, sems):
    me = lax.axis_index("tp")
    copies = []
    for i, offset in enumerate(offsets):
        block = pl.ds(pl.multiple_of((me ^ offset) * width, width), width)
        copies.append(
            pltpu.make_async_copy(
                weight_ref.at[block], out_ref.at[pl.ds(i * width, width)], sems.at[i]
            )
        )
        copies[-1].start()
    return copies


def cache_kernel(
    lengths_ref,
    query_ref,
    key_ref,
    value_ref,
    gain_ref,
    bias_ref,
    hidden_ref,
    gain_out,
    bias_out,
    hidden_out,
    query_out,
    acc_out,
    top_out,
    total_out,
    lengths,
    queries,
    gain_buffer,
    key_buffer,
    value_buffer,
    score_buffer,
    sems,
):
    steps, rows, query_width = query_ref.shape
    cache_span = key_ref.shape[1]
    groups = key_ref.shape[2] // HD
    per_group = query_width // HD // groups
    lines = steps * per_group
    half_rows = rows // 2
    halves = [pl.ds(0, half_rows), pl.ds(half_rows, half_rows)]
    copies = [
        (lengths_ref, lengths),
        (query_ref, queries),
        (key_ref.at[halves[0]], key_buffer.at[halves[0]]),
        (key_ref.at[halves[1]], key_buffer.at[halves[1]]),
        (value_ref.at[halves[0]], value_buffer.at[halves[0]]),
        (value_ref.at[halves[1]], value_buffer.at[halves[1]]),
        (gain_ref, gain_buffer),
        (bias_ref, bias_out),
        (hidden_ref, hidden_out),
    ]
    copies = [pltpu.make_async_copy(*pair, sems.at[i]) for i, pair in enumerate(copies)]
    for copy in copies:
        copy.start()

    copies[0].wait()
    copies[1].wait()
    for group in range(groups):
        query_out[group] = query_block(queries, group, per_group)

    place = lax.broadcasted_iota(jnp.int32, (lines, cache_span), 1)
    for i in range(2):
        copies[2 + i].wait()
        for row in range(i * half_rows, (i + 1) * half_rows):
            for group in range(groups):
                query = query_out[group, pl.ds(row, lines, stride=rows), :].astype(jnp.bfloat16)
                score_buffer[row * groups + group] = lax.dot_general(
                    query,
                    key_buffer[row, :, pl.ds(group * HD, HD)],
                    (((1,), (1,)), ((), ())),
                    preferred_element_type=jnp.float32,
                )
    for i in range(2):
        copies[4 + i].wait()
        for row in range(i * half_rows, (i + 1) * half_rows):
            live = place < lengths[row]
            for group in range(groups):
                mine = pl.ds(row, lines, stride=rows)
                scores = score_buffer[row * groups + group]
                scores = jnp.where(live, scores * score_scale, masked_score)
                top = jnp.max(scores, axis=1, keepdims=True)
                exps = jnp.exp(scores - top)
                total = jnp.sum(exps, axis=1, keepdims=True)
                acc = jnp.dot(
                    exps.astype(jnp.bfloat16),
                    value_buffer[row, :, pl.ds(group * HD, HD)],
                    preferred_element_type=jnp.float32,
                )
                acc_out[group, mine, :] = acc
                top_out[group, mine, :] = jnp.broadcast_to(top, acc.shape)
                total_out[group, mine, :] = jnp.broadcast_to(total, acc.shape)
    copies[6].wait()
    gain_out[...] = gain_buffer[...].astype(jnp.float32)
    for copy in copies[7:]:
        copy.wait()


def cache_call(lengths, queries, keys, values, gain, bias, hidden):
    steps, rows, query_width = queries.shape
    cache_span, key_width = keys.shape[1:]
    groups = key_width // HD
    lines = steps * (query_width // key_width)
    block = (groups, lines * rows, HD)
    operands = (lengths, queries, keys, values, gain, bias, hidden)
    return pl.pallas_call(
        cache_kernel,
        out_shape=(
            pltpu.VMEM(gain.shape, jnp.float32),
            pltpu.VMEM(bias.shape, bias.dtype),
            pltpu.VMEM(hidden.shape, hidden.dtype),
            pltpu.VMEM(block, jnp.float32),
            pltpu.VMEM(block, jnp.float32),
            pltpu.VMEM(block, jnp.float32),
            pltpu.VMEM(block, jnp.float32),
        ),
        in_specs=[HBM] * len(operands),
        out_specs=(VMEM,) * 7,
        scratch_shapes=[
            pltpu.SMEM(lengths.shape, jnp.int32),
            pltpu.VMEM(queries.shape, queries.dtype),
            pltpu.VMEM(gain.shape, gain.dtype),
            pltpu.VMEM(keys.shape, keys.dtype),
            pltpu.VMEM(values.shape, values.dtype),
            pltpu.VMEM((rows * groups, lines, cache_span), jnp.float32),
            pltpu.SemaphoreType.DMA((9,)),
        ],
        compiler_params=pltpu.CompilerParams(vmem_limit_bytes=16 << 20),
        cost_estimate=pl.CostEstimate(flops=2 * 67 << 20, bytes_accessed=5 << 20, transcendentals=0),
        name="cache_attention",
    )(*[pltpu.with_memory_space_constraint(x, pltpu.HBM) for x in operands])


def rows_of(ref):
    return jnp.concatenate([ref[s].astype(jnp.float32) for s in range(ref.shape[0])], axis=0)


def pack_kernel(down_ref, up_ref, out_ref, sems):
    share = out_ref.shape[1]
    width = down_ref.shape[2]
    at = pl.ds(pl.multiple_of(lax.axis_index("tp") * share, share), share)
    copies = [(up_ref, out_ref.at[:, :, pl.ds(width, up_ref.shape[2])])]
    half = width // 2
    for kind in range(down_ref.shape[0]):
        for first in (0, half):
            lanes = pl.ds(first, half)
            copies.append((down_ref.at[kind, at, lanes], out_ref.at[kind, :, lanes]))
    copies = [pltpu.make_async_copy(*pair, sems.at[i]) for i, pair in enumerate(copies)]
    for copy in copies:
        copy.start()
    for copy in copies:
        copy.wait()


def pack_call(down, up):
    kinds, share, columns = up.shape
    return pl.pallas_call(
        pack_kernel,
        out_shape=pltpu.VMEM((kinds, share, down.shape[2] + columns), down.dtype),
        in_specs=[HBM] * 2,
        out_specs=VMEM,
        scratch_shapes=[pltpu.SemaphoreType.DMA((1 + 2 * kinds,))],
        name="pack_factors",
    )(*[pltpu.with_memory_space_constraint(x, pltpu.HBM) for x in (down, up)])


def scaled_block(part, gain_ref, block):
    steps, rows, width = part.shape
    chunks = width // HD
    gain = gain_ref[pl.ds(pl.multiple_of(block * chunks, chunks), chunks)]
    values = rows_of(part)
    squares = jnp.zeros((steps * rows, HD), jnp.float32)
    scaled = []
    for i in range(chunks):
        chunk = values[:, i * HD : (i + 1) * HD]
        squares += chunk * chunk
        scaled.append((chunk * gain[i : i + 1]).astype(jnp.bfloat16))
    return jnp.concatenate(scaled, axis=1), squares


def rotation_tables(lengths, steps, rows, cos_out, sin_out):
    lane = lax.broadcasted_iota(jnp.int32, (rows, HD), 1)
    half = HD // 2
    second = lane >= half
    index = jnp.where(second, lane - half, lane).astype(jnp.float32)
    inv_freq = jnp.exp(index * (-2.0 * math.log(rope_base) / HD))
    row_index = lax.broadcasted_iota(jnp.int32, (rows, HD), 0)
    row_lengths = jnp.zeros((rows, HD), jnp.int32)
    for row in range(rows):
        row_lengths = jnp.where(row_index == row, lengths[row], row_lengths)
    for step in range(steps):
        angles = (row_lengths + step).astype(jnp.float32) * inv_freq
        sine = jnp.sin(angles)
        cos_out[pl.ds(step * rows, rows)] = jnp.cos(angles)
        sin_out[pl.ds(step * rows, rows)] = jnp.where(second, sine, -sine)


def scale_kernel(early, near, far, lengths_ref, weight_ref, gain_ref, *rest):
    scaled_out, early_out, square_out, near_weight, far_weight, cos_out, sin_out = rest[-11:-4]
    lengths, length_sem, near_sems, far_sems = rest[-4:]
    parts = rest[:-11]
    steps, rows, width = parts[0].shape
    length_copy = pltpu.make_async_copy(lengths_ref, lengths, length_sem)
    length_copy.start()
    copies = copy_blocks(near, width, weight_ref, near_weight, near_sems)
    copies += copy_blocks(far, width, weight_ref, far_weight, far_sems)
    me = lax.axis_index("tp")
    scaled_out[...] = jnp.zeros_like(scaled_out)
    total = None
    for k, (offset, part) in enumerate(zip(early, parts)):
        block = me ^ offset
        scaled, squares = scaled_block(part, gain_ref, block)
        total = squares if total is None else total + squares
        scaled_out[:, pl.ds(pl.multiple_of(block * width, width), width)] = scaled
        early_out[:, k * width : (k + 1) * width] = scaled
    square_out[...] = total
    length_copy.wait()
    rotation_tables(lengths, steps, rows, cos_out, sin_out)
    for copy in copies:
        copy.wait()


def scale_call(early, near, far, lengths, weight, gain, parts):
    steps, rows, width = parts[0].shape
    count = steps * rows
    return pl.pallas_call(
        functools.partial(scale_kernel, early, near, far),
        out_shape=(
            pltpu.VMEM((count, (len(near) + len(far)) * width), jnp.bfloat16),
            pltpu.VMEM((count, len(early) * width), jnp.bfloat16),
            pltpu.VMEM((count, HD), jnp.float32),
            pltpu.VMEM((len(near) * width,) + weight.shape[1:], weight.dtype),
            pltpu.VMEM((len(far) * width,) + weight.shape[1:], weight.dtype),
            pltpu.VMEM((count, HD), jnp.float32),
            pltpu.VMEM((count, HD), jnp.float32),
        ),
        in_specs=[HBM] * 2 + [VMEM] * (1 + len(parts)),
        out_specs=(VMEM,) * 7,
        scratch_shapes=[
            pltpu.SMEM(lengths.shape, jnp.int32),
            pltpu.SemaphoreType.DMA,
            pltpu.SemaphoreType.DMA((len(near),)),
            pltpu.SemaphoreType.DMA((len(far),)),
        ],
        compiler_params=pltpu.CompilerParams(vmem_limit_bytes=8 << 20),
        cost_estimate=pl.CostEstimate(flops=0, bytes_accessed=9 << 20, transcendentals=0),
        name="scale_features",
    )(*[pltpu.with_memory_space_constraint(x, pltpu.HBM) for x in (lengths, weight)], gain, *parts)


def inner_kernel(late, scaled_ref, early_ref, square_ref, gain_ref, *rest):
    parts, rest = rest[: len(late)], rest[len(late) :]
    outs, square_out = rest[-1 - len(late) : -1], rest[-1]
    packs, inner_out = (rest[: -2 - len(late)], rest[-2 - len(late)]) if len(rest) > 1 + len(late) else ((), None)
    squares = square_ref[...]
    blocks = []
    for k, (offset, part) in enumerate(zip(late, parts)):
        block = lax.axis_index("tp") ^ offset
        scaled, more = scaled_block(part, gain_ref, block)
        squares += more
        blocks.append((block, scaled))
        width = scaled.shape[1]
        outs[k][:, :width] = early_ref[:, k * width : (k + 1) * width]
        outs[k][:, width:] = scaled
    squares = jnp.sum(squares, axis=1, keepdims=True)
    square_out[...] = jnp.broadcast_to(squares, square_out.shape)
    if not packs:
        return
    me = lax.axis_index("wide")
    total = []
    for offset, pack in enumerate(packs):
        mine = me ^ offset
        rows = scaled_ref[:, pl.ds(pl.multiple_of(mine * width, width), width)]
        for block, scaled in blocks:
            rows = jnp.where(mine == block, scaled, rows)
        total.append(
            lax.dot_general(
                rows,
                pack[:, :, :width].reshape(inner_out.shape[1], width),
                (((1,), (1,)), ((), ())),
                preferred_element_type=jnp.float32,
            )
        )
    inner_out[...] = sum(total[1:], total[0])


def inner_call(late, scaled, early, square, gain, parts, packs):
    count, width = scaled.shape[0], parts[0].shape[2]
    shapes = [pltpu.VMEM((count, 2 * width), scaled.dtype) for _ in late]
    shapes.append(pltpu.VMEM(square.shape, jnp.float32))
    if packs:
        kinds, share, _ = packs[0].shape
        shapes = [pltpu.VMEM((count, kinds * share), jnp.float32)] + shapes
    return pl.pallas_call(
        functools.partial(inner_kernel, late),
        out_shape=tuple(shapes),
        in_specs=[VMEM] * (4 + len(parts) + len(packs)),
        out_specs=(VMEM,) * len(shapes),
        compiler_params=pltpu.CompilerParams(vmem_limit_bytes=8 << 20),
        name="rank_inner",
    )(scaled, early, square, gain, *parts, *packs)


def up_kernel(*refs):
    packs, up_out = refs[:-1], refs[-1]
    kinds, share, pack_width = packs[0].shape
    columns = up_out.shape[1] // kinds
    me = lax.axis_index("wide") if len(packs) > 1 else 0
    up_out[...] = jnp.zeros_like(up_out)
    for offset, pack in enumerate(packs):
        for kind in range(kinds):
            at = pl.multiple_of(((me ^ offset) * kinds + kind) * share, share)
            up_out[pl.ds(at, share), kind * columns : (kind + 1) * columns] = pack[
                kind, :, pack_width - columns :
            ]


def up_call(packs, columns):
    kinds, share, _ = packs[0].shape
    return pl.pallas_call(
        up_kernel,
        out_shape=pltpu.VMEM((len(packs) * kinds * share, kinds * columns), packs[0].dtype),
        in_specs=[VMEM] * len(packs),
        out_specs=VMEM,
        compiler_params=pltpu.CompilerParams(vmem_limit_bytes=8 << 20),
        name="lay_out_up",
    )(*packs)


def final_kernel(width, blocks, near_ref, far_ref, square_ref, bias_ref, *rest):
    query_ref, acc_ref, top_ref, total_ref, cos_ref, sin_ref = rest[:6]
    inner_refs = rest[6 : 6 + blocks]
    up_ref, keys_out, values_out, attended_out, inner_buffer = rest[6 + blocks :]
    steps, rows, columns = keys_out.shape
    count = steps * rows
    groups, size, _ = query_ref.shape
    per_group = size // count
    kinds = bias_ref.shape[0]
    row_scale = lax.rsqrt(square_ref[:, :1] * (1.0 / width) + norm_eps)
    me = lax.axis_index("tp") if blocks > 1 else 0
    for i in range(blocks):
        inner_buffer[me ^ i] = inner_refs[i][...]
    inner = jnp.concatenate([inner_buffer[i] for i in range(blocks)], axis=1)
    high = inner.astype(jnp.bfloat16)
    low = (inner - high.astype(jnp.float32)).astype(jnp.bfloat16)
    lora = jnp.dot(
        jnp.concatenate([high, low], axis=0), up_ref[...], preferred_element_type=jnp.float32
    )
    lora = lora[:count] + lora[count:]
    bias = bias_ref[...].astype(jnp.float32)
    linear = []
    for kind in range(kinds):
        base = near_ref[kind] + far_ref[kind]
        part = lora[:, kind * columns : (kind + 1) * columns]
        linear.append((base + adapter_scale * part) * row_scale + bias[kind : kind + 1])
    cosine, sine = cos_ref[...], sin_ref[...]
    line = lax.broadcasted_iota(jnp.int32, (size, count), 0)
    other = lax.broadcasted_iota(jnp.int32, (size, count), 1)
    live = (line % rows == other % rows) & (other // rows <= line // rows % steps)
    for group in range(groups):
        at = slice(group * HD, (group + 1) * HD)
        key = linear[0][:, at]
        key = (key * cosine + pltpu.roll(key, HD // 2, 1) * sine).astype(jnp.bfloat16)
        value = linear[1][:, at].astype(jnp.bfloat16)
        for step in range(steps):
            keys_out[step, :, at] = key[step * rows : (step + 1) * rows]
            values_out[step, :, at] = value[step * rows : (step + 1) * rows]
        scores = lax.dot_general(
            query_ref[group].astype(jnp.bfloat16),
            key,
            (((1,), (1,)), ((), ())),
            preferred_element_type=jnp.float32,
        )
        scores = jnp.where(live, scores * score_scale, masked_score)
        old_top = top_ref[group][:, :1]
        top = jnp.maximum(old_top, jnp.max(scores, axis=1, keepdims=True))
        exps = jnp.exp(scores - top)
        keep = jnp.exp(old_top - top)
        total = total_ref[group][:, :1] * keep + jnp.sum(exps, axis=1, keepdims=True)
        acc = acc_ref[group] * keep + jnp.dot(
            exps.astype(jnp.bfloat16), value, preferred_element_type=jnp.float32
        )
        attended = (acc / total).astype(jnp.bfloat16)
        for head in range(per_group):
            lanes = pl.ds((group * per_group + head) * HD, HD)
            for step in range(steps):
                tile = (head * steps + step) * rows
                attended_out[step, :, lanes] = attended[tile : tile + rows]


def final_call(shape, width, near, far, square, bias, cached, inner, up):
    steps, rows, query_width = shape
    columns = near.shape[2]
    small = jax.ShapeDtypeStruct((steps, rows, columns), jnp.bfloat16)
    return pl.pallas_call(
        functools.partial(final_kernel, width, len(inner)),
        out_shape=(small, small, jax.ShapeDtypeStruct(shape, jnp.bfloat16)),
        in_specs=[VMEM] * (5 + len(cached) + len(inner)),
        out_specs=(VMEM,) * 3,
        scratch_shapes=[pltpu.VMEM((len(inner),) + inner[0].shape, jnp.float32)],
        compiler_params=pltpu.CompilerParams(vmem_limit_bytes=8 << 20),
        name="fresh_attention",
    )(near, far, square, bias, *cached, *inner, up)


def dot(rows, weight):
    return jnp.einsum("md,dkc->kmc", rows, weight, preferred_element_type=jnp.float32)


def swap(block, axis, offset, count):
    return lax.ppermute(block, axis, [(i, i ^ offset) for i in range(count)])


def on_device(
    wide_count,
    tp_count,
    hidden,
    input_norm_gain,
    key_value_weight,
    key_value_bias,
    adapter_down_factor,
    adapter_up_factor,
    queries,
    stored_rotated_keys,
    stored_value_rows,
    lengths,
):
    steps, rows, part_width = hidden.shape
    width = part_width * tp_count
    kinds, ranks, down_width = adapter_down_factor.shape
    gain = input_norm_gain.reshape(width // HD, HD)
    up_part = jnp.transpose(adapter_up_factor, (0, 2, 1))
    direct = wide_count == tp_count == 4
    beside, crossed = [swap(hidden, "tp", offset, tp_count) for offset in (1, 2)]
    if direct:
        pack = pack_call(adapter_down_factor, up_part)
        second = swap(pack, "wide", 2, wide_count)
        first = swap(pack, "wide", 1, wide_count)
    near, far = (0, 1), (2, 3)
    early, late = (0, 2), (1, 3)
    gain_rows, bias, mine, *cached = cache_call(
        lengths, queries, stored_rotated_keys, stored_value_rows, gain, key_value_bias, hidden
    )
    relayed, gain_rows = lax.optimization_barrier((crossed, gain_rows))
    relayed = swap(relayed, "tp", 1, tp_count)
    if direct:
        third, gain_rows = lax.optimization_barrier((second, gain_rows))
        packs = [pack, first, second, swap(third, "wide", 1, wide_count)]
    scaled, early_scaled, square, near_weight, far_weight, *tables = scale_call(
        early, near, far, lengths, key_value_weight, gain_rows, (mine, crossed)
    )
    late_parts = (beside, relayed)
    if direct:
        inner, near_scaled, far_scaled, square = inner_call(
            late, scaled, early_scaled, square, gain_rows, late_parts, packs
        )
        inner, far_scaled, near_scaled, packs = lax.optimization_barrier(
            (inner, far_scaled, near_scaled, packs)
        )
        inner = [inner] + [swap(inner, "tp", offset, tp_count) for offset in (1, 2, 3)]
    else:
        near_scaled, far_scaled, square = inner_call(
            late, scaled, early_scaled, square, gain_rows, late_parts, []
        )
        down = lax.all_gather(adapter_down_factor, "wide", axis=2, tiled=True)
        rows_full = lax.all_gather(hidden, "tp", axis=2, tiled=True).astype(jnp.float32)
        rows_full = (rows_full * input_norm_gain.astype(jnp.float32)).astype(jnp.bfloat16)
        inner = jnp.einsum("srd,kad->srka", rows_full, down, preferred_element_type=jnp.float32)
        inner = [inner.reshape(steps * rows, kinds * ranks)]
        packs = [lax.all_gather(up_part, "wide", axis=1, tiled=True)]
    near_base = dot(near_scaled, near_weight)
    far_base = dot(far_scaled, far_weight)
    up = up_call(packs, bias.shape[1])
    return final_call(
        queries.shape, width, near_base, far_base, square, bias, cached + tables, inner, up
    )


def solution(mesh):
    in_specs = (
        P(None, ("groups", "wide"), "tp"),
        P(),
        P(None, None, "tp"),
        P(None, "tp"),
        P("groups", None, "wide"),
        P("groups", "tp", "wide"),
        P(None, ("groups", "wide"), "tp"),
        P(("groups", "wide"), None, "tp"),
        P(("groups", "wide"), None, "tp"),
        P(("groups", "wide")),
    )
    out_specs = (
        P(None, ("groups", "wide"), "tp"),
        P(None, ("groups", "wide"), "tp"),
        P(None, ("groups", "wide"), "tp"),
    )
    body = functools.partial(on_device, mesh.shape["wide"], mesh.shape["tp"])
    return jax.shard_map(
        body, mesh=mesh, in_specs=in_specs, out_specs=out_specs, check_vma=False
    )
```

```python
import functools
import math

import jax
import jax.numpy as jnp
from jax import lax
from jax.experimental import pallas as pl
from jax.experimental.pallas import tpu as pltpu
from jax.sharding import PartitionSpec as P

HD = 128


norm_eps = 1e-06
adapter_scale = 2.0
rope_base = 1000000.0
masked_score = -1e30
score_scale = 1.0 / math.sqrt(HD)

VMEM = pl.BlockSpec(memory_space=pltpu.VMEM)
HBM = pl.BlockSpec(memory_space=pltpu.HBM)


def query_block(query_ref, group, per_group):
    steps = query_ref.shape[0]
    tiles = []
    for head in range(per_group):
        at = (group * per_group + head) * HD
        for step in range(steps):
            tiles.append(query_ref[step, :, at : at + HD].astype(jnp.float32))
    return jnp.concatenate(tiles, axis=0)


def copy_blocks(offsets, width, weight_ref, out_ref, sems):
    me = lax.axis_index("tp")
    copies = []
    for i, offset in enumerate(offsets):
        block = pl.ds(pl.multiple_of((me ^ offset) * width, width), width)
        copies.append(
            pltpu.make_async_copy(
                weight_ref.at[block], out_ref.at[pl.ds(i * width, width)], sems.at[i]
            )
        )
        copies[-1].start()
    return copies


def cache_kernel(
    near,
    lengths_ref,
    query_ref,
    key_ref,
    value_ref,
    gain_ref,
    bias_ref,
    hidden_ref,
    weight_ref,
    near_out,
    gain_out,
    bias_out,
    hidden_out,
    query_out,
    acc_out,
    top_out,
    total_out,
    lengths,
    queries,
    gain_buffer,
    key_buffer,
    value_buffer,
    score_buffer,
    sems,
    weight_sems,
):
    steps, rows, query_width = query_ref.shape
    cache_span = key_ref.shape[1]
    groups = key_ref.shape[2] // HD
    per_group = query_width // HD // groups
    lines = steps * per_group
    half_rows = rows // 2
    halves = [pl.ds(0, half_rows), pl.ds(half_rows, half_rows)]
    copies = [
        (lengths_ref, lengths),
        (query_ref, queries),
        (key_ref.at[halves[0]], key_buffer.at[halves[0]]),
        (key_ref.at[halves[1]], key_buffer.at[halves[1]]),
        (value_ref.at[halves[0]], value_buffer.at[halves[0]]),
        (value_ref.at[halves[1]], value_buffer.at[halves[1]]),
        (gain_ref, gain_buffer),
        (bias_ref, bias_out),
        (hidden_ref, hidden_out),
    ]
    copies = [pltpu.make_async_copy(*pair, sems.at[i]) for i, pair in enumerate(copies)]
    for copy in copies:
        copy.start()
    copies += copy_blocks(near, hidden_ref.shape[2], weight_ref, near_out, weight_sems)

    copies[0].wait()
    copies[1].wait()
    for group in range(groups):
        query_out[group] = query_block(queries, group, per_group)

    place = lax.broadcasted_iota(jnp.int32, (lines, cache_span), 1)
    for i in range(2):
        copies[2 + i].wait()
        for row in range(i * half_rows, (i + 1) * half_rows):
            for group in range(groups):
                query = query_out[group, pl.ds(row, lines, stride=rows), :].astype(jnp.bfloat16)
                score_buffer[row * groups + group] = lax.dot_general(
                    query,
                    key_buffer[row, :, pl.ds(group * HD, HD)],
                    (((1,), (1,)), ((), ())),
                    preferred_element_type=jnp.float32,
                )
    for i in range(2):
        copies[4 + i].wait()
        for row in range(i * half_rows, (i + 1) * half_rows):
            live = place < lengths[row]
            for group in range(groups):
                mine = pl.ds(row, lines, stride=rows)
                scores = score_buffer[row * groups + group]
                scores = jnp.where(live, scores * score_scale, masked_score)
                top = jnp.max(scores, axis=1, keepdims=True)
                exps = jnp.exp(scores - top)
                total = jnp.sum(exps, axis=1, keepdims=True)
                acc = jnp.dot(
                    exps.astype(jnp.bfloat16),
                    value_buffer[row, :, pl.ds(group * HD, HD)],
                    preferred_element_type=jnp.float32,
                )
                acc_out[group, mine, :] = acc
                top_out[group, mine, :] = jnp.broadcast_to(top, acc.shape)
                total_out[group, mine, :] = jnp.broadcast_to(total, acc.shape)
    copies[6].wait()
    gain_out[...] = gain_buffer[...].astype(jnp.float32)
    for copy in copies[7:]:
        copy.wait()


def cache_call(near, lengths, queries, keys, values, gain, bias, hidden, weight):
    steps, rows, query_width = queries.shape
    cache_span, key_width = keys.shape[1:]
    groups = key_width // HD
    lines = steps * (query_width // key_width)
    block = (groups, lines * rows, HD)
    operands = (lengths, queries, keys, values, gain, bias, hidden, weight)
    near_weight = (len(near) * hidden.shape[2],) + weight.shape[1:]
    return pl.pallas_call(
        functools.partial(cache_kernel, near),
        out_shape=(
            pltpu.VMEM(near_weight, weight.dtype),
            pltpu.VMEM(gain.shape, jnp.float32),
            pltpu.VMEM(bias.shape, bias.dtype),
            pltpu.VMEM(hidden.shape, hidden.dtype),
            pltpu.VMEM(block, jnp.float32),
            pltpu.VMEM(block, jnp.float32),
            pltpu.VMEM(block, jnp.float32),
            pltpu.VMEM(block, jnp.float32),
        ),
        in_specs=[HBM] * len(operands),
        out_specs=(VMEM,) * 8,
        scratch_shapes=[
            pltpu.SMEM(lengths.shape, jnp.int32),
            pltpu.VMEM(queries.shape, queries.dtype),
            pltpu.VMEM(gain.shape, gain.dtype),
            pltpu.VMEM(keys.shape, keys.dtype),
            pltpu.VMEM(values.shape, values.dtype),
            pltpu.VMEM((rows * groups, lines, cache_span), jnp.float32),
            pltpu.SemaphoreType.DMA((9,)),
            pltpu.SemaphoreType.DMA((len(near),)),
        ],
        compiler_params=pltpu.CompilerParams(vmem_limit_bytes=16 << 20),
        cost_estimate=pl.CostEstimate(flops=2 * 67 << 20, bytes_accessed=5 << 20, transcendentals=0),
        name="cache_attention",
    )(*[pltpu.with_memory_space_constraint(x, pltpu.HBM) for x in operands])


def rows_of(ref):
    return jnp.concatenate([ref[s].astype(jnp.float32) for s in range(ref.shape[0])], axis=0)


def pack_kernel(down_ref, up_ref, out_ref, sems):
    share = out_ref.shape[1]
    width = down_ref.shape[2]
    at = pl.ds(pl.multiple_of(lax.axis_index("tp") * share, share), share)
    copies = [(up_ref, out_ref.at[:, :, pl.ds(width, up_ref.shape[2])])]
    half = width // 2
    for kind in range(down_ref.shape[0]):
        for first in (0, half):
            lanes = pl.ds(first, half)
            copies.append((down_ref.at[kind, at, lanes], out_ref.at[kind, :, lanes]))
    copies = [pltpu.make_async_copy(*pair, sems.at[i]) for i, pair in enumerate(copies)]
    for copy in copies:
        copy.start()
    for copy in copies:
        copy.wait()


def pack_call(down, up):
    kinds, share, columns = up.shape
    return pl.pallas_call(
        pack_kernel,
        out_shape=pltpu.VMEM((kinds, share, down.shape[2] + columns), down.dtype),
        in_specs=[HBM] * 2,
        out_specs=VMEM,
        scratch_shapes=[pltpu.SemaphoreType.DMA((1 + 2 * kinds,))],
        name="pack_factors",
    )(*[pltpu.with_memory_space_constraint(x, pltpu.HBM) for x in (down, up)])


def scaled_block(part, gain_ref, block):
    steps, rows, width = part.shape
    chunks = width // HD
    gain = gain_ref[pl.ds(pl.multiple_of(block * chunks, chunks), chunks)]
    values = rows_of(part)
    squares = jnp.zeros((steps * rows, HD), jnp.float32)
    scaled = []
    for i in range(chunks):
        chunk = values[:, i * HD : (i + 1) * HD]
        squares += chunk * chunk
        scaled.append((chunk * gain[i : i + 1]).astype(jnp.bfloat16))
    return jnp.concatenate(scaled, axis=1), squares


def rotation_tables(lengths, steps, rows, cos_out, sin_out):
    lane = lax.broadcasted_iota(jnp.int32, (rows, HD), 1)
    half = HD // 2
    second = lane >= half
    index = jnp.where(second, lane - half, lane).astype(jnp.float32)
    inv_freq = jnp.exp(index * (-2.0 * math.log(rope_base) / HD))
    row_index = lax.broadcasted_iota(jnp.int32, (rows, HD), 0)
    row_lengths = jnp.zeros((rows, HD), jnp.int32)
    for row in range(rows):
        row_lengths = jnp.where(row_index == row, lengths[row], row_lengths)
    for step in range(steps):
        angles = (row_lengths + step).astype(jnp.float32) * inv_freq
        sine = jnp.sin(angles)
        cos_out[pl.ds(step * rows, rows)] = jnp.cos(angles)
        sin_out[pl.ds(step * rows, rows)] = jnp.where(second, sine, -sine)


def scale_kernel(early, far, lengths_ref, weight_ref, gain_ref, *rest):
    scaled_out, early_out, square_out, far_weight, cos_out, sin_out = rest[-9:-3]
    lengths, length_sem, far_sems = rest[-3:]
    parts = rest[:-9]
    steps, rows, width = parts[0].shape
    length_copy = pltpu.make_async_copy(lengths_ref, lengths, length_sem)
    length_copy.start()
    copies = copy_blocks(far, width, weight_ref, far_weight, far_sems)
    me = lax.axis_index("tp")
    scaled_out[...] = jnp.zeros_like(scaled_out)
    total = None
    for k, (offset, part) in enumerate(zip(early, parts)):
        block = me ^ offset
        scaled, squares = scaled_block(part, gain_ref, block)
        total = squares if total is None else total + squares
        scaled_out[:, pl.ds(pl.multiple_of(block * width, width), width)] = scaled
        early_out[:, k * width : (k + 1) * width] = scaled
    square_out[...] = total
    length_copy.wait()
    rotation_tables(lengths, steps, rows, cos_out, sin_out)
    for copy in copies:
        copy.wait()


def scale_call(early, blocks, far, lengths, weight, gain, parts):
    steps, rows, width = parts[0].shape
    count = steps * rows
    return pl.pallas_call(
        functools.partial(scale_kernel, early, far),
        out_shape=(
            pltpu.VMEM((count, blocks * width), jnp.bfloat16),
            pltpu.VMEM((count, len(early) * width), jnp.bfloat16),
            pltpu.VMEM((count, HD), jnp.float32),
            pltpu.VMEM((len(far) * width,) + weight.shape[1:], weight.dtype),
            pltpu.VMEM((count, HD), jnp.float32),
            pltpu.VMEM((count, HD), jnp.float32),
        ),
        in_specs=[HBM] * 2 + [VMEM] * (1 + len(parts)),
        out_specs=(VMEM,) * 6,
        scratch_shapes=[
            pltpu.SMEM(lengths.shape, jnp.int32),
            pltpu.SemaphoreType.DMA,
            pltpu.SemaphoreType.DMA((len(far),)),
        ],
        compiler_params=pltpu.CompilerParams(vmem_limit_bytes=8 << 20),
        cost_estimate=pl.CostEstimate(flops=0, bytes_accessed=9 << 20, transcendentals=0),
        name="scale_features",
    )(*[pltpu.with_memory_space_constraint(x, pltpu.HBM) for x in (lengths, weight)], gain, *parts)


def inner_kernel(late, scaled_ref, early_ref, square_ref, gain_ref, *rest):
    parts, rest = rest[: len(late)], rest[len(late) :]
    outs, square_out = rest[-1 - len(late) : -1], rest[-1]
    packs, inner_out = (rest[: -2 - len(late)], rest[-2 - len(late)]) if len(rest) > 1 + len(late) else ((), None)
    squares = square_ref[...]
    blocks = []
    for k, (offset, part) in enumerate(zip(late, parts)):
        block = lax.axis_index("tp") ^ offset
        scaled, more = scaled_block(part, gain_ref, block)
        squares += more
        blocks.append((block, scaled))
        width = scaled.shape[1]
        outs[k][:, :width] = early_ref[:, k * width : (k + 1) * width]
        outs[k][:, width:] = scaled
    squares = jnp.sum(squares, axis=1, keepdims=True)
    square_out[...] = jnp.broadcast_to(squares, square_out.shape)
    if not packs:
        return
    me = lax.axis_index("wide")
    total = []
    for offset, pack in enumerate(packs):
        mine = me ^ offset
        rows = scaled_ref[:, pl.ds(pl.multiple_of(mine * width, width), width)]
        for block, scaled in blocks:
            rows = jnp.where(mine == block, scaled, rows)
        total.append(
            lax.dot_general(
                rows,
                pack[:, :, :width].reshape(inner_out.shape[1], width),
                (((1,), (1,)), ((), ())),
                preferred_element_type=jnp.float32,
            )
        )
    inner_out[...] = sum(total[1:], total[0])


def inner_call(late, scaled, early, square, gain, parts, packs):
    count, width = scaled.shape[0], parts[0].shape[2]
    shapes = [pltpu.VMEM((count, 2 * width), scaled.dtype) for _ in late]
    shapes.append(pltpu.VMEM(square.shape, jnp.float32))
    if packs:
        kinds, share, _ = packs[0].shape
        shapes = [pltpu.VMEM((count, kinds * share), jnp.float32)] + shapes
    return pl.pallas_call(
        functools.partial(inner_kernel, late),
        out_shape=tuple(shapes),
        in_specs=[VMEM] * (4 + len(parts) + len(packs)),
        out_specs=(VMEM,) * len(shapes),
        compiler_params=pltpu.CompilerParams(vmem_limit_bytes=8 << 20),
        name="rank_inner",
    )(scaled, early, square, gain, *parts, *packs)


def up_kernel(*refs):
    packs, up_out = refs[:-1], refs[-1]
    kinds, share, pack_width = packs[0].shape
    columns = up_out.shape[1] // kinds
    me = lax.axis_index("wide") if len(packs) > 1 else 0
    up_out[...] = jnp.zeros_like(up_out)
    for offset, pack in enumerate(packs):
        for kind in range(kinds):
            at = pl.multiple_of(((me ^ offset) * kinds + kind) * share, share)
            up_out[pl.ds(at, share), kind * columns : (kind + 1) * columns] = pack[
                kind, :, pack_width - columns :
            ]


def up_call(packs, columns):
    kinds, share, _ = packs[0].shape
    return pl.pallas_call(
        up_kernel,
        out_shape=pltpu.VMEM((len(packs) * kinds * share, kinds * columns), packs[0].dtype),
        in_specs=[VMEM] * len(packs),
        out_specs=VMEM,
        compiler_params=pltpu.CompilerParams(vmem_limit_bytes=8 << 20),
        name="lay_out_up",
    )(*packs)


def final_kernel(width, blocks, near_ref, far_ref, square_ref, bias_ref, *rest):
    query_ref, acc_ref, top_ref, total_ref, cos_ref, sin_ref = rest[:6]
    inner_refs = rest[6 : 6 + blocks]
    up_ref, keys_out, values_out, attended_out, inner_buffer = rest[6 + blocks :]
    steps, rows, columns = keys_out.shape
    count = steps * rows
    groups, size, _ = query_ref.shape
    per_group = size // count
    kinds = bias_ref.shape[0]
    row_scale = lax.rsqrt(square_ref[:, :1] * (1.0 / width) + norm_eps)
    me = lax.axis_index("tp") if blocks > 1 else 0
    for i in range(blocks):
        inner_buffer[me ^ i] = inner_refs[i][...]
    inner = jnp.concatenate([inner_buffer[i] for i in range(blocks)], axis=1)
    high = inner.astype(jnp.bfloat16)
    low = (inner - high.astype(jnp.float32)).astype(jnp.bfloat16)
    lora = jnp.dot(
        jnp.concatenate([high, low], axis=0), up_ref[...], preferred_element_type=jnp.float32
    )
    lora = lora[:count] + lora[count:]
    bias = bias_ref[...].astype(jnp.float32)
    linear = []
    for kind in range(kinds):
        base = near_ref[kind] + far_ref[kind]
        part = lora[:, kind * columns : (kind + 1) * columns]
        linear.append((base + adapter_scale * part) * row_scale + bias[kind : kind + 1])
    cosine, sine = cos_ref[...], sin_ref[...]
    line = lax.broadcasted_iota(jnp.int32, (size, count), 0)
    other = lax.broadcasted_iota(jnp.int32, (size, count), 1)
    live = (line % rows == other % rows) & (other // rows <= line // rows % steps)
    for group in range(groups):
        at = slice(group * HD, (group + 1) * HD)
        key = linear[0][:, at]
        key = (key * cosine + pltpu.roll(key, HD // 2, 1) * sine).astype(jnp.bfloat16)
        value = linear[1][:, at].astype(jnp.bfloat16)
        for step in range(steps):
            keys_out[step, :, at] = key[step * rows : (step + 1) * rows]
            values_out[step, :, at] = value[step * rows : (step + 1) * rows]
        scores = lax.dot_general(
            query_ref[group].astype(jnp.bfloat16),
            key,
            (((1,), (1,)), ((), ())),
            preferred_element_type=jnp.float32,
        )
        scores = jnp.where(live, scores * score_scale, masked_score)
        old_top = top_ref[group][:, :1]
        top = jnp.maximum(old_top, jnp.max(scores, axis=1, keepdims=True))
        exps = jnp.exp(scores - top)
        keep = jnp.exp(old_top - top)
        total = total_ref[group][:, :1] * keep + jnp.sum(exps, axis=1, keepdims=True)
        acc = acc_ref[group] * keep + jnp.dot(
            exps.astype(jnp.bfloat16), value, preferred_element_type=jnp.float32
        )
        attended = (acc / total).astype(jnp.bfloat16)
        for head in range(per_group):
            lanes = pl.ds((group * per_group + head) * HD, HD)
            for step in range(steps):
                tile = (head * steps + step) * rows
                attended_out[step, :, lanes] = attended[tile : tile + rows]


def final_call(shape, width, near, far, square, bias, cached, inner, up):
    steps, rows, query_width = shape
    columns = near.shape[2]
    small = jax.ShapeDtypeStruct((steps, rows, columns), jnp.bfloat16)
    return pl.pallas_call(
        functools.partial(final_kernel, width, len(inner)),
        out_shape=(small, small, jax.ShapeDtypeStruct(shape, jnp.bfloat16)),
        in_specs=[VMEM] * (5 + len(cached) + len(inner)),
        out_specs=(VMEM,) * 3,
        scratch_shapes=[pltpu.VMEM((len(inner),) + inner[0].shape, jnp.float32)],
        compiler_params=pltpu.CompilerParams(vmem_limit_bytes=8 << 20),
        name="fresh_attention",
    )(near, far, square, bias, *cached, *inner, up)


def dot(rows, weight):
    return jnp.einsum("md,dkc->kmc", rows, weight, preferred_element_type=jnp.float32)


def swap(block, axis, offset, count):
    return lax.ppermute(block, axis, [(i, i ^ offset) for i in range(count)])


def on_device(
    wide_count,
    tp_count,
    hidden,
    input_norm_gain,
    key_value_weight,
    key_value_bias,
    adapter_down_factor,
    adapter_up_factor,
    queries,
    stored_rotated_keys,
    stored_value_rows,
    lengths,
):
    steps, rows, part_width = hidden.shape
    width = part_width * tp_count
    kinds, ranks, down_width = adapter_down_factor.shape
    gain = input_norm_gain.reshape(width // HD, HD)
    up_part = jnp.transpose(adapter_up_factor, (0, 2, 1))
    direct = wide_count == tp_count == 4
    beside, crossed = [swap(hidden, "tp", offset, tp_count) for offset in (1, 2)]
    if direct:
        pack = pack_call(adapter_down_factor, up_part)
        second = swap(pack, "wide", 2, wide_count)
        first = swap(pack, "wide", 1, wide_count)
    near, far = (0, 1), (2, 3)
    early, late = (0, 2), (1, 3)
    near_weight, gain_rows, bias, mine, *cached = cache_call(
        near,
        lengths,
        queries,
        stored_rotated_keys,
        stored_value_rows,
        gain,
        key_value_bias,
        hidden,
        key_value_weight,
    )
    relayed, gain_rows = lax.optimization_barrier((crossed, gain_rows))
    relayed = swap(relayed, "tp", 1, tp_count)
    if direct:
        third, gain_rows = lax.optimization_barrier((second, gain_rows))
        packs = [pack, first, second, swap(third, "wide", 1, wide_count)]
    scaled, early_scaled, square, far_weight, *tables = scale_call(
        early, tp_count, far, lengths, key_value_weight, gain_rows, (mine, crossed)
    )
    late_parts = (beside, relayed)
    if direct:
        inner, near_scaled, far_scaled, square = inner_call(
            late, scaled, early_scaled, square, gain_rows, late_parts, packs
        )
        inner, far_scaled, near_scaled, packs = lax.optimization_barrier(
            (inner, far_scaled, near_scaled, packs)
        )
        inner = [inner] + [swap(inner, "tp", offset, tp_count) for offset in (1, 2, 3)]
    else:
        near_scaled, far_scaled, square = inner_call(
            late, scaled, early_scaled, square, gain_rows, late_parts, []
        )
        down = lax.all_gather(adapter_down_factor, "wide", axis=2, tiled=True)
        rows_full = lax.all_gather(hidden, "tp", axis=2, tiled=True).astype(jnp.float32)
        rows_full = (rows_full * input_norm_gain.astype(jnp.float32)).astype(jnp.bfloat16)
        inner = jnp.einsum("srd,kad->srka", rows_full, down, preferred_element_type=jnp.float32)
        inner = [inner.reshape(steps * rows, kinds * ranks)]
        packs = [lax.all_gather(up_part, "wide", axis=1, tiled=True)]
    near_base = dot(near_scaled, near_weight)
    far_base = dot(far_scaled, far_weight)
    up = up_call(packs, bias.shape[1])
    return final_call(
        queries.shape, width, near_base, far_base, square, bias, cached + tables, inner, up
    )


def solution(mesh):
    in_specs = (
        P(None, ("groups", "wide"), "tp"),
        P(),
        P(None, None, "tp"),
        P(None, "tp"),
        P("groups", None, "wide"),
        P("groups", "tp", "wide"),
        P(None, ("groups", "wide"), "tp"),
        P(("groups", "wide"), None, "tp"),
        P(("groups", "wide"), None, "tp"),
        P(("groups", "wide")),
    )
    out_specs = (
        P(None, ("groups", "wide"), "tp"),
        P(None, ("groups", "wide"), "tp"),
        P(None, ("groups", "wide"), "tp"),
    )
    body = functools.partial(on_device, mesh.shape["wide"], mesh.shape["tp"])
    return jax.shard_map(
        body, mesh=mesh, in_specs=in_specs, out_specs=out_specs, check_vma=False
    )
```

```python
import functools
import math

import jax
import jax.numpy as jnp
from jax import lax
from jax.experimental import pallas as pl
from jax.experimental.pallas import tpu as pltpu
from jax.sharding import PartitionSpec as P

HD = 128


norm_eps = 1e-06
adapter_scale = 2.0
rope_base = 1000000.0
masked_score = -1e30
score_scale = 1.0 / math.sqrt(HD)

VMEM = pl.BlockSpec(memory_space=pltpu.VMEM)
HBM = pl.BlockSpec(memory_space=pltpu.HBM)


def query_block(query_ref, group, per_group):
    steps = query_ref.shape[0]
    tiles = []
    for head in range(per_group):
        at = (group * per_group + head) * HD
        for step in range(steps):
            tiles.append(query_ref[step, :, at : at + HD].astype(jnp.float32))
    return jnp.concatenate(tiles, axis=0)


def copy_blocks(offsets, width, weight_ref, out_ref, sems):
    me = lax.axis_index("tp")
    copies = []
    for i, offset in enumerate(offsets):
        block = pl.ds(pl.multiple_of((me ^ offset) * width, width), width)
        copies.append(
            pltpu.make_async_copy(
                weight_ref.at[block], out_ref.at[pl.ds(i * width, width)], sems.at[i]
            )
        )
        copies[-1].start()
    return copies


def cache_kernel(
    near,
    lengths_ref,
    query_ref,
    key_ref,
    value_ref,
    gain_ref,
    bias_ref,
    hidden_ref,
    weight_ref,
    near_out,
    gain_out,
    bias_out,
    hidden_out,
    query_out,
    acc_out,
    top_out,
    total_out,
    lengths,
    queries,
    gain_buffer,
    key_buffer,
    value_buffer,
    score_buffer,
    sems,
    weight_sems,
):
    steps, rows, query_width = query_ref.shape
    cache_span = key_ref.shape[1]
    groups = key_ref.shape[2] // HD
    per_group = query_width // HD // groups
    lines = steps * per_group
    half_rows = rows // 2
    halves = [pl.ds(0, half_rows), pl.ds(half_rows, half_rows)]
    copies = [
        (lengths_ref, lengths),
        (query_ref, queries),
        (key_ref.at[halves[0]], key_buffer.at[halves[0]]),
        (key_ref.at[halves[1]], key_buffer.at[halves[1]]),
        (value_ref.at[halves[0]], value_buffer.at[halves[0]]),
        (value_ref.at[halves[1]], value_buffer.at[halves[1]]),
        (gain_ref, gain_buffer),
        (bias_ref, bias_out),
        (hidden_ref, hidden_out),
    ]
    copies = [pltpu.make_async_copy(*pair, sems.at[i]) for i, pair in enumerate(copies)]
    for copy in copies:
        copy.start()
    copies += copy_blocks(near, hidden_ref.shape[2], weight_ref, near_out, weight_sems)

    copies[0].wait()
    copies[1].wait()
    for group in range(groups):
        query_out[group] = query_block(queries, group, per_group)

    place = lax.broadcasted_iota(jnp.int32, (lines, cache_span), 1)
    for i in range(2):
        copies[2 + i].wait()
        for row in range(i * half_rows, (i + 1) * half_rows):
            for group in range(groups):
                query = query_out[group, pl.ds(row, lines, stride=rows), :].astype(jnp.bfloat16)
                score_buffer[row * groups + group] = lax.dot_general(
                    query,
                    key_buffer[row, :, pl.ds(group * HD, HD)],
                    (((1,), (1,)), ((), ())),
                    preferred_element_type=jnp.float32,
                )
    for i in range(2):
        copies[4 + i].wait()
        for row in range(i * half_rows, (i + 1) * half_rows):
            live = place < lengths[row]
            for group in range(groups):
                mine = pl.ds(row, lines, stride=rows)
                scores = score_buffer[row * groups + group]
                scores = jnp.where(live, scores * score_scale, masked_score)
                top = jnp.max(scores, axis=1, keepdims=True)
                exps = jnp.exp(scores - top)
                total = jnp.sum(exps, axis=1, keepdims=True)
                acc = jnp.dot(
                    exps.astype(jnp.bfloat16),
                    value_buffer[row, :, pl.ds(group * HD, HD)],
                    preferred_element_type=jnp.float32,
                )
                acc_out[group, mine, :] = acc
                top_out[group, mine, :] = jnp.broadcast_to(top, acc.shape)
                total_out[group, mine, :] = jnp.broadcast_to(total, acc.shape)
    copies[6].wait()
    gain_out[...] = gain_buffer[...].astype(jnp.float32)
    for copy in copies[7:]:
        copy.wait()


def cache_call(near, lengths, queries, keys, values, gain, bias, hidden, weight):
    steps, rows, query_width = queries.shape
    cache_span, key_width = keys.shape[1:]
    groups = key_width // HD
    lines = steps * (query_width // key_width)
    block = (groups, lines * rows, HD)
    operands = (lengths, queries, keys, values, gain, bias, hidden, weight)
    near_weight = (len(near) * hidden.shape[2],) + weight.shape[1:]
    return pl.pallas_call(
        functools.partial(cache_kernel, near),
        out_shape=(
            pltpu.VMEM(near_weight, weight.dtype),
            pltpu.VMEM(gain.shape, jnp.float32),
            pltpu.VMEM(bias.shape, bias.dtype),
            pltpu.VMEM(hidden.shape, hidden.dtype),
            pltpu.VMEM(block, jnp.float32),
            pltpu.VMEM(block, jnp.float32),
            pltpu.VMEM(block, jnp.float32),
            pltpu.VMEM(block, jnp.float32),
        ),
        in_specs=[HBM] * len(operands),
        out_specs=(VMEM,) * 8,
        scratch_shapes=[
            pltpu.SMEM(lengths.shape, jnp.int32),
            pltpu.VMEM(queries.shape, queries.dtype),
            pltpu.VMEM(gain.shape, gain.dtype),
            pltpu.VMEM(keys.shape, keys.dtype),
            pltpu.VMEM(values.shape, values.dtype),
            pltpu.VMEM((rows * groups, lines, cache_span), jnp.float32),
            pltpu.SemaphoreType.DMA((9,)),
            pltpu.SemaphoreType.DMA((len(near),)),
        ],
        compiler_params=pltpu.CompilerParams(vmem_limit_bytes=16 << 20),
        cost_estimate=pl.CostEstimate(flops=2 * 67 << 20, bytes_accessed=5 << 20, transcendentals=0),
        name="cache_attention",
    )(*[pltpu.with_memory_space_constraint(x, pltpu.HBM) for x in operands])


def rows_of(ref):
    return jnp.concatenate([ref[s].astype(jnp.float32) for s in range(ref.shape[0])], axis=0)


def pack_kernel(down_ref, up_ref, out_ref, sems):
    share = out_ref.shape[1]
    width = down_ref.shape[2]
    at = pl.ds(pl.multiple_of(lax.axis_index("tp") * share, share), share)
    copies = [(up_ref, out_ref.at[:, :, pl.ds(width, up_ref.shape[2])])]
    half = width // 2
    for kind in range(down_ref.shape[0]):
        for first in (0, half):
            lanes = pl.ds(first, half)
            copies.append((down_ref.at[kind, at, lanes], out_ref.at[kind, :, lanes]))
    copies = [pltpu.make_async_copy(*pair, sems.at[i]) for i, pair in enumerate(copies)]
    for copy in copies:
        copy.start()
    for copy in copies:
        copy.wait()


def pack_call(down, up):
    kinds, share, columns = up.shape
    return pl.pallas_call(
        pack_kernel,
        out_shape=pltpu.VMEM((kinds, share, down.shape[2] + columns), down.dtype),
        in_specs=[HBM] * 2,
        out_specs=VMEM,
        scratch_shapes=[pltpu.SemaphoreType.DMA((1 + 2 * kinds,))],
        name="pack_factors",
    )(*[pltpu.with_memory_space_constraint(x, pltpu.HBM) for x in (down, up)])


def scaled_block(part, gain_ref, block):
    steps, rows, width = part.shape
    chunks = width // HD
    gain = gain_ref[pl.ds(pl.multiple_of(block * chunks, chunks), chunks)]
    values = rows_of(part)
    squares = jnp.zeros((steps * rows, HD), jnp.float32)
    scaled = []
    for i in range(chunks):
        chunk = values[:, i * HD : (i + 1) * HD]
        squares += chunk * chunk
        scaled.append((chunk * gain[i : i + 1]).astype(jnp.bfloat16))
    return jnp.concatenate(scaled, axis=1), squares


def rotation_tables(lengths, steps, rows, cos_out, sin_out):
    lane = lax.broadcasted_iota(jnp.int32, (rows, HD), 1)
    half = HD // 2
    second = lane >= half
    index = jnp.where(second, lane - half, lane).astype(jnp.float32)
    inv_freq = jnp.exp(index * (-2.0 * math.log(rope_base) / HD))
    row_index = lax.broadcasted_iota(jnp.int32, (rows, HD), 0)
    row_lengths = jnp.zeros((rows, HD), jnp.int32)
    for row in range(rows):
        row_lengths = jnp.where(row_index == row, lengths[row], row_lengths)
    for step in range(steps):
        angles = (row_lengths + step).astype(jnp.float32) * inv_freq
        sine = jnp.sin(angles)
        cos_out[pl.ds(step * rows, rows)] = jnp.cos(angles)
        sin_out[pl.ds(step * rows, rows)] = jnp.where(second, sine, -sine)


def scale_kernel(early, far, lengths_ref, weight_ref, gain_ref, *rest):
    scaled_out, early_out, square_out, far_weight, cos_out, sin_out = rest[-9:-3]
    lengths, length_sem, far_sems = rest[-3:]
    parts = rest[:-9]
    steps, rows, width = parts[0].shape
    length_copy = pltpu.make_async_copy(lengths_ref, lengths, length_sem)
    length_copy.start()
    copies = copy_blocks(far, width, weight_ref, far_weight, far_sems)
    me = lax.axis_index("tp")
    scaled_out[...] = jnp.zeros_like(scaled_out)
    total = None
    for k, (offset, part) in enumerate(zip(early, parts)):
        block = me ^ offset
        scaled, squares = scaled_block(part, gain_ref, block)
        total = squares if total is None else total + squares
        scaled_out[:, pl.ds(pl.multiple_of(block * width, width), width)] = scaled
        early_out[:, k * width : (k + 1) * width] = scaled
    square_out[...] = total
    length_copy.wait()
    rotation_tables(lengths, steps, rows, cos_out, sin_out)
    for copy in copies:
        copy.wait()


def scale_call(early, blocks, far, lengths, weight, gain, parts):
    steps, rows, width = parts[0].shape
    count = steps * rows
    return pl.pallas_call(
        functools.partial(scale_kernel, early, far),
        out_shape=(
            pltpu.VMEM((count, blocks * width), jnp.bfloat16),
            pltpu.VMEM((count, len(early) * width), jnp.bfloat16),
            pltpu.VMEM((count, HD), jnp.float32),
            pltpu.VMEM((len(far) * width,) + weight.shape[1:], weight.dtype),
            pltpu.VMEM((count, HD), jnp.float32),
            pltpu.VMEM((count, HD), jnp.float32),
        ),
        in_specs=[HBM] * 2 + [VMEM] * (1 + len(parts)),
        out_specs=(VMEM,) * 6,
        scratch_shapes=[
            pltpu.SMEM(lengths.shape, jnp.int32),
            pltpu.SemaphoreType.DMA,
            pltpu.SemaphoreType.DMA((len(far),)),
        ],
        compiler_params=pltpu.CompilerParams(vmem_limit_bytes=8 << 20),
        cost_estimate=pl.CostEstimate(flops=0, bytes_accessed=9 << 20, transcendentals=0),
        name="scale_features",
    )(*[pltpu.with_memory_space_constraint(x, pltpu.HBM) for x in (lengths, weight)], gain, *parts)


def inner_kernel(late, scaled_ref, early_ref, square_ref, gain_ref, *rest):
    parts, rest = rest[: len(late)], rest[len(late) :]
    outs, square_out = rest[-1 - len(late) : -1], rest[-1]
    packs, inner_out = (rest[: -2 - len(late)], rest[-2 - len(late)]) if len(rest) > 1 + len(late) else ((), None)
    squares = square_ref[...]
    blocks = []
    for k, (offset, part) in enumerate(zip(late, parts)):
        block = lax.axis_index("tp") ^ offset
        scaled, more = scaled_block(part, gain_ref, block)
        squares += more
        blocks.append((block, scaled))
        width = scaled.shape[1]
        outs[k][:, :width] = early_ref[:, k * width : (k + 1) * width]
        outs[k][:, width:] = scaled
    squares = jnp.sum(squares, axis=1, keepdims=True)
    square_out[...] = jnp.broadcast_to(squares, square_out.shape)
    if not packs:
        return
    me = lax.axis_index("wide")
    total = []
    for offset, pack in enumerate(packs):
        mine = me ^ offset
        rows = scaled_ref[:, pl.ds(pl.multiple_of(mine * width, width), width)]
        for block, scaled in blocks:
            rows = jnp.where(mine == block, scaled, rows)
        total.append(
            lax.dot_general(
                rows,
                pack[:, :, :width].reshape(inner_out.shape[1], width),
                (((1,), (1,)), ((), ())),
                preferred_element_type=jnp.float32,
            )
        )
    inner_out[...] = sum(total[1:], total[0])


def inner_call(late, scaled, early, square, gain, parts, packs):
    count, width = scaled.shape[0], parts[0].shape[2]
    shapes = [pltpu.VMEM((count, 2 * width), scaled.dtype) for _ in late]
    shapes.append(pltpu.VMEM(square.shape, jnp.float32))
    if packs:
        kinds, share, _ = packs[0].shape
        shapes = [pltpu.VMEM((count, kinds * share), jnp.float32)] + shapes
    return pl.pallas_call(
        functools.partial(inner_kernel, late),
        out_shape=tuple(shapes),
        in_specs=[VMEM] * (4 + len(parts) + len(packs)),
        out_specs=(VMEM,) * len(shapes),
        compiler_params=pltpu.CompilerParams(vmem_limit_bytes=8 << 20),
        name="rank_inner",
    )(scaled, early, square, gain, *parts, *packs)


def up_kernel(*refs):
    packs, up_out = refs[:-1], refs[-1]
    kinds, share, pack_width = packs[0].shape
    columns = up_out.shape[1] // kinds
    me = lax.axis_index("wide") if len(packs) > 1 else 0
    up_out[...] = jnp.zeros_like(up_out)
    for offset, pack in enumerate(packs):
        for kind in range(kinds):
            at = pl.multiple_of(((me ^ offset) * kinds + kind) * share, share)
            up_out[pl.ds(at, share), kind * columns : (kind + 1) * columns] = pack[
                kind, :, pack_width - columns :
            ]


def up_call(packs, columns):
    kinds, share, _ = packs[0].shape
    return pl.pallas_call(
        up_kernel,
        out_shape=pltpu.VMEM((len(packs) * kinds * share, kinds * columns), packs[0].dtype),
        in_specs=[VMEM] * len(packs),
        out_specs=VMEM,
        compiler_params=pltpu.CompilerParams(vmem_limit_bytes=8 << 20),
        name="lay_out_up",
    )(*packs)


def split_index(index, count):
    if count & (count - 1) == 0:
        return index >> (count.bit_length() - 1), index & (count - 1)
    return index // count, index % count


def final_kernel(width, blocks, near_ref, far_ref, square_ref, bias_ref, *rest):
    query_ref, acc_ref, top_ref, total_ref, cos_ref, sin_ref = rest[:6]
    inner_refs = rest[6 : 6 + blocks]
    up_ref, keys_out, values_out, attended_out, inner_buffer = rest[6 + blocks :]
    steps, rows, columns = keys_out.shape
    count = steps * rows
    groups, size, _ = query_ref.shape
    per_group = size // count
    kinds = bias_ref.shape[0]
    row_scale = lax.rsqrt(square_ref[:, :1] * (1.0 / width) + norm_eps)
    me = lax.axis_index("tp") if blocks > 1 else 0
    for i in range(blocks):
        inner_buffer[me ^ i] = inner_refs[i][...]
    inner = jnp.concatenate([inner_buffer[i] for i in range(blocks)], axis=1)
    high = inner.astype(jnp.bfloat16)
    low = (inner - high.astype(jnp.float32)).astype(jnp.bfloat16)
    lora = jnp.dot(
        jnp.concatenate([high, low], axis=0), up_ref[...], preferred_element_type=jnp.float32
    )
    lora = lora[:count] + lora[count:]
    bias = bias_ref[...].astype(jnp.float32)
    linear = []
    for kind in range(kinds):
        base = near_ref[kind] + far_ref[kind]
        part = lora[:, kind * columns : (kind + 1) * columns]
        linear.append((base + adapter_scale * part) * row_scale + bias[kind : kind + 1])
    cosine, sine = cos_ref[...], sin_ref[...]
    line = lax.broadcasted_iota(jnp.int32, (size, count), 0)
    other = lax.broadcasted_iota(jnp.int32, (size, count), 1)
    line_step, line_row = split_index(line, rows)
    other_step, other_row = split_index(other, rows)
    line_step = split_index(line_step, steps)[1]
    live = (line_row == other_row) & (other_step <= line_step)
    for group in range(groups):
        at = slice(group * HD, (group + 1) * HD)
        key = linear[0][:, at]
        key = (key * cosine + pltpu.roll(key, HD // 2, 1) * sine).astype(jnp.bfloat16)
        value = linear[1][:, at].astype(jnp.bfloat16)
        for step in range(steps):
            keys_out[step, :, at] = key[step * rows : (step + 1) * rows]
            values_out[step, :, at] = value[step * rows : (step + 1) * rows]
        scores = lax.dot_general(
            query_ref[group].astype(jnp.bfloat16),
            key,
            (((1,), (1,)), ((), ())),
            preferred_element_type=jnp.float32,
        )
        scores = jnp.where(live, scores * score_scale, masked_score)
        old_top = top_ref[group][:, :1]
        top = jnp.maximum(old_top, jnp.max(scores, axis=1, keepdims=True))
        exps = jnp.exp(scores - top)
        keep = jnp.exp(old_top - top)
        total = total_ref[group][:, :1] * keep + jnp.sum(exps, axis=1, keepdims=True)
        acc = acc_ref[group] * keep + jnp.dot(
            exps.astype(jnp.bfloat16), value, preferred_element_type=jnp.float32
        )
        attended = (acc * (1.0 / total)).astype(jnp.bfloat16)
        for head in range(per_group):
            lanes = pl.ds((group * per_group + head) * HD, HD)
            for step in range(steps):
                tile = (head * steps + step) * rows
                attended_out[step, :, lanes] = attended[tile : tile + rows]


def final_call(shape, width, near, far, square, bias, cached, inner, up):
    steps, rows, query_width = shape
    columns = near.shape[2]
    small = jax.ShapeDtypeStruct((steps, rows, columns), jnp.bfloat16)
    return pl.pallas_call(
        functools.partial(final_kernel, width, len(inner)),
        out_shape=(small, small, jax.ShapeDtypeStruct(shape, jnp.bfloat16)),
        in_specs=[VMEM] * (5 + len(cached) + len(inner)),
        out_specs=(VMEM,) * 3,
        scratch_shapes=[pltpu.VMEM((len(inner),) + inner[0].shape, jnp.float32)],
        compiler_params=pltpu.CompilerParams(vmem_limit_bytes=8 << 20),
        name="fresh_attention",
    )(near, far, square, bias, *cached, *inner, up)


def dot(rows, weight):
    return jnp.einsum("md,dkc->kmc", rows, weight, preferred_element_type=jnp.float32)


def swap(block, axis, offset, count):
    return lax.ppermute(block, axis, [(i, i ^ offset) for i in range(count)])


def on_device(
    wide_count,
    tp_count,
    hidden,
    input_norm_gain,
    key_value_weight,
    key_value_bias,
    adapter_down_factor,
    adapter_up_factor,
    queries,
    stored_rotated_keys,
    stored_value_rows,
    lengths,
):
    steps, rows, part_width = hidden.shape
    width = part_width * tp_count
    kinds, ranks, down_width = adapter_down_factor.shape
    gain = input_norm_gain.reshape(width // HD, HD)
    up_part = jnp.transpose(adapter_up_factor, (0, 2, 1))
    direct = wide_count == tp_count == 4
    beside, crossed = [swap(hidden, "tp", offset, tp_count) for offset in (1, 2)]
    if direct:
        pack = pack_call(adapter_down_factor, up_part)
        second = swap(pack, "wide", 2, wide_count)
        first = swap(pack, "wide", 1, wide_count)
    near, far = (0, 1), (2, 3)
    early, late = (0, 2), (1, 3)
    near_weight, gain_rows, bias, mine, *cached = cache_call(
        near,
        lengths,
        queries,
        stored_rotated_keys,
        stored_value_rows,
        gain,
        key_value_bias,
        hidden,
        key_value_weight,
    )
    relayed, gain_rows = lax.optimization_barrier((crossed, gain_rows))
    relayed = swap(relayed, "tp", 1, tp_count)
    if direct:
        third, gain_rows = lax.optimization_barrier((second, gain_rows))
        packs = [pack, first, second, swap(third, "wide", 1, wide_count)]
    scaled, early_scaled, square, far_weight, *tables = scale_call(
        early, tp_count, far, lengths, key_value_weight, gain_rows, (mine, crossed)
    )
    late_parts = (beside, relayed)
    if direct:
        inner, near_scaled, far_scaled, square = inner_call(
            late, scaled, early_scaled, square, gain_rows, late_parts, packs
        )
        inner, far_scaled, near_scaled, packs = lax.optimization_barrier(
            (inner, far_scaled, near_scaled, packs)
        )
        inner = [inner] + [swap(inner, "tp", offset, tp_count) for offset in (1, 2, 3)]
    else:
        near_scaled, far_scaled, square = inner_call(
            late, scaled, early_scaled, square, gain_rows, late_parts, []
        )
        down = lax.all_gather(adapter_down_factor, "wide", axis=2, tiled=True)
        rows_full = lax.all_gather(hidden, "tp", axis=2, tiled=True).astype(jnp.float32)
        rows_full = (rows_full * input_norm_gain.astype(jnp.float32)).astype(jnp.bfloat16)
        inner = jnp.einsum("srd,kad->srka", rows_full, down, preferred_element_type=jnp.float32)
        inner = [inner.reshape(steps * rows, kinds * ranks)]
        packs = [lax.all_gather(up_part, "wide", axis=1, tiled=True)]
    near_base = dot(near_scaled, near_weight)
    far_base = dot(far_scaled, far_weight)
    up = up_call(packs, bias.shape[1])
    return final_call(
        queries.shape, width, near_base, far_base, square, bias, cached + tables, inner, up
    )


def solution(mesh):
    in_specs = (
        P(None, ("groups", "wide"), "tp"),
        P(),
        P(None, None, "tp"),
        P(None, "tp"),
        P("groups", None, "wide"),
        P("groups", "tp", "wide"),
        P(None, ("groups", "wide"), "tp"),
        P(("groups", "wide"), None, "tp"),
        P(("groups", "wide"), None, "tp"),
        P(("groups", "wide")),
    )
    out_specs = (
        P(None, ("groups", "wide"), "tp"),
        P(None, ("groups", "wide"), "tp"),
        P(None, ("groups", "wide"), "tp"),
    )
    body = functools.partial(on_device, mesh.shape["wide"], mesh.shape["tp"])
    return jax.shard_map(
        body, mesh=mesh, in_specs=in_specs, out_specs=out_specs, check_vma=False
    )
```

```python
import functools
import math

import jax
import jax.numpy as jnp
from jax import lax
from jax.experimental import pallas as pl
from jax.experimental.pallas import tpu as pltpu
from jax.sharding import PartitionSpec as P

HD = 128


norm_eps = 1e-06
adapter_scale = 2.0
rope_base = 1000000.0
masked_score = -1e30
score_scale = 1.0 / math.sqrt(HD)

VMEM = pl.BlockSpec(memory_space=pltpu.VMEM)
HBM = pl.BlockSpec(memory_space=pltpu.HBM)


def query_block(query_ref, group, per_group):
    steps = query_ref.shape[0]
    tiles = []
    for head in range(per_group):
        at = (group * per_group + head) * HD
        for step in range(steps):
            tiles.append(query_ref[step, :, at : at + HD].astype(jnp.float32))
    return jnp.concatenate(tiles, axis=0)


def copy_blocks(offsets, width, weight_ref, out_ref, sems):
    me = lax.axis_index("tp")
    copies = []
    for i, offset in enumerate(offsets):
        block = pl.ds(pl.multiple_of((me ^ offset) * width, width), width)
        copies.append(
            pltpu.make_async_copy(
                weight_ref.at[block], out_ref.at[pl.ds(i * width, width)], sems.at[i]
            )
        )
        copies[-1].start()
    return copies


def cache_kernel(
    near,
    lengths_ref,
    query_ref,
    key_ref,
    value_ref,
    gain_ref,
    bias_ref,
    hidden_ref,
    weight_ref,
    near_out,
    gain_out,
    bias_out,
    hidden_out,
    query_out,
    acc_out,
    top_out,
    total_out,
    lengths,
    queries,
    gain_buffer,
    key_buffer,
    value_buffer,
    score_buffer,
    sems,
    weight_sems,
):
    steps, rows, query_width = query_ref.shape
    cache_span = key_ref.shape[1]
    groups = key_ref.shape[2] // HD
    per_group = query_width // HD // groups
    lines = steps * per_group
    half_rows = rows // 2
    halves = [pl.ds(0, half_rows), pl.ds(half_rows, half_rows)]
    copies = [
        (lengths_ref, lengths),
        (query_ref, queries),
        (key_ref.at[halves[0]], key_buffer.at[halves[0]]),
        (key_ref.at[halves[1]], key_buffer.at[halves[1]]),
        (value_ref.at[halves[0]], value_buffer.at[halves[0]]),
        (value_ref.at[halves[1]], value_buffer.at[halves[1]]),
        (gain_ref, gain_buffer),
        (bias_ref, bias_out),
        (hidden_ref, hidden_out),
    ]
    copies = [pltpu.make_async_copy(*pair, sems.at[i]) for i, pair in enumerate(copies)]
    for copy in copies:
        copy.start()
    copies += copy_blocks(near, hidden_ref.shape[2], weight_ref, near_out, weight_sems)

    copies[0].wait()
    copies[1].wait()
    for group in range(groups):
        query_out[group] = query_block(queries, group, per_group)

    place = lax.broadcasted_iota(jnp.int32, (lines, cache_span), 1)
    for i in range(2):
        copies[2 + i].wait()
        for row in range(i * half_rows, (i + 1) * half_rows):
            for group in range(groups):
                query = query_out[group, pl.ds(row, lines, stride=rows), :].astype(jnp.bfloat16)
                score_buffer[row * groups + group] = lax.dot_general(
                    query,
                    key_buffer[row, :, pl.ds(group * HD, HD)],
                    (((1,), (1,)), ((), ())),
                    preferred_element_type=jnp.float32,
                )
    for i in range(2):
        copies[4 + i].wait()
        for row in range(i * half_rows, (i + 1) * half_rows):
            live = place < lengths[row]
            for group in range(groups):
                mine = pl.ds(row, lines, stride=rows)
                scores = score_buffer[row * groups + group]
                scores = jnp.where(live, scores * score_scale, masked_score)
                top = jnp.max(scores, axis=1, keepdims=True)
                exps = jnp.exp(scores - top)
                total = jnp.sum(exps, axis=1, keepdims=True)
                acc = jnp.dot(
                    exps.astype(jnp.bfloat16),
                    value_buffer[row, :, pl.ds(group * HD, HD)],
                    preferred_element_type=jnp.float32,
                )
                acc_out[group, mine, :] = acc
                top_out[group, mine, :] = jnp.broadcast_to(top, acc.shape)
                total_out[group, mine, :] = jnp.broadcast_to(total, acc.shape)
    copies[6].wait()
    gain_out[...] = gain_buffer[...].astype(jnp.float32)
    for copy in copies[7:]:
        copy.wait()


def cache_call(near, lengths, queries, keys, values, gain, bias, hidden, weight):
    steps, rows, query_width = queries.shape
    cache_span, key_width = keys.shape[1:]
    groups = key_width // HD
    lines = steps * (query_width // key_width)
    block = (groups, lines * rows, HD)
    operands = (lengths, queries, keys, values, gain, bias, hidden, weight)
    near_weight = (len(near) * hidden.shape[2],) + weight.shape[1:]
    return pl.pallas_call(
        functools.partial(cache_kernel, near),
        out_shape=(
            pltpu.VMEM(near_weight, weight.dtype),
            pltpu.VMEM(gain.shape, jnp.float32),
            pltpu.VMEM(bias.shape, bias.dtype),
            pltpu.VMEM(hidden.shape, hidden.dtype),
            pltpu.VMEM(block, jnp.float32),
            pltpu.VMEM(block, jnp.float32),
            pltpu.VMEM(block, jnp.float32),
            pltpu.VMEM(block, jnp.float32),
        ),
        in_specs=[HBM] * len(operands),
        out_specs=(VMEM,) * 8,
        scratch_shapes=[
            pltpu.SMEM(lengths.shape, jnp.int32),
            pltpu.VMEM(queries.shape, queries.dtype),
            pltpu.VMEM(gain.shape, gain.dtype),
            pltpu.VMEM(keys.shape, keys.dtype),
            pltpu.VMEM(values.shape, values.dtype),
            pltpu.VMEM((rows * groups, lines, cache_span), jnp.float32),
            pltpu.SemaphoreType.DMA((9,)),
            pltpu.SemaphoreType.DMA((len(near),)),
        ],
        compiler_params=pltpu.CompilerParams(vmem_limit_bytes=16 << 20),
        cost_estimate=pl.CostEstimate(flops=2 * 67 << 20, bytes_accessed=5 << 20, transcendentals=0),
        name="cache_attention",
    )(*[pltpu.with_memory_space_constraint(x, pltpu.HBM) for x in operands])


def rows_of(ref):
    return jnp.concatenate([ref[s].astype(jnp.float32) for s in range(ref.shape[0])], axis=0)


def pack_kernel(down_ref, up_ref, out_ref, sems):
    share = out_ref.shape[1]
    width = down_ref.shape[2]
    at = pl.ds(pl.multiple_of(lax.axis_index("tp") * share, share), share)
    copies = [(up_ref, out_ref.at[:, :, pl.ds(width, up_ref.shape[2])])]
    half = width // 2
    for kind in range(down_ref.shape[0]):
        for first in (0, half):
            lanes = pl.ds(first, half)
            copies.append((down_ref.at[kind, at, lanes], out_ref.at[kind, :, lanes]))
    copies = [pltpu.make_async_copy(*pair, sems.at[i]) for i, pair in enumerate(copies)]
    for copy in copies:
        copy.start()
    for copy in copies:
        copy.wait()


def pack_call(down, up):
    kinds, share, columns = up.shape
    return pl.pallas_call(
        pack_kernel,
        out_shape=pltpu.VMEM((kinds, share, down.shape[2] + columns), down.dtype),
        in_specs=[HBM] * 2,
        out_specs=VMEM,
        scratch_shapes=[pltpu.SemaphoreType.DMA((1 + 2 * kinds,))],
        name="pack_factors",
    )(*[pltpu.with_memory_space_constraint(x, pltpu.HBM) for x in (down, up)])


def scaled_block(part, gain_ref, block):
    steps, rows, width = part.shape
    chunks = width // HD
    gain = gain_ref[pl.ds(pl.multiple_of(block * chunks, chunks), chunks)]
    values = rows_of(part)
    squares = jnp.zeros((steps * rows, HD), jnp.float32)
    scaled = []
    for i in range(chunks):
        chunk = values[:, i * HD : (i + 1) * HD]
        squares += chunk * chunk
        scaled.append((chunk * gain[i : i + 1]).astype(jnp.bfloat16))
    return jnp.concatenate(scaled, axis=1), squares


def rotation_tables(lengths, steps, rows, cos_out, sin_out):
    lane = lax.broadcasted_iota(jnp.int32, (rows, HD), 1)
    half = HD // 2
    second = lane >= half
    index = jnp.where(second, lane - half, lane).astype(jnp.float32)
    inv_freq = jnp.exp(index * (-2.0 * math.log(rope_base) / HD))
    row_index = lax.broadcasted_iota(jnp.int32, (rows, HD), 0)
    row_lengths = jnp.zeros((rows, HD), jnp.int32)
    for row in range(rows):
        row_lengths = jnp.where(row_index == row, lengths[row], row_lengths)
    for step in range(steps):
        angles = (row_lengths + step).astype(jnp.float32) * inv_freq
        sine = jnp.sin(angles)
        cos_out[pl.ds(step * rows, rows)] = jnp.cos(angles)
        sin_out[pl.ds(step * rows, rows)] = jnp.where(second, sine, -sine)


def scale_kernel(early, far, lengths_ref, weight_ref, gain_ref, *rest):
    scaled_out, early_out, square_out, far_weight, cos_out, sin_out = rest[-9:-3]
    lengths, length_sem, far_sems = rest[-3:]
    parts = rest[:-9]
    steps, rows, width = parts[0].shape
    length_copy = pltpu.make_async_copy(lengths_ref, lengths, length_sem)
    length_copy.start()
    copies = copy_blocks(far, width, weight_ref, far_weight, far_sems)
    me = lax.axis_index("tp")
    scaled_out[...] = jnp.zeros_like(scaled_out)
    total = None
    for k, (offset, part) in enumerate(zip(early, parts)):
        block = me ^ offset
        scaled, squares = scaled_block(part, gain_ref, block)
        total = squares if total is None else total + squares
        scaled_out[:, pl.ds(pl.multiple_of(block * width, width), width)] = scaled
        early_out[:, k * width : (k + 1) * width] = scaled
    square_out[...] = total
    length_copy.wait()
    rotation_tables(lengths, steps, rows, cos_out, sin_out)
    for copy in copies:
        copy.wait()


def scale_call(early, blocks, far, lengths, weight, gain, parts):
    steps, rows, width = parts[0].shape
    count = steps * rows
    return pl.pallas_call(
        functools.partial(scale_kernel, early, far),
        out_shape=(
            pltpu.VMEM((count, blocks * width), jnp.bfloat16),
            pltpu.VMEM((count, len(early) * width), jnp.bfloat16),
            pltpu.VMEM((count, HD), jnp.float32),
            pltpu.VMEM((len(far) * width,) + weight.shape[1:], weight.dtype),
            pltpu.VMEM((count, HD), jnp.float32),
            pltpu.VMEM((count, HD), jnp.float32),
        ),
        in_specs=[HBM] * 2 + [VMEM] * (1 + len(parts)),
        out_specs=(VMEM,) * 6,
        scratch_shapes=[
            pltpu.SMEM(lengths.shape, jnp.int32),
            pltpu.SemaphoreType.DMA,
            pltpu.SemaphoreType.DMA((len(far),)),
        ],
        compiler_params=pltpu.CompilerParams(vmem_limit_bytes=8 << 20),
        cost_estimate=pl.CostEstimate(flops=0, bytes_accessed=9 << 20, transcendentals=0),
        name="scale_features",
    )(*[pltpu.with_memory_space_constraint(x, pltpu.HBM) for x in (lengths, weight)], gain, *parts)


def inner_kernel(late, scaled_ref, early_ref, square_ref, gain_ref, *rest):
    parts, rest = rest[: len(late)], rest[len(late) :]
    outs, square_out = rest[-1 - len(late) : -1], rest[-1]
    packs, inner_out = (rest[: -2 - len(late)], rest[-2 - len(late)]) if len(rest) > 1 + len(late) else ((), None)
    squares = square_ref[...]
    blocks = []
    for k, (offset, part) in enumerate(zip(late, parts)):
        block = lax.axis_index("tp") ^ offset
        scaled, more = scaled_block(part, gain_ref, block)
        squares += more
        blocks.append((block, scaled))
        width = scaled.shape[1]
        outs[k][:, :width] = early_ref[:, k * width : (k + 1) * width]
        outs[k][:, width:] = scaled
    squares = jnp.sum(squares, axis=1, keepdims=True)
    square_out[...] = jnp.broadcast_to(squares, square_out.shape)
    if not packs:
        return
    me = lax.axis_index("wide")
    total = []
    for offset, pack in enumerate(packs):
        mine = me ^ offset
        rows = scaled_ref[:, pl.ds(pl.multiple_of(mine * width, width), width)]
        for block, scaled in blocks:
            rows = jnp.where(mine == block, scaled, rows)
        total.append(
            lax.dot_general(
                rows,
                pack[:, :, :width].reshape(inner_out.shape[1], width),
                (((1,), (1,)), ((), ())),
                preferred_element_type=jnp.float32,
            )
        )
    inner_out[...] = sum(total[1:], total[0])


def inner_call(late, scaled, early, square, gain, parts, packs):
    count, width = scaled.shape[0], parts[0].shape[2]
    shapes = [pltpu.VMEM((count, 2 * width), scaled.dtype) for _ in late]
    shapes.append(pltpu.VMEM(square.shape, jnp.float32))
    if packs:
        kinds, share, _ = packs[0].shape
        shapes = [pltpu.VMEM((count, kinds * share), jnp.float32)] + shapes
    return pl.pallas_call(
        functools.partial(inner_kernel, late),
        out_shape=tuple(shapes),
        in_specs=[VMEM] * (4 + len(parts) + len(packs)),
        out_specs=(VMEM,) * len(shapes),
        compiler_params=pltpu.CompilerParams(vmem_limit_bytes=8 << 20),
        name="rank_inner",
    )(scaled, early, square, gain, *parts, *packs)


def up_kernel(*refs):
    packs, up_out = refs[:-1], refs[-1]
    kinds, share, pack_width = packs[0].shape
    columns = up_out.shape[1] // kinds
    me = lax.axis_index("wide") if len(packs) > 1 else 0
    up_out[...] = jnp.zeros_like(up_out)
    for offset, pack in enumerate(packs):
        for kind in range(kinds):
            at = pl.multiple_of(((me ^ offset) * kinds + kind) * share, share)
            up_out[pl.ds(at, share), kind * columns : (kind + 1) * columns] = pack[
                kind, :, pack_width - columns :
            ]


def up_call(packs, columns):
    kinds, share, _ = packs[0].shape
    return pl.pallas_call(
        up_kernel,
        out_shape=pltpu.VMEM((len(packs) * kinds * share, kinds * columns), packs[0].dtype),
        in_specs=[VMEM] * len(packs),
        out_specs=VMEM,
        compiler_params=pltpu.CompilerParams(vmem_limit_bytes=8 << 20),
        name="lay_out_up",
    )(*packs)


def split_index(index, count):
    if count & (count - 1) == 0:
        return index >> (count.bit_length() - 1), index & (count - 1)
    return index // count, index % count


def final_kernel(width, blocks, near_ref, far_ref, square_ref, bias_ref, *rest):
    query_ref, acc_ref, top_ref, total_ref, cos_ref, sin_ref = rest[:6]
    inner_refs = rest[6 : 6 + blocks]
    up_ref, keys_ref, values_ref, attended_ref = rest[6 + blocks : 10 + blocks]
    inner_buffer, keys_out, values_out, attended_out, sems = rest[10 + blocks :]
    steps, rows, columns = keys_out.shape
    count = steps * rows
    groups, size, _ = query_ref.shape
    per_group = size // count
    kinds = bias_ref.shape[0]
    row_scale = lax.rsqrt(square_ref[:, :1] * (1.0 / width) + norm_eps)
    me = lax.axis_index("tp") if blocks > 1 else 0
    for i in range(blocks):
        inner_buffer[me ^ i] = inner_refs[i][...]
    inner = jnp.concatenate([inner_buffer[i] for i in range(blocks)], axis=1)
    high = inner.astype(jnp.bfloat16)
    low = (inner - high.astype(jnp.float32)).astype(jnp.bfloat16)
    lora = jnp.dot(
        jnp.concatenate([high, low], axis=0), up_ref[...], preferred_element_type=jnp.float32
    )
    lora = lora[:count] + lora[count:]
    bias = bias_ref[...].astype(jnp.float32)
    linear = []
    for kind in range(kinds):
        base = near_ref[kind] + far_ref[kind]
        part = lora[:, kind * columns : (kind + 1) * columns]
        linear.append((base + adapter_scale * part) * row_scale + bias[kind : kind + 1])
    cosine, sine = cos_ref[...], sin_ref[...]
    line = lax.broadcasted_iota(jnp.int32, (size, count), 0)
    other = lax.broadcasted_iota(jnp.int32, (size, count), 1)
    line_step, line_row = split_index(line, rows)
    other_step, other_row = split_index(other, rows)
    line_step = split_index(line_step, steps)[1]
    live = (line_row == other_row) & (other_step <= line_step)
    copies = []

    def send(source, target):
        copies.append(pltpu.make_async_copy(source, target, sems.at[len(copies)]))
        copies[-1].start()

    keys, values = [], []
    for group in range(groups):
        at = slice(group * HD, (group + 1) * HD)
        key = linear[0][:, at]
        key = (key * cosine + pltpu.roll(key, HD // 2, 1) * sine).astype(jnp.bfloat16)
        value = linear[1][:, at].astype(jnp.bfloat16)
        for step in range(steps):
            keys_out[step, :, at] = key[step * rows : (step + 1) * rows]
            values_out[step, :, at] = value[step * rows : (step + 1) * rows]
        keys.append(key)
        values.append(value)
    send(keys_out, keys_ref)
    send(values_out, values_ref)
    for group in range(groups):
        scores = lax.dot_general(
            query_ref[group].astype(jnp.bfloat16),
            keys[group],
            (((1,), (1,)), ((), ())),
            preferred_element_type=jnp.float32,
        )
        scores = jnp.where(live, scores * score_scale, masked_score)
        old_top = top_ref[group][:, :1]
        top = jnp.maximum(old_top, jnp.max(scores, axis=1, keepdims=True))
        exps = jnp.exp(scores - top)
        keep = jnp.exp(old_top - top)
        total = total_ref[group][:, :1] * keep + jnp.sum(exps, axis=1, keepdims=True)
        acc = acc_ref[group] * keep + jnp.dot(
            exps.astype(jnp.bfloat16), values[group], preferred_element_type=jnp.float32
        )
        attended = (acc * (1.0 / total)).astype(jnp.bfloat16)
        for head in range(per_group):
            lanes = pl.ds((group * per_group + head) * HD, HD)
            for step in range(steps):
                tile = (head * steps + step) * rows
                attended_out[step, :, lanes] = attended[tile : tile + rows]
    for group in range(groups):
        lanes = pl.ds(group * per_group * HD, per_group * HD)
        for step in range(steps):
            send(attended_out.at[step, :, lanes], attended_ref.at[step, :, lanes])
    for copy in copies:
        copy.wait()


def final_call(shape, width, near, far, square, bias, cached, inner, up):
    steps, rows, query_width = shape
    columns = near.shape[2]
    small = jax.ShapeDtypeStruct((steps, rows, columns), jnp.bfloat16)
    return pl.pallas_call(
        functools.partial(final_kernel, width, len(inner)),
        out_shape=(small, small, jax.ShapeDtypeStruct(shape, jnp.bfloat16)),
        in_specs=[VMEM] * (5 + len(cached) + len(inner)),
        out_specs=(HBM,) * 3,
        scratch_shapes=[
            pltpu.VMEM((len(inner),) + inner[0].shape, jnp.float32),
            pltpu.VMEM(small.shape, small.dtype),
            pltpu.VMEM(small.shape, small.dtype),
            pltpu.VMEM(shape, jnp.bfloat16),
            pltpu.SemaphoreType.DMA((2 + columns // HD * steps,)),
        ],
        compiler_params=pltpu.CompilerParams(vmem_limit_bytes=8 << 20),
        name="fresh_attention",
    )(near, far, square, bias, *cached, *inner, up)


def dot(rows, weight):
    return jnp.einsum("md,dkc->kmc", rows, weight, preferred_element_type=jnp.float32)


def swap(block, axis, offset, count):
    return lax.ppermute(block, axis, [(i, i ^ offset) for i in range(count)])


def on_device(
    wide_count,
    tp_count,
    hidden,
    input_norm_gain,
    key_value_weight,
    key_value_bias,
    adapter_down_factor,
    adapter_up_factor,
    queries,
    stored_rotated_keys,
    stored_value_rows,
    lengths,
):
    steps, rows, part_width = hidden.shape
    width = part_width * tp_count
    kinds, ranks, down_width = adapter_down_factor.shape
    gain = input_norm_gain.reshape(width // HD, HD)
    up_part = jnp.transpose(adapter_up_factor, (0, 2, 1))
    direct = wide_count == tp_count == 4
    beside, crossed = [swap(hidden, "tp", offset, tp_count) for offset in (1, 2)]
    if direct:
        pack = pack_call(adapter_down_factor, up_part)
        second = swap(pack, "wide", 2, wide_count)
        first = swap(pack, "wide", 1, wide_count)
    near, far = (0, 1), (2, 3)
    early, late = (0, 2), (1, 3)
    near_weight, gain_rows, bias, mine, *cached = cache_call(
        near,
        lengths,
        queries,
        stored_rotated_keys,
        stored_value_rows,
        gain,
        key_value_bias,
        hidden,
        key_value_weight,
    )
    relayed, gain_rows = lax.optimization_barrier((crossed, gain_rows))
    relayed = swap(relayed, "tp", 1, tp_count)
    if direct:
        third, gain_rows = lax.optimization_barrier((second, gain_rows))
        packs = [pack, first, second, swap(third, "wide", 1, wide_count)]
    scaled, early_scaled, square, far_weight, *tables = scale_call(
        early, tp_count, far, lengths, key_value_weight, gain_rows, (mine, crossed)
    )
    late_parts = (beside, relayed)
    if direct:
        inner, near_scaled, far_scaled, square = inner_call(
            late, scaled, early_scaled, square, gain_rows, late_parts, packs
        )
        inner, far_scaled, near_scaled, packs = lax.optimization_barrier(
            (inner, far_scaled, near_scaled, packs)
        )
        inner = [inner] + [swap(inner, "tp", offset, tp_count) for offset in (1, 2, 3)]
    else:
        near_scaled, far_scaled, square = inner_call(
            late, scaled, early_scaled, square, gain_rows, late_parts, []
        )
        down = lax.all_gather(adapter_down_factor, "wide", axis=2, tiled=True)
        rows_full = lax.all_gather(hidden, "tp", axis=2, tiled=True).astype(jnp.float32)
        rows_full = (rows_full * input_norm_gain.astype(jnp.float32)).astype(jnp.bfloat16)
        inner = jnp.einsum("srd,kad->srka", rows_full, down, preferred_element_type=jnp.float32)
        inner = [inner.reshape(steps * rows, kinds * ranks)]
        packs = [lax.all_gather(up_part, "wide", axis=1, tiled=True)]
    near_base = dot(near_scaled, near_weight)
    far_base = dot(far_scaled, far_weight)
    up = up_call(packs, bias.shape[1])
    return final_call(
        queries.shape, width, near_base, far_base, square, bias, cached + tables, inner, up
    )


def solution(mesh):
    in_specs = (
        P(None, ("groups", "wide"), "tp"),
        P(),
        P(None, None, "tp"),
        P(None, "tp"),
        P("groups", None, "wide"),
        P("groups", "tp", "wide"),
        P(None, ("groups", "wide"), "tp"),
        P(("groups", "wide"), None, "tp"),
        P(("groups", "wide"), None, "tp"),
        P(("groups", "wide")),
    )
    out_specs = (
        P(None, ("groups", "wide"), "tp"),
        P(None, ("groups", "wide"), "tp"),
        P(None, ("groups", "wide"), "tp"),
    )
    body = functools.partial(on_device, mesh.shape["wide"], mesh.shape["tp"])
    return jax.shard_map(
        body, mesh=mesh, in_specs=in_specs, out_specs=out_specs, check_vma=False
    )
```

```python
import functools
import math

import jax
import jax.numpy as jnp
from jax import lax
from jax.experimental import pallas as pl
from jax.experimental.pallas import tpu as pltpu
from jax.sharding import PartitionSpec as P

HD = 128


norm_eps = 1e-06
adapter_scale = 2.0
rope_base = 1000000.0
masked_score = -1e30
score_scale = 1.0 / math.sqrt(HD)

VMEM = pl.BlockSpec(memory_space=pltpu.VMEM)
HBM = pl.BlockSpec(memory_space=pltpu.HBM)


def query_block(query_ref, group, per_group):
    steps = query_ref.shape[0]
    tiles = []
    for head in range(per_group):
        at = (group * per_group + head) * HD
        for step in range(steps):
            tiles.append(query_ref[step, :, at : at + HD].astype(jnp.float32))
    return jnp.concatenate(tiles, axis=0)


def copy_blocks(offsets, width, weight_ref, out_ref, sems):
    me = lax.axis_index("tp")
    copies = []
    for i, offset in enumerate(offsets):
        block = pl.ds(pl.multiple_of((me ^ offset) * width, width), width)
        copies.append(
            pltpu.make_async_copy(
                weight_ref.at[block], out_ref.at[pl.ds(i * width, width)], sems.at[i]
            )
        )
        copies[-1].start()
    return copies


def cache_kernel(
    near,
    lengths_ref,
    query_ref,
    key_ref,
    value_ref,
    gain_ref,
    bias_ref,
    hidden_ref,
    weight_ref,
    near_out,
    gain_out,
    bias_out,
    hidden_out,
    query_out,
    acc_out,
    top_out,
    total_out,
    lengths,
    queries,
    gain_buffer,
    key_buffer,
    value_buffer,
    score_buffer,
    sems,
    weight_sems,
):
    steps, rows, query_width = query_ref.shape
    cache_span = key_ref.shape[1]
    groups = key_ref.shape[2] // HD
    per_group = query_width // HD // groups
    lines = steps * per_group
    half_rows = rows // 2
    halves = [pl.ds(0, half_rows), pl.ds(half_rows, half_rows)]
    copies = [
        (lengths_ref, lengths),
        (query_ref, queries),
        (key_ref.at[halves[0]], key_buffer.at[halves[0]]),
        (key_ref.at[halves[1]], key_buffer.at[halves[1]]),
        (value_ref.at[halves[0]], value_buffer.at[halves[0]]),
        (value_ref.at[halves[1]], value_buffer.at[halves[1]]),
        (gain_ref, gain_buffer),
        (bias_ref, bias_out),
        (hidden_ref, hidden_out),
    ]
    copies = [pltpu.make_async_copy(*pair, sems.at[i]) for i, pair in enumerate(copies)]
    for copy in copies:
        copy.start()
    copies += copy_blocks(near, hidden_ref.shape[2], weight_ref, near_out, weight_sems)

    copies[0].wait()
    copies[1].wait()
    for group in range(groups):
        query_out[group] = query_block(queries, group, per_group)

    place = lax.broadcasted_iota(jnp.int32, (lines, cache_span), 1)
    for i in range(2):
        copies[2 + i].wait()
        for row in range(i * half_rows, (i + 1) * half_rows):
            for group in range(groups):
                query = query_out[group, pl.ds(row, lines, stride=rows), :].astype(jnp.bfloat16)
                score_buffer[row * groups + group] = lax.dot_general(
                    query,
                    key_buffer[row, :, pl.ds(group * HD, HD)],
                    (((1,), (1,)), ((), ())),
                    preferred_element_type=jnp.float32,
                )
    for i in range(2):
        copies[4 + i].wait()
        for row in range(i * half_rows, (i + 1) * half_rows):
            live = place < lengths[row]
            for group in range(groups):
                mine = pl.ds(row, lines, stride=rows)
                scores = score_buffer[row * groups + group]
                scores = jnp.where(live, scores * score_scale, masked_score)
                top = jnp.max(scores, axis=1, keepdims=True)
                exps = jnp.exp(scores - top)
                total = jnp.sum(exps, axis=1, keepdims=True)
                acc = jnp.dot(
                    exps.astype(jnp.bfloat16),
                    value_buffer[row, :, pl.ds(group * HD, HD)],
                    preferred_element_type=jnp.float32,
                )
                acc_out[group, mine, :] = acc
                top_out[group, mine, :] = jnp.broadcast_to(top, acc.shape)
                total_out[group, mine, :] = jnp.broadcast_to(total, acc.shape)
    copies[6].wait()
    gain_out[...] = gain_buffer[...].astype(jnp.float32)
    for copy in copies[7:]:
        copy.wait()


def cache_call(near, lengths, queries, keys, values, gain, bias, hidden, weight):
    steps, rows, query_width = queries.shape
    cache_span, key_width = keys.shape[1:]
    groups = key_width // HD
    lines = steps * (query_width // key_width)
    block = (groups, lines * rows, HD)
    operands = (lengths, queries, keys, values, gain, bias, hidden, weight)
    near_weight = (len(near) * hidden.shape[2],) + weight.shape[1:]
    return pl.pallas_call(
        functools.partial(cache_kernel, near),
        out_shape=(
            pltpu.VMEM(near_weight, weight.dtype),
            pltpu.VMEM(gain.shape, jnp.float32),
            pltpu.VMEM(bias.shape, bias.dtype),
            pltpu.VMEM(hidden.shape, hidden.dtype),
            pltpu.VMEM(block, jnp.float32),
            pltpu.VMEM(block, jnp.float32),
            pltpu.VMEM(block, jnp.float32),
            pltpu.VMEM(block, jnp.float32),
        ),
        in_specs=[HBM] * len(operands),
        out_specs=(VMEM,) * 8,
        scratch_shapes=[
            pltpu.SMEM(lengths.shape, jnp.int32),
            pltpu.VMEM(queries.shape, queries.dtype),
            pltpu.VMEM(gain.shape, gain.dtype),
            pltpu.VMEM(keys.shape, keys.dtype),
            pltpu.VMEM(values.shape, values.dtype),
            pltpu.VMEM((rows * groups, lines, cache_span), jnp.float32),
            pltpu.SemaphoreType.DMA((9,)),
            pltpu.SemaphoreType.DMA((len(near),)),
        ],
        compiler_params=pltpu.CompilerParams(vmem_limit_bytes=16 << 20),
        cost_estimate=pl.CostEstimate(flops=2 * 67 << 20, bytes_accessed=5 << 20, transcendentals=0),
        name="cache_attention",
    )(*[pltpu.with_memory_space_constraint(x, pltpu.HBM) for x in operands])


def rows_of(ref):
    return jnp.concatenate([ref[s].astype(jnp.float32) for s in range(ref.shape[0])], axis=0)


def pack_kernel(down_ref, up_ref, out_ref, sems):
    share = out_ref.shape[1]
    width = down_ref.shape[2]
    at = pl.ds(pl.multiple_of(lax.axis_index("tp") * share, share), share)
    copies = [(up_ref, out_ref.at[:, :, pl.ds(width, up_ref.shape[2])])]
    half = width // 2
    for kind in range(down_ref.shape[0]):
        for first in (0, half):
            lanes = pl.ds(first, half)
            copies.append((down_ref.at[kind, at, lanes], out_ref.at[kind, :, lanes]))
    copies = [pltpu.make_async_copy(*pair, sems.at[i]) for i, pair in enumerate(copies)]
    for copy in copies:
        copy.start()
    for copy in copies:
        copy.wait()


def pack_call(down, up):
    kinds, share, columns = up.shape
    return pl.pallas_call(
        pack_kernel,
        out_shape=pltpu.VMEM((kinds, share, down.shape[2] + columns), down.dtype),
        in_specs=[HBM] * 2,
        out_specs=VMEM,
        scratch_shapes=[pltpu.SemaphoreType.DMA((1 + 2 * kinds,))],
        name="pack_factors",
    )(*[pltpu.with_memory_space_constraint(x, pltpu.HBM) for x in (down, up)])


def scaled_block(part, gain_ref, block):
    steps, rows, width = part.shape
    chunks = width // HD
    gain = gain_ref[pl.ds(pl.multiple_of(block * chunks, chunks), chunks)]
    values = rows_of(part)
    squares = jnp.zeros((steps * rows, HD), jnp.float32)
    scaled = []
    for i in range(chunks):
        chunk = values[:, i * HD : (i + 1) * HD]
        squares += chunk * chunk
        scaled.append((chunk * gain[i : i + 1]).astype(jnp.bfloat16))
    return jnp.concatenate(scaled, axis=1), squares


def rotation_tables(lengths, steps, rows, cos_out, sin_out):
    lane = lax.broadcasted_iota(jnp.int32, (rows, HD), 1)
    half = HD // 2
    second = lane >= half
    index = jnp.where(second, lane - half, lane).astype(jnp.float32)
    inv_freq = jnp.exp(index * (-2.0 * math.log(rope_base) / HD))
    row_index = lax.broadcasted_iota(jnp.int32, (rows, HD), 0)
    row_lengths = jnp.zeros((rows, HD), jnp.int32)
    for row in range(rows):
        row_lengths = jnp.where(row_index == row, lengths[row], row_lengths)
    for step in range(steps):
        angles = (row_lengths + step).astype(jnp.float32) * inv_freq
        sine = jnp.sin(angles)
        cos_out[pl.ds(step * rows, rows)] = jnp.cos(angles)
        sin_out[pl.ds(step * rows, rows)] = jnp.where(second, sine, -sine)


def scale_kernel(early, far, lengths_ref, weight_ref, gain_ref, *rest):
    scaled_out, early_out, square_out, far_weight, cos_out, sin_out = rest[-9:-3]
    lengths, length_sem, far_sems = rest[-3:]
    parts = rest[:-9]
    steps, rows, width = parts[0].shape
    length_copy = pltpu.make_async_copy(lengths_ref, lengths, length_sem)
    length_copy.start()
    copies = copy_blocks(far, width, weight_ref, far_weight, far_sems)
    me = lax.axis_index("tp")
    scaled_out[...] = jnp.zeros_like(scaled_out)
    total = None
    for k, (offset, part) in enumerate(zip(early, parts)):
        block = me ^ offset
        scaled, squares = scaled_block(part, gain_ref, block)
        total = squares if total is None else total + squares
        scaled_out[:, pl.ds(pl.multiple_of(block * width, width), width)] = scaled
        early_out[:, k * width : (k + 1) * width] = scaled
    square_out[...] = total
    length_copy.wait()
    rotation_tables(lengths, steps, rows, cos_out, sin_out)
    for copy in copies:
        copy.wait()


def scale_call(early, blocks, far, lengths, weight, gain, parts):
    steps, rows, width = parts[0].shape
    count = steps * rows
    return pl.pallas_call(
        functools.partial(scale_kernel, early, far),
        out_shape=(
            pltpu.VMEM((count, blocks * width), jnp.bfloat16),
            pltpu.VMEM((count, len(early) * width), jnp.bfloat16),
            pltpu.VMEM((count, HD), jnp.float32),
            pltpu.VMEM((len(far) * width,) + weight.shape[1:], weight.dtype),
            pltpu.VMEM((count, HD), jnp.float32),
            pltpu.VMEM((count, HD), jnp.float32),
        ),
        in_specs=[HBM] * 2 + [VMEM] * (1 + len(parts)),
        out_specs=(VMEM,) * 6,
        scratch_shapes=[
            pltpu.SMEM(lengths.shape, jnp.int32),
            pltpu.SemaphoreType.DMA,
            pltpu.SemaphoreType.DMA((len(far),)),
        ],
        compiler_params=pltpu.CompilerParams(vmem_limit_bytes=8 << 20),
        cost_estimate=pl.CostEstimate(flops=0, bytes_accessed=9 << 20, transcendentals=0),
        name="scale_features",
    )(*[pltpu.with_memory_space_constraint(x, pltpu.HBM) for x in (lengths, weight)], gain, *parts)


def inner_kernel(late, scaled_ref, early_ref, square_ref, gain_ref, *rest):
    parts, rest = rest[: len(late)], rest[len(late) :]
    outs, square_out = rest[-1 - len(late) : -1], rest[-1]
    packs, inner_out = (rest[: -2 - len(late)], rest[-2 - len(late)]) if len(rest) > 1 + len(late) else ((), None)
    squares = square_ref[...]
    blocks = []
    for k, (offset, part) in enumerate(zip(late, parts)):
        block = lax.axis_index("tp") ^ offset
        scaled, more = scaled_block(part, gain_ref, block)
        squares += more
        blocks.append((block, scaled))
        width = scaled.shape[1]
        outs[k][:, :width] = early_ref[:, k * width : (k + 1) * width]
        outs[k][:, width:] = scaled
    squares = jnp.sum(squares, axis=1, keepdims=True)
    square_out[...] = jnp.broadcast_to(squares, square_out.shape)
    if not packs:
        return
    me = lax.axis_index("wide")
    total = []
    for offset, pack in enumerate(packs):
        mine = me ^ offset
        rows = scaled_ref[:, pl.ds(pl.multiple_of(mine * width, width), width)]
        for block, scaled in blocks:
            rows = jnp.where(mine == block, scaled, rows)
        total.append(
            lax.dot_general(
                rows,
                pack[:, :, :width].reshape(inner_out.shape[1], width),
                (((1,), (1,)), ((), ())),
                preferred_element_type=jnp.float32,
            )
        )
    inner_out[...] = sum(total[1:], total[0])


def inner_call(late, scaled, early, square, gain, parts, packs):
    count, width = scaled.shape[0], parts[0].shape[2]
    shapes = [pltpu.VMEM((count, 2 * width), scaled.dtype) for _ in late]
    shapes.append(pltpu.VMEM(square.shape, jnp.float32))
    if packs:
        kinds, share, _ = packs[0].shape
        shapes = [pltpu.VMEM((count, kinds * share), jnp.float32)] + shapes
    return pl.pallas_call(
        functools.partial(inner_kernel, late),
        out_shape=tuple(shapes),
        in_specs=[VMEM] * (4 + len(parts) + len(packs)),
        out_specs=(VMEM,) * len(shapes),
        compiler_params=pltpu.CompilerParams(vmem_limit_bytes=8 << 20),
        name="rank_inner",
    )(scaled, early, square, gain, *parts, *packs)


def up_kernel(*refs):
    packs, up_out = refs[:-1], refs[-1]
    kinds, share, pack_width = packs[0].shape
    columns = up_out.shape[1] // kinds
    me = lax.axis_index("wide") if len(packs) > 1 else 0
    up_out[...] = jnp.zeros_like(up_out)
    for offset, pack in enumerate(packs):
        for kind in range(kinds):
            at = pl.multiple_of(((me ^ offset) * kinds + kind) * share, share)
            up_out[pl.ds(at, share), kind * columns : (kind + 1) * columns] = pack[
                kind, :, pack_width - columns :
            ]


def up_call(packs, columns):
    kinds, share, _ = packs[0].shape
    return pl.pallas_call(
        up_kernel,
        out_shape=pltpu.VMEM((len(packs) * kinds * share, kinds * columns), packs[0].dtype),
        in_specs=[VMEM] * len(packs),
        out_specs=VMEM,
        compiler_params=pltpu.CompilerParams(vmem_limit_bytes=8 << 20),
        name="lay_out_up",
    )(*packs)


def split_index(index, count):
    if count & (count - 1) == 0:
        return index >> (count.bit_length() - 1), index & (count - 1)
    return index // count, index % count


def final_kernel(width, blocks, near_ref, far_ref, square_ref, bias_ref, *rest):
    query_ref, acc_ref, top_ref, total_ref, cos_ref, sin_ref = rest[:6]
    inner_refs = rest[6 : 6 + blocks]
    up_ref, keys_out, values_out, attended_out, inner_buffer = rest[6 + blocks :]
    steps, rows, columns = keys_out.shape
    count = steps * rows
    groups, size, _ = query_ref.shape
    per_group = size // count
    kinds = bias_ref.shape[0]
    row_scale = lax.rsqrt(square_ref[...] * (1.0 / width) + norm_eps)
    row_scale = jnp.concatenate([row_scale] * groups, axis=1)
    me = lax.axis_index("tp") if blocks > 1 else 0
    for i in range(blocks):
        inner_buffer[me ^ i] = inner_refs[i][...]
    inner = jnp.concatenate([inner_buffer[i] for i in range(blocks)], axis=1)
    high = inner.astype(jnp.bfloat16)
    low = (inner - high.astype(jnp.float32)).astype(jnp.bfloat16)
    lora = jnp.dot(
        jnp.concatenate([high, low], axis=0), up_ref[...], preferred_element_type=jnp.float32
    )
    lora = lora[:count] + lora[count:]
    bias = bias_ref[...].astype(jnp.float32)
    linear = []
    for kind in range(kinds):
        base = near_ref[kind] + far_ref[kind]
        part = lora[:, kind * columns : (kind + 1) * columns]
        linear.append((base + adapter_scale * part) * row_scale + bias[kind : kind + 1])
    cosine, sine = cos_ref[...], sin_ref[...]
    line = lax.broadcasted_iota(jnp.int32, (size, count), 0)
    other = lax.broadcasted_iota(jnp.int32, (size, count), 1)
    line_step, line_row = split_index(line, rows)
    other_step, other_row = split_index(other, rows)
    line_step = split_index(line_step, steps)[1]
    live = (line_row == other_row) & (other_step <= line_step)
    for group in range(groups):
        at = slice(group * HD, (group + 1) * HD)
        key = linear[0][:, at]
        key = (key * cosine + pltpu.roll(key, HD // 2, 1) * sine).astype(jnp.bfloat16)
        value = linear[1][:, at].astype(jnp.bfloat16)
        for step in range(steps):
            keys_out[step, :, at] = key[step * rows : (step + 1) * rows]
            values_out[step, :, at] = value[step * rows : (step + 1) * rows]
        scores = lax.dot_general(
            query_ref[group].astype(jnp.bfloat16),
            key,
            (((1,), (1,)), ((), ())),
            preferred_element_type=jnp.float32,
        )
        scores = jnp.where(live, scores * score_scale, masked_score)
        old_top = top_ref[group]
        top = jnp.maximum(old_top, jnp.max(scores, axis=1, keepdims=True))
        exps = jnp.exp(scores - top[:, :count])
        keep = jnp.exp(old_top - top)
        total = total_ref[group] * keep + jnp.sum(exps, axis=1, keepdims=True)
        acc = acc_ref[group] * keep + jnp.dot(
            exps.astype(jnp.bfloat16), value, preferred_element_type=jnp.float32
        )
        attended = (acc * (1.0 / total)).astype(jnp.bfloat16)
        for head in range(per_group):
            lanes = pl.ds((group * per_group + head) * HD, HD)
            for step in range(steps):
                tile = (head * steps + step) * rows
                attended_out[step, :, lanes] = attended[tile : tile + rows]


def final_call(shape, width, near, far, square, bias, cached, inner, up):
    steps, rows, query_width = shape
    columns = near.shape[2]
    small = jax.ShapeDtypeStruct((steps, rows, columns), jnp.bfloat16)
    return pl.pallas_call(
        functools.partial(final_kernel, width, len(inner)),
        out_shape=(small, small, jax.ShapeDtypeStruct(shape, jnp.bfloat16)),
        in_specs=[VMEM] * (5 + len(cached) + len(inner)),
        out_specs=(VMEM,) * 3,
        scratch_shapes=[pltpu.VMEM((len(inner),) + inner[0].shape, jnp.float32)],
        compiler_params=pltpu.CompilerParams(vmem_limit_bytes=8 << 20),
        name="fresh_attention",
    )(near, far, square, bias, *cached, *inner, up)


def dot(rows, weight):
    return jnp.einsum("md,dkc->kmc", rows, weight, preferred_element_type=jnp.float32)


def swap(block, axis, offset, count):
    return lax.ppermute(block, axis, [(i, i ^ offset) for i in range(count)])


def on_device(
    wide_count,
    tp_count,
    hidden,
    input_norm_gain,
    key_value_weight,
    key_value_bias,
    adapter_down_factor,
    adapter_up_factor,
    queries,
    stored_rotated_keys,
    stored_value_rows,
    lengths,
):
    steps, rows, part_width = hidden.shape
    width = part_width * tp_count
    kinds, ranks, down_width = adapter_down_factor.shape
    gain = input_norm_gain.reshape(width // HD, HD)
    up_part = jnp.transpose(adapter_up_factor, (0, 2, 1))
    direct = wide_count == tp_count == 4
    beside, crossed = [swap(hidden, "tp", offset, tp_count) for offset in (1, 2)]
    if direct:
        pack = pack_call(adapter_down_factor, up_part)
        second = swap(pack, "wide", 2, wide_count)
        first = swap(pack, "wide", 1, wide_count)
    near, far = (0, 1), (2, 3)
    early, late = (0, 2), (1, 3)
    near_weight, gain_rows, bias, mine, *cached = cache_call(
        near,
        lengths,
        queries,
        stored_rotated_keys,
        stored_value_rows,
        gain,
        key_value_bias,
        hidden,
        key_value_weight,
    )
    relayed, gain_rows = lax.optimization_barrier((crossed, gain_rows))
    relayed = swap(relayed, "tp", 1, tp_count)
    if direct:
        third, gain_rows = lax.optimization_barrier((second, gain_rows))
        packs = [pack, first, second, swap(third, "wide", 1, wide_count)]
    scaled, early_scaled, square, far_weight, *tables = scale_call(
        early, tp_count, far, lengths, key_value_weight, gain_rows, (mine, crossed)
    )
    late_parts = (beside, relayed)
    if direct:
        inner, near_scaled, far_scaled, square = inner_call(
            late, scaled, early_scaled, square, gain_rows, late_parts, packs
        )
        inner, far_scaled, near_scaled, packs = lax.optimization_barrier(
            (inner, far_scaled, near_scaled, packs)
        )
        inner = [inner] + [swap(inner, "tp", offset, tp_count) for offset in (1, 2, 3)]
    else:
        near_scaled, far_scaled, square = inner_call(
            late, scaled, early_scaled, square, gain_rows, late_parts, []
        )
        down = lax.all_gather(adapter_down_factor, "wide", axis=2, tiled=True)
        rows_full = lax.all_gather(hidden, "tp", axis=2, tiled=True).astype(jnp.float32)
        rows_full = (rows_full * input_norm_gain.astype(jnp.float32)).astype(jnp.bfloat16)
        inner = jnp.einsum("srd,kad->srka", rows_full, down, preferred_element_type=jnp.float32)
        inner = [inner.reshape(steps * rows, kinds * ranks)]
        packs = [lax.all_gather(up_part, "wide", axis=1, tiled=True)]
    near_base = dot(near_scaled, near_weight)
    far_base = dot(far_scaled, far_weight)
    up = up_call(packs, bias.shape[1])
    return final_call(
        queries.shape, width, near_base, far_base, square, bias, cached + tables, inner, up
    )


def solution(mesh):
    in_specs = (
        P(None, ("groups", "wide"), "tp"),
        P(),
        P(None, None, "tp"),
        P(None, "tp"),
        P("groups", None, "wide"),
        P("groups", "tp", "wide"),
        P(None, ("groups", "wide"), "tp"),
        P(("groups", "wide"), None, "tp"),
        P(("groups", "wide"), None, "tp"),
        P(("groups", "wide")),
    )
    out_specs = (
        P(None, ("groups", "wide"), "tp"),
        P(None, ("groups", "wide"), "tp"),
        P(None, ("groups", "wide"), "tp"),
    )
    body = functools.partial(on_device, mesh.shape["wide"], mesh.shape["tp"])
    return jax.shard_map(
        body, mesh=mesh, in_specs=in_specs, out_specs=out_specs, check_vma=False
    )
```

```python
import functools
import math

import jax
import jax.numpy as jnp
from jax import lax
from jax.experimental import pallas as pl
from jax.experimental.pallas import tpu as pltpu
from jax.sharding import PartitionSpec as P

HD = 128


norm_eps = 1e-06
adapter_scale = 2.0
rope_base = 1000000.0
masked_score = -1e30
score_scale = 1.0 / math.sqrt(HD)

VMEM = pl.BlockSpec(memory_space=pltpu.VMEM)
HBM = pl.BlockSpec(memory_space=pltpu.HBM)


def query_block(query_ref, group, per_group):
    steps = query_ref.shape[0]
    tiles = []
    for head in range(per_group):
        at = (group * per_group + head) * HD
        for step in range(steps):
            tiles.append(query_ref[step, :, at : at + HD].astype(jnp.float32))
    return jnp.concatenate(tiles, axis=0)


def copy_blocks(offsets, width, weight_ref, out_ref, sems):
    me = lax.axis_index("tp")
    copies = []
    for i, offset in enumerate(offsets):
        block = pl.ds(pl.multiple_of((me ^ offset) * width, width), width)
        copies.append(
            pltpu.make_async_copy(
                weight_ref.at[block], out_ref.at[pl.ds(i * width, width)], sems.at[i]
            )
        )
        copies[-1].start()
    return copies


def cache_kernel(
    near,
    lengths_ref,
    query_ref,
    key_ref,
    value_ref,
    gain_ref,
    bias_ref,
    hidden_ref,
    weight_ref,
    near_out,
    gain_out,
    bias_out,
    hidden_out,
    query_out,
    acc_out,
    top_out,
    total_out,
    lengths,
    queries,
    gain_buffer,
    key_buffer,
    value_buffer,
    score_buffer,
    sems,
    weight_sems,
):
    steps, rows, query_width = query_ref.shape
    cache_span = key_ref.shape[1]
    groups = key_ref.shape[2] // HD
    per_group = query_width // HD // groups
    lines = steps * per_group
    half_rows = rows // 2
    halves = [pl.ds(0, half_rows), pl.ds(half_rows, half_rows)]
    copies = [
        (lengths_ref, lengths),
        (query_ref, queries),
        (key_ref.at[halves[0]], key_buffer.at[halves[0]]),
        (key_ref.at[halves[1]], key_buffer.at[halves[1]]),
        (value_ref.at[halves[0]], value_buffer.at[halves[0]]),
        (value_ref.at[halves[1]], value_buffer.at[halves[1]]),
        (gain_ref, gain_buffer),
        (bias_ref, bias_out),
        (hidden_ref, hidden_out),
    ]
    copies = [pltpu.make_async_copy(*pair, sems.at[i]) for i, pair in enumerate(copies)]
    for copy in copies:
        copy.start()
    copies += copy_blocks(near, hidden_ref.shape[2], weight_ref, near_out, weight_sems)

    copies[0].wait()
    copies[1].wait()
    for group in range(groups):
        query_out[group] = query_block(queries, group, per_group)

    place = lax.broadcasted_iota(jnp.int32, (lines, cache_span), 1)
    for i in range(2):
        copies[2 + i].wait()
        for row in range(i * half_rows, (i + 1) * half_rows):
            for group in range(groups):
                query = query_out[group, pl.ds(row, lines, stride=rows), :].astype(jnp.bfloat16)
                score_buffer[row * groups + group] = lax.dot_general(
                    query,
                    key_buffer[row, :, pl.ds(group * HD, HD)],
                    (((1,), (1,)), ((), ())),
                    preferred_element_type=jnp.float32,
                )
    for i in range(2):
        copies[4 + i].wait()
        for row in range(i * half_rows, (i + 1) * half_rows):
            live = place < lengths[row]
            for group in range(groups):
                mine = pl.ds(row, lines, stride=rows)
                scores = score_buffer[row * groups + group]
                scores = jnp.where(live, scores * score_scale, masked_score)
                top = jnp.max(scores, axis=1, keepdims=True)
                exps = jnp.exp(scores - top)
                total = jnp.sum(exps, axis=1, keepdims=True)
                acc = jnp.dot(
                    exps.astype(jnp.bfloat16),
                    value_buffer[row, :, pl.ds(group * HD, HD)],
                    preferred_element_type=jnp.float32,
                )
                acc_out[group, mine, :] = acc
                top_out[group, mine, :] = jnp.broadcast_to(top, acc.shape)
                total_out[group, mine, :] = jnp.broadcast_to(total, acc.shape)
    copies[6].wait()
    gain_out[...] = gain_buffer[...].astype(jnp.float32)
    for copy in copies[7:]:
        copy.wait()


def cache_call(near, lengths, queries, keys, values, gain, bias, hidden, weight):
    steps, rows, query_width = queries.shape
    cache_span, key_width = keys.shape[1:]
    groups = key_width // HD
    lines = steps * (query_width // key_width)
    block = (groups, lines * rows, HD)
    operands = (lengths, queries, keys, values, gain, bias, hidden, weight)
    near_weight = (len(near) * hidden.shape[2],) + weight.shape[1:]
    return pl.pallas_call(
        functools.partial(cache_kernel, near),
        out_shape=(
            pltpu.VMEM(near_weight, weight.dtype),
            pltpu.VMEM(gain.shape, jnp.float32),
            pltpu.VMEM(bias.shape, bias.dtype),
            pltpu.VMEM(hidden.shape, hidden.dtype),
            pltpu.VMEM(block, jnp.float32),
            pltpu.VMEM(block, jnp.float32),
            pltpu.VMEM(block, jnp.float32),
            pltpu.VMEM(block, jnp.float32),
        ),
        in_specs=[HBM] * len(operands),
        out_specs=(VMEM,) * 8,
        scratch_shapes=[
            pltpu.SMEM(lengths.shape, jnp.int32),
            pltpu.VMEM(queries.shape, queries.dtype),
            pltpu.VMEM(gain.shape, gain.dtype),
            pltpu.VMEM(keys.shape, keys.dtype),
            pltpu.VMEM(values.shape, values.dtype),
            pltpu.VMEM((rows * groups, lines, cache_span), jnp.float32),
            pltpu.SemaphoreType.DMA((9,)),
            pltpu.SemaphoreType.DMA((len(near),)),
        ],
        compiler_params=pltpu.CompilerParams(vmem_limit_bytes=16 << 20),
        cost_estimate=pl.CostEstimate(flops=2 * 67 << 20, bytes_accessed=5 << 20, transcendentals=0),
        name="cache_attention",
    )(*[pltpu.with_memory_space_constraint(x, pltpu.HBM) for x in operands])


def rows_of(ref):
    return jnp.concatenate([ref[s].astype(jnp.float32) for s in range(ref.shape[0])], axis=0)


def pack_kernel(down_ref, up_ref, out_ref, sems):
    share = out_ref.shape[1]
    width = down_ref.shape[2]
    at = pl.ds(pl.multiple_of(lax.axis_index("tp") * share, share), share)
    copies = [(up_ref, out_ref.at[:, :, pl.ds(width, up_ref.shape[2])])]
    half = width // 2
    for kind in range(down_ref.shape[0]):
        for first in (0, half):
            lanes = pl.ds(first, half)
            copies.append((down_ref.at[kind, at, lanes], out_ref.at[kind, :, lanes]))
    copies = [pltpu.make_async_copy(*pair, sems.at[i]) for i, pair in enumerate(copies)]
    for copy in copies:
        copy.start()
    for copy in copies:
        copy.wait()


def pack_call(down, up):
    kinds, share, columns = up.shape
    return pl.pallas_call(
        pack_kernel,
        out_shape=pltpu.VMEM((kinds, share, down.shape[2] + columns), down.dtype),
        in_specs=[HBM] * 2,
        out_specs=VMEM,
        scratch_shapes=[pltpu.SemaphoreType.DMA((1 + 2 * kinds,))],
        name="pack_factors",
    )(*[pltpu.with_memory_space_constraint(x, pltpu.HBM) for x in (down, up)])


def scaled_block(part, gain_ref, block):
    steps, rows, width = part.shape
    chunks = width // HD
    gain = gain_ref[pl.ds(pl.multiple_of(block * chunks, chunks), chunks)]
    values = rows_of(part)
    squares = jnp.zeros((steps * rows, HD), jnp.float32)
    scaled = []
    for i in range(chunks):
        chunk = values[:, i * HD : (i + 1) * HD]
        squares += chunk * chunk
        scaled.append((chunk * gain[i : i + 1]).astype(jnp.bfloat16))
    return jnp.concatenate(scaled, axis=1), squares


def rotation_tables(lengths, steps, rows, cos_out, sin_out):
    lane = lax.broadcasted_iota(jnp.int32, (rows, HD), 1)
    half = HD // 2
    second = lane >= half
    index = jnp.where(second, lane - half, lane).astype(jnp.float32)
    inv_freq = jnp.exp(index * (-2.0 * math.log(rope_base) / HD))
    row_index = lax.broadcasted_iota(jnp.int32, (rows, HD), 0)
    row_lengths = jnp.zeros((rows, HD), jnp.int32)
    for row in range(rows):
        row_lengths = jnp.where(row_index == row, lengths[row], row_lengths)
    for step in range(steps):
        angles = (row_lengths + step).astype(jnp.float32) * inv_freq
        sine = jnp.sin(angles)
        cos_out[pl.ds(step * rows, rows)] = jnp.cos(angles)
        sin_out[pl.ds(step * rows, rows)] = jnp.where(second, sine, -sine)


def scale_kernel(early, far, lengths_ref, weight_ref, gain_ref, query_ref, *rest):
    scaled_out, early_out, square_out, far_weight, query_out, cos_out, sin_out = rest[-10:-3]
    lengths, length_sem, far_sems = rest[-3:]
    parts = rest[:-10]
    steps, rows, width = parts[0].shape
    length_copy = pltpu.make_async_copy(lengths_ref, lengths, length_sem)
    length_copy.start()
    copies = copy_blocks(far, width, weight_ref, far_weight, far_sems)
    me = lax.axis_index("tp")
    scaled_out[...] = jnp.zeros_like(scaled_out)
    total = None
    for k, (offset, part) in enumerate(zip(early, parts)):
        block = me ^ offset
        scaled, squares = scaled_block(part, gain_ref, block)
        total = squares if total is None else total + squares
        scaled_out[:, pl.ds(pl.multiple_of(block * width, width), width)] = scaled
        early_out[:, k * width : (k + 1) * width] = scaled
    square_out[...] = total
    query_out[...] = query_ref[...].astype(query_out.dtype)
    length_copy.wait()
    rotation_tables(lengths, steps, rows, cos_out, sin_out)
    for copy in copies:
        copy.wait()


def scale_call(early, blocks, far, lengths, weight, gain, queries, parts):
    steps, rows, width = parts[0].shape
    count = steps * rows
    return pl.pallas_call(
        functools.partial(scale_kernel, early, far),
        out_shape=(
            pltpu.VMEM((count, blocks * width), jnp.bfloat16),
            pltpu.VMEM((count, len(early) * width), jnp.bfloat16),
            pltpu.VMEM((count, HD), jnp.float32),
            pltpu.VMEM((len(far) * width,) + weight.shape[1:], weight.dtype),
            pltpu.VMEM(queries.shape, jnp.bfloat16),
            pltpu.VMEM((count, HD), jnp.float32),
            pltpu.VMEM((count, HD), jnp.float32),
        ),
        in_specs=[HBM] * 2 + [VMEM] * (2 + len(parts)),
        out_specs=(VMEM,) * 7,
        scratch_shapes=[
            pltpu.SMEM(lengths.shape, jnp.int32),
            pltpu.SemaphoreType.DMA,
            pltpu.SemaphoreType.DMA((len(far),)),
        ],
        compiler_params=pltpu.CompilerParams(vmem_limit_bytes=8 << 20),
        cost_estimate=pl.CostEstimate(flops=0, bytes_accessed=9 << 20, transcendentals=0),
        name="scale_features",
    )(*[pltpu.with_memory_space_constraint(x, pltpu.HBM) for x in (lengths, weight)], gain, queries, *parts)


def inner_kernel(late, scaled_ref, early_ref, square_ref, gain_ref, *rest):
    parts, rest = rest[: len(late)], rest[len(late) :]
    outs, square_out = rest[-1 - len(late) : -1], rest[-1]
    packs, inner_out = (rest[: -2 - len(late)], rest[-2 - len(late)]) if len(rest) > 1 + len(late) else ((), None)
    squares = square_ref[...]
    blocks = []
    for k, (offset, part) in enumerate(zip(late, parts)):
        block = lax.axis_index("tp") ^ offset
        scaled, more = scaled_block(part, gain_ref, block)
        squares += more
        blocks.append((block, scaled))
        width = scaled.shape[1]
        outs[k][:, :width] = early_ref[:, k * width : (k + 1) * width]
        outs[k][:, width:] = scaled
    squares = jnp.sum(squares, axis=1, keepdims=True)
    square_out[...] = jnp.broadcast_to(squares, square_out.shape)
    if not packs:
        return
    me = lax.axis_index("wide")
    total = []
    for offset, pack in enumerate(packs):
        mine = me ^ offset
        rows = scaled_ref[:, pl.ds(pl.multiple_of(mine * width, width), width)]
        for block, scaled in blocks:
            rows = jnp.where(mine == block, scaled, rows)
        total.append(
            lax.dot_general(
                rows,
                pack[:, :, :width].reshape(inner_out.shape[1], width),
                (((1,), (1,)), ((), ())),
                preferred_element_type=jnp.float32,
            )
        )
    inner_out[...] = sum(total[1:], total[0])


def inner_call(late, scaled, early, square, gain, parts, packs):
    count, width = scaled.shape[0], parts[0].shape[2]
    shapes = [pltpu.VMEM((count, 2 * width), scaled.dtype) for _ in late]
    shapes.append(pltpu.VMEM(square.shape, jnp.float32))
    if packs:
        kinds, share, _ = packs[0].shape
        shapes = [pltpu.VMEM((count, kinds * share), jnp.float32)] + shapes
    return pl.pallas_call(
        functools.partial(inner_kernel, late),
        out_shape=tuple(shapes),
        in_specs=[VMEM] * (4 + len(parts) + len(packs)),
        out_specs=(VMEM,) * len(shapes),
        compiler_params=pltpu.CompilerParams(vmem_limit_bytes=8 << 20),
        name="rank_inner",
    )(scaled, early, square, gain, *parts, *packs)


def up_kernel(*refs):
    packs, up_out = refs[:-1], refs[-1]
    kinds, share, pack_width = packs[0].shape
    columns = up_out.shape[1] // kinds
    me = lax.axis_index("wide") if len(packs) > 1 else 0
    up_out[...] = jnp.zeros_like(up_out)
    for offset, pack in enumerate(packs):
        for kind in range(kinds):
            at = pl.multiple_of(((me ^ offset) * kinds + kind) * share, share)
            up_out[pl.ds(at, share), kind * columns : (kind + 1) * columns] = pack[
                kind, :, pack_width - columns :
            ]


def up_call(packs, columns):
    kinds, share, _ = packs[0].shape
    return pl.pallas_call(
        up_kernel,
        out_shape=pltpu.VMEM((len(packs) * kinds * share, kinds * columns), packs[0].dtype),
        in_specs=[VMEM] * len(packs),
        out_specs=VMEM,
        compiler_params=pltpu.CompilerParams(vmem_limit_bytes=8 << 20),
        name="lay_out_up",
    )(*packs)


def split_index(index, count):
    if count & (count - 1) == 0:
        return index >> (count.bit_length() - 1), index & (count - 1)
    return index // count, index % count


def final_kernel(width, blocks, near_ref, far_ref, square_ref, bias_ref, *rest):
    query_ref, acc_ref, top_ref, total_ref, cos_ref, sin_ref = rest[:6]
    inner_refs = rest[6 : 6 + blocks]
    up_ref, keys_out, values_out, attended_out = rest[6 + blocks :]
    steps, rows, columns = keys_out.shape
    count = steps * rows
    groups, size, _ = query_ref.shape
    per_group = size // count
    kinds = bias_ref.shape[0]
    row_scale = lax.rsqrt(square_ref[...] * (1.0 / width) + norm_eps)
    row_scale = jnp.concatenate([row_scale] * groups, axis=1)
    me = lax.axis_index("tp") if blocks > 1 else 0
    share = inner_refs[0].shape[1]
    products = []
    for i in range(blocks):
        inner = inner_refs[i][...]
        high = inner.astype(jnp.bfloat16)
        low = (inner - high.astype(jnp.float32)).astype(jnp.bfloat16)
        at = pl.multiple_of((me ^ i) * share, share)
        products.append(
            jnp.dot(
                jnp.concatenate([high, low], axis=0),
                up_ref[pl.ds(at, share), :],
                preferred_element_type=jnp.float32,
            )
        )
    lora = sum(products[1:], products[0])
    lora = lora[:count] + lora[count:]
    bias = bias_ref[...].astype(jnp.float32)
    linear = []
    for kind in range(kinds):
        base = near_ref[kind] + far_ref[kind]
        part = lora[:, kind * columns : (kind + 1) * columns]
        linear.append((base + adapter_scale * part) * row_scale + bias[kind : kind + 1])
    cosine, sine = cos_ref[...], sin_ref[...]
    line = lax.broadcasted_iota(jnp.int32, (size, count), 0)
    other = lax.broadcasted_iota(jnp.int32, (size, count), 1)
    line_step, line_row = split_index(line, rows)
    other_step, other_row = split_index(other, rows)
    line_step = split_index(line_step, steps)[1]
    live = (line_row == other_row) & (other_step <= line_step)
    for group in range(groups):
        at = slice(group * HD, (group + 1) * HD)
        key = linear[0][:, at]
        key = (key * cosine + pltpu.roll(key, HD // 2, 1) * sine).astype(jnp.bfloat16)
        value = linear[1][:, at].astype(jnp.bfloat16)
        for step in range(steps):
            keys_out[step, :, at] = key[step * rows : (step + 1) * rows]
            values_out[step, :, at] = value[step * rows : (step + 1) * rows]
        scores = lax.dot_general(
            query_ref[group],
            key,
            (((1,), (1,)), ((), ())),
            preferred_element_type=jnp.float32,
        )
        scores = jnp.where(live, scores * score_scale, masked_score)
        old_top = top_ref[group]
        top = jnp.maximum(old_top, jnp.max(scores, axis=1, keepdims=True))
        exps = jnp.exp(scores - top[:, :count])
        keep = jnp.exp(old_top - top)
        total = total_ref[group] * keep + jnp.sum(exps, axis=1, keepdims=True)
        acc = acc_ref[group] * keep + jnp.dot(
            exps.astype(jnp.bfloat16), value, preferred_element_type=jnp.float32
        )
        attended = (acc * (1.0 / total)).astype(jnp.bfloat16)
        for head in range(per_group):
            lanes = pl.ds((group * per_group + head) * HD, HD)
            for step in range(steps):
                tile = (head * steps + step) * rows
                attended_out[step, :, lanes] = attended[tile : tile + rows]


def final_call(shape, width, near, far, square, bias, cached, inner, up):
    steps, rows, query_width = shape
    columns = near.shape[2]
    small = jax.ShapeDtypeStruct((steps, rows, columns), jnp.bfloat16)
    return pl.pallas_call(
        functools.partial(final_kernel, width, len(inner)),
        out_shape=(small, small, jax.ShapeDtypeStruct(shape, jnp.bfloat16)),
        in_specs=[VMEM] * (5 + len(cached) + len(inner)),
        out_specs=(VMEM,) * 3,
        compiler_params=pltpu.CompilerParams(vmem_limit_bytes=8 << 20),
        name="fresh_attention",
    )(near, far, square, bias, *cached, *inner, up)


def dot(rows, weight):
    return jnp.einsum("md,dkc->kmc", rows, weight, preferred_element_type=jnp.float32)


def swap(block, axis, offset, count):
    return lax.ppermute(block, axis, [(i, i ^ offset) for i in range(count)])


def on_device(
    wide_count,
    tp_count,
    hidden,
    input_norm_gain,
    key_value_weight,
    key_value_bias,
    adapter_down_factor,
    adapter_up_factor,
    queries,
    stored_rotated_keys,
    stored_value_rows,
    lengths,
):
    steps, rows, part_width = hidden.shape
    width = part_width * tp_count
    kinds, ranks, down_width = adapter_down_factor.shape
    gain = input_norm_gain.reshape(width // HD, HD)
    up_part = jnp.transpose(adapter_up_factor, (0, 2, 1))
    direct = wide_count == tp_count == 4
    beside, crossed = [swap(hidden, "tp", offset, tp_count) for offset in (1, 2)]
    if direct:
        pack = pack_call(adapter_down_factor, up_part)
        second = swap(pack, "wide", 2, wide_count)
        first = swap(pack, "wide", 1, wide_count)
    near, far = (0, 1), (2, 3)
    early, late = (0, 2), (1, 3)
    near_weight, gain_rows, bias, mine, query_rows, *cached = cache_call(
        near,
        lengths,
        queries,
        stored_rotated_keys,
        stored_value_rows,
        gain,
        key_value_bias,
        hidden,
        key_value_weight,
    )
    relayed, gain_rows = lax.optimization_barrier((crossed, gain_rows))
    relayed = swap(relayed, "tp", 1, tp_count)
    if direct:
        third, gain_rows = lax.optimization_barrier((second, gain_rows))
        packs = [pack, first, second, swap(third, "wide", 1, wide_count)]
    scaled, early_scaled, square, far_weight, query_rows, *tables = scale_call(
        early, tp_count, far, lengths, key_value_weight, gain_rows, query_rows, (mine, crossed)
    )
    late_parts = (beside, relayed)
    if direct:
        inner, near_scaled, far_scaled, square = inner_call(
            late, scaled, early_scaled, square, gain_rows, late_parts, packs
        )
        inner, far_scaled, near_scaled, packs = lax.optimization_barrier(
            (inner, far_scaled, near_scaled, packs)
        )
        inner = [inner] + [swap(inner, "tp", offset, tp_count) for offset in (1, 2, 3)]
    else:
        near_scaled, far_scaled, square = inner_call(
            late, scaled, early_scaled, square, gain_rows, late_parts, []
        )
        down = lax.all_gather(adapter_down_factor, "wide", axis=2, tiled=True)
        rows_full = lax.all_gather(hidden, "tp", axis=2, tiled=True).astype(jnp.float32)
        rows_full = (rows_full * input_norm_gain.astype(jnp.float32)).astype(jnp.bfloat16)
        inner = jnp.einsum("srd,kad->srka", rows_full, down, preferred_element_type=jnp.float32)
        inner = [inner.reshape(steps * rows, kinds * ranks)]
        packs = [lax.all_gather(up_part, "wide", axis=1, tiled=True)]
    near_base = dot(near_scaled, near_weight)
    far_base = dot(far_scaled, far_weight)
    up = up_call(packs, bias.shape[1])
    return final_call(
        queries.shape, width, near_base, far_base, square, bias, [query_rows] + cached + tables, inner, up
    )


def solution(mesh):
    in_specs = (
        P(None, ("groups", "wide"), "tp"),
        P(),
        P(None, None, "tp"),
        P(None, "tp"),
        P("groups", None, "wide"),
        P("groups", "tp", "wide"),
        P(None, ("groups", "wide"), "tp"),
        P(("groups", "wide"), None, "tp"),
        P(("groups", "wide"), None, "tp"),
        P(("groups", "wide")),
    )
    out_specs = (
        P(None, ("groups", "wide"), "tp"),
        P(None, ("groups", "wide"), "tp"),
        P(None, ("groups", "wide"), "tp"),
    )
    body = functools.partial(on_device, mesh.shape["wide"], mesh.shape["tp"])
    return jax.shard_map(
        body, mesh=mesh, in_specs=in_specs, out_specs=out_specs, check_vma=False
    )
```

```python
import functools
import math

import jax
import jax.numpy as jnp
from jax import lax
from jax.experimental import pallas as pl
from jax.experimental.pallas import tpu as pltpu
from jax.sharding import PartitionSpec as P

HD = 128


norm_eps = 1e-06
adapter_scale = 2.0
rope_base = 1000000.0
masked_score = -1e30
score_scale = 1.0 / math.sqrt(HD)

VMEM = pl.BlockSpec(memory_space=pltpu.VMEM)
HBM = pl.BlockSpec(memory_space=pltpu.HBM)


def query_block(query_ref, group, per_group):
    steps = query_ref.shape[0]
    tiles = []
    for head in range(per_group):
        at = (group * per_group + head) * HD
        for step in range(steps):
            tiles.append(query_ref[step, :, at : at + HD].astype(jnp.float32))
    return jnp.concatenate(tiles, axis=0)


def copy_blocks(offsets, width, weight_ref, out_ref, sems):
    me = lax.axis_index("tp")
    copies = []
    for i, offset in enumerate(offsets):
        block = pl.ds(pl.multiple_of((me ^ offset) * width, width), width)
        copies.append(
            pltpu.make_async_copy(
                weight_ref.at[block], out_ref.at[pl.ds(i * width, width)], sems.at[i]
            )
        )
        copies[-1].start()
    return copies


def cache_kernel(
    near,
    lengths_ref,
    query_ref,
    key_ref,
    value_ref,
    gain_ref,
    bias_ref,
    hidden_ref,
    weight_ref,
    near_out,
    gain_out,
    bias_out,
    hidden_out,
    query_out,
    acc_out,
    top_out,
    total_out,
    lengths,
    queries,
    gain_buffer,
    key_buffer,
    value_buffer,
    score_buffer,
    sems,
    weight_sems,
):
    steps, rows, query_width = query_ref.shape
    cache_span = key_ref.shape[1]
    groups = key_ref.shape[2] // HD
    per_group = query_width // HD // groups
    lines = steps * per_group
    half_rows = rows // 2
    halves = [pl.ds(0, half_rows), pl.ds(half_rows, half_rows)]
    copies = [
        (lengths_ref, lengths),
        (query_ref, queries),
        (key_ref.at[halves[0]], key_buffer.at[halves[0]]),
        (key_ref.at[halves[1]], key_buffer.at[halves[1]]),
        (value_ref.at[halves[0]], value_buffer.at[halves[0]]),
        (value_ref.at[halves[1]], value_buffer.at[halves[1]]),
        (gain_ref, gain_buffer),
        (bias_ref, bias_out),
        (hidden_ref, hidden_out),
    ]
    copies = [pltpu.make_async_copy(*pair, sems.at[i]) for i, pair in enumerate(copies)]
    for copy in copies:
        copy.start()
    copies += copy_blocks(near, hidden_ref.shape[2], weight_ref, near_out, weight_sems)

    copies[0].wait()
    copies[1].wait()
    for group in range(groups):
        query_out[group] = query_block(queries, group, per_group)

    place = lax.broadcasted_iota(jnp.int32, (lines, cache_span), 1)
    for i in range(2):
        copies[2 + i].wait()
        for row in range(i * half_rows, (i + 1) * half_rows):
            for group in range(groups):
                query = query_out[group, pl.ds(row, lines, stride=rows), :].astype(jnp.bfloat16)
                score_buffer[row * groups + group] = lax.dot_general(
                    query,
                    key_buffer[row, :, pl.ds(group * HD, HD)],
                    (((1,), (1,)), ((), ())),
                    preferred_element_type=jnp.float32,
                )
    for i in range(2):
        copies[4 + i].wait()
        for row in range(i * half_rows, (i + 1) * half_rows):
            live = place < lengths[row]
            for group in range(groups):
                mine = pl.ds(row, lines, stride=rows)
                scores = score_buffer[row * groups + group]
                scores = jnp.where(live, scores * score_scale, masked_score)
                top = jnp.max(scores, axis=1, keepdims=True)
                exps = jnp.exp(scores - top)
                total = jnp.sum(exps, axis=1, keepdims=True)
                acc = jnp.dot(
                    exps.astype(jnp.bfloat16),
                    value_buffer[row, :, pl.ds(group * HD, HD)],
                    preferred_element_type=jnp.float32,
                )
                acc_out[group, mine, :] = acc
                top_out[group, mine, :] = jnp.broadcast_to(top, acc.shape)
                total_out[group, mine, :] = jnp.broadcast_to(total, acc.shape)
    copies[6].wait()
    gain_out[...] = gain_buffer[...].astype(jnp.float32)
    for copy in copies[7:]:
        copy.wait()


def cache_call(near, lengths, queries, keys, values, gain, bias, hidden, weight):
    steps, rows, query_width = queries.shape
    cache_span, key_width = keys.shape[1:]
    groups = key_width // HD
    lines = steps * (query_width // key_width)
    block = (groups, lines * rows, HD)
    operands = (lengths, queries, keys, values, gain, bias, hidden, weight)
    near_weight = (len(near) * hidden.shape[2],) + weight.shape[1:]
    return pl.pallas_call(
        functools.partial(cache_kernel, near),
        out_shape=(
            pltpu.VMEM(near_weight, weight.dtype),
            pltpu.VMEM(gain.shape, jnp.float32),
            pltpu.VMEM(bias.shape, bias.dtype),
            pltpu.VMEM(hidden.shape, hidden.dtype),
            pltpu.VMEM(block, jnp.float32),
            pltpu.VMEM(block, jnp.float32),
            pltpu.VMEM(block, jnp.float32),
            pltpu.VMEM(block, jnp.float32),
        ),
        in_specs=[HBM] * len(operands),
        out_specs=(VMEM,) * 8,
        scratch_shapes=[
            pltpu.SMEM(lengths.shape, jnp.int32),
            pltpu.VMEM(queries.shape, queries.dtype),
            pltpu.VMEM(gain.shape, gain.dtype),
            pltpu.VMEM(keys.shape, keys.dtype),
            pltpu.VMEM(values.shape, values.dtype),
            pltpu.VMEM((rows * groups, lines, cache_span), jnp.float32),
            pltpu.SemaphoreType.DMA((9,)),
            pltpu.SemaphoreType.DMA((len(near),)),
        ],
        compiler_params=pltpu.CompilerParams(vmem_limit_bytes=16 << 20),
        cost_estimate=pl.CostEstimate(flops=2 * 67 << 20, bytes_accessed=5 << 20, transcendentals=0),
        name="cache_attention",
    )(*[pltpu.with_memory_space_constraint(x, pltpu.HBM) for x in operands])


def rows_of(ref):
    return jnp.concatenate([ref[s].astype(jnp.float32) for s in range(ref.shape[0])], axis=0)


def pack_kernel(down_ref, up_ref, out_ref, sems):
    share = out_ref.shape[1]
    width = down_ref.shape[2]
    at = pl.ds(pl.multiple_of(lax.axis_index("tp") * share, share), share)
    copies = [(up_ref, out_ref.at[:, :, pl.ds(width, up_ref.shape[2])])]
    half = width // 2
    for kind in range(down_ref.shape[0]):
        for first in (0, half):
            lanes = pl.ds(first, half)
            copies.append((down_ref.at[kind, at, lanes], out_ref.at[kind, :, lanes]))
    copies = [pltpu.make_async_copy(*pair, sems.at[i]) for i, pair in enumerate(copies)]
    for copy in copies:
        copy.start()
    for copy in copies:
        copy.wait()


def pack_call(down, up):
    kinds, share, columns = up.shape
    return pl.pallas_call(
        pack_kernel,
        out_shape=pltpu.VMEM((kinds, share, down.shape[2] + columns), down.dtype),
        in_specs=[HBM] * 2,
        out_specs=VMEM,
        scratch_shapes=[pltpu.SemaphoreType.DMA((1 + 2 * kinds,))],
        name="pack_factors",
    )(*[pltpu.with_memory_space_constraint(x, pltpu.HBM) for x in (down, up)])


def scaled_block(part, gain_ref, block):
    steps, rows, width = part.shape
    chunks = width // HD
    gain = gain_ref[pl.ds(pl.multiple_of(block * chunks, chunks), chunks)]
    values = rows_of(part)
    squares = jnp.zeros((steps * rows, HD), jnp.float32)
    scaled = []
    for i in range(chunks):
        chunk = values[:, i * HD : (i + 1) * HD]
        squares += chunk * chunk
        scaled.append((chunk * gain[i : i + 1]).astype(jnp.bfloat16))
    return jnp.concatenate(scaled, axis=1), squares


def rotation_tables(lengths, steps, rows, cos_out, sin_out):
    lane = lax.broadcasted_iota(jnp.int32, (rows, HD), 1)
    half = HD // 2
    second = lane >= half
    index = jnp.where(second, lane - half, lane).astype(jnp.float32)
    inv_freq = jnp.exp(index * (-2.0 * math.log(rope_base) / HD))
    row_index = lax.broadcasted_iota(jnp.int32, (rows, HD), 0)
    row_lengths = jnp.zeros((rows, HD), jnp.int32)
    for row in range(rows):
        row_lengths = jnp.where(row_index == row, lengths[row], row_lengths)
    for step in range(steps):
        angles = (row_lengths + step).astype(jnp.float32) * inv_freq
        sine = jnp.sin(angles)
        cos_out[pl.ds(step * rows, rows)] = jnp.cos(angles)
        sin_out[pl.ds(step * rows, rows)] = jnp.where(second, sine, -sine)


def scale_kernel(early, far, lengths_ref, weight_ref, gain_ref, query_ref, *rest):
    scaled_out, early_out, square_out, far_weight, query_out, cos_out, sin_out = rest[-10:-3]
    lengths, length_sem, far_sems = rest[-3:]
    parts = rest[:-10]
    steps, rows, width = parts[0].shape
    length_copy = pltpu.make_async_copy(lengths_ref, lengths, length_sem)
    length_copy.start()
    copies = copy_blocks(far, width, weight_ref, far_weight, far_sems)
    me = lax.axis_index("tp")
    scaled_out[...] = jnp.zeros_like(scaled_out)
    total = None
    for k, (offset, part) in enumerate(zip(early, parts)):
        block = me ^ offset
        scaled, squares = scaled_block(part, gain_ref, block)
        total = squares if total is None else total + squares
        scaled_out[:, pl.ds(pl.multiple_of(block * width, width), width)] = scaled
        early_out[:, k * width : (k + 1) * width] = scaled
    square_out[...] = total
    query_out[...] = query_ref[...].astype(query_out.dtype)
    length_copy.wait()
    rotation_tables(lengths, steps, rows, cos_out, sin_out)
    for copy in copies:
        copy.wait()


def scale_call(early, blocks, far, lengths, weight, gain, queries, parts):
    steps, rows, width = parts[0].shape
    count = steps * rows
    return pl.pallas_call(
        functools.partial(scale_kernel, early, far),
        out_shape=(
            pltpu.VMEM((count, blocks * width), jnp.bfloat16),
            pltpu.VMEM((count, len(early) * width), jnp.bfloat16),
            pltpu.VMEM((count, HD), jnp.float32),
            pltpu.VMEM((len(far) * width,) + weight.shape[1:], weight.dtype),
            pltpu.VMEM(queries.shape, jnp.bfloat16),
            pltpu.VMEM((count, HD), jnp.float32),
            pltpu.VMEM((count, HD), jnp.float32),
        ),
        in_specs=[HBM] * 2 + [VMEM] * (2 + len(parts)),
        out_specs=(VMEM,) * 7,
        scratch_shapes=[
            pltpu.SMEM(lengths.shape, jnp.int32),
            pltpu.SemaphoreType.DMA,
            pltpu.SemaphoreType.DMA((len(far),)),
        ],
        compiler_params=pltpu.CompilerParams(vmem_limit_bytes=8 << 20),
        cost_estimate=pl.CostEstimate(flops=0, bytes_accessed=9 << 20, transcendentals=0),
        name="scale_features",
    )(*[pltpu.with_memory_space_constraint(x, pltpu.HBM) for x in (lengths, weight)], gain, queries, *parts)


def inner_kernel(late, scaled_ref, square_ref, gain_ref, *rest):
    parts, rest = rest[: len(late)], rest[len(late) :]
    late_out, square_out = rest[-2:]
    packs, inner_out = (rest[:-3], rest[-3]) if len(rest) > 2 else ((), None)
    squares = square_ref[...]
    blocks = []
    for k, (offset, part) in enumerate(zip(late, parts)):
        block = lax.axis_index("tp") ^ offset
        scaled, more = scaled_block(part, gain_ref, block)
        squares += more
        blocks.append((block, scaled))
        width = scaled.shape[1]
        late_out[:, k * width : (k + 1) * width] = scaled
    squares = jnp.sum(squares, axis=1, keepdims=True)
    square_out[...] = jnp.broadcast_to(squares, square_out.shape)
    if not packs:
        return
    me = lax.axis_index("wide")
    total = []
    for offset, pack in enumerate(packs):
        mine = me ^ offset
        rows = scaled_ref[:, pl.ds(pl.multiple_of(mine * width, width), width)]
        for block, scaled in blocks:
            rows = jnp.where(mine == block, scaled, rows)
        total.append(
            lax.dot_general(
                rows,
                pack[:, :, :width].reshape(inner_out.shape[1], width),
                (((1,), (1,)), ((), ())),
                preferred_element_type=jnp.float32,
            )
        )
    inner_out[...] = sum(total[1:], total[0])


def inner_call(late, scaled, square, gain, parts, packs):
    count, width = scaled.shape[0], parts[0].shape[2]
    shapes = [
        pltpu.VMEM((count, len(late) * width), scaled.dtype),
        pltpu.VMEM(square.shape, jnp.float32),
    ]
    if packs:
        kinds, share, _ = packs[0].shape
        shapes = [pltpu.VMEM((count, kinds * share), jnp.float32)] + shapes
    return pl.pallas_call(
        functools.partial(inner_kernel, late),
        out_shape=tuple(shapes),
        in_specs=[VMEM] * (3 + len(parts) + len(packs)),
        out_specs=(VMEM,) * len(shapes),
        compiler_params=pltpu.CompilerParams(vmem_limit_bytes=8 << 20),
        name="rank_inner",
    )(scaled, square, gain, *parts, *packs)


def up_kernel(*refs):
    packs, up_out = refs[:-1], refs[-1]
    kinds, share, pack_width = packs[0].shape
    columns = up_out.shape[1] // kinds
    me = lax.axis_index("wide") if len(packs) > 1 else 0
    up_out[...] = jnp.zeros_like(up_out)
    for offset, pack in enumerate(packs):
        for kind in range(kinds):
            at = pl.multiple_of(((me ^ offset) * kinds + kind) * share, share)
            up_out[pl.ds(at, share), kind * columns : (kind + 1) * columns] = pack[
                kind, :, pack_width - columns :
            ]


def up_call(packs, columns):
    kinds, share, _ = packs[0].shape
    return pl.pallas_call(
        up_kernel,
        out_shape=pltpu.VMEM((len(packs) * kinds * share, kinds * columns), packs[0].dtype),
        in_specs=[VMEM] * len(packs),
        out_specs=VMEM,
        compiler_params=pltpu.CompilerParams(vmem_limit_bytes=8 << 20),
        name="lay_out_up",
    )(*packs)


def split_index(index, count):
    if count & (count - 1) == 0:
        return index >> (count.bit_length() - 1), index & (count - 1)
    return index // count, index % count


def final_kernel(width, blocks, near_ref, far_ref, square_ref, bias_ref, *rest):
    query_ref, acc_ref, top_ref, total_ref, cos_ref, sin_ref = rest[:6]
    inner_refs = rest[6 : 6 + blocks]
    up_ref, keys_out, values_out, attended_out = rest[6 + blocks :]
    steps, rows, columns = keys_out.shape
    count = steps * rows
    groups, size, _ = query_ref.shape
    per_group = size // count
    kinds = bias_ref.shape[0]
    row_scale = lax.rsqrt(square_ref[...] * (1.0 / width) + norm_eps)
    row_scale = jnp.concatenate([row_scale] * groups, axis=1)
    me = lax.axis_index("tp") if blocks > 1 else 0
    share = inner_refs[0].shape[1]
    products = []
    for i in range(blocks):
        inner = inner_refs[i][...]
        high = inner.astype(jnp.bfloat16)
        low = (inner - high.astype(jnp.float32)).astype(jnp.bfloat16)
        at = pl.multiple_of((me ^ i) * share, share)
        products.append(
            jnp.dot(
                jnp.concatenate([high, low], axis=0),
                up_ref[pl.ds(at, share), :],
                preferred_element_type=jnp.float32,
            )
        )
    lora = sum(products[1:], products[0])
    lora = lora[:count] + lora[count:]
    bias = bias_ref[...].astype(jnp.float32)
    linear = []
    for kind in range(kinds):
        base = near_ref[kind] + far_ref[kind]
        part = lora[:, kind * columns : (kind + 1) * columns]
        linear.append((base + adapter_scale * part) * row_scale + bias[kind : kind + 1])
    cosine, sine = cos_ref[...], sin_ref[...]
    line = lax.broadcasted_iota(jnp.int32, (size, count), 0)
    other = lax.broadcasted_iota(jnp.int32, (size, count), 1)
    line_step, line_row = split_index(line, rows)
    other_step, other_row = split_index(other, rows)
    line_step = split_index(line_step, steps)[1]
    live = (line_row == other_row) & (other_step <= line_step)
    for group in range(groups):
        at = slice(group * HD, (group + 1) * HD)
        key = linear[0][:, at]
        key = (key * cosine + pltpu.roll(key, HD // 2, 1) * sine).astype(jnp.bfloat16)
        value = linear[1][:, at].astype(jnp.bfloat16)
        for step in range(steps):
            keys_out[step, :, at] = key[step * rows : (step + 1) * rows]
            values_out[step, :, at] = value[step * rows : (step + 1) * rows]
        scores = lax.dot_general(
            query_ref[group],
            key,
            (((1,), (1,)), ((), ())),
            preferred_element_type=jnp.float32,
        )
        scores = jnp.where(live, scores * score_scale, masked_score)
        old_top = top_ref[group]
        top = jnp.maximum(old_top, jnp.max(scores, axis=1, keepdims=True))
        exps = jnp.exp(scores - top[:, :count])
        keep = jnp.exp(old_top - top)
        total = total_ref[group] * keep + jnp.sum(exps, axis=1, keepdims=True)
        acc = acc_ref[group] * keep + jnp.dot(
            exps.astype(jnp.bfloat16), value, preferred_element_type=jnp.float32
        )
        attended = (acc * (1.0 / total)).astype(jnp.bfloat16)
        for head in range(per_group):
            lanes = pl.ds((group * per_group + head) * HD, HD)
            for step in range(steps):
                tile = (head * steps + step) * rows
                attended_out[step, :, lanes] = attended[tile : tile + rows]


def final_call(shape, width, near, far, square, bias, cached, inner, up):
    steps, rows, query_width = shape
    columns = near.shape[2]
    small = jax.ShapeDtypeStruct((steps, rows, columns), jnp.bfloat16)
    return pl.pallas_call(
        functools.partial(final_kernel, width, len(inner)),
        out_shape=(small, small, jax.ShapeDtypeStruct(shape, jnp.bfloat16)),
        in_specs=[VMEM] * (5 + len(cached) + len(inner)),
        out_specs=(VMEM,) * 3,
        compiler_params=pltpu.CompilerParams(vmem_limit_bytes=8 << 20),
        name="fresh_attention",
    )(near, far, square, bias, *cached, *inner, up)


def dot(rows, weight):
    return jnp.einsum("md,dkc->kmc", rows, weight, preferred_element_type=jnp.float32)


def swap(block, axis, offset, count):
    return lax.ppermute(block, axis, [(i, i ^ offset) for i in range(count)])


def on_device(
    wide_count,
    tp_count,
    hidden,
    input_norm_gain,
    key_value_weight,
    key_value_bias,
    adapter_down_factor,
    adapter_up_factor,
    queries,
    stored_rotated_keys,
    stored_value_rows,
    lengths,
):
    steps, rows, part_width = hidden.shape
    width = part_width * tp_count
    kinds, ranks, down_width = adapter_down_factor.shape
    gain = input_norm_gain.reshape(width // HD, HD)
    up_part = jnp.transpose(adapter_up_factor, (0, 2, 1))
    direct = wide_count == tp_count == 4
    crossed = swap(hidden, "tp", 2, tp_count)
    if direct:
        pack = pack_call(adapter_down_factor, up_part)
        second = swap(pack, "wide", 2, wide_count)
        first = swap(pack, "wide", 1, wide_count)
    early, late = (0, 2), (1, 3)
    early_weight, gain_rows, bias, mine, query_rows, *cached = cache_call(
        early,
        lengths,
        queries,
        stored_rotated_keys,
        stored_value_rows,
        gain,
        key_value_bias,
        hidden,
        key_value_weight,
    )
    beside = swap(mine, "tp", 1, tp_count)
    if direct:
        relayed, third, gain_rows = lax.optimization_barrier((crossed, second, gain_rows))
    else:
        relayed = crossed
    relayed = swap(relayed, "tp", 1, tp_count)
    if direct:
        packs = [pack, first, second, swap(third, "wide", 1, wide_count)]
    scaled, early_scaled, square, late_weight, query_rows, *tables = scale_call(
        early, tp_count, late, lengths, key_value_weight, gain_rows, query_rows, (mine, crossed)
    )
    late_parts = (beside, relayed)
    early_base = dot(early_scaled, early_weight)
    if direct:
        scaled, early_base = lax.optimization_barrier((scaled, early_base))
        inner, late_scaled, square = inner_call(
            late, scaled, square, gain_rows, late_parts, packs
        )
        inner, late_scaled, packs = lax.optimization_barrier((inner, late_scaled, packs))
        diagonal = swap(inner, "tp", 3, tp_count)
        across = swap(inner, "tp", 2, tp_count)
        beside = swap(inner, "tp", 1, tp_count)
        both, beside = lax.optimization_barrier((diagonal + across, beside))
        inner = [inner, beside, across, diagonal]
    else:
        late_scaled, square = inner_call(late, scaled, square, gain_rows, late_parts, [])
        down = lax.all_gather(adapter_down_factor, "wide", axis=2, tiled=True)
        rows_full = lax.all_gather(hidden, "tp", axis=2, tiled=True).astype(jnp.float32)
        rows_full = (rows_full * input_norm_gain.astype(jnp.float32)).astype(jnp.bfloat16)
        inner = jnp.einsum("srd,kad->srka", rows_full, down, preferred_element_type=jnp.float32)
        inner = [inner.reshape(steps * rows, kinds * ranks)]
        packs = [lax.all_gather(up_part, "wide", axis=1, tiled=True)]
    late_base = dot(late_scaled, late_weight)
    up = up_call(packs, bias.shape[1])
    return final_call(
        queries.shape, width, early_base, late_base, square, bias, [query_rows] + cached + tables, inner, up
    )


def solution(mesh):
    in_specs = (
        P(None, ("groups", "wide"), "tp"),
        P(),
        P(None, None, "tp"),
        P(None, "tp"),
        P("groups", None, "wide"),
        P("groups", "tp", "wide"),
        P(None, ("groups", "wide"), "tp"),
        P(("groups", "wide"), None, "tp"),
        P(("groups", "wide"), None, "tp"),
        P(("groups", "wide")),
    )
    out_specs = (
        P(None, ("groups", "wide"), "tp"),
        P(None, ("groups", "wide"), "tp"),
        P(None, ("groups", "wide"), "tp"),
    )
    body = functools.partial(on_device, mesh.shape["wide"], mesh.shape["tp"])
    return jax.shard_map(
        body, mesh=mesh, in_specs=in_specs, out_specs=out_specs, check_vma=False
    )
```

```python
import functools
import math

import jax
import jax.numpy as jnp
from jax import lax
from jax.experimental import pallas as pl
from jax.experimental.pallas import tpu as pltpu
from jax.sharding import PartitionSpec as P

HD = 128


norm_eps = 1e-06
adapter_scale = 2.0
rope_base = 1000000.0
masked_score = -1e30
score_scale = 1.0 / math.sqrt(HD)

VMEM = pl.BlockSpec(memory_space=pltpu.VMEM)
HBM = pl.BlockSpec(memory_space=pltpu.HBM)


def query_block(query_ref, group, per_group):
    steps = query_ref.shape[0]
    tiles = []
    for head in range(per_group):
        at = (group * per_group + head) * HD
        for step in range(steps):
            tiles.append(query_ref[step, :, at : at + HD].astype(jnp.float32))
    return jnp.concatenate(tiles, axis=0)


def copy_blocks(offsets, width, weight_ref, out_ref, sems):
    me = lax.axis_index("tp")
    copies = []
    for i, offset in enumerate(offsets):
        block = pl.ds(pl.multiple_of((me ^ offset) * width, width), width)
        copies.append(
            pltpu.make_async_copy(
                weight_ref.at[block], out_ref.at[pl.ds(i * width, width)], sems.at[i]
            )
        )
        copies[-1].start()
    return copies


def cache_kernel(
    near,
    lengths_ref,
    query_ref,
    key_ref,
    value_ref,
    gain_ref,
    bias_ref,
    hidden_ref,
    weight_ref,
    near_out,
    gain_out,
    bias_out,
    hidden_out,
    query_out,
    acc_out,
    top_out,
    total_out,
    lengths,
    queries,
    gain_buffer,
    key_buffer,
    value_buffer,
    score_buffer,
    sems,
    weight_sems,
):
    steps, rows, query_width = query_ref.shape
    cache_span = key_ref.shape[1]
    groups = key_ref.shape[2] // HD
    per_group = query_width // HD // groups
    lines = steps * per_group
    half_rows = rows // 2
    halves = [pl.ds(0, half_rows), pl.ds(half_rows, half_rows)]
    copies = [
        (lengths_ref, lengths),
        (query_ref, queries),
        (key_ref.at[halves[0]], key_buffer.at[halves[0]]),
        (key_ref.at[halves[1]], key_buffer.at[halves[1]]),
        (value_ref.at[halves[0]], value_buffer.at[halves[0]]),
        (value_ref.at[halves[1]], value_buffer.at[halves[1]]),
        (gain_ref, gain_buffer),
        (bias_ref, bias_out),
        (hidden_ref, hidden_out),
    ]
    copies = [pltpu.make_async_copy(*pair, sems.at[i]) for i, pair in enumerate(copies)]
    for copy in copies:
        copy.start()
    copies += copy_blocks(near, hidden_ref.shape[2], weight_ref, near_out, weight_sems)

    copies[0].wait()
    copies[1].wait()
    for group in range(groups):
        query_out[group] = query_block(queries, group, per_group)

    place = lax.broadcasted_iota(jnp.int32, (lines, cache_span), 1)
    for i in range(2):
        copies[2 + i].wait()
        for row in range(i * half_rows, (i + 1) * half_rows):
            for group in range(groups):
                query = query_out[group, pl.ds(row, lines, stride=rows), :].astype(jnp.bfloat16)
                score_buffer[row * groups + group] = lax.dot_general(
                    query,
                    key_buffer[row, :, pl.ds(group * HD, HD)],
                    (((1,), (1,)), ((), ())),
                    preferred_element_type=jnp.float32,
                )
    for i in range(2):
        copies[4 + i].wait()
        for row in range(i * half_rows, (i + 1) * half_rows):
            live = place < lengths[row]
            for group in range(groups):
                mine = pl.ds(row, lines, stride=rows)
                scores = score_buffer[row * groups + group]
                scores = jnp.where(live, scores * score_scale, masked_score)
                top = jnp.max(scores, axis=1, keepdims=True)
                exps = jnp.exp(scores - top)
                total = jnp.sum(exps, axis=1, keepdims=True)
                acc = jnp.dot(
                    exps.astype(jnp.bfloat16),
                    value_buffer[row, :, pl.ds(group * HD, HD)],
                    preferred_element_type=jnp.float32,
                )
                acc_out[group, mine, :] = acc
                top_out[group, mine, :] = jnp.broadcast_to(top, acc.shape)
                total_out[group, mine, :] = jnp.broadcast_to(total, acc.shape)
    copies[6].wait()
    gain_out[...] = gain_buffer[...].astype(jnp.float32)
    for copy in copies[7:]:
        copy.wait()


def cache_call(near, lengths, queries, keys, values, gain, bias, hidden, weight):
    steps, rows, query_width = queries.shape
    cache_span, key_width = keys.shape[1:]
    groups = key_width // HD
    lines = steps * (query_width // key_width)
    block = (groups, lines * rows, HD)
    operands = (lengths, queries, keys, values, gain, bias, hidden, weight)
    near_weight = (len(near) * hidden.shape[2],) + weight.shape[1:]
    return pl.pallas_call(
        functools.partial(cache_kernel, near),
        out_shape=(
            pltpu.VMEM(near_weight, weight.dtype),
            pltpu.VMEM(gain.shape, jnp.float32),
            pltpu.VMEM(bias.shape, bias.dtype),
            pltpu.VMEM(hidden.shape, hidden.dtype),
            pltpu.VMEM(block, jnp.float32),
            pltpu.VMEM(block, jnp.float32),
            pltpu.VMEM(block, jnp.float32),
            pltpu.VMEM(block, jnp.float32),
        ),
        in_specs=[HBM] * len(operands),
        out_specs=(VMEM,) * 8,
        scratch_shapes=[
            pltpu.SMEM(lengths.shape, jnp.int32),
            pltpu.VMEM(queries.shape, queries.dtype),
            pltpu.VMEM(gain.shape, gain.dtype),
            pltpu.VMEM(keys.shape, keys.dtype),
            pltpu.VMEM(values.shape, values.dtype),
            pltpu.VMEM((rows * groups, lines, cache_span), jnp.float32),
            pltpu.SemaphoreType.DMA((9,)),
            pltpu.SemaphoreType.DMA((len(near),)),
        ],
        compiler_params=pltpu.CompilerParams(vmem_limit_bytes=16 << 20),
        cost_estimate=pl.CostEstimate(flops=2 * 67 << 20, bytes_accessed=5 << 20, transcendentals=0),
        name="cache_attention",
    )(*[pltpu.with_memory_space_constraint(x, pltpu.HBM) for x in operands])


def rows_of(ref):
    return jnp.concatenate([ref[s].astype(jnp.float32) for s in range(ref.shape[0])], axis=0)


def pack_kernel(down_ref, up_ref, out_ref, sems):
    share = out_ref.shape[1]
    width = down_ref.shape[2]
    at = pl.ds(pl.multiple_of(lax.axis_index("tp") * share, share), share)
    copies = [(up_ref, out_ref.at[:, :, pl.ds(width, up_ref.shape[2])])]
    half = width // 2
    for kind in range(down_ref.shape[0]):
        for first in (0, half):
            lanes = pl.ds(first, half)
            copies.append((down_ref.at[kind, at, lanes], out_ref.at[kind, :, lanes]))
    copies = [pltpu.make_async_copy(*pair, sems.at[i]) for i, pair in enumerate(copies)]
    for copy in copies:
        copy.start()
    for copy in copies:
        copy.wait()


def pack_call(down, up):
    kinds, share, columns = up.shape
    return pl.pallas_call(
        pack_kernel,
        out_shape=pltpu.VMEM((kinds, share, down.shape[2] + columns), down.dtype),
        in_specs=[HBM] * 2,
        out_specs=VMEM,
        scratch_shapes=[pltpu.SemaphoreType.DMA((1 + 2 * kinds,))],
        name="pack_factors",
    )(*[pltpu.with_memory_space_constraint(x, pltpu.HBM) for x in (down, up)])


def scaled_block(part, gain_ref, block):
    steps, rows, width = part.shape
    chunks = width // HD
    gain = gain_ref[pl.ds(pl.multiple_of(block * chunks, chunks), chunks)]
    values = rows_of(part)
    squares = jnp.zeros((steps * rows, HD), jnp.float32)
    scaled = []
    for i in range(chunks):
        chunk = values[:, i * HD : (i + 1) * HD]
        squares += chunk * chunk
        scaled.append((chunk * gain[i : i + 1]).astype(jnp.bfloat16))
    return jnp.concatenate(scaled, axis=1), squares


def rotation_tables(lengths, steps, rows, cos_out, sin_out):
    lane = lax.broadcasted_iota(jnp.int32, (rows, HD), 1)
    half = HD // 2
    second = lane >= half
    index = jnp.where(second, lane - half, lane).astype(jnp.float32)
    inv_freq = jnp.exp(index * (-2.0 * math.log(rope_base) / HD))
    row_index = lax.broadcasted_iota(jnp.int32, (rows, HD), 0)
    row_lengths = jnp.zeros((rows, HD), jnp.int32)
    for row in range(rows):
        row_lengths = jnp.where(row_index == row, lengths[row], row_lengths)
    for step in range(steps):
        angles = (row_lengths + step).astype(jnp.float32) * inv_freq
        sine = jnp.sin(angles)
        cos_out[pl.ds(step * rows, rows)] = jnp.cos(angles)
        sin_out[pl.ds(step * rows, rows)] = jnp.where(second, sine, -sine)


def scale_kernel(early, far, lengths_ref, weight_ref, gain_ref, query_ref, *rest):
    scaled_out, early_out, square_out, far_weight, query_out, cos_out, sin_out = rest[-10:-3]
    lengths, length_sem, far_sems = rest[-3:]
    parts = rest[:-10]
    steps, rows, width = parts[0].shape
    length_copy = pltpu.make_async_copy(lengths_ref, lengths, length_sem)
    length_copy.start()
    copies = copy_blocks(far, width, weight_ref, far_weight, far_sems)
    me = lax.axis_index("tp")
    scaled_out[...] = jnp.zeros_like(scaled_out)
    total = None
    for k, (offset, part) in enumerate(zip(early, parts)):
        block = me ^ offset
        scaled, squares = scaled_block(part, gain_ref, block)
        total = squares if total is None else total + squares
        scaled_out[:, pl.ds(pl.multiple_of(block * width, width), width)] = scaled
        early_out[:, k * width : (k + 1) * width] = scaled
    square_out[...] = total
    query_out[...] = query_ref[...].astype(query_out.dtype)
    length_copy.wait()
    rotation_tables(lengths, steps, rows, cos_out, sin_out)
    for copy in copies:
        copy.wait()


def scale_call(early, blocks, far, lengths, weight, gain, queries, parts):
    steps, rows, width = parts[0].shape
    count = steps * rows
    return pl.pallas_call(
        functools.partial(scale_kernel, early, far),
        out_shape=(
            pltpu.VMEM((count, blocks * width), jnp.bfloat16),
            pltpu.VMEM((count, len(early) * width), jnp.bfloat16),
            pltpu.VMEM((count, HD), jnp.float32),
            pltpu.VMEM((len(far) * width,) + weight.shape[1:], weight.dtype),
            pltpu.VMEM(queries.shape, jnp.bfloat16),
            pltpu.VMEM((count, HD), jnp.float32),
            pltpu.VMEM((count, HD), jnp.float32),
        ),
        in_specs=[HBM] * 2 + [VMEM] * (2 + len(parts)),
        out_specs=(VMEM,) * 7,
        scratch_shapes=[
            pltpu.SMEM(lengths.shape, jnp.int32),
            pltpu.SemaphoreType.DMA,
            pltpu.SemaphoreType.DMA((len(far),)),
        ],
        compiler_params=pltpu.CompilerParams(vmem_limit_bytes=8 << 20),
        cost_estimate=pl.CostEstimate(flops=0, bytes_accessed=9 << 20, transcendentals=0),
        name="scale_features",
    )(*[pltpu.with_memory_space_constraint(x, pltpu.HBM) for x in (lengths, weight)], gain, queries, *parts)


def inner_kernel(late, scaled_ref, square_ref, gain_ref, *rest):
    parts, rest = rest[: len(late)], rest[len(late) :]
    late_out, square_out = rest[-2:]
    packs, inner_out = (rest[:-3], rest[-3]) if len(rest) > 2 else ((), None)
    squares = square_ref[...]
    blocks = []
    for k, (offset, part) in enumerate(zip(late, parts)):
        block = lax.axis_index("tp") ^ offset
        scaled, more = scaled_block(part, gain_ref, block)
        squares += more
        blocks.append((block, scaled))
        width = scaled.shape[1]
        late_out[:, k * width : (k + 1) * width] = scaled
    squares = jnp.sum(squares, axis=1, keepdims=True)
    square_out[...] = jnp.broadcast_to(squares, square_out.shape)
    if not packs:
        return
    me = lax.axis_index("wide")
    total = []
    for offset, pack in enumerate(packs):
        mine = me ^ offset
        rows = scaled_ref[:, pl.ds(pl.multiple_of(mine * width, width), width)]
        for block, scaled in blocks:
            rows = jnp.where(mine == block, scaled, rows)
        total.append(
            lax.dot_general(
                rows,
                pack[:, :, :width].reshape(inner_out.shape[1], width),
                (((1,), (1,)), ((), ())),
                preferred_element_type=jnp.float32,
            )
        )
    inner_out[...] = sum(total[1:], total[0])


def inner_call(late, scaled, square, gain, parts, packs):
    count, width = scaled.shape[0], parts[0].shape[2]
    shapes = [
        pltpu.VMEM((count, len(late) * width), scaled.dtype),
        pltpu.VMEM(square.shape, jnp.float32),
    ]
    if packs:
        kinds, share, _ = packs[0].shape
        shapes = [pltpu.VMEM((count, kinds * share), jnp.float32)] + shapes
    return pl.pallas_call(
        functools.partial(inner_kernel, late),
        out_shape=tuple(shapes),
        in_specs=[VMEM] * (3 + len(parts) + len(packs)),
        out_specs=(VMEM,) * len(shapes),
        compiler_params=pltpu.CompilerParams(vmem_limit_bytes=8 << 20),
        name="rank_inner",
    )(scaled, square, gain, *parts, *packs)


def up_kernel(*refs):
    packs, up_out = refs[:-1], refs[-1]
    kinds, share, pack_width = packs[0].shape
    columns = up_out.shape[1] // kinds
    me = lax.axis_index("wide") if len(packs) > 1 else 0
    up_out[...] = jnp.zeros_like(up_out)
    for offset, pack in enumerate(packs):
        for kind in range(kinds):
            at = pl.multiple_of(((me ^ offset) * kinds + kind) * share, share)
            up_out[pl.ds(at, share), kind * columns : (kind + 1) * columns] = pack[
                kind, :, pack_width - columns :
            ]


def up_call(packs, columns):
    kinds, share, _ = packs[0].shape
    return pl.pallas_call(
        up_kernel,
        out_shape=pltpu.VMEM((len(packs) * kinds * share, kinds * columns), packs[0].dtype),
        in_specs=[VMEM] * len(packs),
        out_specs=VMEM,
        compiler_params=pltpu.CompilerParams(vmem_limit_bytes=8 << 20),
        name="lay_out_up",
    )(*packs)


def split_index(index, count):
    if count & (count - 1) == 0:
        return index >> (count.bit_length() - 1), index & (count - 1)
    return index // count, index % count


def final_kernel(width, blocks, near_ref, far_ref, square_ref, bias_ref, *rest):
    query_ref, acc_ref, top_ref, total_ref, cos_ref, sin_ref = rest[:6]
    inner_refs = rest[6 : 6 + blocks]
    up_ref, keys_out, values_out, attended_out = rest[6 + blocks :]
    steps, rows, columns = keys_out.shape
    count = steps * rows
    groups, size, _ = query_ref.shape
    per_group = size // count
    kinds = bias_ref.shape[0]
    row_scale = lax.rsqrt(square_ref[...] * (1.0 / width) + norm_eps)
    row_scale = jnp.concatenate([row_scale] * groups, axis=1)
    me = lax.axis_index("tp") if blocks > 1 else 0
    share = inner_refs[0].shape[1]
    products = []
    for i in range(blocks):
        inner = inner_refs[i][...]
        high = inner.astype(jnp.bfloat16)
        low = (inner - high.astype(jnp.float32)).astype(jnp.bfloat16)
        at = pl.multiple_of((me ^ i) * share, share)
        products.append(
            jnp.dot(
                jnp.concatenate([high, low], axis=0),
                up_ref[pl.ds(at, share), :],
                preferred_element_type=jnp.float32,
            )
        )
    lora = sum(products[1:], products[0])
    lora = lora[:count] + lora[count:]
    bias = bias_ref[...].astype(jnp.float32)
    linear = []
    for kind in range(kinds):
        base = near_ref[kind] + far_ref[kind]
        part = lora[:, kind * columns : (kind + 1) * columns]
        linear.append((base + adapter_scale * part) * row_scale + bias[kind : kind + 1])
    cosine, sine = cos_ref[...], sin_ref[...]
    line = lax.broadcasted_iota(jnp.int32, (size, count), 0)
    other = lax.broadcasted_iota(jnp.int32, (size, count), 1)
    line_step, line_row = split_index(line, rows)
    other_step, other_row = split_index(other, rows)
    line_step = split_index(line_step, steps)[1]
    live = (line_row == other_row) & (other_step <= line_step)
    for group in range(groups):
        at = slice(group * HD, (group + 1) * HD)
        key = linear[0][:, at]
        key = (key * cosine + pltpu.roll(key, HD // 2, 1) * sine).astype(jnp.bfloat16)
        value = linear[1][:, at].astype(jnp.bfloat16)
        for step in range(steps):
            keys_out[step, :, at] = key[step * rows : (step + 1) * rows]
            values_out[step, :, at] = value[step * rows : (step + 1) * rows]
        scores = lax.dot_general(
            query_ref[group],
            key,
            (((1,), (1,)), ((), ())),
            preferred_element_type=jnp.float32,
        )
        scores = jnp.where(live, scores * score_scale, masked_score)
        old_top = top_ref[group]
        top = jnp.maximum(old_top, jnp.max(scores, axis=1, keepdims=True))
        exps = jnp.exp(scores - top[:, :count])
        keep = jnp.exp(old_top - top)
        total = total_ref[group] * keep + jnp.sum(exps, axis=1, keepdims=True)
        acc = acc_ref[group] * keep + jnp.dot(
            exps.astype(jnp.bfloat16), value, preferred_element_type=jnp.float32
        )
        attended = (acc * (1.0 / total)).astype(jnp.bfloat16)
        for head in range(per_group):
            lanes = pl.ds((group * per_group + head) * HD, HD)
            for step in range(steps):
                tile = (head * steps + step) * rows
                attended_out[step, :, lanes] = attended[tile : tile + rows]


def final_call(shape, width, near, far, square, bias, cached, inner, up):
    steps, rows, query_width = shape
    columns = near.shape[2]
    small = jax.ShapeDtypeStruct((steps, rows, columns), jnp.bfloat16)
    return pl.pallas_call(
        functools.partial(final_kernel, width, len(inner)),
        out_shape=(small, small, jax.ShapeDtypeStruct(shape, jnp.bfloat16)),
        in_specs=[VMEM] * (5 + len(cached) + len(inner)),
        out_specs=(VMEM,) * 3,
        compiler_params=pltpu.CompilerParams(vmem_limit_bytes=8 << 20),
        name="fresh_attention",
    )(near, far, square, bias, *cached, *inner, up)


def dot(rows, weight):
    return jnp.einsum("md,dkc->kmc", rows, weight, preferred_element_type=jnp.float32)


def swap(block, axis, offset, count):
    return lax.ppermute(block, axis, [(i, i ^ offset) for i in range(count)])


def on_device(
    wide_count,
    tp_count,
    hidden,
    input_norm_gain,
    key_value_weight,
    key_value_bias,
    adapter_down_factor,
    adapter_up_factor,
    queries,
    stored_rotated_keys,
    stored_value_rows,
    lengths,
):
    steps, rows, part_width = hidden.shape
    width = part_width * tp_count
    kinds, ranks, down_width = adapter_down_factor.shape
    gain = input_norm_gain.reshape(width // HD, HD)
    up_part = jnp.transpose(adapter_up_factor, (0, 2, 1))
    direct = wide_count == tp_count == 4
    beside, crossed = [swap(hidden, "tp", offset, tp_count) for offset in (1, 2)]
    if direct:
        pack = pack_call(adapter_down_factor, up_part)
        second = swap(pack, "wide", 2, wide_count)
        first = swap(pack, "wide", 1, wide_count)
    early, late = (0, 2), (1, 3)
    early_weight, gain_rows, bias, mine, query_rows, *cached = cache_call(
        early,
        lengths,
        queries,
        stored_rotated_keys,
        stored_value_rows,
        gain,
        key_value_bias,
        hidden,
        key_value_weight,
    )
    if direct:
        relayed, third, gain_rows = lax.optimization_barrier((crossed, second, gain_rows))
    else:
        relayed = crossed
    relayed = swap(relayed, "tp", 1, tp_count)
    if direct:
        packs = [pack, first, second, swap(third, "wide", 1, wide_count)]
    scaled, early_scaled, square, late_weight, query_rows, *tables = scale_call(
        early, tp_count, late, lengths, key_value_weight, gain_rows, query_rows, (mine, crossed)
    )
    late_parts = (beside, relayed)
    early_base = dot(early_scaled, early_weight)
    if direct:
        scaled, early_base = lax.optimization_barrier((scaled, early_base))
        inner, late_scaled, square = inner_call(
            late, scaled, square, gain_rows, late_parts, packs
        )
        inner, late_scaled, packs = lax.optimization_barrier((inner, late_scaled, packs))
        diagonal = swap(inner, "tp", 3, tp_count)
        across = swap(inner, "tp", 2, tp_count)
        beside = swap(inner, "tp", 1, tp_count)
        both, beside = lax.optimization_barrier((diagonal + across, beside))
        inner = [inner, beside, across, diagonal]
    else:
        late_scaled, square = inner_call(late, scaled, square, gain_rows, late_parts, [])
        down = lax.all_gather(adapter_down_factor, "wide", axis=2, tiled=True)
        rows_full = lax.all_gather(hidden, "tp", axis=2, tiled=True).astype(jnp.float32)
        rows_full = (rows_full * input_norm_gain.astype(jnp.float32)).astype(jnp.bfloat16)
        inner = jnp.einsum("srd,kad->srka", rows_full, down, preferred_element_type=jnp.float32)
        inner = [inner.reshape(steps * rows, kinds * ranks)]
        packs = [lax.all_gather(up_part, "wide", axis=1, tiled=True)]
    late_base = dot(late_scaled, late_weight)
    up = up_call(packs, bias.shape[1])
    return final_call(
        queries.shape, width, early_base, late_base, square, bias, [query_rows] + cached + tables, inner, up
    )


def solution(mesh):
    in_specs = (
        P(None, ("groups", "wide"), "tp"),
        P(),
        P(None, None, "tp"),
        P(None, "tp"),
        P("groups", None, "wide"),
        P("groups", "tp", "wide"),
        P(None, ("groups", "wide"), "tp"),
        P(("groups", "wide"), None, "tp"),
        P(("groups", "wide"), None, "tp"),
        P(("groups", "wide")),
    )
    out_specs = (
        P(None, ("groups", "wide"), "tp"),
        P(None, ("groups", "wide"), "tp"),
        P(None, ("groups", "wide"), "tp"),
    )
    body = functools.partial(on_device, mesh.shape["wide"], mesh.shape["tp"])
    return jax.shard_map(
        body, mesh=mesh, in_specs=in_specs, out_specs=out_specs, check_vma=False
    )
```

```python
import functools
import math

import jax
import jax.numpy as jnp
from jax import lax
from jax.experimental import pallas as pl
from jax.experimental.pallas import tpu as pltpu
from jax.sharding import PartitionSpec as P

HD = 128


norm_eps = 1e-06
adapter_scale = 2.0
rope_base = 1000000.0
masked_score = -1e30
score_scale = 1.0 / math.sqrt(HD)

VMEM = pl.BlockSpec(memory_space=pltpu.VMEM)
HBM = pl.BlockSpec(memory_space=pltpu.HBM)


def query_block(query_ref, group, per_group):
    steps = query_ref.shape[0]
    tiles = []
    for head in range(per_group):
        at = (group * per_group + head) * HD
        for step in range(steps):
            tiles.append(query_ref[step, :, at : at + HD].astype(jnp.float32))
    return jnp.concatenate(tiles, axis=0)


def copy_blocks(offsets, width, weight_ref, out_ref, sems):
    me = lax.axis_index("tp")
    copies = []
    for i, offset in enumerate(offsets):
        block = pl.ds(pl.multiple_of((me ^ offset) * width, width), width)
        copies.append(
            pltpu.make_async_copy(
                weight_ref.at[block], out_ref.at[pl.ds(i * width, width)], sems.at[i]
            )
        )
        copies[-1].start()
    return copies


def cache_kernel(
    near,
    lengths_ref,
    query_ref,
    key_ref,
    value_ref,
    gain_ref,
    bias_ref,
    hidden_ref,
    weight_ref,
    near_out,
    gain_out,
    bias_out,
    hidden_out,
    query_out,
    acc_out,
    top_out,
    total_out,
    lengths,
    queries,
    gain_buffer,
    key_buffer,
    value_buffer,
    score_buffer,
    sems,
    weight_sems,
):
    steps, rows, query_width = query_ref.shape
    cache_span = key_ref.shape[1]
    groups = key_ref.shape[2] // HD
    per_group = query_width // HD // groups
    lines = steps * per_group
    half_rows = rows // 2
    halves = [pl.ds(0, half_rows), pl.ds(half_rows, half_rows)]
    copies = [
        (lengths_ref, lengths),
        (query_ref, queries),
        (key_ref.at[halves[0]], key_buffer.at[halves[0]]),
        (key_ref.at[halves[1]], key_buffer.at[halves[1]]),
        (value_ref.at[halves[0]], value_buffer.at[halves[0]]),
        (value_ref.at[halves[1]], value_buffer.at[halves[1]]),
        (gain_ref, gain_buffer),
        (bias_ref, bias_out),
        (hidden_ref, hidden_out),
    ]
    copies = [pltpu.make_async_copy(*pair, sems.at[i]) for i, pair in enumerate(copies)]
    for copy in copies:
        copy.start()
    copies += copy_blocks(near, hidden_ref.shape[2], weight_ref, near_out, weight_sems)

    copies[0].wait()
    copies[1].wait()
    for group in range(groups):
        query_out[group] = query_block(queries, group, per_group)

    place = lax.broadcasted_iota(jnp.int32, (lines, cache_span), 1)
    for i in range(2):
        copies[2 + i].wait()
        for row in range(i * half_rows, (i + 1) * half_rows):
            for group in range(groups):
                query = query_out[group, pl.ds(row, lines, stride=rows), :].astype(jnp.bfloat16)
                score_buffer[row * groups + group] = lax.dot_general(
                    query,
                    key_buffer[row, :, pl.ds(group * HD, HD)],
                    (((1,), (1,)), ((), ())),
                    preferred_element_type=jnp.float32,
                )
    for i in range(2):
        copies[4 + i].wait()
        for row in range(i * half_rows, (i + 1) * half_rows):
            live = place < lengths[row]
            for group in range(groups):
                mine = pl.ds(row, lines, stride=rows)
                scores = score_buffer[row * groups + group]
                scores = jnp.where(live, scores * score_scale, masked_score)
                top = jnp.max(scores, axis=1, keepdims=True)
                exps = jnp.exp(scores - top)
                total = jnp.sum(exps, axis=1, keepdims=True)
                acc = jnp.dot(
                    exps.astype(jnp.bfloat16),
                    value_buffer[row, :, pl.ds(group * HD, HD)],
                    preferred_element_type=jnp.float32,
                )
                acc_out[group, mine, :] = acc
                top_out[group, mine, :] = jnp.broadcast_to(top, acc.shape)
                total_out[group, mine, :] = jnp.broadcast_to(total, acc.shape)
    copies[6].wait()
    gain_out[...] = gain_buffer[...].astype(jnp.float32)
    for copy in copies[7:]:
        copy.wait()


def cache_call(near, lengths, queries, keys, values, gain, bias, hidden, weight):
    steps, rows, query_width = queries.shape
    cache_span, key_width = keys.shape[1:]
    groups = key_width // HD
    lines = steps * (query_width // key_width)
    block = (groups, lines * rows, HD)
    operands = (lengths, queries, keys, values, gain, bias, hidden, weight)
    near_weight = (len(near) * hidden.shape[2],) + weight.shape[1:]
    return pl.pallas_call(
        functools.partial(cache_kernel, near),
        out_shape=(
            pltpu.VMEM(near_weight, weight.dtype),
            pltpu.VMEM(gain.shape, jnp.float32),
            pltpu.VMEM(bias.shape, bias.dtype),
            pltpu.VMEM(hidden.shape, hidden.dtype),
            pltpu.VMEM(block, jnp.float32),
            pltpu.VMEM(block, jnp.float32),
            pltpu.VMEM(block, jnp.float32),
            pltpu.VMEM(block, jnp.float32),
        ),
        in_specs=[HBM] * len(operands),
        out_specs=(VMEM,) * 8,
        scratch_shapes=[
            pltpu.SMEM(lengths.shape, jnp.int32),
            pltpu.VMEM(queries.shape, queries.dtype),
            pltpu.VMEM(gain.shape, gain.dtype),
            pltpu.VMEM(keys.shape, keys.dtype),
            pltpu.VMEM(values.shape, values.dtype),
            pltpu.VMEM((rows * groups, lines, cache_span), jnp.float32),
            pltpu.SemaphoreType.DMA((9,)),
            pltpu.SemaphoreType.DMA((len(near),)),
        ],
        compiler_params=pltpu.CompilerParams(vmem_limit_bytes=16 << 20),
        cost_estimate=pl.CostEstimate(flops=2 * 67 << 20, bytes_accessed=5 << 20, transcendentals=0),
        name="cache_attention",
    )(*[pltpu.with_memory_space_constraint(x, pltpu.HBM) for x in operands])


def rows_of(ref):
    return jnp.concatenate([ref[s].astype(jnp.float32) for s in range(ref.shape[0])], axis=0)


def pack_kernel(down_ref, up_ref, out_ref, sems):
    share = out_ref.shape[1]
    width = down_ref.shape[2]
    at = pl.ds(pl.multiple_of(lax.axis_index("tp") * share, share), share)
    copies = [(up_ref, out_ref.at[:, :, pl.ds(width, up_ref.shape[2])])]
    half = width // 2
    for kind in range(down_ref.shape[0]):
        for first in (0, half):
            lanes = pl.ds(first, half)
            copies.append((down_ref.at[kind, at, lanes], out_ref.at[kind, :, lanes]))
    copies = [pltpu.make_async_copy(*pair, sems.at[i]) for i, pair in enumerate(copies)]
    for copy in copies:
        copy.start()
    for copy in copies:
        copy.wait()


def pack_call(down, up):
    kinds, share, columns = up.shape
    return pl.pallas_call(
        pack_kernel,
        out_shape=pltpu.VMEM((kinds, share, down.shape[2] + columns), down.dtype),
        in_specs=[HBM] * 2,
        out_specs=VMEM,
        scratch_shapes=[pltpu.SemaphoreType.DMA((1 + 2 * kinds,))],
        name="pack_factors",
    )(*[pltpu.with_memory_space_constraint(x, pltpu.HBM) for x in (down, up)])


def scaled_block(part, gain_ref, block):
    steps, rows, width = part.shape
    chunks = width // HD
    gain = gain_ref[pl.ds(pl.multiple_of(block * chunks, chunks), chunks)]
    values = rows_of(part)
    squares = jnp.zeros((steps * rows, HD), jnp.float32)
    scaled = []
    for i in range(chunks):
        chunk = values[:, i * HD : (i + 1) * HD]
        squares += chunk * chunk
        scaled.append((chunk * gain[i : i + 1]).astype(jnp.bfloat16))
    return jnp.concatenate(scaled, axis=1), squares


def rotation_tables(lengths, steps, rows, cos_out, sin_out):
    lane = lax.broadcasted_iota(jnp.int32, (rows, HD), 1)
    half = HD // 2
    second = lane >= half
    index = jnp.where(second, lane - half, lane).astype(jnp.float32)
    inv_freq = jnp.exp(index * (-2.0 * math.log(rope_base) / HD))
    row_index = lax.broadcasted_iota(jnp.int32, (rows, HD), 0)
    row_lengths = jnp.zeros((rows, HD), jnp.int32)
    for row in range(rows):
        row_lengths = jnp.where(row_index == row, lengths[row], row_lengths)
    for step in range(steps):
        angles = (row_lengths + step).astype(jnp.float32) * inv_freq
        sine = jnp.sin(angles)
        cos_out[pl.ds(step * rows, rows)] = jnp.cos(angles)
        sin_out[pl.ds(step * rows, rows)] = jnp.where(second, sine, -sine)


def scale_kernel(early, far, lengths_ref, weight_ref, gain_ref, query_ref, *rest):
    scaled_out, early_out, square_out, far_weight, query_out, cos_out, sin_out = rest[-10:-3]
    lengths, length_sem, far_sems = rest[-3:]
    parts = rest[:-10]
    steps, rows, width = parts[0].shape
    length_copy = pltpu.make_async_copy(lengths_ref, lengths, length_sem)
    length_copy.start()
    copies = copy_blocks(far, width, weight_ref, far_weight, far_sems)
    me = lax.axis_index("tp")
    scaled_out[...] = jnp.zeros_like(scaled_out)
    total = None
    for k, (offset, part) in enumerate(zip(early, parts)):
        block = me ^ offset
        scaled, squares = scaled_block(part, gain_ref, block)
        total = squares if total is None else total + squares
        scaled_out[:, pl.ds(pl.multiple_of(block * width, width), width)] = scaled
        early_out[:, k * width : (k + 1) * width] = scaled
    square_out[...] = total
    query_out[...] = query_ref[...].astype(query_out.dtype)
    length_copy.wait()
    rotation_tables(lengths, steps, rows, cos_out, sin_out)
    for copy in copies:
        copy.wait()


def scale_call(early, blocks, far, lengths, weight, gain, queries, parts):
    steps, rows, width = parts[0].shape
    count = steps * rows
    return pl.pallas_call(
        functools.partial(scale_kernel, early, far),
        out_shape=(
            pltpu.VMEM((count, blocks * width), jnp.bfloat16),
            pltpu.VMEM((count, len(early) * width), jnp.bfloat16),
            pltpu.VMEM((count, HD), jnp.float32),
            pltpu.VMEM((len(far) * width,) + weight.shape[1:], weight.dtype),
            pltpu.VMEM(queries.shape, jnp.bfloat16),
            pltpu.VMEM((count, HD), jnp.float32),
            pltpu.VMEM((count, HD), jnp.float32),
        ),
        in_specs=[HBM] * 2 + [VMEM] * (2 + len(parts)),
        out_specs=(VMEM,) * 7,
        scratch_shapes=[
            pltpu.SMEM(lengths.shape, jnp.int32),
            pltpu.SemaphoreType.DMA,
            pltpu.SemaphoreType.DMA((len(far),)),
        ],
        compiler_params=pltpu.CompilerParams(vmem_limit_bytes=8 << 20),
        cost_estimate=pl.CostEstimate(flops=0, bytes_accessed=9 << 20, transcendentals=0),
        name="scale_features",
    )(*[pltpu.with_memory_space_constraint(x, pltpu.HBM) for x in (lengths, weight)], gain, queries, *parts)


def inner_kernel(late, scaled_ref, early_ref, square_ref, gain_ref, *rest):
    parts, rest = rest[: len(late)], rest[len(late) :]
    outs, square_out = rest[-1 - len(late) : -1], rest[-1]
    packs, inner_out = (rest[: -2 - len(late)], rest[-2 - len(late)]) if len(rest) > 1 + len(late) else ((), None)
    squares = square_ref[...]
    blocks = []
    for k, (offset, part) in enumerate(zip(late, parts)):
        block = lax.axis_index("tp") ^ offset
        scaled, more = scaled_block(part, gain_ref, block)
        squares += more
        blocks.append((block, scaled))
        width = scaled.shape[1]
        outs[k][:, :width] = early_ref[:, k * width : (k + 1) * width]
        outs[k][:, width:] = scaled
    squares = jnp.sum(squares, axis=1, keepdims=True)
    square_out[...] = jnp.broadcast_to(squares, square_out.shape)
    if not packs:
        return
    me = lax.axis_index("wide")
    total = []
    for offset, pack in enumerate(packs):
        mine = me ^ offset
        rows = scaled_ref[:, pl.ds(pl.multiple_of(mine * width, width), width)]
        for block, scaled in blocks:
            rows = jnp.where(mine == block, scaled, rows)
        total.append(
            lax.dot_general(
                rows,
                pack[:, :, :width].reshape(inner_out.shape[1], width),
                (((1,), (1,)), ((), ())),
                preferred_element_type=jnp.float32,
            )
        )
    inner_out[...] = sum(total[1:], total[0])


def inner_call(late, scaled, early, square, gain, parts, packs):
    count, width = scaled.shape[0], parts[0].shape[2]
    shapes = [pltpu.VMEM((count, 2 * width), scaled.dtype) for _ in late]
    shapes.append(pltpu.VMEM(square.shape, jnp.float32))
    if packs:
        kinds, share, _ = packs[0].shape
        shapes = [pltpu.VMEM((count, kinds * share), jnp.float32)] + shapes
    return pl.pallas_call(
        functools.partial(inner_kernel, late),
        out_shape=tuple(shapes),
        in_specs=[VMEM] * (4 + len(parts) + len(packs)),
        out_specs=(VMEM,) * len(shapes),
        compiler_params=pltpu.CompilerParams(vmem_limit_bytes=8 << 20),
        name="rank_inner",
    )(scaled, early, square, gain, *parts, *packs)


def up_kernel(*refs):
    packs, up_out = refs[:-1], refs[-1]
    kinds, share, pack_width = packs[0].shape
    columns = up_out.shape[1] // kinds
    me = lax.axis_index("wide") if len(packs) > 1 else 0
    up_out[...] = jnp.zeros_like(up_out)
    for offset, pack in enumerate(packs):
        for kind in range(kinds):
            at = pl.multiple_of(((me ^ offset) * kinds + kind) * share, share)
            up_out[pl.ds(at, share), kind * columns : (kind + 1) * columns] = pack[
                kind, :, pack_width - columns :
            ]


def up_call(packs, columns):
    kinds, share, _ = packs[0].shape
    return pl.pallas_call(
        up_kernel,
        out_shape=pltpu.VMEM((len(packs) * kinds * share, kinds * columns), packs[0].dtype),
        in_specs=[VMEM] * len(packs),
        out_specs=VMEM,
        compiler_params=pltpu.CompilerParams(vmem_limit_bytes=8 << 20),
        name="lay_out_up",
    )(*packs)


def split_index(index, count):
    if count & (count - 1) == 0:
        return index >> (count.bit_length() - 1), index & (count - 1)
    return index // count, index % count


def final_kernel(width, blocks, near_ref, far_ref, square_ref, bias_ref, *rest):
    query_ref, acc_ref, top_ref, total_ref, cos_ref, sin_ref = rest[:6]
    inner_refs = rest[6 : 6 + blocks]
    up_ref, keys_out, values_out, attended_out = rest[6 + blocks :]
    steps, rows, columns = keys_out.shape
    count = steps * rows
    groups, size, _ = query_ref.shape
    per_group = size // count
    kinds = bias_ref.shape[0]
    row_scale = lax.rsqrt(square_ref[...] * (1.0 / width) + norm_eps)
    row_scale = jnp.concatenate([row_scale] * groups, axis=1)
    me = lax.axis_index("tp") if blocks > 1 else 0
    share = inner_refs[0].shape[1]
    products = []
    for i in range(blocks):
        inner = inner_refs[i][...]
        high = inner.astype(jnp.bfloat16)
        low = (inner - high.astype(jnp.float32)).astype(jnp.bfloat16)
        at = pl.multiple_of((me ^ i) * share, share)
        products.append(
            jnp.dot(
                jnp.concatenate([high, low], axis=0),
                up_ref[pl.ds(at, share), :],
                preferred_element_type=jnp.float32,
            )
        )
    lora = sum(products[1:], products[0])
    lora = lora[:count] + lora[count:]
    bias = bias_ref[...].astype(jnp.float32)
    linear = []
    for kind in range(kinds):
        base = near_ref[kind] + far_ref[kind]
        part = lora[:, kind * columns : (kind + 1) * columns]
        linear.append((base + adapter_scale * part) * row_scale + bias[kind : kind + 1])
    cosine, sine = cos_ref[...], sin_ref[...]
    line = lax.broadcasted_iota(jnp.int32, (size, count), 0)
    other = lax.broadcasted_iota(jnp.int32, (size, count), 1)
    line_step, line_row = split_index(line, rows)
    other_step, other_row = split_index(other, rows)
    line_step = split_index(line_step, steps)[1]
    live = (line_row == other_row) & (other_step <= line_step)
    for group in range(groups):
        at = slice(group * HD, (group + 1) * HD)
        key = linear[0][:, at]
        key = (key * cosine + pltpu.roll(key, HD // 2, 1) * sine).astype(jnp.bfloat16)
        value = linear[1][:, at].astype(jnp.bfloat16)
        for step in range(steps):
            keys_out[step, :, at] = key[step * rows : (step + 1) * rows]
            values_out[step, :, at] = value[step * rows : (step + 1) * rows]
        scores = lax.dot_general(
            query_ref[group],
            key,
            (((1,), (1,)), ((), ())),
            preferred_element_type=jnp.float32,
        )
        scores = jnp.where(live, scores * score_scale, masked_score)
        old_top = top_ref[group]
        top = jnp.maximum(old_top, jnp.max(scores, axis=1, keepdims=True))
        exps = jnp.exp(scores - top[:, :count])
        keep = jnp.exp(old_top - top)
        total = total_ref[group] * keep + jnp.sum(exps, axis=1, keepdims=True)
        acc = acc_ref[group] * keep + jnp.dot(
            exps.astype(jnp.bfloat16), value, preferred_element_type=jnp.float32
        )
        attended = (acc * (1.0 / total)).astype(jnp.bfloat16)
        for head in range(per_group):
            lanes = pl.ds((group * per_group + head) * HD, HD)
            for step in range(steps):
                tile = (head * steps + step) * rows
                attended_out[step, :, lanes] = attended[tile : tile + rows]


def final_call(shape, width, near, far, square, bias, cached, inner, up):
    steps, rows, query_width = shape
    columns = near.shape[2]
    small = jax.ShapeDtypeStruct((steps, rows, columns), jnp.bfloat16)
    return pl.pallas_call(
        functools.partial(final_kernel, width, len(inner)),
        out_shape=(small, small, jax.ShapeDtypeStruct(shape, jnp.bfloat16)),
        in_specs=[VMEM] * (5 + len(cached) + len(inner)),
        out_specs=(VMEM,) * 3,
        compiler_params=pltpu.CompilerParams(vmem_limit_bytes=8 << 20),
        name="fresh_attention",
    )(near, far, square, bias, *cached, *inner, up)


def dot(rows, weight):
    return jnp.einsum("md,dkc->kmc", rows, weight, preferred_element_type=jnp.float32)


def swap(block, axis, offset, count):
    return lax.ppermute(block, axis, [(i, i ^ offset) for i in range(count)])


def on_device(
    wide_count,
    tp_count,
    hidden,
    input_norm_gain,
    key_value_weight,
    key_value_bias,
    adapter_down_factor,
    adapter_up_factor,
    queries,
    stored_rotated_keys,
    stored_value_rows,
    lengths,
):
    steps, rows, part_width = hidden.shape
    width = part_width * tp_count
    kinds, ranks, down_width = adapter_down_factor.shape
    gain = input_norm_gain.reshape(width // HD, HD)
    up_part = jnp.transpose(adapter_up_factor, (0, 2, 1))
    direct = wide_count == tp_count == 4
    crossed = swap(hidden, "tp", 2, tp_count)
    if direct:
        pack = pack_call(adapter_down_factor, up_part)
        second = swap(pack, "wide", 2, wide_count)
        first = swap(pack, "wide", 1, wide_count)
    near, far = (0, 1), (2, 3)
    early, late = (0, 2), (1, 3)
    near_weight, gain_rows, bias, mine, query_rows, *cached = cache_call(
        near,
        lengths,
        queries,
        stored_rotated_keys,
        stored_value_rows,
        gain,
        key_value_bias,
        hidden,
        key_value_weight,
    )
    beside = swap(mine, "tp", 1, tp_count)
    relayed, gain_rows = lax.optimization_barrier((crossed, gain_rows))
    relayed = swap(relayed, "tp", 1, tp_count)
    if direct:
        third, gain_rows = lax.optimization_barrier((second, gain_rows))
        packs = [pack, first, second, swap(third, "wide", 1, wide_count)]
    scaled, early_scaled, square, far_weight, query_rows, *tables = scale_call(
        early, tp_count, far, lengths, key_value_weight, gain_rows, query_rows, (mine, crossed)
    )
    late_parts = (beside, relayed)
    if direct:
        inner, near_scaled, far_scaled, square = inner_call(
            late, scaled, early_scaled, square, gain_rows, late_parts, packs
        )
        inner, far_scaled, near_scaled, packs = lax.optimization_barrier(
            (inner, far_scaled, near_scaled, packs)
        )
        inner = [inner] + [swap(inner, "tp", offset, tp_count) for offset in (1, 2, 3)]
    else:
        near_scaled, far_scaled, square = inner_call(
            late, scaled, early_scaled, square, gain_rows, late_parts, []
        )
        down = lax.all_gather(adapter_down_factor, "wide", axis=2, tiled=True)
        rows_full = lax.all_gather(hidden, "tp", axis=2, tiled=True).astype(jnp.float32)
        rows_full = (rows_full * input_norm_gain.astype(jnp.float32)).astype(jnp.bfloat16)
        inner = jnp.einsum("srd,kad->srka", rows_full, down, preferred_element_type=jnp.float32)
        inner = [inner.reshape(steps * rows, kinds * ranks)]
        packs = [lax.all_gather(up_part, "wide", axis=1, tiled=True)]
    near_base = dot(near_scaled, near_weight)
    far_base = dot(far_scaled, far_weight)
    up = up_call(packs, bias.shape[1])
    return final_call(
        queries.shape, width, near_base, far_base, square, bias, [query_rows] + cached + tables, inner, up
    )


def solution(mesh):
    in_specs = (
        P(None, ("groups", "wide"), "tp"),
        P(),
        P(None, None, "tp"),
        P(None, "tp"),
        P("groups", None, "wide"),
        P("groups", "tp", "wide"),
        P(None, ("groups", "wide"), "tp"),
        P(("groups", "wide"), None, "tp"),
        P(("groups", "wide"), None, "tp"),
        P(("groups", "wide")),
    )
    out_specs = (
        P(None, ("groups", "wide"), "tp"),
        P(None, ("groups", "wide"), "tp"),
        P(None, ("groups", "wide"), "tp"),
    )
    body = functools.partial(on_device, mesh.shape["wide"], mesh.shape["tp"])
    return jax.shard_map(
        body, mesh=mesh, in_specs=in_specs, out_specs=out_specs, check_vma=False
    )
```
